32 devices in a mesh: dp: 4 (over z), row: 2 (over y), col: 4 (over x, core).
Axes of the slice: x: 2, y: 2, z: 4, core: 2. Of those that a mesh axis runs over, the one named last changes fastest.
Arguments:
- tokens: bfloat16 [16384, 2048], P(('dp', 'col'), 'row'), may hold values from -6 to 6
- norm1_gain: float32 [2048], P('row'), may hold values from 0.25 to 1.75
- w_query: bfloat16 [2048, 1280], P('row', 'col'), may hold values from -0.125 to 0.125
- w_key: bfloat16 [2048, 320], P('row', 'col'), may hold values from -0.125 to 0.125
- w_value: bfloat16 [2048, 320], P('row', 'col'), may hold values from -0.125 to 0.125
- query_gain: float32 [64], replicated, may hold values from 0.25 to 1.75
- key_gain: float32 [64], replicated, may hold values from 0.25 to 1.75
- w_out: bfloat16 [1280, 2048], P('col', 'row'), may hold values from -0.625 to 0.625
- norm2_gain: float32 [2048], P('row'), may hold values from 0.25 to 1.75
- w_gate: bfloat16 [2048, 5120], P('row', 'col'), may hold values from -0.125 to 0.125
- w_up: bfloat16 [2048, 5120], P('row', 'col'), may hold values from -0.125 to 0.125
- w_down: bfloat16 [5120, 2048], P('col', 'row'), may hold values from -0.078125 to 0.078125
- teacher: bfloat16 [16384, 2048], P(('dp', 'col'), 'row'), may hold values from -6 to 6
- positions: int32 [16384], P('dp'), may hold values from 0 to 3453, as said below
- token_count: int32 [1], replicated, may hold values from 8192 to 16384
Outputs:
- block_out: bfloat16 [16384, 2048], P(('dp', 'col'), 'row')
- grad_input: float32 [16384, 2048], P(('dp', 'col'), 'row')
- grad_norm1: float32 [2048], P('row')
- grad_query: float32 [2048, 1280], P('row', 'col')
- grad_key: float32 [2048, 320], P('row', 'col')
- grad_value: float32 [2048, 320], P('row', 'col')
- grad_query_gain: float32 [64], replicated
- grad_key_gain: float32 [64], replicated
- grad_out: float32 [1280, 2048], P('col', 'row')
- grad_norm2: float32 [2048], P('row')
- grad_gate: float32 [2048, 5120], P('row', 'col')
- grad_up: float32 [2048, 5120], P('row', 'col')
- grad_down: float32 [5120, 2048], P('col', 'row')
The draws below stay inside these ranges and needn't reach their ends.
Inputs may be any that keep to these rules, and one draw needn't show every extreme that they name: Within each group of 2048 tokens the prompt's 1024 positions count up by one from a start of the group; each continuation's 128 positions count up by one from a start at or after the prompt's last position plus one.
All inputs are finite; a program needn't handle non-finite values.
Results may differ from the reference program's by a relative error of at most 0.015.
Values may be sent and summed in bfloat16 or wider, within the bound.
A program may use at most 320 MiB of HBM per device.

```python
import math
import jax
import jax.numpy as jnp
from jax import lax

D = 2048
QH = 20
KVH = 5
HD = 64
FF = 5120
PROMPT = 1024
CONT = 128
NCONT = 8
GROUP_LEN = 2048
GROUPS = 8
TOKENS = 16384


def draw_positions(key, part):
    groups = TOKENS // GROUP_LEN
    key_start = jax.random.fold_in(key, 11)
    key_skip = jax.random.fold_in(key, 23)
    group_index = jnp.arange(groups)[:, None]
    start = jax.random.randint(key_start, (groups, 1), 0, 2048)
    start = jnp.where(group_index == 0, 0, start)
    start = jnp.where(group_index == groups - 1, 2047, start)
    skips = jax.random.randint(key_skip, (groups, NCONT), 0, 2 * CONT)
    last_slot = (group_index == groups - 1) & (jnp.arange(NCONT)[None, :] == NCONT - 1)
    skips = jnp.where(last_slot, 2 * CONT - 1, skips)
    index = jnp.arange(GROUP_LEN)
    slot = jnp.clip((index - PROMPT) // CONT, 0, NCONT - 1)
    inside = (index - PROMPT) % CONT
    later = PROMPT + skips[:, slot] + inside[None, :]
    places = jnp.where(index[None, :] < PROMPT, index[None, :], later) + start
    return places.reshape(TOKENS).astype(jnp.int32)


def block_levels(stream_key, extent, split, smallest, high):
    factor_of = 1.0
    for dim, parts in split:
        draws = jax.random.uniform(jax.random.fold_in(jax.random.fold_in(stream_key, 6), dim), (parts,), jnp.float32, smallest / len(split), high / len(split))
        factor_of = factor_of * jnp.repeat(jnp.exp(draws), extent[dim] // parts).reshape((-1,) + (1,) * (len(extent) - 1 - dim))
    return factor_of


def gaussian(key, shape, scale, most, cuts=(), held_as=jnp.bfloat16):
    level = block_levels(key, shape, cuts, -0.22, 0.18) if cuts else 1.0
    values = jax.random.normal(key, shape, jnp.float32) * scale * level
    return jnp.minimum(jnp.maximum(values, -most), most).astype(held_as)


def setup_inputs(seed: int = 0) -> dict:
    streams_of = jax.random.split(jax.random.key(seed), 16)
    return {
        "tokens": gaussian(streams_of[0], (TOKENS, D), 1.0, 6.0, ((0, 16), (1, 2))),
        "norm1_gain": jnp.clip(1.0 + 0.15 * jax.random.normal(streams_of[1], (D,), jnp.float32), 0.25, 1.75),
        "w_query": gaussian(streams_of[2], (D, QH * HD), D ** -0.5, 0.125, ((0, 2), (1, 4))),
        "w_key": gaussian(streams_of[3], (D, KVH * HD), D ** -0.5, 0.125, ((0, 2), (1, 4))),
        "w_value": gaussian(streams_of[4], (D, KVH * HD), D ** -0.5, 0.125, ((0, 2), (1, 4))),
        "query_gain": jnp.clip(1.0 + 0.15 * jax.random.normal(streams_of[5], (HD,), jnp.float32), 0.25, 1.75),
        "key_gain": jnp.clip(1.0 + 0.15 * jax.random.normal(streams_of[6], (HD,), jnp.float32), 0.25, 1.75),
        "w_out": gaussian(streams_of[7], (QH * HD, D), (QH * HD // 16) ** -0.5, 0.625, ((0, 4), (1, 2))),
        "norm2_gain": jnp.clip(1.0 + 0.15 * jax.random.normal(streams_of[8], (D,), jnp.float32), 0.25, 1.75),
        "w_gate": gaussian(streams_of[9], (D, FF), D ** -0.5, 0.125, ((0, 2), (1, 4))),
        "w_up": gaussian(streams_of[10], (D, FF), D ** -0.5, 0.125, ((0, 2), (1, 4))),
        "w_down": gaussian(streams_of[11], (FF, D), FF ** -0.5, 0.078125, ((0, 4), (1, 2))),
        "teacher": gaussian(streams_of[12], (TOKENS, D), 1.0, 6.0, ((0, 16), (1, 2))),
        "positions": draw_positions(jax.random.fold_in(streams_of[15], 71), 0),
        "token_count": jax.random.randint(streams_of[14], (1,), TOKENS // 2, TOKENS + 1).astype(jnp.int32),
    }


EPSILON = 1e-06
NEG_FILL = -1e+30
HIGHEST = lax.Precision.HIGHEST

@jax.custom_vjp
def low(v):
    return lax.optimization_barrier(v.astype(jnp.bfloat16)).astype(jnp.float32)

@jax.custom_vjp
def low_back(v):
    return v

def low_keep(v):
    return (low(v), None)

def low_pass(kept, grad):
    return (grad,)

def back_keep(v):
    return (v, None)

def back_low(kept, grad):
    return (low(grad),)
low.defvjp(low_keep, low_pass)
low_back.defvjp(back_keep, back_low)

def matmul_high(left, right):
    return jnp.dot(left, right, precision=HIGHEST, preferred_element_type=jnp.float32)

def head_norm(values, gain):
    return values * lax.rsqrt(lax.optimization_barrier(jnp.mean(values * values, axis=-1, keepdims=True)) + EPSILON) * gain

def rotate(values, places):
    half = values.shape[-1] // 2
    freq = jnp.exp(jnp.arange(half, dtype=jnp.float32) * (-2.0 * math.log(10000.0) / values.shape[-1]))
    angle = places.astype(jnp.float32)[:, None] * freq[None, :]
    cosine = jnp.cos(angle)[:, None, :]
    sine = jnp.sin(angle)[:, None, :]
    first = values[..., :half]
    second = values[..., half:]
    return jnp.concatenate([first * cosine - second * sine, second * cosine + first * sine], axis=-1)

def allowed_keys(query_index, key_index):
    query_seg = jnp.where(query_index < PROMPT, -1, (query_index - PROMPT) // CONT)
    key_seg = jnp.where(key_index < PROMPT, -1, (key_index - PROMPT) // CONT)
    causal = key_index[None, :] <= query_index[:, None]
    visible = (key_index[None, :] < PROMPT) | (key_seg[None, :] == query_seg[:, None])
    return causal & visible

def group_out(params, states, places):
    norm_one, wq, wk, wv, gain_q, gain_k, wo, norm_two, wg, wu, wd = params
    inverse_one = lax.rsqrt(lax.optimization_barrier(jnp.mean(states * states, axis=-1, keepdims=True)) + EPSILON)
    normed_one = low(states * inverse_one * norm_one)
    query_raw = low_back(matmul_high(normed_one, wq))
    key_raw = low_back(matmul_high(normed_one, wk))
    value_raw = low_back(matmul_high(normed_one, wv))
    key_sent = low(key_raw)
    value_sent = low(value_raw)
    query_use = low(rotate(head_norm(query_raw.reshape(GROUP_LEN, QH, HD), gain_q), places))
    key_use = low(rotate(head_norm(key_sent.reshape(GROUP_LEN, KVH, HD), gain_k), places))
    key_wide = jnp.repeat(key_use, QH // KVH, axis=1)
    value_wide = jnp.repeat(value_sent.reshape(GROUP_LEN, KVH, HD), QH // KVH, axis=1)
    block = min(512, GROUP_LEN)
    key_index = jnp.arange(GROUP_LEN)
    scale = 1.0 / math.sqrt(HD)

    def attend(start):
        query_block = lax.dynamic_slice_in_dim(query_use, start, block, 0)
        query_index = start + jnp.arange(block)
        scores = low_back(jnp.einsum('qhd,khd->hqk', query_block, key_wide, precision=HIGHEST) * scale)
        scores = jnp.where(allowed_keys(query_index, key_index)[None], scores, NEG_FILL)
        top = lax.optimization_barrier(jnp.max(scores, axis=-1, keepdims=True))
        expo = jnp.exp(scores - top)
        weights = low(expo / lax.optimization_barrier(jnp.sum(expo, axis=-1, keepdims=True)))
        return jnp.einsum('hqk,khd->qhd', weights, value_wide, precision=HIGHEST)
    starts = (jnp.arange(GROUP_LEN // block) * block).astype(jnp.int32)
    mixed = lax.map(jax.checkpoint(attend), starts).reshape(GROUP_LEN, QH * HD)
    mixed = low(low_back(mixed))
    hidden = states + low_back(matmul_high(mixed, wo))
    inverse_two = lax.rsqrt(lax.optimization_barrier(jnp.mean(hidden * hidden, axis=-1, keepdims=True)) + EPSILON)
    normed_two = low(hidden * inverse_two * norm_two)
    gate = low_back(matmul_high(normed_two, wg))
    up = low_back(matmul_high(normed_two, wu))
    activated = low(jax.nn.silu(gate) * up)
    return hidden + low_back(matmul_high(activated, wd))

def reference(tokens, norm1_gain, w_query, w_key, w_value, query_gain, key_gain, w_out, norm2_gain, w_gate, w_up, w_down, teacher, positions, token_count):
    params = tuple((item.astype(jnp.float32) for item in (norm1_gain, w_query, w_key, w_value, query_gain, key_gain, w_out, norm2_gain, w_gate, w_up, w_down)))
    states_all = tokens.astype(jnp.float32).reshape(GROUPS, GROUP_LEN, D)
    target_all = teacher.astype(jnp.float32).reshape(GROUPS, GROUP_LEN, D)
    places_all = positions.reshape(GROUPS, GROUP_LEN)
    count = token_count[0].astype(jnp.float32)
    cell = jax.checkpoint(group_out)

    def total_loss(states_in, weights_in):

        def step(accum, item):
            states, target, places = item
            result = cell(weights_in, states, places)
            diff = result - target
            return (accum + jnp.sum(diff * diff), result)
        accum, results = lax.scan(step, jnp.zeros((), jnp.float32), (states_in, target_all, places_all))
        return (accum * (TOKENS / (2.0 * count)), results)
    (loss, results), pull = jax.vjp(total_loss, states_all, params)
    grad_states, grads = pull((jnp.ones((), jnp.float32), jnp.zeros_like(results)))
    block_out = results.reshape(TOKENS, D).astype(jnp.bfloat16)
    return (block_out, grad_states.reshape(TOKENS, D), grads[0], grads[1], grads[2], grads[3], grads[4], grads[5], grads[6], grads[7], grads[8], grads[9], grads[10])
```

```python
import functools
import math

import jax
import jax.numpy as jnp
from jax import lax
from jax.experimental import pallas as pl
from jax.experimental.pallas import tpu as pltpu
from jax.sharding import Mesh
from jax.sharding import PartitionSpec as P

D = 2048
QH = 20
KVH = 5
HD = 64
PROMPT = 1024
CONT = 128
NCONT = 8
GROUP = PROMPT + NCONT * CONT
REP = QH // KVH
KEYS = 256

EPSILON = 1e-06
BF = jnp.bfloat16
F32 = jnp.float32


def dot(left, right, dims=((1,), (0,))):
    return lax.dot_general(left, right, (dims, ((), ())), preferred_element_type=F32)


def rms(values):
    return lax.rsqrt(jnp.mean(values * values, axis=1, keepdims=True) + EPSILON)


def norm_back(states, inverse, gain, d_normed):
    mean = jnp.mean(states * gain * d_normed, axis=1, keepdims=True)
    return inverse * gain * d_normed - states * inverse**3 * mean


def prepare(raw, gain, cosine, sine):
    values = raw * lax.rsqrt(jnp.mean(raw * raw, axis=1, keepdims=True) + EPSILON)
    values = values * gain[None, :, None]
    half = HD // 2
    first, second = values[:, :half], values[:, half:]
    return jnp.concatenate(
        [first * cosine - second * sine, second * cosine + first * sine], axis=1
    )


def allowed(first_query, first_key, span, rows):
    key = first_key + lax.broadcasted_iota(jnp.int32, (KEYS, rows), 0)
    query = first_query + lax.broadcasted_iota(jnp.int32, (KEYS, rows), 1) % span
    return (key <= query) & ((key < PROMPT) | (key // CONT == query // CONT))


def side_by_side(ref, index, span):
    return jnp.concatenate(
        [ref[0, head, :, index * span : (index + 1) * span] for head in range(REP)], axis=1
    )


def tiles_of(first_query):
    last = first_query // KEYS
    return jnp.minimum(last, PROMPT // KEYS), last


def attend_kernel(chunks, span, first_ref, query_ref, key_ref, value_ref, out_ref, log_ref):
    rows = REP * span
    for index in range(chunks):
        query = side_by_side(query_ref, index, span)
        first_query = first_ref[index]
        full, last = tiles_of(first_query)

        def tile(where, accum, masked):
            first_key = pl.multiple_of(where * KEYS, KEYS)
            scores = dot(key_ref[0, pl.ds(first_key, KEYS), :], query)
            expo = jnp.exp(scores)
            if masked:
                expo = jnp.where(allowed(first_query, first_key, span, rows), expo, 0.0)
            return accum + dot(value_ref[0, :, pl.ds(first_key, KEYS)], expo.astype(BF))

        accum = tile(last, jnp.zeros((value_ref.shape[1], rows), F32), True)
        accum = lax.fori_loop(0, full, lambda where, total: tile(where, total, False), accum)
        total = accum[HD : HD + 1]
        mixed = accum[:HD] / total
        logs = jnp.log(total)
        for head in range(REP):
            cut = slice(head * span, (head + 1) * span)
            out_ref[0, head, :, index * span : (index + 1) * span] = mixed[:, cut]
            log_ref[0, head : head + 1, index * span : (index + 1) * span] = logs[:, cut]


def attend_back_kernel(
    chunks,
    span,
    first_ref,
    query_ref,
    d_out_ref,
    log_ref,
    delta_ref,
    key_ref,
    value_ref,
    key_t_ref,
    d_query_ref,
    d_key_ref,
    d_value_ref,
):
    rows = REP * span
    d_key_ref[...] = jnp.zeros_like(d_key_ref)
    d_value_ref[...] = jnp.zeros_like(d_value_ref)
    for index in range(chunks):
        query = side_by_side(query_ref, index, span)
        d_out = side_by_side(d_out_ref, index, span)
        query_t = query.T
        d_out_t = d_out.T
        cut = slice(index * span, (index + 1) * span)
        logs = jnp.concatenate([log_ref[0, h : h + 1, cut] for h in range(REP)], axis=1)
        delta = jnp.concatenate([delta_ref[0, h : h + 1, cut] for h in range(REP)], axis=1)
        first_query = first_ref[index]
        full, last = tiles_of(first_query)

        def tile(where, accum, masked):
            first_key = pl.multiple_of(where * KEYS, KEYS)
            here = pl.ds(first_key, KEYS)
            probs = jnp.exp(dot(key_ref[0, here, :], query) - logs)
            if masked:
                probs = jnp.where(allowed(first_query, first_key, span, rows), probs, 0.0)
            d_probs = dot(value_ref[0, here, :], d_out)
            d_scores = (probs * (d_probs - delta)).astype(BF)
            d_value_ref[0, here, :] += dot(probs.astype(BF), d_out_t)
            d_key_ref[0, here, :] += dot(d_scores, query_t)
            return accum + dot(key_t_ref[0, :, here], d_scores)

        accum = tile(last, jnp.zeros((HD, rows), F32), True)
        accum = lax.fori_loop(0, full, lambda where, total: tile(where, total, False), accum)
        for head in range(REP):
            part = accum[:, head * span : (head + 1) * span]
            d_query_ref[0, head, :, cut] = part


def per_head(shape):
    return pl.BlockSpec((1,) + shape, lambda head, first: (head,) + (0,) * len(shape))


def attend(first, query, key, value_t):
    tokens = query.shape[-1]
    chunks = first.shape[0]
    return pl.pallas_call(
        functools.partial(attend_kernel, chunks, tokens // chunks),
        out_shape=(
            jax.ShapeDtypeStruct((KVH, REP, HD, tokens), F32),
            jax.ShapeDtypeStruct((KVH, REP, tokens), F32),
        ),
        grid_spec=pltpu.PrefetchScalarGridSpec(
            num_scalar_prefetch=1,
            grid=(KVH,),
            in_specs=[
                per_head((REP, HD, tokens)),
                per_head((GROUP, HD)),
                per_head((value_t.shape[1], GROUP)),
            ],
            out_specs=[per_head((REP, HD, tokens)), per_head((REP, tokens))],
        ),
        compiler_params=pltpu.CompilerParams(vmem_limit_bytes=32 * 1024 * 1024),
        name="attend",
    )(first, query, key, value_t)


def attend_back(first, query, d_out, logs, delta, key, value, key_t):
    tokens = query.shape[-1]
    chunks = first.shape[0]
    return pl.pallas_call(
        functools.partial(attend_back_kernel, chunks, tokens // chunks),
        out_shape=(
            jax.ShapeDtypeStruct((KVH, REP, HD, tokens), F32),
            jax.ShapeDtypeStruct((KVH, GROUP, HD), F32),
            jax.ShapeDtypeStruct((KVH, GROUP, HD), F32),
        ),
        grid_spec=pltpu.PrefetchScalarGridSpec(
            num_scalar_prefetch=1,
            grid=(KVH,),
            in_specs=[
                per_head((REP, HD, tokens)),
                per_head((REP, HD, tokens)),
                per_head((REP, tokens)),
                per_head((REP, tokens)),
                per_head((GROUP, HD)),
                per_head((GROUP, HD)),
                per_head((HD, GROUP)),
            ],
            out_specs=[
                per_head((REP, HD, tokens)),
                per_head((GROUP, HD)),
                per_head((GROUP, HD)),
            ],
        ),
        compiler_params=pltpu.CompilerParams(vmem_limit_bytes=32 * 1024 * 1024),
        name="attend_back",
    )(first, query, d_out, logs, delta, key, value, key_t)


def body(
    tokens,
    norm1_gain,
    w_query,
    w_key,
    w_value,
    query_gain,
    key_gain,
    w_out,
    norm2_gain,
    w_gate,
    w_up,
    w_down,
    teacher,
    positions,
    token_count,
):
    rows = lax.axis_size("row")
    cores = lax.axis_size("side")
    cols = lax.axis_size("group") * cores
    row_index = lax.axis_index("row")
    group_index = lax.axis_index("group")
    members = rows * cores
    member = row_index * cores + lax.axis_index("side")
    shard, width = tokens.shape
    pieces = 2 * members
    span = shard // pieces
    mine = shard // members * cores
    q_width, k_width = w_query.shape[1], w_key.shape[1]
    ff = w_gate.shape[1]

    def to_members(block):
        parts = block.reshape(pieces, span, width)
        parts = jnp.stack([parts[:members], parts[members:][::-1]], axis=1)
        moved = lax.all_to_all(parts, ("row", "side"), 0, 0, tiled=True)
        moved = moved.reshape(rows, cores, 2 * span, width).transpose(1, 2, 0, 3)
        return moved.reshape(mine, rows * width)

    def from_members(block):
        parts = block.reshape(cores, 2, span, rows, width).transpose(3, 0, 1, 2, 4)
        parts = parts.reshape(members, 2, span, width)
        moved = lax.all_to_all(parts, ("row", "side"), 0, 0, tiled=True)
        moved = jnp.concatenate([moved[:, 0], moved[:, 1][::-1]], axis=0)
        return moved.reshape(shard, width)

    def pick(values):
        part = lax.dynamic_slice_in_dim(values.reshape(-1, cores, pieces, span), group_index, 1, 0)[0]
        low = lax.dynamic_slice_in_dim(part, member, 1, 1)
        high = lax.dynamic_slice_in_dim(part, pieces - 1 - member, 1, 1)
        return jnp.concatenate([low, high], axis=1).reshape(-1)

    first_tokens = (
        jnp.array([0, 0, shard, shard], jnp.int32)
        + jnp.stack([member, pieces - 1 - member] * 2).astype(jnp.int32) * span
    )

    w_project = jnp.concatenate([w_query, w_key, w_value], axis=1)
    w_project = lax.all_gather(w_project, ("group", "side", "row"), axis=0, tiled=True)
    w_project = w_project.reshape(cols, D, q_width + 2 * k_width)
    states = to_members(tokens).astype(F32)
    w_out_all = lax.all_gather(w_out, ("group", "side", "row"), axis=0)
    w_out_all = w_out_all.reshape(cols, rows, q_width, width).transpose(0, 2, 1, 3)
    w_out_all = w_out_all.reshape(QH * HD, D)
    w_gate_all = lax.all_gather(w_gate, "row", axis=0, tiled=True)
    w_up_all = lax.all_gather(w_up, "row", axis=0, tiled=True)
    w_down_all = lax.all_gather(w_down, "row", axis=0).transpose(1, 0, 2).reshape(ff, D)
    gain_one = lax.all_gather(norm1_gain, "row", axis=0, tiled=True)
    gain_two = lax.all_gather(norm2_gain, "row", axis=0, tiled=True)
    target = to_members(teacher)

    half = HD // 2
    freq = jnp.exp(jnp.arange(half, dtype=F32) * (-2.0 * math.log(10000.0) / HD))
    angle = freq[:, None] * pick(positions).astype(F32)[None, :]
    cosine, sine = jnp.cos(angle), jnp.sin(angle)
    inverse_one = rms(states)
    normed_one = (states * inverse_one * gain_one).astype(BF)
    projected = dot(w_project, normed_one, ((1,), (1,)))
    query_raw = projected[:, :q_width].reshape(QH, HD, mine)
    key_sent = projected[:, q_width : q_width + k_width].reshape(KVH, HD, mine).astype(BF)
    value_sent = projected[:, q_width + k_width :].reshape(KVH, HD, mine).astype(BF)
    query_rot, query_back = jax.vjp(
        lambda raw, gain: prepare(raw, gain, cosine, sine), query_raw, query_gain
    )
    key_rot, key_back = jax.vjp(
        lambda raw, gain: prepare(raw, gain, cosine, sine), key_sent.astype(F32), key_gain
    )
    scale = 1.0 / math.sqrt(HD)
    query_use = (query_rot.astype(BF) * BF(scale)).reshape(KVH, REP, HD, mine)
    pair = jnp.stack([key_rot.astype(BF), value_sent])
    pair = lax.all_gather(pair, ("row", "side"), axis=0)

    def natural(stacked):
        lead = stacked.shape[1:-1]
        parts = stacked.reshape((members,) + lead + (cores, 2, span))
        low, high = parts[..., 0, :], parts[..., 1, :]
        both = jnp.concatenate([low, high[::-1]], axis=0)
        return jnp.moveaxis(both, 0, -2).reshape(lead + (GROUP,))

    def dealt(full):
        lead, entry = full.shape[:-2], full.shape[-1]
        parts = full.reshape(lead + (cores, pieces, span, entry))
        low = parts[..., :members, :, :]
        high = parts[..., members:, :, :][..., ::-1, :, :]
        both = jnp.stack([low, high], axis=-3)
        both = jnp.moveaxis(both, -4, 0)
        return both.reshape((members,) + lead + (mine, entry))

    pair = natural(pair)
    key_t, value_t = pair[0], pair[1]
    key_n, value_n = key_t.transpose(0, 2, 1), value_t.transpose(0, 2, 1)
    value_one = jnp.concatenate([value_t, jnp.ones((KVH, 16, GROUP), BF)], axis=1)
    mixed_f, logs = attend(first_tokens, query_use, key_n, value_one)
    mixed = mixed_f.reshape(QH * HD, mine).astype(BF)
    hidden = states + dot(mixed, w_out_all, ((0,), (0,)))

    inverse_two = rms(hidden)
    normed_two = (hidden * inverse_two * gain_two).astype(BF)
    normed_all = lax.all_gather(normed_two, ("group", "side"), axis=0, tiled=True)
    gate = dot(normed_all, w_gate_all)
    up = dot(normed_all, w_up_all)
    sig = jax.nn.sigmoid(gate)
    activated = (gate * sig * up).astype(BF)
    ffn_out = dot(activated, w_down_all).astype(BF)
    ffn_out = lax.psum_scatter(ffn_out, ("group", "side"), scatter_dimension=0, tiled=True)
    result = hidden + ffn_out.astype(F32)
    block_out = from_members(result.astype(BF))

    total_tokens = shard * cols * lax.axis_size("dp")
    loss_scale = total_tokens / token_count[0].astype(F32)
    d_result = loss_scale * (result - target.astype(F32))
    d_low = lax.all_gather(d_result.astype(BF), ("group", "side"), axis=0, tiled=True)
    d_act = dot(d_low, w_down_all, ((1,), (1,)))
    grad_down = dot(activated, d_low, ((0,), (0,))).astype(BF)
    d_up = (d_act * gate * sig).astype(BF)
    d_gate = (d_act * up * sig * (1.0 + gate * (1.0 - sig))).astype(BF)
    d_normed = dot(d_gate, w_gate_all, ((1,), (1,))) + dot(d_up, w_up_all, ((1,), (1,)))
    d_normed = lax.psum_scatter(
        d_normed.astype(BF), ("group", "side"), scatter_dimension=0, tiled=True
    ).astype(F32)
    grad_gate = dot(normed_all, d_gate, ((0,), (0,))).astype(BF)
    grad_up = dot(normed_all, d_up, ((0,), (0,))).astype(BF)
    grad_down = lax.psum_scatter(grad_down, "row", scatter_dimension=1, tiled=True)
    grad_gate = lax.psum_scatter(grad_gate, "row", scatter_dimension=0, tiled=True)
    grad_up = lax.psum_scatter(grad_up, "row", scatter_dimension=0, tiled=True)
    grad_down = lax.psum(grad_down, "dp")
    grad_gate, grad_up, _ = lax.optimization_barrier((grad_gate, grad_up, grad_down))
    grad_gate, grad_up = lax.psum((grad_gate, grad_up), "dp")

    norm_two_part = jnp.sum(d_normed * hidden * inverse_two, axis=0)
    d_hidden = d_result + norm_back(hidden, inverse_two, gain_two, d_normed)
    d_hidden_low = d_hidden.astype(BF)
    grad_out = dot(mixed, d_hidden_low, ((1,), (0,))).astype(BF)
    d_mixed = dot(w_out_all, d_hidden_low, ((1,), (1,))).astype(BF)
    d_mixed = d_mixed.reshape(KVH, REP, HD, mine)
    delta = jnp.sum(d_mixed.astype(F32) * mixed_f, axis=2)
    d_query, d_key_n, d_value_n = attend_back(
        first_tokens, query_use, d_mixed, logs, delta, key_n, value_n, key_t
    )
    d_pair = dealt(jnp.stack([d_key_n, d_value_n])).astype(BF)
    d_pair = lax.psum_scatter(d_pair, ("row", "side"), scatter_dimension=0, tiled=True)[0]
    d_pair = d_pair.astype(F32).transpose(0, 1, 3, 2)
    d_query_raw, query_gain_part = query_back(d_query.reshape(QH, HD, mine) * scale)
    d_key_raw, key_gain_part = key_back(d_pair[0])
    d_projected = jnp.concatenate(
        [
            d_query_raw.reshape(cols, q_width, mine),
            d_key_raw.reshape(cols, k_width, mine),
            d_pair[1].reshape(cols, k_width, mine),
        ],
        axis=1,
    ).astype(BF)
    d_normed_one = dot(d_projected, w_project, ((0, 1), (0, 2)))
    grad_input = d_hidden + norm_back(states, inverse_one, gain_one, d_normed_one)
    norm_one_part = jnp.sum(d_normed_one * states * inverse_one, axis=0)
    grad_input = from_members(grad_input)

    grad_project = lax.dot_general(
        d_projected, normed_one, (((2,), (0,)), ((), ())), preferred_element_type=F32
    )
    grad_project = grad_project.astype(BF).transpose(0, 2, 1)
    grad_project = lax.psum_scatter(
        grad_project.reshape(cols * D, -1),
        ("group", "side", "row"),
        scatter_dimension=0,
        tiled=True,
    )
    grad_out = grad_out.reshape(cols, q_width, rows, width).transpose(0, 2, 1, 3)
    grad_out = lax.psum_scatter(
        grad_out.reshape(cols * rows * q_width, width),
        ("group", "side", "row"),
        scatter_dimension=0,
        tiled=True,
    )
    grad_project, grad_out, _ = lax.optimization_barrier((grad_project, grad_out, grad_gate))
    grad_project, grad_out = lax.psum((grad_project, grad_out), "dp")
    small = jnp.concatenate([norm_one_part, norm_two_part, query_gain_part, key_gain_part])
    small = lax.psum(small, ("dp", "row", "group", "side"))
    grad_norm1 = lax.dynamic_slice_in_dim(small, row_index * width, width, 0)
    grad_norm2 = lax.dynamic_slice_in_dim(small, D + row_index * width, width, 0)
    grad_project = grad_project.astype(F32)
    return (
        block_out,
        grad_input,
        grad_norm1,
        grad_project[:, :q_width],
        grad_project[:, q_width : q_width + k_width],
        grad_project[:, q_width + k_width :],
        small[2 * D : 2 * D + HD],
        small[2 * D + HD :],
        grad_out.astype(F32),
        grad_norm2,
        grad_gate.astype(F32),
        grad_up.astype(F32),
        grad_down.astype(F32),
    )


def solution(mesh):
    dp, row, col = mesh.shape["dp"], mesh.shape["row"], mesh.shape["col"]

    def call(*args):
        side = GROUP * dp * col // args[0].shape[0]
        fine = Mesh(
            mesh.devices.reshape(dp, row, col // side, side), ("dp", "row", "group", "side")
        )
        col_axes = ("group", "side")
        token_spec = P(("dp", "group", "side"), "row")
        wide = P("row", col_axes)
        tall = P(col_axes, "row")
        return jax.shard_map(
            body,
            mesh=fine,
            in_specs=(
                token_spec,
                P("row"),
                wide,
                wide,
                wide,
                P(),
                P(),
                tall,
                P("row"),
                wide,
                wide,
                tall,
                token_spec,
                P("dp"),
                P(),
            ),
            out_specs=(
                token_spec,
                token_spec,
                P("row"),
                wide,
                wide,
                wide,
                P(),
                P(),
                tall,
                P("row"),
                wide,
                wide,
                tall,
            ),
            check_vma=False,
        )(*args)

    return call
```

```python
import functools
import math

import jax
import jax.numpy as jnp
from jax import lax
from jax.experimental import pallas as pl
from jax.experimental.pallas import tpu as pltpu
from jax.sharding import Mesh
from jax.sharding import PartitionSpec as P

D = 2048
QH = 20
KVH = 5
HD = 64
PROMPT = 1024
CONT = 128
NCONT = 8
GROUP = PROMPT + NCONT * CONT
REP = QH // KVH
KEYS = 256

EPSILON = 1e-06
BF = jnp.bfloat16
F32 = jnp.float32


def dot(left, right, dims=((1,), (0,))):
    return lax.dot_general(left, right, (dims, ((), ())), preferred_element_type=F32)


def rms(values):
    return lax.rsqrt(jnp.mean(values * values, axis=1, keepdims=True) + EPSILON)


def norm_back(states, inverse, gain, d_normed):
    mean = jnp.mean(states * gain * d_normed, axis=1, keepdims=True)
    return inverse * gain * d_normed - states * inverse**3 * mean


def prepare(raw, gain, cosine, sine):
    values = raw * lax.rsqrt(jnp.mean(raw * raw, axis=1, keepdims=True) + EPSILON)
    values = values * gain[None, :, None]
    half = HD // 2
    first, second = values[:, :half], values[:, half:]
    return jnp.concatenate(
        [first * cosine - second * sine, second * cosine + first * sine], axis=1
    )


def allowed(first_query, first_key, span, rows):
    key = first_key + lax.broadcasted_iota(jnp.int32, (KEYS, rows), 0)
    query = first_query + lax.broadcasted_iota(jnp.int32, (KEYS, rows), 1) % span
    return (key <= query) & ((key < PROMPT) | (key // CONT == query // CONT))


def side_by_side(ref, index, span):
    return jnp.concatenate(
        [ref[0, head, :, index * span : (index + 1) * span] for head in range(REP)], axis=1
    )


def tiles_of(first_query):
    last = first_query // KEYS
    return jnp.minimum(last, PROMPT // KEYS), last


def attend_kernel(chunks, span, first_ref, query_ref, key_ref, value_ref, out_ref, log_ref):
    rows = REP * span
    for index in range(chunks):
        query = side_by_side(query_ref, index, span)
        first_query = first_ref[index]
        full, last = tiles_of(first_query)

        def tile(where, accum, masked):
            first_key = pl.multiple_of(where * KEYS, KEYS)
            scores = dot(key_ref[0, pl.ds(first_key, KEYS), :], query)
            expo = jnp.exp(scores)
            if masked:
                expo = jnp.where(allowed(first_query, first_key, span, rows), expo, 0.0)
            return accum + dot(value_ref[0, :, pl.ds(first_key, KEYS)], expo.astype(BF))

        accum = tile(last, jnp.zeros((value_ref.shape[1], rows), F32), True)
        accum = lax.fori_loop(0, full, lambda where, total: tile(where, total, False), accum)
        total = accum[HD : HD + 1]
        mixed = accum[:HD] / total
        logs = jnp.log(total)
        for head in range(REP):
            cut = slice(head * span, (head + 1) * span)
            out_ref[0, head, :, index * span : (index + 1) * span] = mixed[:, cut]
            log_ref[0, head : head + 1, index * span : (index + 1) * span] = logs[:, cut]


def attend_back_kernel(
    chunks,
    span,
    first_ref,
    query_ref,
    d_out_ref,
    log_ref,
    delta_ref,
    key_ref,
    value_ref,
    key_t_ref,
    d_query_ref,
    d_key_ref,
    d_value_ref,
):
    rows = REP * span
    d_key_ref[...] = jnp.zeros_like(d_key_ref)
    d_value_ref[...] = jnp.zeros_like(d_value_ref)
    for index in range(chunks):
        query = side_by_side(query_ref, index, span)
        d_out = side_by_side(d_out_ref, index, span)
        query_t = query.T
        d_out_t = d_out.T
        cut = slice(index * span, (index + 1) * span)
        logs = jnp.concatenate([log_ref[0, h : h + 1, cut] for h in range(REP)], axis=1)
        delta = jnp.concatenate([delta_ref[0, h : h + 1, cut] for h in range(REP)], axis=1)
        first_query = first_ref[index]
        full, last = tiles_of(first_query)

        def tile(where, accum, masked):
            first_key = pl.multiple_of(where * KEYS, KEYS)
            here = pl.ds(first_key, KEYS)
            probs = jnp.exp(dot(key_ref[0, here, :], query) - logs)
            if masked:
                probs = jnp.where(allowed(first_query, first_key, span, rows), probs, 0.0)
            d_probs = dot(value_ref[0, here, :], d_out)
            d_scores = (probs * (d_probs - delta)).astype(BF)
            d_value_ref[0, here, :] += dot(probs.astype(BF), d_out_t)
            d_key_ref[0, here, :] += dot(d_scores, query_t)
            return accum + dot(key_t_ref[0, :, here], d_scores)

        accum = tile(last, jnp.zeros((HD, rows), F32), True)
        accum = lax.fori_loop(0, full, lambda where, total: tile(where, total, False), accum)
        for head in range(REP):
            part = accum[:, head * span : (head + 1) * span]
            d_query_ref[0, head, :, cut] = part


def per_head(shape):
    return pl.BlockSpec((1,) + shape, lambda head, first: (head,) + (0,) * len(shape))


def attend(first, query, key, value_t):
    tokens = query.shape[-1]
    chunks = first.shape[0]
    return pl.pallas_call(
        functools.partial(attend_kernel, chunks, tokens // chunks),
        out_shape=(
            jax.ShapeDtypeStruct((KVH, REP, HD, tokens), F32),
            jax.ShapeDtypeStruct((KVH, REP, tokens), F32),
        ),
        grid_spec=pltpu.PrefetchScalarGridSpec(
            num_scalar_prefetch=1,
            grid=(KVH,),
            in_specs=[
                per_head((REP, HD, tokens)),
                per_head((GROUP, HD)),
                per_head((value_t.shape[1], GROUP)),
            ],
            out_specs=[per_head((REP, HD, tokens)), per_head((REP, tokens))],
        ),
        compiler_params=pltpu.CompilerParams(vmem_limit_bytes=32 * 1024 * 1024),
        name="attend",
    )(first, query, key, value_t)


def attend_back(first, query, d_out, logs, delta, key, value, key_t):
    tokens = query.shape[-1]
    chunks = first.shape[0]
    return pl.pallas_call(
        functools.partial(attend_back_kernel, chunks, tokens // chunks),
        out_shape=(
            jax.ShapeDtypeStruct((KVH, REP, HD, tokens), F32),
            jax.ShapeDtypeStruct((KVH, GROUP, HD), F32),
            jax.ShapeDtypeStruct((KVH, GROUP, HD), F32),
        ),
        grid_spec=pltpu.PrefetchScalarGridSpec(
            num_scalar_prefetch=1,
            grid=(KVH,),
            in_specs=[
                per_head((REP, HD, tokens)),
                per_head((REP, HD, tokens)),
                per_head((REP, tokens)),
                per_head((REP, tokens)),
                per_head((GROUP, HD)),
                per_head((GROUP, HD)),
                per_head((HD, GROUP)),
            ],
            out_specs=[
                per_head((REP, HD, tokens)),
                per_head((GROUP, HD)),
                per_head((GROUP, HD)),
            ],
        ),
        compiler_params=pltpu.CompilerParams(vmem_limit_bytes=32 * 1024 * 1024),
        name="attend_back",
    )(first, query, d_out, logs, delta, key, value, key_t)


AHEAD = 4


class Part:
    def __init__(self, axis, rows, cols, count, base):
        self.axis, self.rows, self.cols, self.count, self.base = axis, rows, cols, count, base

    def cut(self, ref, index, half):
        first = index * self.rows
        if self.axis == 0:
            return ref.at[pl.ds(half * self.rows * self.count + first, self.rows), :]
        return ref.at[pl.ds(first, self.rows), pl.ds(half * self.cols, self.cols)]


def reduce_kernel(parts, planes, *refs):
    count = len(parts)
    grads, outs, own, near, far, wide = (refs[i * count : (i + 1) * count] for i in range(6))
    own_sem, out_sem, row_send, row_recv, in_send, far_recv, mid_send, wide_recv = refs[6 * count :]
    plane = lax.axis_index("dp")
    row = lax.axis_index("row")
    other_row = {"row": 1 - row}
    at_end = (plane == 0) | (plane == planes - 1)
    low = plane < planes // 2
    end_next = {"dp": jnp.where(low, 1, planes - 2)}
    mid_outer = {"dp": jnp.where(low, 0, planes - 1)}
    mid_other = {"dp": jnp.where(low, planes // 2, planes // 2 - 1)}

    def remote(source, target, send, recv, where):
        return pltpu.make_async_remote_copy(
            source, target, send, recv, device_id=where, device_id_type=pl.DeviceIdType.MESH
        )

    barrier = pltpu.get_barrier_semaphore()

    def greet(where):
        pl.semaphore_signal(barrier, 1, device_id=where, device_id_type=pl.DeviceIdType.MESH)

    greet(other_row)

    @pl.when(at_end)
    def _():
        greet(end_next)
        pl.semaphore_wait(barrier, 2)

    @pl.when(jnp.logical_not(at_end))
    def _():
        greet(mid_outer)
        greet(mid_other)
        pl.semaphore_wait(barrier, 3)

    def row_copy(j, index):
        slot = parts[j].base + index
        return remote(
            parts[j].cut(grads[j], index, 1), near[j].at[index], row_send.at[slot], row_recv.at[slot], other_row
        )

    def in_copy(j, index):
        slot = parts[j].base + index
        return remote(near[j].at[index], far[j].at[index], in_send.at[slot], far_recv.at[slot], end_next)

    def mid_copy(j, index):
        slot = parts[j].base + index
        return remote(far[j].at[index], wide[j].at[index], mid_send.at[slot], wide_recv.at[slot], mid_other)

    def back_copy(j, index):
        slot = parts[j].base + index
        return remote(wide[j].at[index], far[j].at[index], in_send.at[slot], far_recv.at[slot], mid_outer)

    def out_copy(j, index, source):
        slot = parts[j].base + index
        return pltpu.make_async_copy(source[j].at[index], parts[j].cut(outs[j], index, 0), out_sem.at[slot])

    def own_copy(j, index):
        slot = parts[j].base + index
        return pltpu.make_async_copy(parts[j].cut(grads[j], index, 0), own[j].at[index], own_sem.at[slot])

    def each(step, action):
        for j, part in enumerate(parts):
            index = step - part.base

            @pl.when((index >= 0) & (index < part.count))
            def _(j=j, index=index):
                action(j, index)

    def add(target, j, index, first, second):
        total = first[j][index].astype(F32) + second[j][index].astype(F32)
        target[j][index] = total.astype(BF)

    def send_row(j, index):
        own_copy(j, index).start()
        row_copy(j, index).start()

    def take_row(j, index):
        own_copy(j, index).wait()
        row_copy(j, index).wait_recv()
        add(near, j, index, near, own)

        @pl.when(at_end)
        def _():
            in_copy(j, index).start()

    def take_far(j, index):
        back_copy(j, index).wait_recv()
        add(far, j, index, far, near)
        mid_copy(j, index).start()

    def take_wide(j, index):
        mid_copy(j, index).wait_recv()
        add(wide, j, index, wide, far)
        back_copy(j, index).start()
        out_copy(j, index, wide).start()

    def take_back(j, index):
        in_copy(j, index).wait_recv()
        out_copy(j, index, far).start()

    def finish_end(j, index):
        row_copy(j, index).wait_send()
        in_copy(j, index).wait_send()
        out_copy(j, index, far).wait()

    def finish_mid(j, index):
        row_copy(j, index).wait_send()
        mid_copy(j, index).wait_send()
        back_copy(j, index).wait_send()
        out_copy(j, index, wide).wait()

    total = sum(part.count for part in parts)

    @pl.loop(0, AHEAD)
    def _(step):
        each(step, send_row)

    @pl.loop(0, total + 4)
    def _(step):
        each(step + AHEAD, send_row)
        each(step, take_row)

        @pl.when(at_end)
        def _():
            each(step - 4, take_back)

        @pl.when(jnp.logical_not(at_end))
        def _():
            each(step - 1, take_far)
            each(step - 2, take_wide)

    @pl.when(at_end)
    def _():
        @pl.loop(0, total)
        def _(step):
            each(step, finish_end)

    @pl.when(jnp.logical_not(at_end))
    def _():
        @pl.loop(0, total)
        def _(step):
            each(step, finish_mid)


def reduce_all(planes, grads):
    parts, base = [], 0
    for grad, axis, rows in grads:
        height = grad.shape[0] // (2 if axis == 0 else 1)
        width = grad.shape[1] // (1 if axis == 0 else 2)
        parts.append(Part(axis, rows, width, height // rows, base))
        base += height // rows
    shapes = [(part.count, part.rows, part.cols) for part in parts]
    anywhere = pl.BlockSpec(memory_space=pl.ANY)
    return pl.pallas_call(
        functools.partial(reduce_kernel, parts, planes),
        out_shape=[jax.ShapeDtypeStruct((n * r, c), BF) for n, r, c in shapes],
        in_specs=[anywhere] * len(parts),
        out_specs=[anywhere] * len(parts),
        scratch_shapes=[pltpu.VMEM(shape, BF) for _ in range(4) for shape in shapes]
        + [pltpu.SemaphoreType.DMA((base,)) for _ in range(8)],
        compiler_params=pltpu.CompilerParams(
            collective_id=0, has_side_effects=True, vmem_limit_bytes=56 * 1024 * 1024
        ),
        name="reduce_grads",
    )(*[grad for grad, _, _ in grads])


def body(
    tokens,
    norm1_gain,
    w_query,
    w_key,
    w_value,
    query_gain,
    key_gain,
    w_out,
    norm2_gain,
    w_gate,
    w_up,
    w_down,
    teacher,
    positions,
    token_count,
):
    rows = lax.axis_size("row")
    cores = lax.axis_size("side")
    cols = lax.axis_size("group") * cores
    row_index = lax.axis_index("row")
    group_index = lax.axis_index("group")
    members = rows * cores
    member = row_index * cores + lax.axis_index("side")
    shard, width = tokens.shape
    pieces = 2 * members
    span = shard // pieces
    mine = shard // members * cores
    q_width, k_width = w_query.shape[1], w_key.shape[1]
    ff = w_gate.shape[1]

    def from_row(block, ahead):
        pairs = [((r + ahead) % rows, r) for r in range(rows)]
        return lax.ppermute(block, "row", pairs)

    def gather_rows(block, axis):
        parts = [block] + [from_row(block, ahead) for ahead in range(1, rows)]
        return jnp.concatenate(parts, axis=axis)

    def scatter_rows(block, axis):
        size = block.shape[axis] // rows
        total = lax.slice_in_dim(block, 0, size, axis=axis).astype(F32)
        for ahead in range(1, rows):
            part = lax.slice_in_dim(block, ahead * size, (ahead + 1) * size, axis=axis)
            total = total + from_row(part, rows - ahead).astype(F32)
        return total.astype(BF)

    def sum_planes(block, cuts):
        planes = lax.axis_size("dp")
        plane = lax.axis_index("dp")
        half = planes // 2
        edge = jnp.minimum(plane, planes - 1 - plane)
        done = []
        for part in jnp.split(block, cuts, axis=0):
            for step in range(half - 1):
                pairs = [(step, step + 1), (planes - 1 - step, planes - 2 - step)]
                come = lax.ppermute(part, "dp", pairs)
                part = (part.astype(F32) + come.astype(F32)).astype(BF)
            come = lax.ppermute(part, "dp", [(half - 1, half), (half, half - 1)])
            part = (part.astype(F32) + come.astype(F32)).astype(BF)
            for step in reversed(range(half - 1)):
                pairs = [(step + 1, step), (planes - 2 - step, planes - 1 - step)]
                come = lax.ppermute(part, "dp", pairs)
                part = jnp.where(edge == step, come, part)
            done.append(part)
        return jnp.concatenate(done, axis=0)

    def to_members(block):
        parts = block.reshape(pieces, span, width)
        parts = jnp.stack([parts[:members], parts[members:][::-1]], axis=1)
        moved = lax.all_to_all(parts, ("row", "side"), 0, 0, tiled=True)
        moved = jnp.roll(moved.reshape(rows, cores, 2 * span, width), -row_index, 0)
        moved = moved.transpose(1, 2, 0, 3)
        return moved.reshape(mine, rows * width)

    def from_members(block):
        parts = block.reshape(cores, 2, span, rows, width).transpose(3, 0, 1, 2, 4)
        parts = jnp.roll(parts, row_index, 0).reshape(members, 2, span, width)
        moved = lax.all_to_all(parts, ("row", "side"), 0, 0, tiled=True)
        moved = jnp.concatenate([moved[:, 0], moved[:, 1][::-1]], axis=0)
        return moved.reshape(shard, width)

    def pick(values):
        part = lax.dynamic_slice_in_dim(values.reshape(-1, cores, pieces, span), group_index, 1, 0)[0]
        low = lax.dynamic_slice_in_dim(part, member, 1, 1)
        high = lax.dynamic_slice_in_dim(part, pieces - 1 - member, 1, 1)
        return jnp.concatenate([low, high], axis=1).reshape(-1)

    first_tokens = (
        jnp.array([0, 0, shard, shard], jnp.int32)
        + jnp.stack([member, pieces - 1 - member] * 2).astype(jnp.int32) * span
    )

    states = to_members(tokens).astype(F32)
    gain_one = gather_rows(norm1_gain, 0)
    gain_two = gather_rows(norm2_gain, 0)
    w_project = jnp.concatenate([w_query, w_key, w_value], axis=1)
    w_project = gather_rows(w_project, 0)
    w_project = lax.all_gather(w_project, ("group", "side"), axis=0)
    w_out_all = gather_rows(w_out, 1)
    w_out_all = lax.all_gather(w_out_all, ("group", "side"), axis=0, tiled=True)
    w_gate_all = gather_rows(w_gate, 0)
    w_up_all = gather_rows(w_up, 0)
    w_down_all = gather_rows(w_down, 1)
    target = to_members(teacher)

    half = HD // 2
    freq = jnp.exp(jnp.arange(half, dtype=F32) * (-2.0 * math.log(10000.0) / HD))
    angle = freq[:, None] * pick(positions).astype(F32)[None, :]
    cosine, sine = jnp.cos(angle), jnp.sin(angle)
    inverse_one = rms(states)
    normed_one = (states * inverse_one * gain_one).astype(BF)
    projected = dot(w_project, normed_one, ((1,), (1,)))
    query_raw = projected[:, :q_width].reshape(QH, HD, mine)
    key_sent = projected[:, q_width : q_width + k_width].reshape(KVH, HD, mine).astype(BF)
    value_sent = projected[:, q_width + k_width :].reshape(KVH, HD, mine).astype(BF)
    query_rot, query_back = jax.vjp(
        lambda raw, gain: prepare(raw, gain, cosine, sine), query_raw, query_gain
    )
    key_rot, key_back = jax.vjp(
        lambda raw, gain: prepare(raw, gain, cosine, sine), key_sent.astype(F32), key_gain
    )
    scale = 1.0 / math.sqrt(HD)
    query_use = (query_rot.astype(BF) * BF(scale)).reshape(KVH, REP, HD, mine)
    pair = jnp.stack([key_rot.astype(BF), value_sent])
    pair = lax.all_gather(pair, ("row", "side"), axis=0)

    def natural(stacked):
        lead = stacked.shape[1:-1]
        parts = stacked.reshape((members,) + lead + (cores, 2, span))
        low, high = parts[..., 0, :], parts[..., 1, :]
        both = jnp.concatenate([low, high[::-1]], axis=0)
        return jnp.moveaxis(both, 0, -2).reshape(lead + (GROUP,))

    def dealt(full):
        lead, entry = full.shape[:-2], full.shape[-1]
        parts = full.reshape(lead + (cores, pieces, span, entry))
        low = parts[..., :members, :, :]
        high = parts[..., members:, :, :][..., ::-1, :, :]
        both = jnp.stack([low, high], axis=-3)
        both = jnp.moveaxis(both, -4, 0)
        return both.reshape((members,) + lead + (mine, entry))

    pair = natural(pair)
    key_t, value_t = pair[0], pair[1]
    key_n, value_n = key_t.transpose(0, 2, 1), value_t.transpose(0, 2, 1)
    value_one = jnp.concatenate([value_t, jnp.ones((KVH, 16, GROUP), BF)], axis=1)
    mixed_f, logs = attend(first_tokens, query_use, key_n, value_one)
    mixed = mixed_f.reshape(QH * HD, mine).astype(BF)
    hidden = states + dot(mixed, w_out_all, ((0,), (0,)))

    inverse_two = rms(hidden)
    normed_two = (hidden * inverse_two * gain_two).astype(BF)
    normed_all = lax.all_gather(normed_two, ("group", "side"), axis=0, tiled=True)
    gate = dot(normed_all, w_gate_all)
    up = dot(normed_all, w_up_all)
    sig = jax.nn.sigmoid(gate)
    activated = (gate * sig * up).astype(BF)
    ffn_out = dot(activated, w_down_all).astype(BF)
    ffn_out = lax.psum_scatter(ffn_out, ("group", "side"), scatter_dimension=0, tiled=True)
    result = hidden + ffn_out.astype(F32)
    block_out = from_members(result.astype(BF))

    total_tokens = shard * cols * lax.axis_size("dp")
    loss_scale = total_tokens / token_count[0].astype(F32)
    d_result = loss_scale * (result - target.astype(F32))
    d_low = lax.all_gather(d_result.astype(BF), ("group", "side"), axis=0, tiled=True)
    d_act = dot(d_low, w_down_all, ((1,), (1,)))
    grad_down = dot(activated, d_low, ((0,), (0,))).astype(BF)
    d_up = (d_act * gate * sig).astype(BF)
    d_gate = (d_act * up * sig * (1.0 + gate * (1.0 - sig))).astype(BF)
    d_normed = dot(d_gate, w_gate_all, ((1,), (1,))) + dot(d_up, w_up_all, ((1,), (1,)))
    d_normed = lax.psum_scatter(
        d_normed.astype(BF), ("group", "side"), scatter_dimension=0, tiled=True
    ).astype(F32)
    d_gate_up = jnp.concatenate([d_gate, d_up], axis=1)
    grad_gate_up = dot(normed_all, d_gate_up, ((0,), (0,))).astype(BF)

    norm_two_part = jnp.sum(d_normed * hidden * inverse_two, axis=0)
    d_hidden = d_result + norm_back(hidden, inverse_two, gain_two, d_normed)
    d_hidden_low = d_hidden.astype(BF)
    grad_out = dot(mixed, d_hidden_low, ((1,), (0,))).astype(BF)
    d_mixed = dot(w_out_all, d_hidden_low, ((1,), (1,))).astype(BF)
    d_mixed = d_mixed.reshape(KVH, REP, HD, mine)
    delta = jnp.sum(d_mixed.astype(F32) * mixed_f, axis=2)
    d_query, d_key_n, d_value_n = attend_back(
        first_tokens, query_use, d_mixed, logs, delta, key_n, value_n, key_t
    )
    d_pair = dealt(jnp.stack([d_key_n, d_value_n])).astype(BF)
    d_pair = lax.psum_scatter(d_pair, ("row", "side"), scatter_dimension=0, tiled=True)[0]
    d_pair = d_pair.astype(F32).transpose(0, 1, 3, 2)
    d_query_raw, query_gain_part = query_back(d_query.reshape(QH, HD, mine) * scale)
    d_key_raw, key_gain_part = key_back(d_pair[0])
    d_projected = jnp.concatenate(
        [
            d_query_raw.reshape(cols, q_width, mine),
            d_key_raw.reshape(cols, k_width, mine),
            d_pair[1].reshape(cols, k_width, mine),
        ],
        axis=1,
    ).astype(BF)
    d_normed_one = dot(d_projected, w_project, ((0, 1), (0, 2)))
    grad_input = d_hidden + norm_back(states, inverse_one, gain_one, d_normed_one)
    norm_one_part = jnp.sum(d_normed_one * states * inverse_one, axis=0)
    grad_input = from_members(grad_input)

    grad_project = lax.dot_general(
        d_projected, normed_one, (((2,), (0,)), ((), ())), preferred_element_type=F32
    )
    grad_project = grad_project.astype(BF).transpose(0, 2, 1)
    grad_project = lax.psum_scatter(
        grad_project.reshape(cols * D, -1), ("group", "side"), scatter_dimension=0, tiled=True
    )
    grad_out = lax.psum_scatter(grad_out, ("group", "side"), scatter_dimension=0, tiled=True)
    if rows == 2 and lax.axis_size("dp") == 4:
        grad_down, grad_gate_up, grad_out, grad_project = reduce_all(
            4, [(grad_down, 1, 128), (grad_gate_up, 0, 64), (grad_out, 1, 64), (grad_project, 0, 256)]
        )
    else:
        grad_down = sum_planes(scatter_rows(grad_down, 1), 2)
        grad_gate_up = sum_planes(scatter_rows(grad_gate_up, 0), 4)
        grad_out = sum_planes(scatter_rows(grad_out, 1), 1)
        grad_project = sum_planes(scatter_rows(grad_project, 0), 2)
    norm_one_part = jnp.roll(norm_one_part.reshape(rows, width), row_index, 0).reshape(D)
    norm_two_part = jnp.roll(norm_two_part.reshape(rows, width), row_index, 0).reshape(D)
    small = jnp.concatenate([norm_one_part, norm_two_part, query_gain_part, key_gain_part])
    small = lax.psum(small, ("dp", "row", "group", "side"))
    grad_norm1 = lax.dynamic_slice_in_dim(small, row_index * width, width, 0)
    grad_norm2 = lax.dynamic_slice_in_dim(small, D + row_index * width, width, 0)
    grad_project = grad_project.astype(F32)
    return (
        block_out,
        grad_input,
        grad_norm1,
        grad_project[:, :q_width],
        grad_project[:, q_width : q_width + k_width],
        grad_project[:, q_width + k_width :],
        small[2 * D : 2 * D + HD],
        small[2 * D + HD :],
        grad_out.astype(F32),
        grad_norm2,
        grad_gate_up[:, :ff].astype(F32),
        grad_gate_up[:, ff:].astype(F32),
        grad_down.astype(F32),
    )


def solution(mesh):
    dp, row, col = mesh.shape["dp"], mesh.shape["row"], mesh.shape["col"]

    def call(*args):
        side = GROUP * dp * col // args[0].shape[0]
        fine = Mesh(
            mesh.devices.reshape(dp, row, col // side, side), ("dp", "row", "group", "side")
        )
        col_axes = ("group", "side")
        token_spec = P(("dp", "group", "side"), "row")
        wide = P("row", col_axes)
        tall = P(col_axes, "row")
        return jax.shard_map(
            body,
            mesh=fine,
            in_specs=(
                token_spec,
                P("row"),
                wide,
                wide,
                wide,
                P(),
                P(),
                tall,
                P("row"),
                wide,
                wide,
                tall,
                token_spec,
                P("dp"),
                P(),
            ),
            out_specs=(
                token_spec,
                token_spec,
                P("row"),
                wide,
                wide,
                wide,
                P(),
                P(),
                tall,
                P("row"),
                wide,
                wide,
                tall,
            ),
            check_vma=False,
        )(*args)

    return call
```

```python
import functools
import math

import jax
import jax.numpy as jnp
from jax import lax
from jax.experimental import pallas as pl
from jax.experimental.pallas import tpu as pltpu
from jax.sharding import Mesh
from jax.sharding import PartitionSpec as P

D = 2048
QH = 20
KVH = 5
HD = 64
PROMPT = 1024
CONT = 128
NCONT = 8
GROUP = PROMPT + NCONT * CONT
REP = QH // KVH
KEYS = 256

EPSILON = 1e-06
BF = jnp.bfloat16
F32 = jnp.float32


def dot(left, right, dims=((1,), (0,))):
    return lax.dot_general(left, right, (dims, ((), ())), preferred_element_type=F32)


def rms(values):
    return lax.rsqrt(jnp.mean(values * values, axis=1, keepdims=True) + EPSILON)


def norm_back(states, inverse, gain, d_normed):
    mean = jnp.mean(states * gain * d_normed, axis=1, keepdims=True)
    return inverse * gain * d_normed - states * inverse**3 * mean


def prepare(raw, gain, cosine, sine):
    values = raw * lax.rsqrt(jnp.mean(raw * raw, axis=1, keepdims=True) + EPSILON)
    values = values * gain[None, :, None]
    half = HD // 2
    first, second = values[:, :half], values[:, half:]
    return jnp.concatenate(
        [first * cosine - second * sine, second * cosine + first * sine], axis=1
    )


def allowed(first_query, first_key, span, rows):
    key = first_key + lax.broadcasted_iota(jnp.int32, (KEYS, rows), 0)
    query = first_query + lax.broadcasted_iota(jnp.int32, (KEYS, rows), 1) % span
    return (key <= query) & ((key < PROMPT) | (key // CONT == query // CONT))


def side_by_side(ref, index, span):
    return jnp.concatenate(
        [ref[0, head, :, index * span : (index + 1) * span] for head in range(REP)], axis=1
    )


def tiles_of(first_query):
    last = first_query // KEYS
    return jnp.minimum(last, PROMPT // KEYS), last


def attend_kernel(chunks, span, first_ref, query_ref, key_ref, value_ref, out_ref, log_ref):
    rows = REP * span
    for index in range(chunks):
        query = side_by_side(query_ref, index, span)
        first_query = first_ref[index]
        full, last = tiles_of(first_query)

        def tile(where, accum, masked):
            first_key = pl.multiple_of(where * KEYS, KEYS)
            scores = dot(key_ref[0, pl.ds(first_key, KEYS), :], query)
            expo = jnp.exp(scores)
            if masked:
                expo = jnp.where(allowed(first_query, first_key, span, rows), expo, 0.0)
            return accum + dot(value_ref[0, :, pl.ds(first_key, KEYS)], expo.astype(BF))

        accum = tile(last, jnp.zeros((value_ref.shape[1], rows), F32), True)
        accum = lax.fori_loop(0, full, lambda where, total: tile(where, total, False), accum)
        total = accum[HD : HD + 1]
        mixed = accum[:HD] / total
        logs = jnp.log(total)
        for head in range(REP):
            cut = slice(head * span, (head + 1) * span)
            out_ref[0, head, :, index * span : (index + 1) * span] = mixed[:, cut]
            log_ref[0, head : head + 1, index * span : (index + 1) * span] = logs[:, cut]


def attend_back_kernel(
    chunks,
    span,
    first_ref,
    query_ref,
    d_out_ref,
    log_ref,
    delta_ref,
    key_ref,
    value_ref,
    key_t_ref,
    d_query_ref,
    d_key_ref,
    d_value_ref,
):
    rows = REP * span
    d_key_ref[...] = jnp.zeros_like(d_key_ref)
    d_value_ref[...] = jnp.zeros_like(d_value_ref)
    for index in range(chunks):
        query = side_by_side(query_ref, index, span)
        d_out = side_by_side(d_out_ref, index, span)
        query_t = query.T
        d_out_t = d_out.T
        cut = slice(index * span, (index + 1) * span)
        logs = jnp.concatenate([log_ref[0, h : h + 1, cut] for h in range(REP)], axis=1)
        delta = jnp.concatenate([delta_ref[0, h : h + 1, cut] for h in range(REP)], axis=1)
        first_query = first_ref[index]
        full, last = tiles_of(first_query)

        def tile(where, accum, masked):
            first_key = pl.multiple_of(where * KEYS, KEYS)
            here = pl.ds(first_key, KEYS)
            probs = jnp.exp(dot(key_ref[0, here, :], query) - logs)
            if masked:
                probs = jnp.where(allowed(first_query, first_key, span, rows), probs, 0.0)
            d_probs = dot(value_ref[0, here, :], d_out)
            d_scores = (probs * (d_probs - delta)).astype(BF)
            d_value_ref[0, here, :] += dot(probs.astype(BF), d_out_t)
            d_key_ref[0, here, :] += dot(d_scores, query_t)
            return accum + dot(key_t_ref[0, :, here], d_scores)

        accum = tile(last, jnp.zeros((HD, rows), F32), True)
        accum = lax.fori_loop(0, full, lambda where, total: tile(where, total, False), accum)
        for head in range(REP):
            part = accum[:, head * span : (head + 1) * span]
            d_query_ref[0, head, :, cut] = part


def per_head(shape):
    return pl.BlockSpec((1,) + shape, lambda head, first: (head,) + (0,) * len(shape))


def attend(first, query, key, value_t):
    tokens = query.shape[-1]
    chunks = first.shape[0]
    return pl.pallas_call(
        functools.partial(attend_kernel, chunks, tokens // chunks),
        out_shape=(
            jax.ShapeDtypeStruct((KVH, REP, HD, tokens), F32),
            jax.ShapeDtypeStruct((KVH, REP, tokens), F32),
        ),
        grid_spec=pltpu.PrefetchScalarGridSpec(
            num_scalar_prefetch=1,
            grid=(KVH,),
            in_specs=[
                per_head((REP, HD, tokens)),
                per_head((GROUP, HD)),
                per_head((value_t.shape[1], GROUP)),
            ],
            out_specs=[per_head((REP, HD, tokens)), per_head((REP, tokens))],
        ),
        compiler_params=pltpu.CompilerParams(vmem_limit_bytes=32 * 1024 * 1024),
        name="attend",
    )(first, query, key, value_t)


def attend_back(first, query, d_out, logs, delta, key, value, key_t):
    tokens = query.shape[-1]
    chunks = first.shape[0]
    return pl.pallas_call(
        functools.partial(attend_back_kernel, chunks, tokens // chunks),
        out_shape=(
            jax.ShapeDtypeStruct((KVH, REP, HD, tokens), F32),
            jax.ShapeDtypeStruct((KVH, GROUP, HD), F32),
            jax.ShapeDtypeStruct((KVH, GROUP, HD), F32),
        ),
        grid_spec=pltpu.PrefetchScalarGridSpec(
            num_scalar_prefetch=1,
            grid=(KVH,),
            in_specs=[
                per_head((REP, HD, tokens)),
                per_head((REP, HD, tokens)),
                per_head((REP, tokens)),
                per_head((REP, tokens)),
                per_head((GROUP, HD)),
                per_head((GROUP, HD)),
                per_head((HD, GROUP)),
            ],
            out_specs=[
                per_head((REP, HD, tokens)),
                per_head((GROUP, HD)),
                per_head((GROUP, HD)),
            ],
        ),
        compiler_params=pltpu.CompilerParams(vmem_limit_bytes=32 * 1024 * 1024),
        name="attend_back",
    )(first, query, d_out, logs, delta, key, value, key_t)


AHEAD = 4
SLOTS = AHEAD + 2
LAG = 4
SMALL = 40


class Part:
    def __init__(self, axis, rows, cols, count, base, col):
        self.axis, self.rows, self.cols = axis, rows, cols
        self.count, self.base, self.col = count, base, col

    def cut(self, ref, index, half, lead=()):
        first = pl.ds(index * self.rows, self.rows)
        if self.axis == 0:
            first = pl.ds((half * self.count + index) * self.rows, self.rows)
            return ref.at[(*lead, first, slice(None))]
        return ref.at[(*lead, first, pl.ds(half * self.cols, self.cols))]


def reduce_kernel(parts, planes, *refs):
    count = len(parts)
    refs = list(refs)

    def take(number):
        taken = refs[:number]
        del refs[:number]
        return taken

    grads = take(count)
    (small_ref,) = take(1)
    outs = take(count)
    (small_out,) = take(1)
    near, far, wide, own = take(count), take(count), take(count), take(count)
    col_parts = [j for j in range(count) if parts[j].col]
    mate_in = dict(zip(col_parts, take(len(col_parts))))
    far_in = dict(zip(col_parts, take(len(col_parts))))
    own_sem, out_sem, row_send, row_recv, in_send, far_recv, mid_send, wide_recv = take(8)
    col_own, col_send, col_recv, x_send, x_recv, small_local, small_send, small_recv = take(8)
    small_in, small_sum = take(2)
    plane, row = lax.axis_index("dp"), lax.axis_index("row")
    group, side = lax.axis_index("group"), lax.axis_index("side")
    other_row, mate, far_dev = {"row": 1 - row}, {"side": 1 - side}, {"group": 1 - group}
    at_end = (plane == 0) | (plane == planes - 1)
    low = plane < planes // 2
    end_next = {"dp": jnp.where(low, 1, planes - 2)}
    mid_outer = {"dp": jnp.where(low, 0, planes - 1)}
    mid_other = {"dp": jnp.where(low, planes // 2, planes // 2 - 1)}

    def remote(source, target, send, recv, where):
        return pltpu.make_async_remote_copy(
            source, target, send, recv, device_id=where, device_id_type=pl.DeviceIdType.MESH
        )

    barrier = pltpu.get_barrier_semaphore()

    def greet(where):
        pl.semaphore_signal(barrier, 1, device_id=where, device_id_type=pl.DeviceIdType.MESH)

    for where in (other_row, mate, far_dev):
        greet(where)

    @pl.when(at_end)
    def _():
        greet(end_next)
        pl.semaphore_wait(barrier, 4)

    @pl.when(jnp.logical_not(at_end))
    def _():
        greet(mid_outer)
        greet(mid_other)
        pl.semaphore_wait(barrier, 5)

    def col_slot(j, half, index):
        before = sum(2 * parts[i].count for i in col_parts if i < j)
        return before + half * parts[j].count + index

    def col_own_copy(j, half, index, target):
        return pltpu.make_async_copy(
            parts[j].cut(grads[j], index, half, (2 * target + side,)),
            own[j].at[target, half, index],
            col_own.at[target, col_slot(j, half, index)],
        )

    def col_copy(j, half, index, target):
        slot = col_slot(j, half, index)
        return remote(
            parts[j].cut(grads[j], index, half, (2 * target + 1 - side,)),
            mate_in[j].at[target, half, index],
            col_send.at[target, slot],
            col_recv.at[target, slot],
            mate,
        )

    def x_copy(j, half, index):
        slot = col_slot(j, half, index)
        return remote(
            mate_in[j].at[1 - group, half, index],
            far_in[j].at[half, index],
            x_send.at[slot],
            x_recv.at[slot],
            far_dev,
        )

    def take_col(j, half, index):
        for target in range(2):
            col_own_copy(j, half, index, target).wait()
            col_copy(j, half, index, target).wait_recv()
            total = own[j][target, half, index].astype(F32)
            total += mate_in[j][target, half, index].astype(F32)
            mate_in[j][target, half, index] = total.astype(BF)
        x_copy(j, half, index).start()

    def take_x(j, half, index):
        x_copy(j, half, index).wait_recv()
        total = far_in[j][half, index].astype(F32) + mate_in[j][group, half, index].astype(F32)
        far_in[j][half, index] = total.astype(BF)

    def row_copy(j, index):
        slot = parts[j].base + index
        source = far_in[j].at[1, index] if parts[j].col else parts[j].cut(grads[j], index, 1)
        return remote(source, near[j].at[index], row_send.at[slot], row_recv.at[slot], other_row)

    def in_copy(j, index):
        slot = parts[j].base + index
        return remote(near[j].at[index], far[j].at[index], in_send.at[slot], far_recv.at[slot], end_next)

    def mid_copy(j, index):
        slot = parts[j].base + index
        return remote(far[j].at[index], wide[j].at[index], mid_send.at[slot], wide_recv.at[slot], mid_other)

    def back_copy(j, index):
        slot = parts[j].base + index
        return remote(wide[j].at[index], far[j].at[index], in_send.at[slot], far_recv.at[slot], mid_outer)

    def out_copy(j, index, source):
        slot = parts[j].base + index
        return pltpu.make_async_copy(source[j].at[index], parts[j].cut(outs[j], index, 0), out_sem.at[slot])

    def own_copy(j, index):
        slot = parts[j].base + index
        return pltpu.make_async_copy(
            parts[j].cut(grads[j], index, 0), own[j].at[index % SLOTS], own_sem.at[slot]
        )

    def each(step, action):
        for j, part in enumerate(parts):
            index = step - part.base

            @pl.when((index >= 0) & (index < part.count))
            def _(j=j, index=index):
                action(j, index)

    def send_row(j, index):
        if not parts[j].col:
            own_copy(j, index).start()
        row_copy(j, index).start()

    def take_row(j, index):
        row_copy(j, index).wait_recv()
        if parts[j].col:
            mine = far_in[j][0, index]
        else:
            own_copy(j, index).wait()
            mine = own[j][index % SLOTS]
        near[j][index] = (near[j][index].astype(F32) + mine.astype(F32)).astype(BF)

        @pl.when(at_end)
        def _():
            in_copy(j, index).start()

    def take_far(j, index):
        back_copy(j, index).wait_recv()
        far[j][index] = (far[j][index].astype(F32) + near[j][index].astype(F32)).astype(BF)
        mid_copy(j, index).start()

    def take_wide(j, index):
        mid_copy(j, index).wait_recv()
        wide[j][index] = (wide[j][index].astype(F32) + far[j][index].astype(F32)).astype(BF)
        back_copy(j, index).start()
        out_copy(j, index, wide).start()

    def take_back(j, index):
        in_copy(j, index).wait_recv()
        out_copy(j, index, far).start()

    def finish_end(j, index):
        row_copy(j, index).wait_send()
        in_copy(j, index).wait_send()
        out_copy(j, index, far).wait()

    def finish_mid(j, index):
        row_copy(j, index).wait_send()
        mid_copy(j, index).wait_send()
        back_copy(j, index).wait_send()
        out_copy(j, index, wide).wait()

    def small_copy(stage, source, where):
        return remote(small_sum.at[source], small_in.at[stage], small_send.at[stage], small_recv.at[stage], where)

    plane_hops = [small_copy(0, 0, mate), small_copy(1, 1, far_dev), small_copy(2, 2, other_row)]
    small_end = small_copy(3, 3, end_next)
    small_mid = small_copy(4, 4, mid_other)
    small_back = small_copy(3, 5, mid_outer)
    small_load = pltpu.make_async_copy(small_ref, small_sum.at[0], small_local.at[0])
    small_store = pltpu.make_async_copy(small_sum.at[5], small_out, small_local.at[1])

    total = sum(part.count for part in parts)
    small_load.start()
    for j in col_parts:
        for half in (1, 0):
            for index in range(parts[j].count):
                for target in range(2):
                    col_own_copy(j, half, index, target).start()
                    col_copy(j, half, index, target).start()

    @pl.loop(0, AHEAD)
    def _(step):
        each(step, send_row)

    pieces = [(j, half, index) for j in col_parts for half in (1, 0) for index in range(parts[j].count)]

    @pl.loop(0, total + LAG)
    def _(step):
        each(step + AHEAD, send_row)
        each(step, take_row)

        @pl.when(at_end)
        def _():
            each(step - LAG, take_back)

        @pl.when(jnp.logical_not(at_end))
        def _():
            each(step - 1, take_far)
            each(step - 2, take_wide)

        for place, piece in enumerate(pieces):
            @pl.when(step == place + 1)
            def _(piece=piece):
                take_col(*piece)

            @pl.when(step == place + 5)
            def _(piece=piece):
                take_x(*piece)

        @pl.when(step == 0)
        def _():
            small_load.wait()
            plane_hops[0].start()

        for hop in range(3):
            @pl.when(step == hop + 1)
            def _(hop=hop):
                plane_hops[hop].wait_recv()
                small_sum[hop + 1] = small_sum[hop] + small_in[hop]
                if hop < 2:
                    plane_hops[hop + 1].start()

        @pl.when(at_end & (step == 3))
        def _():
            small_end.start()

        @pl.when(at_end & (step == 10))
        def _():
            small_end.wait_recv()
            small_sum[5] = small_in[3]
            small_store.start()

        @pl.when(jnp.logical_not(at_end) & (step == 5))
        def _():
            small_back.wait_recv()
            small_sum[4] = small_sum[3] + small_in[3]
            small_mid.start()

        @pl.when(jnp.logical_not(at_end) & (step == 7))
        def _():
            small_mid.wait_recv()
            small_sum[5] = small_sum[4] + small_in[4]
            small_back.start()
            small_store.start()

    for copy in plane_hops:
        copy.wait_send()
    small_store.wait()
    for j, half, index in pieces:
        for target in range(2):
            col_copy(j, half, index, target).wait_send()
        x_copy(j, half, index).wait_send()

    @pl.when(at_end)
    def _():
        small_end.wait_send()

        @pl.loop(0, total)
        def _(step):
            each(step, finish_end)

    @pl.when(jnp.logical_not(at_end))
    def _():
        small_mid.wait_send()
        small_back.wait_send()

        @pl.loop(0, total)
        def _(step):
            each(step, finish_mid)


def reduce_all(planes, grads, small):
    parts, base = [], 0
    for grad, axis, rows in grads:
        height, width = grad.shape[-2:]
        height, width = (height // 2, width) if axis == 0 else (height, width // 2)
        parts.append(Part(axis, rows, width, height // rows, base, grad.ndim == 3))
        base += height // rows
    shapes = [(part.count, part.rows, part.cols) for part in parts]
    col_shapes = [(2, *shape) for part, shape in zip(parts, shapes) if part.col]
    pieces = sum(shape[1] * 2 for shape in col_shapes)
    own_shapes = [
        (2, 2, *shape) if part.col else (SLOTS, *shape[1:]) for part, shape in zip(parts, shapes)
    ]
    anywhere = pl.BlockSpec(memory_space=pl.ANY)
    dma = pltpu.SemaphoreType.DMA
    return pl.pallas_call(
        functools.partial(reduce_kernel, parts, planes),
        out_shape=[jax.ShapeDtypeStruct((n * r, c), BF) for n, r, c in shapes]
        + [jax.ShapeDtypeStruct(small.shape, F32)],
        in_specs=[anywhere] * (len(parts) + 1),
        out_specs=[anywhere] * (len(parts) + 1),
        scratch_shapes=[pltpu.VMEM(shape, BF) for _ in range(3) for shape in shapes]
        + [pltpu.VMEM(shape, BF) for shape in own_shapes]
        + [pltpu.VMEM((2, *shape), BF) for shape in col_shapes]
        + [pltpu.VMEM(shape, BF) for shape in col_shapes]
        + [dma((base,)) for _ in range(8)]
        + [dma((2, pieces)), dma((2, pieces)), dma((2, pieces)), dma((pieces,)), dma((pieces,))]
        + [dma((2,)), dma((5,)), dma((5,))]
        + [pltpu.VMEM((5, *small.shape), F32), pltpu.VMEM((6, *small.shape), F32)],
        compiler_params=pltpu.CompilerParams(
            collective_id=0, has_side_effects=True, vmem_limit_bytes=60 * 1024 * 1024
        ),
        name="reduce_grads",
    )(*[grad for grad, _, _ in grads], small)


TILE = 256
STEPS = 8


def spread_kernel(forward, *refs):
    if forward:
        mine_ref, *weights = refs[:7]
        all_ref, gate_ref, up_ref, act_ref, out_ref = refs[7:12]
        rest = refs[12:]
    else:
        mine_ref, *weights = refs[:7]
        gate_ref, up_ref = refs[7:9]
        all_ref, d_gate_up_ref, out_ref = refs[9:12]
        rest = refs[12:]
    block, w_gate, w_up, w_down, kept, to_mate, from_mate, far_part, to_far, from_mate_far, far_sum, from_far = rest[:12]
    (
        weight_sem, block_sem, out_sem, mate_send, mate_recv, x_send, x_recv, pass_send, pass_recv,
        sum_send, sum_recv, part_send, part_recv, back_send, back_recv,
    ) = rest[12:27]
    stage = rest[27:]
    tokens, depth = mine_ref.shape
    quarter = tokens // 4
    width = w_gate.shape[1]
    group, side = lax.axis_index("group"), lax.axis_index("side")
    mate, far = {"side": 1 - side}, {"group": 1 - group}

    def remote(source, target, send, recv, where):
        return pltpu.make_async_remote_copy(
            source, target, send, recv, device_id=where, device_id_type=pl.DeviceIdType.MESH
        )

    barrier = pltpu.get_barrier_semaphore()
    for where in (mate, far):
        pl.semaphore_signal(barrier, 1, device_id=where, device_id_type=pl.DeviceIdType.MESH)

    half = depth // 2
    loads = []
    for index, (source, target) in enumerate(
        [
            (weights[0], w_gate.at[pl.ds(0, half), :]),
            (weights[1], w_gate.at[pl.ds(half, half), :]),
            (weights[2], w_up.at[pl.ds(0, half), :]),
            (weights[3], w_up.at[pl.ds(half, half), :]),
            (weights[4], w_down.at[:, pl.ds(0, half)]),
            (weights[5], w_down.at[:, pl.ds(half, half)]),
        ]
    ):
        loads.append(pltpu.make_async_copy(source, target, weight_sem.at[index]))
    order = loads if forward else loads[4:] + loads[:4]
    mine_copies = [
        pltpu.make_async_copy(
            mine_ref.at[pl.ds(i * 2 * quarter, 2 * quarter), :], block.at[i], block_sem.at[i]
        )
        for i in range(2)
    ]
    for copy in mine_copies:
        copy.start()
    for copy in order:
        copy.start()
    pl.semaphore_wait(barrier, 2)

    def piece(index):
        return mine_ref.at[pl.ds(index * quarter, quarter), :]

    def mate_copy(index):
        return remote(
            piece(index),
            block.at[2 + index // 2, pl.ds(index % 2 * quarter, quarter), :],
            mate_send.at[index],
            mate_recv.at[index],
            mate,
        )

    def x_copy(index):
        return remote(
            piece(index), block.at[4 + index, pl.ds(0, quarter), :], x_send.at[index], x_recv.at[index], far
        )

    def pass_copy(index):
        return remote(
            block.at[4 + index, pl.ds(0, quarter), :],
            block.at[4 + index, pl.ds(quarter, quarter), :],
            pass_send.at[index],
            pass_recv.at[index],
            mate,
        )

    def sum_copy(index):
        return remote(to_mate.at[index], from_mate.at[index], sum_send.at[index], sum_recv.at[index], mate)

    def part_copy(index):
        return remote(to_far.at[index], from_mate_far.at[index], part_send.at[index], part_recv.at[index], mate)

    def back_copy(index):
        return remote(far_sum.at[index], from_far.at[index], back_send.at[index], back_recv.at[index], far)

    x_copy(0).start()
    for index in range(4):
        mate_copy(index).start()
    x_copy(1).start()
    for copy in mine_copies:
        copy.wait()

    def emit(step, where, part):
        @pl.when(step < 2)
        def _():
            kept[jnp.minimum(step, 1), :, where] = part

        @pl.when((step >= 2) & (step < 4))
        def _():
            to_mate[jnp.clip(step - 2, 0, 1), :, where] = part.astype(BF)

        @pl.when(step >= 4)
        def _():
            far_part[jnp.maximum(step - 4, 0), :, where] = part[:quarter]
            to_far[jnp.maximum(step - 4, 0), :, where] = part[quarter:].astype(BF)

    def all_copy(step):
        return pltpu.make_async_copy(block.at[step], all_ref.at[step], out_sem.at[0, step])

    if forward:
        stage_gate, stage_up, stage_act = stage

        def saves(step):
            slot = step % 2
            return [
                pltpu.make_async_copy(stage_gate.at[slot], gate_ref.at[step], out_sem.at[1, step]),
                pltpu.make_async_copy(stage_up.at[slot], up_ref.at[step], out_sem.at[2, step]),
                pltpu.make_async_copy(stage_act.at[slot], act_ref.at[step], out_sem.at[3, step]),
            ]

        def fetches(step):
            return []

        def first_loads():
            for copy in loads[:4]:
                copy.wait()

        def second_loads():
            for copy in loads[4:]:
                copy.wait()

        def first_half(step):
            slot = step % 2

            @pl.loop(0, width // TILE)
            def _(tile):
                where = pl.ds(pl.multiple_of(tile * TILE, TILE), TILE)
                gate = dot(block[step], w_gate[:, where])
                up = dot(block[step], w_up[:, where])
                stage_gate[slot, :, where] = gate.astype(BF)
                stage_up[slot, :, where] = up.astype(BF)
                stage_act[slot, :, where] = (gate * up / (1.0 + jnp.exp(-gate))).astype(BF)

        def second_half(step):
            slot = step % 2

            @pl.loop(0, depth // TILE)
            def _(tile):
                where = pl.ds(pl.multiple_of(tile * TILE, TILE), TILE)
                emit(step, where, dot(stage_act[slot], w_down[:, where]))

    else:
        stage_gate, stage_up, stage_d, fetch_sem = stage

        def saves(step):
            return [
                pltpu.make_async_copy(stage_d.at[step % 2], d_gate_up_ref.at[step], out_sem.at[1, step])
            ]

        def fetches(step):
            slot = step % 2
            return [
                pltpu.make_async_copy(gate_ref.at[step], stage_gate.at[slot], fetch_sem.at[0, step]),
                pltpu.make_async_copy(up_ref.at[step], stage_up.at[slot], fetch_sem.at[1, step]),
            ]

        def first_loads():
            for copy in loads[4:]:
                copy.wait()

        def second_loads():
            for copy in loads[:4]:
                copy.wait()

        def first_half(step):
            slot = step % 2

            @pl.loop(0, width // TILE)
            def _(tile):
                first = pl.multiple_of(tile * TILE, TILE)
                where = pl.ds(first, TILE)
                d_act = dot(block[step], w_down[where, :], ((1,), (1,)))
                gate = stage_gate[slot, :, where].astype(F32)
                up = stage_up[slot, :, where].astype(F32)
                sig = 1.0 / (1.0 + jnp.exp(-gate))
                d_gate = d_act * up * sig * (1.0 + gate * (1.0 - sig))
                stage_d[slot, :, where] = d_gate.astype(BF)
                stage_d[slot, :, pl.ds(pl.multiple_of(width + first, TILE), TILE)] = (d_act * gate * sig).astype(BF)

        def second_half(step):
            slot = step % 2

            @pl.loop(0, depth // TILE)
            def _(tile):
                where = pl.ds(pl.multiple_of(tile * TILE, TILE), TILE)
                part = dot(stage_d[slot, :, :width], w_gate[where, :], ((1,), (1,)))
                part += dot(stage_d[slot, :, width:], w_up[where, :], ((1,), (1,)))
                emit(step, where, part)

    def finish_far(index):
        part_copy(index).wait_recv()
        total = far_part[index] + from_mate_far[index].astype(F32)
        far_sum[index] = total.astype(BF)
        back_copy(index).start()

    for copy in fetches(0):
        copy.start()

    @pl.loop(0, STEPS)
    def _(step):
        @pl.when((step == 2) | (step == 3))
        def _():
            index = jnp.clip(2 * (step - 2), 0, 2)
            mate_copy(index).wait_recv()
            mate_copy(index + 1).wait_recv()

        @pl.when(step >= 4)
        def _():
            index = jnp.maximum(step - 4, 0)
            x_copy(index).wait_recv()
            pass_copy(index).start()
            pass_copy(index).wait_recv()

        all_copy(step).start()
        for copy in fetches(step):
            copy.wait()

        if not forward:
            @pl.when(step < STEPS - 1)
            def _():
                for copy in fetches(jnp.minimum(step + 1, STEPS - 1)):
                    copy.start()

        @pl.when(step == 0)
        def _():
            first_loads()

        @pl.when(step >= 2)
        def _():
            for copy in saves(jnp.maximum(step - 2, 0)):
                copy.wait()

        first_half(step)

        @pl.when(step == 0)
        def _():
            second_loads()

        second_half(step)
        for copy in saves(step):
            copy.start()

        @pl.when((step == 1) | (step == 3))
        def _():
            x_copy(2 + step // 2).start()

        @pl.when((step >= 2) & (step < 4))
        def _():
            sum_copy(jnp.clip(step - 2, 0, 1)).start()

        @pl.when(step >= 4)
        def _():
            part_copy(jnp.maximum(step - 4, 0)).start()

        @pl.when(step >= 5)
        def _():
            finish_far(jnp.maximum(step - 5, 0))

    finish_far(3)
    for index in range(2):
        sum_copy(index).wait_recv()
        kept[index] = kept[index] + from_mate[index].astype(F32)
    results = []
    for index in range(4):
        back_copy(index).wait_recv()
        rows = pl.ds(index % 2 * quarter, quarter)
        kept[index // 2, rows, :] = kept[index // 2, rows, :] + from_far[index].astype(F32)
        if index % 2:
            copy = pltpu.make_async_copy(kept.at[index // 2], out_ref.at[index // 2], block_sem.at[index // 2])
            copy.start()
            results.append(copy)
    for copy in results:
        copy.wait()

    @pl.loop(0, STEPS)
    def _(step):
        all_copy(step).wait()

        @pl.when(step >= STEPS - 2)
        def _():
            for copy in saves(step):
                copy.wait()

        @pl.when(step < 4)
        def _():
            index = jnp.minimum(step, 3)
            mate_copy(index).wait_send()
            x_copy(index).wait_send()
            pass_copy(index).wait_send()
            part_copy(index).wait_send()
            back_copy(index).wait_send()

        @pl.when(step < 2)
        def _():
            sum_copy(jnp.minimum(step, 1)).wait_send()


def spread(forward, mine, weights, *kept):
    tokens, depth = mine.shape
    quarter, double = tokens // 4, tokens // 2
    width = weights[0].shape[1]
    anywhere = pl.BlockSpec(memory_space=pl.ANY)
    wide = jax.ShapeDtypeStruct((STEPS, double, width), BF)
    whole = jax.ShapeDtypeStruct((STEPS, double, depth), BF)
    out = jax.ShapeDtypeStruct((2, double, depth), F32)
    if forward:
        outs = [whole, wide, wide, wide, out]
        stage = [pltpu.VMEM((2, double, width), BF) for _ in range(3)]
    else:
        outs = [whole, jax.ShapeDtypeStruct((STEPS, double, 2 * width), BF), out]
        stage = [
            pltpu.VMEM((2, double, width), BF),
            pltpu.VMEM((2, double, width), BF),
            pltpu.VMEM((2, double, 2 * width), BF),
            pltpu.SemaphoreType.DMA((2, STEPS)),
        ]
    result = pl.pallas_call(
        functools.partial(spread_kernel, forward),
        out_shape=outs,
        in_specs=[anywhere] * (7 + len(kept)),
        out_specs=[anywhere] * len(outs),
        scratch_shapes=[
            pltpu.VMEM((STEPS, double, depth), BF),
            pltpu.VMEM((depth, width), BF),
            pltpu.VMEM((depth, width), BF),
            pltpu.VMEM((width, depth), BF),
            pltpu.VMEM((2, double, depth), F32),
            pltpu.VMEM((2, double, depth), BF),
            pltpu.VMEM((2, double, depth), BF),
            pltpu.VMEM((4, quarter, depth), F32),
            pltpu.VMEM((4, quarter, depth), BF),
            pltpu.VMEM((4, quarter, depth), BF),
            pltpu.VMEM((4, quarter, depth), BF),
            pltpu.VMEM((4, quarter, depth), BF),
            pltpu.SemaphoreType.DMA((6,)),
            pltpu.SemaphoreType.DMA((2,)),
            pltpu.SemaphoreType.DMA((4, STEPS)),
        ]
        + [pltpu.SemaphoreType.DMA((4,)) for _ in range(6)]
        + [pltpu.SemaphoreType.DMA((2,)) for _ in range(2)]
        + [pltpu.SemaphoreType.DMA((4,)) for _ in range(4)]
        + stage,
        compiler_params=pltpu.CompilerParams(
            collective_id=1 if forward else 2,
            has_side_effects=True,
            vmem_limit_bytes=60 * 1024 * 1024,
        ),
        name="feed_forward" if forward else "feed_forward_back",
    )(mine, *weights, *kept)
    return result


def body(
    tokens,
    norm1_gain,
    w_query,
    w_key,
    w_value,
    query_gain,
    key_gain,
    w_out,
    norm2_gain,
    w_gate,
    w_up,
    w_down,
    teacher,
    positions,
    token_count,
):
    rows = lax.axis_size("row")
    cores = lax.axis_size("side")
    cols = lax.axis_size("group") * cores
    row_index = lax.axis_index("row")
    group_index = lax.axis_index("group")
    members = rows * cores
    member = row_index * cores + lax.axis_index("side")
    shard, width = tokens.shape
    pieces = 2 * members
    span = shard // pieces
    mine = shard // members * cores
    q_width, k_width = w_query.shape[1], w_key.shape[1]
    ff = w_gate.shape[1]

    def from_row(block, ahead):
        pairs = [((r + ahead) % rows, r) for r in range(rows)]
        return lax.ppermute(block, "row", pairs)

    def gather_rows(block, axis):
        parts = [block] + [from_row(block, ahead) for ahead in range(1, rows)]
        return jnp.concatenate(parts, axis=axis)

    def scatter_rows(block, axis):
        size = block.shape[axis] // rows
        total = lax.slice_in_dim(block, 0, size, axis=axis).astype(F32)
        for ahead in range(1, rows):
            part = lax.slice_in_dim(block, ahead * size, (ahead + 1) * size, axis=axis)
            total = total + from_row(part, rows - ahead).astype(F32)
        return total.astype(BF)

    def sum_planes(block, cuts):
        planes = lax.axis_size("dp")
        plane = lax.axis_index("dp")
        half = planes // 2
        edge = jnp.minimum(plane, planes - 1 - plane)
        done = []
        for part in jnp.split(block, cuts, axis=0):
            for step in range(half - 1):
                pairs = [(step, step + 1), (planes - 1 - step, planes - 2 - step)]
                come = lax.ppermute(part, "dp", pairs)
                part = (part.astype(F32) + come.astype(F32)).astype(BF)
            come = lax.ppermute(part, "dp", [(half - 1, half), (half, half - 1)])
            part = (part.astype(F32) + come.astype(F32)).astype(BF)
            for step in reversed(range(half - 1)):
                pairs = [(step + 1, step), (planes - 2 - step, planes - 1 - step)]
                come = lax.ppermute(part, "dp", pairs)
                part = jnp.where(edge == step, come, part)
            done.append(part)
        return jnp.concatenate(done, axis=0)

    def to_members(block):
        parts = block.reshape(pieces, span, width)
        parts = jnp.stack([parts[:members], parts[members:][::-1]], axis=1)
        moved = lax.all_to_all(parts, ("row", "side"), 0, 0, tiled=True)
        moved = jnp.roll(moved.reshape(rows, cores, 2 * span, width), -row_index, 0)
        moved = moved.transpose(1, 2, 0, 3)
        return moved.reshape(mine, rows * width)

    def from_members(block):
        parts = block.reshape(cores, 2, span, rows, width).transpose(3, 0, 1, 2, 4)
        parts = jnp.roll(parts, row_index, 0).reshape(members, 2, span, width)
        moved = lax.all_to_all(parts, ("row", "side"), 0, 0, tiled=True)
        moved = jnp.concatenate([moved[:, 0], moved[:, 1][::-1]], axis=0)
        return moved.reshape(shard, width)

    def pick(values):
        part = lax.dynamic_slice_in_dim(values.reshape(-1, cores, pieces, span), group_index, 1, 0)[0]
        low = lax.dynamic_slice_in_dim(part, member, 1, 1)
        high = lax.dynamic_slice_in_dim(part, pieces - 1 - member, 1, 1)
        return jnp.concatenate([low, high], axis=1).reshape(-1)

    first_tokens = (
        jnp.array([0, 0, shard, shard], jnp.int32)
        + jnp.stack([member, pieces - 1 - member] * 2).astype(jnp.int32) * span
    )

    states = to_members(tokens).astype(F32)
    gain_one = gather_rows(norm1_gain, 0)
    gain_two = gather_rows(norm2_gain, 0)
    w_project = jnp.concatenate([w_query, w_key, w_value], axis=1)
    w_project = gather_rows(w_project, 0)
    w_project = lax.all_gather(w_project, ("group", "side"), axis=0)
    w_out_all = gather_rows(w_out, 1)
    w_out_all = lax.all_gather(w_out_all, ("group", "side"), axis=0, tiled=True)
    def halves(block, axis):
        if rows == 2:
            return [block, from_row(block, 1)]
        return jnp.split(gather_rows(block, axis), 2, axis=axis)

    ffn_weights = halves(w_gate, 0) + halves(w_up, 0) + halves(w_down, 1)
    target = to_members(teacher)

    half = HD // 2
    freq = jnp.exp(jnp.arange(half, dtype=F32) * (-2.0 * math.log(10000.0) / HD))
    angle = freq[:, None] * pick(positions).astype(F32)[None, :]
    cosine, sine = jnp.cos(angle), jnp.sin(angle)
    inverse_one = rms(states)
    normed_one = (states * inverse_one * gain_one).astype(BF)
    projected = dot(w_project, normed_one, ((1,), (1,)))
    query_raw = projected[:, :q_width].reshape(QH, HD, mine)
    key_sent = projected[:, q_width : q_width + k_width].reshape(KVH, HD, mine).astype(BF)
    value_sent = projected[:, q_width + k_width :].reshape(KVH, HD, mine).astype(BF)
    query_rot, query_back = jax.vjp(
        lambda raw, gain: prepare(raw, gain, cosine, sine), query_raw, query_gain
    )
    key_rot, key_back = jax.vjp(
        lambda raw, gain: prepare(raw, gain, cosine, sine), key_sent.astype(F32), key_gain
    )
    scale = 1.0 / math.sqrt(HD)
    query_use = (query_rot.astype(BF) * BF(scale)).reshape(KVH, REP, HD, mine)
    pair = jnp.stack([key_rot.astype(BF), value_sent])
    pair = lax.all_gather(pair, ("row", "side"), axis=0)

    def natural(stacked):
        lead = stacked.shape[1:-1]
        parts = stacked.reshape((members,) + lead + (cores, 2, span))
        low, high = parts[..., 0, :], parts[..., 1, :]
        both = jnp.concatenate([low, high[::-1]], axis=0)
        return jnp.moveaxis(both, 0, -2).reshape(lead + (GROUP,))

    def dealt(full):
        lead, entry = full.shape[:-2], full.shape[-1]
        parts = full.reshape(lead + (cores, pieces, span, entry))
        low = parts[..., :members, :, :]
        high = parts[..., members:, :, :][..., ::-1, :, :]
        both = jnp.stack([low, high], axis=-3)
        both = jnp.moveaxis(both, -4, 0)
        return both.reshape((members,) + lead + (mine, entry))

    pair = natural(pair)
    key_t, value_t = pair[0], pair[1]
    key_n, value_n = key_t.transpose(0, 2, 1), value_t.transpose(0, 2, 1)
    value_one = jnp.concatenate([value_t, jnp.ones((KVH, 16, GROUP), BF)], axis=1)
    mixed_f, logs = attend(first_tokens, query_use, key_n, value_one)
    mixed = mixed_f.reshape(QH * HD, mine).astype(BF)
    hidden = states + dot(mixed, w_out_all, ((0,), (0,)))

    inverse_two = rms(hidden)
    normed_two = (hidden * inverse_two * gain_two).astype(BF)
    normed_all, gate, up, activated, ffn_out = spread(True, normed_two, ffn_weights)
    ffn_out = ffn_out.reshape(mine, D)
    result = hidden + ffn_out
    block_out = from_members(result.astype(BF))

    total_tokens = shard * cols * lax.axis_size("dp")
    loss_scale = total_tokens / token_count[0].astype(F32)
    d_result = loss_scale * (result - target.astype(F32))
    d_low, d_gate_up, d_normed = spread(False, d_result.astype(BF), ffn_weights, gate, up)
    d_normed = d_normed.reshape(mine, D)
    d_low, normed_all = d_low.reshape(-1, D), normed_all.reshape(-1, D)
    grad_down = dot(activated.reshape(-1, ff), d_low, ((0,), (0,))).astype(BF)
    grad_gate_up = dot(normed_all, d_gate_up.reshape(-1, 2 * ff), ((0,), (0,))).astype(BF)

    norm_two_part = jnp.sum(d_normed * hidden * inverse_two, axis=0)
    d_hidden = d_result + norm_back(hidden, inverse_two, gain_two, d_normed)
    d_hidden_low = d_hidden.astype(BF)
    grad_out = dot(mixed, d_hidden_low, ((1,), (0,))).astype(BF)
    d_mixed = dot(w_out_all, d_hidden_low, ((1,), (1,))).astype(BF)
    d_mixed = d_mixed.reshape(KVH, REP, HD, mine)
    delta = jnp.sum(d_mixed.astype(F32) * mixed_f, axis=2)
    d_query, d_key_n, d_value_n = attend_back(
        first_tokens, query_use, d_mixed, logs, delta, key_n, value_n, key_t
    )
    d_pair = dealt(jnp.stack([d_key_n, d_value_n])).astype(BF)
    d_pair = lax.psum_scatter(d_pair, ("row", "side"), scatter_dimension=0, tiled=True)[0]
    d_pair = d_pair.astype(F32).transpose(0, 1, 3, 2)
    d_query_raw, query_gain_part = query_back(d_query.reshape(QH, HD, mine) * scale)
    d_key_raw, key_gain_part = key_back(d_pair[0])
    d_projected = jnp.concatenate(
        [
            d_query_raw.reshape(cols, q_width, mine),
            d_key_raw.reshape(cols, k_width, mine),
            d_pair[1].reshape(cols, k_width, mine),
        ],
        axis=1,
    ).astype(BF)
    d_normed_one = dot(d_projected, w_project, ((0, 1), (0, 2)))
    grad_input = d_hidden + norm_back(states, inverse_one, gain_one, d_normed_one)
    norm_one_part = jnp.sum(d_normed_one * states * inverse_one, axis=0)
    grad_input = from_members(grad_input)

    grad_project = lax.dot_general(
        d_projected, normed_one, (((2,), (0,)), ((), ())), preferred_element_type=F32
    )
    grad_project = grad_project.astype(BF).transpose(0, 2, 1)
    grad_out = grad_out.reshape(cols, q_width, D)
    norm_one_part = jnp.roll(norm_one_part.reshape(rows, width), row_index, 0).reshape(D)
    norm_two_part = jnp.roll(norm_two_part.reshape(rows, width), row_index, 0).reshape(D)
    small = jnp.concatenate([norm_one_part, norm_two_part, query_gain_part, key_gain_part])
    if rows == 2 and cols == 4 and lax.axis_size("dp") == 4:
        padded = jnp.pad(small, (0, SMALL * 128 - small.shape[0])).reshape(SMALL, 128)
        grad_down, grad_gate_up, grad_out, grad_project, small = reduce_all(
            4,
            [(grad_down, 1, 128), (grad_gate_up, 0, 64), (grad_out, 1, 160), (grad_project, 0, 512)],
            padded,
        )
        small = small.reshape(-1)[: 2 * D + 2 * HD]
    else:
        small = lax.psum(small, ("dp", "row", "group", "side"))
        col_axes = ("group", "side")
        grad_project = lax.psum_scatter(grad_project, col_axes, scatter_dimension=0, tiled=True)
        grad_out = lax.psum_scatter(grad_out, col_axes, scatter_dimension=0, tiled=True)
        grad_down = sum_planes(scatter_rows(grad_down, 1), 2)
        grad_gate_up = sum_planes(scatter_rows(grad_gate_up, 0), 4)
        grad_out = sum_planes(scatter_rows(grad_out[0], 1), 1)
        grad_project = sum_planes(scatter_rows(grad_project[0], 0), 2)
    grad_norm1 = lax.dynamic_slice_in_dim(small, row_index * width, width, 0)
    grad_norm2 = lax.dynamic_slice_in_dim(small, D + row_index * width, width, 0)
    grad_project = grad_project.astype(F32)
    return (
        block_out,
        grad_input,
        grad_norm1,
        grad_project[:, :q_width],
        grad_project[:, q_width : q_width + k_width],
        grad_project[:, q_width + k_width :],
        small[2 * D : 2 * D + HD],
        small[2 * D + HD :],
        grad_out.astype(F32),
        grad_norm2,
        grad_gate_up[:, :ff].astype(F32),
        grad_gate_up[:, ff:].astype(F32),
        grad_down.astype(F32),
    )


def solution(mesh):
    dp, row, col = mesh.shape["dp"], mesh.shape["row"], mesh.shape["col"]

    def call(*args):
        side = GROUP * dp * col // args[0].shape[0]
        fine = Mesh(
            mesh.devices.reshape(dp, row, col // side, side), ("dp", "row", "group", "side")
        )
        col_axes = ("group", "side")
        token_spec = P(("dp", "group", "side"), "row")
        wide = P("row", col_axes)
        tall = P(col_axes, "row")
        return jax.shard_map(
            body,
            mesh=fine,
            in_specs=(
                token_spec,
                P("row"),
                wide,
                wide,
                wide,
                P(),
                P(),
                tall,
                P("row"),
                wide,
                wide,
                tall,
                token_spec,
                P("dp"),
                P(),
            ),
            out_specs=(
                token_spec,
                token_spec,
                P("row"),
                wide,
                wide,
                wide,
                P(),
                P(),
                tall,
                P("row"),
                wide,
                wide,
                tall,
            ),
            check_vma=False,
        )(*args)

    return call
```

```python
import functools
import math

import jax
import jax.numpy as jnp
from jax import lax
from jax.experimental import pallas as pl
from jax.experimental.pallas import tpu as pltpu
from jax.sharding import Mesh
from jax.sharding import PartitionSpec as P

D = 2048
QH = 20
KVH = 5
HD = 64
PROMPT = 1024
CONT = 128
NCONT = 8
GROUP = PROMPT + NCONT * CONT
REP = QH // KVH
KEYS = 256

EPSILON = 1e-06
BF = jnp.bfloat16
F32 = jnp.float32


def dot(left, right, dims=((1,), (0,))):
    return lax.dot_general(left, right, (dims, ((), ())), preferred_element_type=F32)


def rms(values):
    return lax.rsqrt(jnp.mean(values * values, axis=1, keepdims=True) + EPSILON)


def norm_back(states, inverse, gain, d_normed):
    mean = jnp.mean(states * gain * d_normed, axis=1, keepdims=True)
    return inverse * gain * d_normed - states * inverse**3 * mean


def prepare(raw, gain, cosine, sine):
    values = raw * lax.rsqrt(jnp.mean(raw * raw, axis=1, keepdims=True) + EPSILON)
    values = values * gain[None, :, None]
    half = HD // 2
    first, second = values[:, :half], values[:, half:]
    return jnp.concatenate(
        [first * cosine - second * sine, second * cosine + first * sine], axis=1
    )


def allowed(first_query, first_key, span, rows):
    key = first_key + lax.broadcasted_iota(jnp.int32, (KEYS, rows), 0)
    query = first_query + lax.broadcasted_iota(jnp.int32, (KEYS, rows), 1) % span
    return (key <= query) & ((key < PROMPT) | (key // CONT == query // CONT))


def side_by_side(ref, index, span):
    return jnp.concatenate(
        [ref[0, head, :, index * span : (index + 1) * span] for head in range(REP)], axis=1
    )


def tiles_of(first_query):
    last = first_query // KEYS
    return jnp.minimum(last, PROMPT // KEYS), last


def attend_kernel(chunks, span, first_ref, query_ref, key_ref, value_ref, out_ref, log_ref):
    rows = REP * span
    for index in range(chunks):
        query = side_by_side(query_ref, index, span)
        first_query = first_ref[index]
        full, last = tiles_of(first_query)

        def tile(where, accum, masked):
            first_key = pl.multiple_of(where * KEYS, KEYS)
            scores = dot(key_ref[0, pl.ds(first_key, KEYS), :], query)
            expo = jnp.exp(scores)
            if masked:
                expo = jnp.where(allowed(first_query, first_key, span, rows), expo, 0.0)
            return accum + dot(value_ref[0, :, pl.ds(first_key, KEYS)], expo.astype(BF))

        accum = tile(last, jnp.zeros((value_ref.shape[1], rows), F32), True)
        accum = lax.fori_loop(0, full, lambda where, total: tile(where, total, False), accum)
        total = accum[HD : HD + 1]
        mixed = accum[:HD] / total
        logs = jnp.log(total)
        for head in range(REP):
            cut = slice(head * span, (head + 1) * span)
            out_ref[0, head, :, index * span : (index + 1) * span] = mixed[:, cut]
            log_ref[0, head : head + 1, index * span : (index + 1) * span] = logs[:, cut]


def attend_back_kernel(
    chunks,
    span,
    first_ref,
    query_ref,
    d_out_ref,
    log_ref,
    delta_ref,
    key_t_ref,
    value_t_ref,
    d_query_ref,
    d_key_ref,
    d_value_ref,
    key_ref,
    value_ref,
):
    rows = REP * span
    key_ref[...] = key_t_ref[0].T
    value_ref[...] = value_t_ref[0].T
    d_key_ref[...] = jnp.zeros_like(d_key_ref)
    d_value_ref[...] = jnp.zeros_like(d_value_ref)
    for index in range(chunks):
        query = side_by_side(query_ref, index, span)
        d_out = side_by_side(d_out_ref, index, span)
        query_t = query.T
        d_out_t = d_out.T
        cut = slice(index * span, (index + 1) * span)
        logs = jnp.concatenate([log_ref[0, h : h + 1, cut] for h in range(REP)], axis=1)
        delta = jnp.concatenate([delta_ref[0, h : h + 1, cut] for h in range(REP)], axis=1)
        first_query = first_ref[index]
        full, last = tiles_of(first_query)

        def tile(where, accum, masked):
            first_key = pl.multiple_of(where * KEYS, KEYS)
            here = pl.ds(first_key, KEYS)
            probs = jnp.exp(dot(key_ref[here, :], query) - logs)
            if masked:
                probs = jnp.where(allowed(first_query, first_key, span, rows), probs, 0.0)
            d_probs = dot(value_ref[here, :], d_out)
            d_scores = (probs * (d_probs - delta)).astype(BF)
            d_value_ref[0, here, :] += dot(probs.astype(BF), d_out_t)
            d_key_ref[0, here, :] += dot(d_scores, query_t)
            return accum + dot(key_t_ref[0, :, here], d_scores)

        accum = tile(last, jnp.zeros((HD, rows), F32), True)
        accum = lax.fori_loop(0, full, lambda where, total: tile(where, total, False), accum)
        for head in range(REP):
            part = accum[:, head * span : (head + 1) * span]
            d_query_ref[0, head, :, cut] = part


def per_head(shape):
    return pl.BlockSpec((1,) + shape, lambda head, first: (head,) + (0,) * len(shape))


def attend(first, query, key, value_t):
    tokens = query.shape[-1]
    chunks = first.shape[0]
    return pl.pallas_call(
        functools.partial(attend_kernel, chunks, tokens // chunks),
        out_shape=(
            jax.ShapeDtypeStruct((KVH, REP, HD, tokens), F32),
            jax.ShapeDtypeStruct((KVH, REP, tokens), F32),
        ),
        grid_spec=pltpu.PrefetchScalarGridSpec(
            num_scalar_prefetch=1,
            grid=(KVH,),
            in_specs=[
                per_head((REP, HD, tokens)),
                per_head((GROUP, HD)),
                per_head((value_t.shape[1], GROUP)),
            ],
            out_specs=[per_head((REP, HD, tokens)), per_head((REP, tokens))],
        ),
        compiler_params=pltpu.CompilerParams(vmem_limit_bytes=32 * 1024 * 1024),
        name="attend",
    )(first, query, key, value_t)


def attend_back(first, query, d_out, logs, delta, key_t, value_t):
    tokens = query.shape[-1]
    chunks = first.shape[0]
    return pl.pallas_call(
        functools.partial(attend_back_kernel, chunks, tokens // chunks),
        out_shape=(
            jax.ShapeDtypeStruct((KVH, REP, HD, tokens), F32),
            jax.ShapeDtypeStruct((KVH, GROUP, HD), F32),
            jax.ShapeDtypeStruct((KVH, GROUP, HD), F32),
        ),
        grid_spec=pltpu.PrefetchScalarGridSpec(
            num_scalar_prefetch=1,
            grid=(KVH,),
            in_specs=[
                per_head((REP, HD, tokens)),
                per_head((REP, HD, tokens)),
                per_head((REP, tokens)),
                per_head((REP, tokens)),
                per_head((HD, GROUP)),
                per_head((HD, GROUP)),
            ],
            out_specs=[
                per_head((REP, HD, tokens)),
                per_head((GROUP, HD)),
                per_head((GROUP, HD)),
            ],
            scratch_shapes=[pltpu.VMEM((GROUP, HD), BF), pltpu.VMEM((GROUP, HD), BF)],
        ),
        compiler_params=pltpu.CompilerParams(vmem_limit_bytes=32 * 1024 * 1024),
        name="attend_back",
    )(first, query, d_out, logs, delta, key_t, value_t)


AHEAD = 4
SLOTS = AHEAD + 2
LAG = 4
SMALL = 40


class Part:
    def __init__(self, axis, rows, cols, count, base, col):
        self.axis, self.rows, self.cols = axis, rows, cols
        self.count, self.base, self.col = count, base, col

    def cut(self, ref, index, half, lead=()):
        first = pl.ds(index * self.rows, self.rows)
        if self.axis == 0:
            first = pl.ds((half * self.count + index) * self.rows, self.rows)
            return ref.at[(*lead, first, slice(None))]
        return ref.at[(*lead, first, pl.ds(half * self.cols, self.cols))]


def reduce_kernel(parts, planes, *refs):
    count = len(parts)
    refs = list(refs)

    def take(number):
        taken = refs[:number]
        del refs[:number]
        return taken

    grads = take(count)
    (small_ref,) = take(1)
    outs = take(count)
    (small_out,) = take(1)
    near, far, wide, own = take(count), take(count), take(count), take(count)
    col_parts = [j for j in range(count) if parts[j].col]
    mate_in = dict(zip(col_parts, take(len(col_parts))))
    far_in = dict(zip(col_parts, take(len(col_parts))))
    own_sem, out_sem, row_send, row_recv, in_send, far_recv, mid_send, wide_recv = take(8)
    col_own, col_send, col_recv, x_send, x_recv, small_local, small_send, small_recv = take(8)
    small_in, small_sum = take(2)
    plane, row = lax.axis_index("dp"), lax.axis_index("row")
    group, side = lax.axis_index("group"), lax.axis_index("side")
    other_row, mate, far_dev = {"row": 1 - row}, {"side": 1 - side}, {"group": 1 - group}
    at_end = (plane == 0) | (plane == planes - 1)
    low = plane < planes // 2
    end_next = {"dp": jnp.where(low, 1, planes - 2)}
    mid_outer = {"dp": jnp.where(low, 0, planes - 1)}
    mid_other = {"dp": jnp.where(low, planes // 2, planes // 2 - 1)}

    def remote(source, target, send, recv, where):
        return pltpu.make_async_remote_copy(
            source, target, send, recv, device_id=where, device_id_type=pl.DeviceIdType.MESH
        )

    barrier = pltpu.get_barrier_semaphore()

    def greet(where):
        pl.semaphore_signal(barrier, 1, device_id=where, device_id_type=pl.DeviceIdType.MESH)

    for where in (other_row, mate, far_dev):
        greet(where)

    @pl.when(at_end)
    def _():
        greet(end_next)
        pl.semaphore_wait(barrier, 4)

    @pl.when(jnp.logical_not(at_end))
    def _():
        greet(mid_outer)
        greet(mid_other)
        pl.semaphore_wait(barrier, 5)

    def col_slot(j, half, index):
        before = sum(2 * parts[i].count for i in col_parts if i < j)
        return before + half * parts[j].count + index

    def col_own_copy(j, half, index, target):
        return pltpu.make_async_copy(
            parts[j].cut(grads[j], index, half, (2 * target + side,)),
            own[j].at[target, half, index],
            col_own.at[target, col_slot(j, half, index)],
        )

    def col_copy(j, half, index, target):
        slot = col_slot(j, half, index)
        return remote(
            parts[j].cut(grads[j], index, half, (2 * target + 1 - side,)),
            mate_in[j].at[target, half, index],
            col_send.at[target, slot],
            col_recv.at[target, slot],
            mate,
        )

    def x_copy(j, half, index):
        slot = col_slot(j, half, index)
        return remote(
            mate_in[j].at[1 - group, half, index],
            far_in[j].at[half, index],
            x_send.at[slot],
            x_recv.at[slot],
            far_dev,
        )

    def take_col(j, half, index):
        for target in range(2):
            col_own_copy(j, half, index, target).wait()
            col_copy(j, half, index, target).wait_recv()
            total = own[j][target, half, index].astype(F32)
            total += mate_in[j][target, half, index].astype(F32)
            mate_in[j][target, half, index] = total.astype(BF)
        x_copy(j, half, index).start()

    def take_x(j, half, index):
        x_copy(j, half, index).wait_recv()
        total = far_in[j][half, index].astype(F32) + mate_in[j][group, half, index].astype(F32)
        far_in[j][half, index] = total.astype(BF)

    def row_copy(j, index):
        slot = parts[j].base + index
        source = far_in[j].at[1, index] if parts[j].col else parts[j].cut(grads[j], index, 1)
        return remote(source, near[j].at[index], row_send.at[slot], row_recv.at[slot], other_row)

    def in_copy(j, index):
        slot = parts[j].base + index
        return remote(near[j].at[index], far[j].at[index], in_send.at[slot], far_recv.at[slot], end_next)

    def mid_copy(j, index):
        slot = parts[j].base + index
        return remote(far[j].at[index], wide[j].at[index], mid_send.at[slot], wide_recv.at[slot], mid_other)

    def back_copy(j, index):
        slot = parts[j].base + index
        return remote(wide[j].at[index], far[j].at[index], in_send.at[slot], far_recv.at[slot], mid_outer)

    def out_copy(j, index, source):
        slot = parts[j].base + index
        return pltpu.make_async_copy(source[j].at[index], parts[j].cut(outs[j], index, 0), out_sem.at[slot])

    def own_copy(j, index):
        slot = parts[j].base + index
        return pltpu.make_async_copy(
            parts[j].cut(grads[j], index, 0), own[j].at[index % SLOTS], own_sem.at[slot]
        )

    def each(step, action):
        for j, part in enumerate(parts):
            index = step - part.base

            @pl.when((index >= 0) & (index < part.count))
            def _(j=j, index=index):
                action(j, index)

    def send_row(j, index):
        if not parts[j].col:
            own_copy(j, index).start()
        row_copy(j, index).start()

    def take_row(j, index):
        row_copy(j, index).wait_recv()
        if parts[j].col:
            mine = far_in[j][0, index]
        else:
            own_copy(j, index).wait()
            mine = own[j][index % SLOTS]
        near[j][index] = (near[j][index].astype(F32) + mine.astype(F32)).astype(BF)

        @pl.when(at_end)
        def _():
            in_copy(j, index).start()

    def take_far(j, index):
        back_copy(j, index).wait_recv()
        far[j][index] = (far[j][index].astype(F32) + near[j][index].astype(F32)).astype(BF)
        mid_copy(j, index).start()

    def take_wide(j, index):
        mid_copy(j, index).wait_recv()
        wide[j][index] = (wide[j][index].astype(F32) + far[j][index].astype(F32)).astype(BF)
        back_copy(j, index).start()
        out_copy(j, index, wide).start()

    def take_back(j, index):
        in_copy(j, index).wait_recv()
        out_copy(j, index, far).start()

    def finish_end(j, index):
        row_copy(j, index).wait_send()
        in_copy(j, index).wait_send()
        out_copy(j, index, far).wait()

    def finish_mid(j, index):
        row_copy(j, index).wait_send()
        mid_copy(j, index).wait_send()
        back_copy(j, index).wait_send()
        out_copy(j, index, wide).wait()

    def small_copy(stage, source, where):
        return remote(small_sum.at[source], small_in.at[stage], small_send.at[stage], small_recv.at[stage], where)

    plane_hops = [small_copy(0, 0, mate), small_copy(1, 1, far_dev), small_copy(2, 2, other_row)]
    small_end = small_copy(3, 3, end_next)
    small_mid = small_copy(4, 4, mid_other)
    small_back = small_copy(3, 5, mid_outer)
    small_load = pltpu.make_async_copy(small_ref, small_sum.at[0], small_local.at[0])
    small_store = pltpu.make_async_copy(small_sum.at[5], small_out, small_local.at[1])

    total = sum(part.count for part in parts)
    small_load.start()
    for j in col_parts:
        for half in (1, 0):
            for index in range(parts[j].count):
                for target in range(2):
                    col_own_copy(j, half, index, target).start()
                    col_copy(j, half, index, target).start()

    @pl.loop(0, AHEAD)
    def _(step):
        each(step, send_row)

    pieces = [(j, half, index) for j in col_parts for half in (1, 0) for index in range(parts[j].count)]

    @pl.loop(0, total + LAG)
    def _(step):
        each(step + AHEAD, send_row)
        each(step, take_row)

        @pl.when(at_end)
        def _():
            each(step - LAG, take_back)

        @pl.when(jnp.logical_not(at_end))
        def _():
            each(step - 1, take_far)
            each(step - 2, take_wide)

        for place, piece in enumerate(pieces):
            @pl.when(step == place + 1)
            def _(piece=piece):
                take_col(*piece)

            @pl.when(step == place + 5)
            def _(piece=piece):
                take_x(*piece)

        @pl.when(step == 0)
        def _():
            small_load.wait()
            plane_hops[0].start()

        for hop in range(3):
            @pl.when(step == hop + 1)
            def _(hop=hop):
                plane_hops[hop].wait_recv()
                small_sum[hop + 1] = small_sum[hop] + small_in[hop]
                if hop < 2:
                    plane_hops[hop + 1].start()

        @pl.when(at_end & (step == 3))
        def _():
            small_end.start()

        @pl.when(at_end & (step == 10))
        def _():
            small_end.wait_recv()
            small_sum[5] = small_in[3]
            small_store.start()

        @pl.when(jnp.logical_not(at_end) & (step == 5))
        def _():
            small_back.wait_recv()
            small_sum[4] = small_sum[3] + small_in[3]
            small_mid.start()

        @pl.when(jnp.logical_not(at_end) & (step == 7))
        def _():
            small_mid.wait_recv()
            small_sum[5] = small_sum[4] + small_in[4]
            small_back.start()
            small_store.start()

    for copy in plane_hops:
        copy.wait_send()
    small_store.wait()
    for j, half, index in pieces:
        for target in range(2):
            col_copy(j, half, index, target).wait_send()
        x_copy(j, half, index).wait_send()

    @pl.when(at_end)
    def _():
        small_end.wait_send()

        @pl.loop(0, total)
        def _(step):
            each(step, finish_end)

    @pl.when(jnp.logical_not(at_end))
    def _():
        small_mid.wait_send()
        small_back.wait_send()

        @pl.loop(0, total)
        def _(step):
            each(step, finish_mid)


def reduce_all(planes, grads, small):
    parts, base = [], 0
    for grad, axis, rows in grads:
        height, width = grad.shape[-2:]
        height, width = (height // 2, width) if axis == 0 else (height, width // 2)
        parts.append(Part(axis, rows, width, height // rows, base, grad.ndim == 3))
        base += height // rows
    shapes = [(part.count, part.rows, part.cols) for part in parts]
    col_shapes = [(2, *shape) for part, shape in zip(parts, shapes) if part.col]
    pieces = sum(shape[1] * 2 for shape in col_shapes)
    own_shapes = [
        (2, 2, *shape) if part.col else (SLOTS, *shape[1:]) for part, shape in zip(parts, shapes)
    ]
    anywhere = pl.BlockSpec(memory_space=pl.ANY)
    dma = pltpu.SemaphoreType.DMA
    return pl.pallas_call(
        functools.partial(reduce_kernel, parts, planes),
        out_shape=[jax.ShapeDtypeStruct((n * r, c), BF) for n, r, c in shapes]
        + [jax.ShapeDtypeStruct(small.shape, F32)],
        in_specs=[anywhere] * (len(parts) + 1),
        out_specs=[anywhere] * (len(parts) + 1),
        scratch_shapes=[pltpu.VMEM(shape, BF) for _ in range(3) for shape in shapes]
        + [pltpu.VMEM(shape, BF) for shape in own_shapes]
        + [pltpu.VMEM((2, *shape), BF) for shape in col_shapes]
        + [pltpu.VMEM(shape, BF) for shape in col_shapes]
        + [dma((base,)) for _ in range(8)]
        + [dma((2, pieces)), dma((2, pieces)), dma((2, pieces)), dma((pieces,)), dma((pieces,))]
        + [dma((2,)), dma((5,)), dma((5,))]
        + [pltpu.VMEM((5, *small.shape), F32), pltpu.VMEM((6, *small.shape), F32)],
        compiler_params=pltpu.CompilerParams(
            collective_id=0, has_side_effects=True, vmem_limit_bytes=60 * 1024 * 1024
        ),
        name="reduce_grads",
    )(*[grad for grad, _, _ in grads], small)


TILE = 256
STEPS = 8


def spread_kernel(forward, fast, *refs):
    refs = list(refs)

    def take(number):
        taken = refs[:number]
        del refs[:number]
        return taken

    (mine_ref,) = take(1)
    weights = take(5 if forward and fast else 6)
    if not forward:
        gate_ref, up_ref = take(2)
    dealt_in = take(1) if fast else None
    if forward:
        all_ref, gate_ref, up_ref, act_ref, out_ref = take(5)
        if fast:
            (down_out,) = take(1)
    else:
        all_ref, d_gate_up_ref, out_ref = take(3)
    dealt_out = take(1) if fast else None
    block, w_gate, w_up, w_down, kept, to_mate, from_mate, far_part, to_far, from_mate_far, far_sum, from_far = take(12)
    (
        weight_sem, block_sem, out_sem, mate_send, mate_recv, x_send, x_recv, pass_send, pass_recv,
        sum_send, sum_recv, part_send, part_recv, back_send, back_recv,
    ) = take(15)
    deal_send, deal_recv, deal_local, row_send, row_recv, plane_send, plane_recv = take(7)
    stage = refs
    tokens, depth = mine_ref.shape
    quarter = tokens // 4
    width = w_gate.shape[1]
    half = depth // 2
    row = lax.axis_index("row")
    group, side = lax.axis_index("group"), lax.axis_index("side")
    mate, far = {"side": 1 - side}, {"group": 1 - group}
    other_row, cross = {"row": 1 - row}, {"row": 1 - row, "side": 1 - side}
    parity = lax.axis_index("dp") % 2
    next_plane = {"dp": lax.axis_index("dp") + 1 - 2 * parity}

    def remote(source, target, send, recv, where):
        return pltpu.make_async_remote_copy(
            source, target, send, recv, device_id=where, device_id_type=pl.DeviceIdType.MESH
        )

    barrier = pltpu.get_barrier_semaphore()
    greeted = [mate, far]
    if fast:
        greeted += [other_row, cross] + ([next_plane] if forward else [])
    for where in greeted:
        pl.semaphore_signal(barrier, 1, device_id=where, device_id_type=pl.DeviceIdType.MESH)

    dealt_own, dealt_sent, down_chunks = [], [], []
    if fast:
        span = tokens // 4
        member = 2 * row + side
        for index, (to_row, to_side, where) in enumerate(
            [(1 - row, side, other_row), (1 - row, 1 - side, cross), (row, 1 - side, mate), (row, side, None)]
        ):
            slot = 0 if index >= 2 else 1
            there = 2 * to_row + to_side
            for high in range(2):
                piece = 7 - there if high else there
                if not forward:
                    piece = 7 - member if high else member
                whole = pl.ds(pl.multiple_of(piece * span, span), span), slice(None)
                of_side = side if forward else to_side
                first = pl.multiple_of(of_side * 2 * span + high * span, span)
                part = pl.ds(first, span), pl.ds(slot * half, half)
                source = dealt_in[0].at[whole] if forward else dealt_in[0].at[part]
                target = dealt_out[0].at[part] if forward else dealt_out[0].at[whole]
                if where is None:
                    dealt_own.append(pltpu.make_async_copy(source, target, deal_local.at[high]))
                else:
                    sems = deal_send.at[index, high], deal_recv.at[index, high]
                    dealt_sent.append(remote(source, target, *sems, where))
        if forward:
            rows = width // 8
            for index in range(4):
                here = pl.ds(pl.multiple_of((4 * parity + index) * rows, 16), rows)
                place = w_down.at[here, pl.ds(half, half)]
                down_chunks.append(
                    (
                        remote(weights[4].at[here, :], place, row_send.at[index], row_recv.at[index], other_row),
                        remote(place, place, plane_send.at[index], plane_recv.at[index], next_plane),
                    )
                )

    loads = []
    for index, (source, target) in enumerate(
        [
            (weights[0], w_gate.at[pl.ds(0, half), :]),
            (weights[1], w_gate.at[pl.ds(half, half), :]),
            (weights[2], w_up.at[pl.ds(0, half), :]),
            (weights[3], w_up.at[pl.ds(half, half), :]),
            (weights[4], w_down.at[:, pl.ds(0, half)]),
        ]
        + ([] if forward and fast else [(weights[5], w_down.at[:, pl.ds(half, half)])])
    ):
        loads.append(pltpu.make_async_copy(source, target, weight_sem.at[index]))
    order = loads if forward else loads[4:] + loads[:4]
    mine_copies = [
        pltpu.make_async_copy(
            mine_ref.at[pl.ds(i * 2 * quarter, 2 * quarter), :], block.at[i], block_sem.at[i]
        )
        for i in range(2)
    ]
    for copy in mine_copies:
        copy.start()
    for copy in order:
        copy.start()
    pl.semaphore_wait(barrier, len(greeted))
    for over_row, over_planes in down_chunks:
        over_row.start()

    def piece(index):
        return mine_ref.at[pl.ds(index * quarter, quarter), :]

    def mate_copy(index):
        return remote(
            piece(index),
            block.at[2 + index // 2, pl.ds(index % 2 * quarter, quarter), :],
            mate_send.at[index],
            mate_recv.at[index],
            mate,
        )

    def x_copy(index):
        return remote(
            piece(index), block.at[4 + index, pl.ds(0, quarter), :], x_send.at[index], x_recv.at[index], far
        )

    def pass_copy(index):
        return remote(
            block.at[4 + index, pl.ds(0, quarter), :],
            block.at[4 + index, pl.ds(quarter, quarter), :],
            pass_send.at[index],
            pass_recv.at[index],
            mate,
        )

    def sum_copy(index):
        return remote(to_mate.at[index], from_mate.at[index], sum_send.at[index], sum_recv.at[index], mate)

    def part_copy(index):
        return remote(to_far.at[index], from_mate_far.at[index], part_send.at[index], part_recv.at[index], mate)

    def back_copy(index):
        return remote(far_sum.at[index], from_far.at[index], back_send.at[index], back_recv.at[index], far)

    x_copy(0).start()
    for index in range(4):
        mate_copy(index).start()
    x_copy(1).start()
    for copy in dealt_sent + dealt_own:
        copy.start()
    for copy in mine_copies:
        copy.wait()

    def emit(step, where, part):
        @pl.when(step < 2)
        def _():
            kept[jnp.minimum(step, 1), :, where] = part

        @pl.when((step >= 2) & (step < 4))
        def _():
            to_mate[jnp.clip(step - 2, 0, 1), :, where] = part.astype(BF)

        @pl.when(step >= 4)
        def _():
            far_part[jnp.maximum(step - 4, 0), :, where] = part[:quarter]
            to_far[jnp.maximum(step - 4, 0), :, where] = part[quarter:].astype(BF)

    def all_copy(step):
        return pltpu.make_async_copy(block.at[step], all_ref.at[step], out_sem.at[0, step])

    if forward:
        stage_gate, stage_up, stage_act = stage

        def saves(step):
            slot = step % 2
            return [
                pltpu.make_async_copy(stage_gate.at[slot], gate_ref.at[step], out_sem.at[1, step]),
                pltpu.make_async_copy(stage_up.at[slot], up_ref.at[step], out_sem.at[2, step]),
                pltpu.make_async_copy(stage_act.at[step], act_ref.at[step], out_sem.at[3, step]),
            ]

        def fetches(step):
            return []

        def first_loads():
            for copy in loads[:4]:
                copy.wait()

        def second_loads():
            for copy in loads[4:]:
                copy.wait()

        def first_half(step):
            slot = step % 2

            @pl.loop(0, width // TILE)
            def _(tile):
                where = pl.ds(pl.multiple_of(tile * TILE, TILE), TILE)
                gate = dot(block[step], w_gate[:, where])
                up = dot(block[step], w_up[:, where])
                stage_gate[slot, :, where] = gate.astype(BF)
                stage_up[slot, :, where] = up.astype(BF)
                stage_act[step, :, where] = (gate * up / (1.0 + jnp.exp(-gate))).astype(BF)

        def second_half(step, first=0, last=depth // TILE):
            @pl.loop(first, last)
            def _(tile):
                where = pl.ds(pl.multiple_of(tile * TILE, TILE), TILE)
                emit(step, where, dot(stage_act[step], w_down[:, where]))

    else:
        stage_gate, stage_up, stage_d, fetch_sem = stage

        def saves(step):
            return [
                pltpu.make_async_copy(stage_d.at[step % 2], d_gate_up_ref.at[step], out_sem.at[1, step])
            ]

        def fetches(step):
            slot = step % 2
            return [
                pltpu.make_async_copy(gate_ref.at[step], stage_gate.at[slot], fetch_sem.at[0, step]),
                pltpu.make_async_copy(up_ref.at[step], stage_up.at[slot], fetch_sem.at[1, step]),
            ]

        def first_loads():
            for copy in loads[4:]:
                copy.wait()

        def second_loads():
            for copy in loads[:4]:
                copy.wait()

        def first_half(step):
            slot = step % 2

            @pl.loop(0, width // TILE)
            def _(tile):
                first = pl.multiple_of(tile * TILE, TILE)
                where = pl.ds(first, TILE)
                d_act = dot(block[step], w_down[where, :], ((1,), (1,)))
                gate = stage_gate[slot, :, where].astype(F32)
                up = stage_up[slot, :, where].astype(F32)
                sig = 1.0 / (1.0 + jnp.exp(-gate))
                d_gate = d_act * up * sig * (1.0 + gate * (1.0 - sig))
                stage_d[slot, :, where] = d_gate.astype(BF)
                stage_d[slot, :, pl.ds(pl.multiple_of(width + first, TILE), TILE)] = (d_act * gate * sig).astype(BF)

        def second_half(step):
            slot = step % 2

            @pl.loop(0, depth // TILE)
            def _(tile):
                where = pl.ds(pl.multiple_of(tile * TILE, TILE), TILE)
                part = dot(stage_d[slot, :, :width], w_gate[where, :], ((1,), (1,)))
                part += dot(stage_d[slot, :, width:], w_up[where, :], ((1,), (1,)))
                emit(step, where, part)

    def finish_far(index):
        part_copy(index).wait_recv()
        total = far_part[index] + from_mate_far[index].astype(F32)
        far_sum[index] = total.astype(BF)
        back_copy(index).start()

    if forward and fast:
        down_saved = pltpu.make_async_copy(w_down.at[:, pl.ds(half, half)], down_out, weight_sem.at[5])
    for copy in fetches(0):
        copy.start()

    @pl.loop(0, STEPS)
    def _(step):
        @pl.when((step == 2) | (step == 3))
        def _():
            index = jnp.clip(2 * (step - 2), 0, 2)
            mate_copy(index).wait_recv()
            mate_copy(index + 1).wait_recv()

        @pl.when(step >= 4)
        def _():
            index = jnp.maximum(step - 4, 0)
            x_copy(index).wait_recv()
            pass_copy(index).start()
            pass_copy(index).wait_recv()

        all_copy(step).start()
        for copy in fetches(step):
            copy.wait()

        if not forward:
            @pl.when(step < STEPS - 1)
            def _():
                for copy in fetches(jnp.minimum(step + 1, STEPS - 1)):
                    copy.start()

        @pl.when(step == 0)
        def _():
            first_loads()

        @pl.when(step >= 2)
        def _():
            for copy in saves(jnp.maximum(step - 2, 0)):
                copy.wait()

        first_half(step)

        @pl.when(step == 0)
        def _():
            second_loads()

        if forward and fast:
            @pl.when(step < 4)
            def _():
                second_half(step, 0, half // TILE)

            for index in range(4):
                @pl.when(step == min(index + 1, 3))
                def _(index=index):
                    down_chunks[index][0].wait_recv()
                    down_chunks[index][1].start()

            @pl.when(step == 3)
            def _():
                for _, over_planes in down_chunks:
                    over_planes.wait_recv()
                down_saved.start()

                @pl.loop(0, 4)
                def _(early):
                    second_half(early, half // TILE)

                sum_copy(0).start()

            @pl.when(step >= 4)
            def _():
                second_half(step)
        else:
            second_half(step)
        for copy in saves(step):
            copy.start()

        @pl.when((step == 1) | (step == 3))
        def _():
            x_copy(2 + step // 2).start()

        @pl.when((step == 3) if forward and fast else ((step >= 2) & (step < 4)))
        def _():
            sum_copy(jnp.clip(step - 2, 0, 1)).start()

        @pl.when(step >= 4)
        def _():
            part_copy(jnp.maximum(step - 4, 0)).start()

        @pl.when(step >= 5)
        def _():
            finish_far(jnp.maximum(step - 5, 0))

    finish_far(3)
    for index in range(2):
        sum_copy(index).wait_recv()
        kept[index] = kept[index] + from_mate[index].astype(F32)
    results = []
    for index in range(4):
        back_copy(index).wait_recv()
        rows = pl.ds(index % 2 * quarter, quarter)
        kept[index // 2, rows, :] = kept[index // 2, rows, :] + from_far[index].astype(F32)
        if index % 2:
            copy = pltpu.make_async_copy(kept.at[index // 2], out_ref.at[index // 2], block_sem.at[index // 2])
            copy.start()
            results.append(copy)
    for copy in results + dealt_own:
        copy.wait()
    for copy in dealt_sent:
        copy.wait()
    for over_row, over_planes in down_chunks:
        over_row.wait_send()
        over_planes.wait_send()
    if forward and fast:
        down_saved.wait()

    @pl.loop(0, STEPS)
    def _(step):
        all_copy(step).wait()

        @pl.when(step >= STEPS - 2)
        def _():
            for copy in saves(step):
                copy.wait()

        @pl.when(step < 4)
        def _():
            index = jnp.minimum(step, 3)
            mate_copy(index).wait_send()
            x_copy(index).wait_send()
            pass_copy(index).wait_send()
            part_copy(index).wait_send()
            back_copy(index).wait_send()

        @pl.when(step < 2)
        def _():
            sum_copy(jnp.minimum(step, 1)).wait_send()


def spread(forward, mine, weights, kept=(), dealt=None):
    tokens, depth = mine.shape
    quarter, double = tokens // 4, tokens // 2
    width = weights[0].shape[1]
    anywhere = pl.BlockSpec(memory_space=pl.ANY)
    wide = jax.ShapeDtypeStruct((STEPS, double, width), BF)
    whole = jax.ShapeDtypeStruct((STEPS, double, depth), BF)
    out = jax.ShapeDtypeStruct((2, double, depth), F32)
    if forward:
        outs = [whole, wide, wide, wide, out]
        if dealt is not None:
            outs.append(jax.ShapeDtypeStruct((width, depth // 2), BF))
            outs.append(jax.ShapeDtypeStruct((tokens, depth), BF))
        stage = [
            pltpu.VMEM((2, double, width), BF),
            pltpu.VMEM((2, double, width), BF),
            pltpu.VMEM((STEPS, double, width), BF),
        ]
    else:
        outs = [whole, jax.ShapeDtypeStruct((STEPS, double, 2 * width), BF), out]
        if dealt is not None:
            outs.append(jax.ShapeDtypeStruct((2 * tokens, depth // 2), BF))
        stage = [
            pltpu.VMEM((2, double, width), BF),
            pltpu.VMEM((2, double, width), BF),
            pltpu.VMEM((2, double, 2 * width), BF),
            pltpu.SemaphoreType.DMA((2, STEPS)),
        ]
    inputs = [mine, *weights, *kept] + ([] if dealt is None else [dealt])
    return pl.pallas_call(
        functools.partial(spread_kernel, forward, dealt is not None),
        out_shape=outs,
        in_specs=[anywhere] * len(inputs),
        out_specs=[anywhere] * len(outs),
        scratch_shapes=[
            pltpu.VMEM((STEPS, double, depth), BF),
            pltpu.VMEM((depth, width), BF),
            pltpu.VMEM((depth, width), BF),
            pltpu.VMEM((width, depth), BF),
            pltpu.VMEM((2, double, depth), F32),
            pltpu.VMEM((2, double, depth), BF),
            pltpu.VMEM((2, double, depth), BF),
            pltpu.VMEM((4, quarter, depth), F32),
            pltpu.VMEM((4, quarter, depth), BF),
            pltpu.VMEM((4, quarter, depth), BF),
            pltpu.VMEM((4, quarter, depth), BF),
            pltpu.VMEM((4, quarter, depth), BF),
            pltpu.SemaphoreType.DMA((6,)),
            pltpu.SemaphoreType.DMA((2,)),
            pltpu.SemaphoreType.DMA((4, STEPS)),
        ]
        + [pltpu.SemaphoreType.DMA((4,)) for _ in range(6)]
        + [pltpu.SemaphoreType.DMA((2,)) for _ in range(2)]
        + [pltpu.SemaphoreType.DMA((4,)) for _ in range(4)]
        + [pltpu.SemaphoreType.DMA((3, 2)), pltpu.SemaphoreType.DMA((3, 2)), pltpu.SemaphoreType.DMA((2,))]
        + [pltpu.SemaphoreType.DMA((4,)) for _ in range(4)]
        + stage,
        compiler_params=pltpu.CompilerParams(
            collective_id=1 if forward else 2,
            has_side_effects=True,
            vmem_limit_bytes=60 * 1024 * 1024,
        ),
        name="feed_forward" if forward else "feed_forward_back",
    )(*inputs)


def front_kernel(*refs):
    refs = list(refs)

    def take(number):
        taken = refs[:number]
        del refs[:number]
        return taken

    tokens_ref, w_project_ref, w_out_ref, gains_ref, gate_ref, up_ref = take(6)
    cos_ref, sin_ref, query_gain_ref, key_gain_ref = take(4)
    (
        states_out, normed_out, raw_out, query_out, key_out, pair_out, mixed_out, logs_out, hidden_out, normed_two_out,
        w_project_out, w_out_out, gate_out, up_out, gains_out,
    ) = take(15)
    states, normed, w_project, raw, key_raw, query, pair_own, pair, key_n, mixed_t, logs, mixed = take(12)
    w_out, hidden, gains = take(3)
    token_send, token_recv, token_local = take(3)
    project_send, project_recv, out_send, out_recv, gain_send, gain_recv = take(6)
    pair_send, pair_recv, row_send, row_recv, plane_send, plane_recv, local, store = take(8)

    plane, row = lax.axis_index("dp"), lax.axis_index("row")
    group, side = lax.axis_index("group"), lax.axis_index("side")
    other_row, mate, far = {"row": 1 - row}, {"side": 1 - side}, {"group": 1 - group}
    cross = {"row": 1 - row, "side": 1 - side}
    parity = plane % 2
    next_plane = {"dp": plane + 1 - 2 * parity}
    shard, width = tokens_ref.shape
    mine, depth = states.shape
    pieces = 8
    span = shard // pieces
    member = 2 * row + side
    kv_rows = key_raw.shape[0]

    def remote(source, target, send, recv, where):
        return pltpu.make_async_remote_copy(
            source, target, send, recv, device_id=where, device_id_type=pl.DeviceIdType.MESH
        )

    barrier = pltpu.get_barrier_semaphore()
    for where in (other_row, mate, far, cross, next_plane):
        pl.semaphore_signal(barrier, 1, device_id=where, device_id_type=pl.DeviceIdType.MESH)

    def token_copies(to_row, to_side, index, where):
        target_member = 2 * to_row + to_side
        slot = 1 if to_row is not row else 0
        copies = []
        for high in range(2):
            piece = pieces - 1 - target_member if high else target_member
            source = tokens_ref.at[pl.ds(pl.multiple_of(piece * span, span), span), :]
            first = pl.multiple_of(side * 2 * span + high * span, span)
            target = states.at[pl.ds(first, span), pl.ds(slot * width, width)]
            if where is None:
                copies.append(pltpu.make_async_copy(source, target, token_local.at[high]))
            else:
                sems = token_send.at[index, high], token_recv.at[index, high]
                copies.append(remote(source, target, *sems, where))
        return copies

    own_tokens = token_copies(row, side, 0, None)
    other = 1 - row
    sent_tokens = token_copies(other, side, 0, other_row)
    sent_tokens += token_copies(other, 1 - side, 1, cross)
    sent_tokens += token_copies(row, 1 - side, 2, mate)

    me, far_col = 2 * group + side, 2 * (1 - group) + side

    class Spread:
        def __init__(self, source, place, send, recv):
            self.copies = []

            def add(origin, target, where):
                index = len(self.copies)
                self.copies.append(remote(origin, target, send.at[index], recv.at[index], where))
                return self.copies[-1]

            here, there = parity, 1 - parity
            rows = source.shape[0] // 2
            first_half = source.at[pl.ds(pl.multiple_of(here * rows, 16), rows), :]
            self.to_row = add(first_half, place(me, 1, here), other_row)
            self.to_plane = add(place(me, 1, here), place(me, 1, here), next_plane)
            self.to_far = [add(source, place(me, 0, None), far)]
            self.to_far += [add(place(me, 1, half), place(me, 1, half), far) for half in (here, there)]
            self.to_mate = [add(source, place(me, 0, None), mate)]
            self.to_mate += [add(place(me, 1, half), place(me, 1, half), mate) for half in (here, there)]
            self.to_mate += [add(place(far_col, 0, None), place(far_col, 0, None), mate)]
            self.to_mate += [
                add(place(far_col, 1, half), place(far_col, 1, half), mate) for half in (here, there)
            ]

        def first(self):
            self.to_row.start()
            self.to_far[0].start()
            self.to_mate[0].start()

        def row_in(self):
            self.to_row.wait_recv()
            for copy in (self.to_plane, self.to_far[1], self.to_mate[1]):
                copy.start()

        def plane_in(self):
            self.to_plane.wait_recv()
            self.to_far[2].start()
            self.to_mate[2].start()

        def far_in(self, index):
            self.to_far[index].wait_recv()
            self.to_mate[3 + index].start()

        def mate_in(self, first, last):
            for copy in self.to_mate[first:last]:
                copy.wait_recv()

        def sent(self):
            for copy in self.copies:
                copy.wait_send()

    q_width = w_out_ref.shape[0]

    def project_place(col, slot, half):
        if half is None:
            return w_project.at[col, slot]
        return w_project.at[col, slot, pl.ds(pl.multiple_of(half * (width // 2), 16), width // 2), :]

    def out_place(col, slot, half):
        first, rows = col * q_width, q_width
        if half is not None:
            rows = q_width // 2
            first = first + half * rows
        return w_out.at[pl.ds(pl.multiple_of(first, 16), rows), pl.ds(slot * width, width)]

    project = Spread(w_project_ref, project_place, project_send, project_recv)
    output = Spread(w_out_ref, out_place, out_send, out_recv)
    own_project = pltpu.make_async_copy(w_project_ref, w_project.at[me, 0], local.at[0])
    own_output = pltpu.make_async_copy(w_out_ref, out_place(me, 0, None), local.at[1])
    own_gains = pltpu.make_async_copy(gains_ref, gains.at[0], local.at[2])
    sent_gains = remote(gains_ref, gains.at[1], gain_send.at[0], gain_recv.at[0], other_row)

    chunks = []
    for index, (source, target) in enumerate([(gate_ref, gate_out), (up_ref, up_out)]):
        rows = source.shape[0] // 4
        for part in range(2):
            here = pl.ds(pl.multiple_of((2 * parity + part) * rows, 64), rows)
            slot = 2 * index + part
            over_row = remote(source.at[here, :], target.at[here, :], row_send.at[slot], row_recv.at[slot], other_row)
            over_planes = remote(
                target.at[here, :], target.at[here, :], plane_send.at[slot], plane_recv.at[slot], next_plane
            )
            chunks.append((over_row, over_planes))

    def pass_on(index):
        chunks[index][0].wait_recv()
        chunks[index][1].start()

    own_copies = [own_gains, *own_tokens, own_project, own_output]
    for copy in own_copies:
        copy.start()
    pl.semaphore_wait(barrier, 5)
    sent_gains.start()
    project.first()
    for copy in sent_tokens:
        copy.start()
    output.first()
    chunks[0][0].start()
    for copy in own_copies:
        copy.wait()
    sent_gains.wait_recv()
    project.row_in()
    for copy in sent_tokens:
        copy.wait_recv()

    stores = []

    def save(source, target):
        copy = pltpu.make_async_copy(source, target, store.at[len(stores)])
        copy.start()
        stores.append(copy)
        return copy

    block = mine // 4

    @pl.loop(0, 4)
    def _(index):
        here = pl.ds(pl.multiple_of(index * block, block), block)
        values = states[here, :].astype(F32)
        inverse = lax.rsqrt(jnp.mean(values * values, axis=1, keepdims=True) + EPSILON)
        for slot in range(2):
            part = values[:, slot * width : (slot + 1) * width] * inverse
            normed[here, slot * width : (slot + 1) * width] = (part * gains[slot, 0:1, :]).astype(BF)

    save(states, states_out)
    normed_saved = save(normed, normed_out)
    save(gains, gains_out)

    def project_col(col):
        part = dot(normed[:, :width], w_project[col, 0]) + dot(normed[:, width:], w_project[col, 1])
        part = part.T
        heads = q_width // HD
        for head in range(heads):
            raw[col * heads + head] = part[head * HD : (head + 1) * HD]
        k_width = kv_rows // 4
        first = pl.multiple_of(col * k_width, 16)
        key_raw[pl.ds(first, k_width), :] = part[q_width : q_width + k_width].astype(BF)
        first = pl.multiple_of(kv_rows + col * k_width, 16)
        pair_own[pl.ds(first, k_width), :] = part[q_width + k_width :].astype(BF)

    project.plane_in()
    project.far_in(0)
    project_col(me)
    project.mate_in(0, 3)
    project_col(2 * group + 1 - side)
    project.far_in(1)
    project.far_in(2)
    project_col(far_col)
    project.mate_in(3, 6)
    project_col(2 * (1 - group) + 1 - side)
    save(raw, raw_out)
    save(key_raw, key_out)
    save(w_project, w_project_out)

    cosine, sine = cos_ref[...], sin_ref[...]

    def turned(values, gain):
        values = values * lax.rsqrt(jnp.mean(values * values, axis=0, keepdims=True) + EPSILON) * gain
        first, second = values[: HD // 2], values[HD // 2 :]
        return jnp.concatenate([first * cosine - second * sine, second * cosine + first * sine], axis=0)

    for head in range(kv_rows // HD):
        cut = slice(head * HD, (head + 1) * HD)
        pair_own[cut, :] = turned(key_raw[cut, :].astype(F32), key_gain_ref[...]).astype(BF)

    def places(who):
        starts = [who, pieces - 1 - who, pieces + who, 2 * pieces - 1 - who]
        return [pair.at[:, pl.ds(pl.multiple_of(start * span, span), span)] for start in starts]

    for index, place in enumerate(places(member)):
        place[...] = pair_own[:, index * span : (index + 1) * span]
    to_mate, to_row, passed = [], [], []
    for index, place in enumerate(places(member)):
        to_row.append(remote(place, place, pair_send.at[0, index], pair_recv.at[0, index], other_row))
        to_mate.append(remote(place, place, pair_send.at[1, index], pair_recv.at[1, index], mate))
    for index, place in enumerate(places(2 * (1 - row) + side)):
        passed.append(remote(place, place, pair_send.at[2, index], pair_recv.at[2, index], mate))
    for copy in to_row + to_mate:
        copy.start()
    chunks[1][0].start()
    output.row_in()
    output.far_in(0)

    @pl.loop(0, raw.shape[0])
    def _(head):
        values = turned(raw[head], query_gain_ref[...]).astype(BF)
        query[head] = values * BF(1.0 / math.sqrt(HD))

    for index in range(4):
        to_row[index].wait_recv()
        passed[index].start()
    chunks[2][0].start()
    output.plane_in()
    pass_on(0)
    for index in range(4):
        to_mate[index].wait_recv()
        passed[index].wait_recv()
    chunks[3][0].start()
    output.far_in(1)
    output.far_in(2)

    firsts = [member, pieces - 1 - member, pieces + member, 2 * pieces - 1 - member]
    rows = REP * span
    ones = jnp.ones((16, KEYS), BF)

    @pl.loop(0, kv_rows // HD)
    def _(head):
        key_n[...] = pair[pl.ds(pl.multiple_of(head * HD, HD), HD), :].T
        value_rows = pl.ds(pl.multiple_of(kv_rows + head * HD, HD), HD)
        for index in range(4):
            cut = slice(index * span, (index + 1) * span)
            query_here = jnp.concatenate([query[head * REP + rep, :, cut] for rep in range(REP)], axis=1)
            first_query = firsts[index] * span
            full, last = tiles_of(first_query)

            def tile(where, accum, masked):
                first_key = pl.multiple_of(where * KEYS, KEYS)
                expo = jnp.exp(dot(key_n[pl.ds(first_key, KEYS), :], query_here))
                if masked:
                    expo = jnp.where(allowed(first_query, first_key, span, rows), expo, 0.0)
                value = jnp.concatenate([pair[value_rows, pl.ds(first_key, KEYS)], ones], axis=0)
                return accum + dot(value, expo.astype(BF))

            accum = tile(last, jnp.zeros((HD + 16, rows), F32), True)
            accum = lax.fori_loop(0, full, lambda where, total: tile(where, total, False), accum)
            total = accum[HD : HD + 1]
            result = accum[:HD] / total
            log = jnp.log(total)
            for rep in range(REP):
                part = slice(rep * span, (rep + 1) * span)
                mixed_t[pl.ds(pl.multiple_of((head * REP + rep) * HD, HD), HD), cut] = result[:, part]
                logs[head, rep : rep + 1, cut] = log[:, part]

        for number, index in ((1, 1), (3, 2)):
            @pl.when(head == number)
            def _(index=index):
                pass_on(index)

    save(query, query_out)
    save(mixed_t, mixed_out)
    save(logs, logs_out)
    save(pair, pair_out)
    pass_on(3)
    output.mate_in(0, 6)
    save(w_out, w_out_out)

    @pl.loop(0, mixed_t.shape[0] // 128)
    def _(index):
        here = pl.ds(pl.multiple_of(index * 128, 128), 128)
        mixed[:, here] = mixed_t[here, :].astype(BF).T

    @pl.loop(0, depth // TILE)
    def _(index):
        here = pl.ds(pl.multiple_of(index * TILE, TILE), TILE)
        hidden[:, here] = states[:, here].astype(F32) + dot(mixed[...], w_out[:, here])

    normed_saved.wait()

    @pl.loop(0, 4)
    def _(index):
        here = pl.ds(pl.multiple_of(index * block, block), block)
        values = hidden[here, :]
        inverse = lax.rsqrt(jnp.mean(values * values, axis=1, keepdims=True) + EPSILON)
        for slot in range(2):
            part = values[:, slot * width : (slot + 1) * width] * inverse
            normed[here, slot * width : (slot + 1) * width] = (part * gains[slot, 1:2, :]).astype(BF)

    save(hidden, hidden_out)
    save(normed, normed_two_out)
    for copy in stores:
        if copy is not normed_saved:
            copy.wait()
    sent_gains.wait_send()
    for copy in sent_tokens + to_row + to_mate + passed:
        copy.wait_send()
    project.sent()
    output.sent()
    for over_row, over_planes in chunks:
        over_row.wait_send()
        over_planes.wait_recv()
        over_planes.wait_send()


def front(tokens, w_project, w_out, gains, w_gate, w_up, cosine, sine, query_gain, key_gain):
    shard, width = tokens.shape
    mine, depth = shard // 2, 2 * width
    q_width, columns = w_out.shape[0], w_project.shape[1]
    kv_rows = KVH * HD
    anywhere = pl.BlockSpec(memory_space=pl.ANY)
    inside = pl.BlockSpec(memory_space=pltpu.VMEM)
    dma = pltpu.SemaphoreType.DMA
    shape = jax.ShapeDtypeStruct
    return pl.pallas_call(
        front_kernel,
        out_shape=[
            shape((mine, depth), BF),
            shape((mine, depth), BF),
            shape((QH, HD, mine), F32),
            shape((QH, HD, mine), BF),
            shape((kv_rows, mine), BF),
            shape((2 * kv_rows, GROUP), BF),
            shape((QH * HD, mine), F32),
            shape((KVH, REP, mine), F32),
            shape((mine, depth), F32),
            shape((mine, depth), BF),
            shape((4, 2, width, columns), BF),
            shape((4 * q_width, depth), BF),
            shape(w_gate.shape, BF),
            shape(w_up.shape, BF),
            shape((2, 2, width), F32),
        ],
        in_specs=[anywhere] * 6 + [inside] * 4,
        out_specs=[anywhere] * 15,
        scratch_shapes=[
            pltpu.VMEM((mine, depth), BF),
            pltpu.VMEM((mine, depth), BF),
            pltpu.VMEM((4, 2, width, columns), BF),
            pltpu.VMEM((QH, HD, mine), F32),
            pltpu.VMEM((kv_rows, mine), BF),
            pltpu.VMEM((QH, HD, mine), BF),
            pltpu.VMEM((2 * kv_rows, mine), BF),
            pltpu.VMEM((2 * kv_rows, GROUP), BF),
            pltpu.VMEM((GROUP, HD), BF),
            pltpu.VMEM((QH * HD, mine), F32),
            pltpu.VMEM((KVH, REP, mine), F32),
            pltpu.VMEM((mine, QH * HD), BF),
            pltpu.VMEM((4 * q_width, depth), BF),
            pltpu.VMEM((mine, depth), F32),
            pltpu.VMEM((2, 2, width), F32),
            dma((3, 2)), dma((3, 2)), dma((2,)),
            dma((11,)), dma((11,)), dma((11,)), dma((11,)), dma((1,)), dma((1,)),
            dma((3, 4)), dma((3, 4)), dma((4,)), dma((4,)), dma((4,)), dma((4,)), dma((3,)), dma((13,)),
        ],
        compiler_params=pltpu.CompilerParams(
            collective_id=3, has_side_effects=True, vmem_limit_bytes=56 * 1024 * 1024
        ),
        name="front",
    )(tokens, w_project, w_out, gains, w_gate, w_up, cosine, sine, query_gain, key_gain)


def body(
    tokens,
    norm1_gain,
    w_query,
    w_key,
    w_value,
    query_gain,
    key_gain,
    w_out,
    norm2_gain,
    w_gate,
    w_up,
    w_down,
    teacher,
    positions,
    token_count,
):
    rows = lax.axis_size("row")
    cores = lax.axis_size("side")
    cols = lax.axis_size("group") * cores
    row_index = lax.axis_index("row")
    group_index = lax.axis_index("group")
    members = rows * cores
    member = row_index * cores + lax.axis_index("side")
    shard, width = tokens.shape
    pieces = 2 * members
    span = shard // pieces
    mine = shard // members * cores
    q_width, k_width = w_query.shape[1], w_key.shape[1]
    ff = w_gate.shape[1]

    def from_row(block, ahead):
        pairs = [((r + ahead) % rows, r) for r in range(rows)]
        return lax.ppermute(block, "row", pairs)

    def gather_rows(block, axis):
        parts = [block] + [from_row(block, ahead) for ahead in range(1, rows)]
        return jnp.concatenate(parts, axis=axis)

    def scatter_rows(block, axis):
        size = block.shape[axis] // rows
        total = lax.slice_in_dim(block, 0, size, axis=axis).astype(F32)
        for ahead in range(1, rows):
            part = lax.slice_in_dim(block, ahead * size, (ahead + 1) * size, axis=axis)
            total = total + from_row(part, rows - ahead).astype(F32)
        return total.astype(BF)

    def sum_planes(block, cuts):
        planes = lax.axis_size("dp")
        plane = lax.axis_index("dp")
        half = planes // 2
        edge = jnp.minimum(plane, planes - 1 - plane)
        done = []
        for part in jnp.split(block, cuts, axis=0):
            for step in range(half - 1):
                pairs = [(step, step + 1), (planes - 1 - step, planes - 2 - step)]
                come = lax.ppermute(part, "dp", pairs)
                part = (part.astype(F32) + come.astype(F32)).astype(BF)
            come = lax.ppermute(part, "dp", [(half - 1, half), (half, half - 1)])
            part = (part.astype(F32) + come.astype(F32)).astype(BF)
            for step in reversed(range(half - 1)):
                pairs = [(step + 1, step), (planes - 2 - step, planes - 1 - step)]
                come = lax.ppermute(part, "dp", pairs)
                part = jnp.where(edge == step, come, part)
            done.append(part)
        return jnp.concatenate(done, axis=0)

    def to_members(block):
        parts = block.reshape(pieces, span, width)
        parts = jnp.stack([parts[:members], parts[members:][::-1]], axis=1)
        moved = lax.all_to_all(parts, ("row", "side"), 0, 0, tiled=True)
        moved = jnp.roll(moved.reshape(rows, cores, 2 * span, width), -row_index, 0)
        moved = moved.transpose(1, 2, 0, 3)
        return moved.reshape(mine, rows * width)

    def from_members(block):
        parts = block.reshape(cores, 2, span, rows, width).transpose(3, 0, 1, 2, 4)
        parts = jnp.roll(parts, row_index, 0).reshape(members, 2, span, width)
        moved = lax.all_to_all(parts, ("row", "side"), 0, 0, tiled=True)
        moved = jnp.concatenate([moved[:, 0], moved[:, 1][::-1]], axis=0)
        return moved.reshape(shard, width)

    def pick(values):
        part = lax.dynamic_slice_in_dim(values.reshape(-1, cores, pieces, span), group_index, 1, 0)[0]
        low = lax.dynamic_slice_in_dim(part, member, 1, 1)
        high = lax.dynamic_slice_in_dim(part, pieces - 1 - member, 1, 1)
        return jnp.concatenate([low, high], axis=1).reshape(-1)

    first_tokens = (
        jnp.array([0, 0, shard, shard], jnp.int32)
        + jnp.stack([member, pieces - 1 - member] * 2).astype(jnp.int32) * span
    )

    half = HD // 2
    freq = jnp.exp(jnp.arange(half, dtype=F32) * (-2.0 * math.log(10000.0) / HD))
    angle = freq[:, None] * pick(positions).astype(F32)[None, :]
    cosine, sine = jnp.cos(angle), jnp.sin(angle)
    def dealt(full):
        lead, entry = full.shape[:-2], full.shape[-1]
        parts = full.reshape(lead + (cores, pieces, span, entry))
        low = parts[..., :members, :, :]
        high = parts[..., members:, :, :][..., ::-1, :, :]
        both = jnp.stack([low, high], axis=-3)
        both = jnp.moveaxis(both, -4, 0)
        return both.reshape((members,) + lead + (mine, entry))

    w_project = jnp.concatenate([w_query, w_key, w_value], axis=1)
    scale = 1.0 / math.sqrt(HD)
    fast = rows == 2 and cols == 4 and lax.axis_size("dp") % 2 == 0 and mine == 4 * span
    if fast:
        (
            states, normed_one, query_raw, query_use, key_sent, pair, mixed_f, logs, hidden,
            normed_two, w_project, w_out_all, gate_other, up_other, gains,
        ) = front(
            tokens, w_project, w_out, jnp.stack([norm1_gain, norm2_gain]), w_gate, w_up,
            cosine, sine, query_gain[:, None], key_gain[:, None],
        )
        states = states.astype(F32)
        inverse_one, inverse_two = rms(states), rms(hidden)
        gain_one, gain_two = gains[:, 0].reshape(D), gains[:, 1].reshape(D)
        key_sent = key_sent.reshape(KVH, HD, mine)
        query_use = query_use.reshape(KVH, REP, HD, mine)
        mixed_f = mixed_f.reshape(KVH, REP, HD, mine)
        pair = pair.reshape(2, KVH, HD, GROUP)
        key_t, value_t = pair[0], pair[1]
        mixed = mixed_f.reshape(QH * HD, mine).astype(BF)
        w_project = w_project.reshape(cols, D, -1)
        ffn_weights = [w_gate, gate_other, w_up, up_other, w_down]
        query_back = jax.vjp(
            lambda raw, gain: prepare(raw, gain, cosine, sine), query_raw, query_gain
        )[1]
        key_back = jax.vjp(
            lambda raw, gain: prepare(raw, gain, cosine, sine), key_sent.astype(F32), key_gain
        )[1]
    else:
        states = to_members(tokens).astype(F32)
        gain_one = gather_rows(norm1_gain, 0)
        gain_two = gather_rows(norm2_gain, 0)
        w_project = gather_rows(w_project, 0)
        w_project = lax.all_gather(w_project, ("group", "side"), axis=0)
        w_out_all = gather_rows(w_out, 1)
        w_out_all = lax.all_gather(w_out_all, ("group", "side"), axis=0, tiled=True)
        def halves(block, axis):
            if rows == 2:
                return [block, from_row(block, 1)]
            return jnp.split(gather_rows(block, axis), 2, axis=axis)

        ffn_weights = halves(w_gate, 0) + halves(w_up, 0) + halves(w_down, 1)
        inverse_one = rms(states)
        normed_one = (states * inverse_one * gain_one).astype(BF)
        projected = dot(w_project, normed_one, ((1,), (1,)))
        query_raw = projected[:, :q_width].reshape(QH, HD, mine)
        key_sent = projected[:, q_width : q_width + k_width].reshape(KVH, HD, mine).astype(BF)
        value_sent = projected[:, q_width + k_width :].reshape(KVH, HD, mine).astype(BF)
        query_rot, query_back = jax.vjp(
            lambda raw, gain: prepare(raw, gain, cosine, sine), query_raw, query_gain
        )
        key_rot, key_back = jax.vjp(
            lambda raw, gain: prepare(raw, gain, cosine, sine), key_sent.astype(F32), key_gain
        )
        query_use = (query_rot.astype(BF) * BF(scale)).reshape(KVH, REP, HD, mine)
        pair = jnp.stack([key_rot.astype(BF), value_sent])
        pair = lax.all_gather(pair, ("row", "side"), axis=0)

        def natural(stacked):
            lead = stacked.shape[1:-1]
            parts = stacked.reshape((members,) + lead + (cores, 2, span))
            low, high = parts[..., 0, :], parts[..., 1, :]
            both = jnp.concatenate([low, high[::-1]], axis=0)
            return jnp.moveaxis(both, 0, -2).reshape(lead + (GROUP,))

        pair = natural(pair)
        key_t, value_t = pair[0], pair[1]
        key_n = key_t.transpose(0, 2, 1)
        value_one = jnp.concatenate([value_t, jnp.ones((KVH, 16, GROUP), BF)], axis=1)
        mixed_f, logs = attend(first_tokens, query_use, key_n, value_one)
        mixed = mixed_f.reshape(QH * HD, mine).astype(BF)
        hidden = states + dot(mixed, w_out_all, ((0,), (0,)))

        inverse_two = rms(hidden)
        normed_two = (hidden * inverse_two * gain_two).astype(BF)

    if fast:
        normed_all, gate, up, activated, ffn_out, down_other, target = spread(
            True, normed_two, ffn_weights, dealt=teacher
        )
        ffn_weights.append(down_other)
    else:
        normed_all, gate, up, activated, ffn_out = spread(True, normed_two, ffn_weights)
        target = to_members(teacher)
    ffn_out = ffn_out.reshape(mine, D)
    result = hidden + ffn_out

    total_tokens = shard * cols * lax.axis_size("dp")
    loss_scale = total_tokens / token_count[0].astype(F32)
    d_result = loss_scale * (result - target.astype(F32))
    if fast:
        d_low, d_gate_up, d_normed, block_out = spread(
            False, d_result.astype(BF), ffn_weights, (gate, up), result.astype(BF)
        )
    else:
        d_low, d_gate_up, d_normed = spread(False, d_result.astype(BF), ffn_weights, (gate, up))
        block_out = from_members(result.astype(BF))
    d_normed = d_normed.reshape(mine, D)
    d_low, normed_all = d_low.reshape(-1, D), normed_all.reshape(-1, D)
    grad_down = dot(activated.reshape(-1, ff), d_low, ((0,), (0,))).astype(BF)
    grad_gate_up = dot(normed_all, d_gate_up.reshape(-1, 2 * ff), ((0,), (0,))).astype(BF)

    norm_two_part = jnp.sum(d_normed * hidden * inverse_two, axis=0)
    d_hidden = d_result + norm_back(hidden, inverse_two, gain_two, d_normed)
    d_hidden_low = d_hidden.astype(BF)
    grad_out = dot(mixed, d_hidden_low, ((1,), (0,))).astype(BF)
    d_mixed = dot(w_out_all, d_hidden_low, ((1,), (1,))).astype(BF)
    d_mixed = d_mixed.reshape(KVH, REP, HD, mine)
    delta = jnp.sum(d_mixed.astype(F32) * mixed_f, axis=2)
    d_query, d_key_n, d_value_n = attend_back(
        first_tokens, query_use, d_mixed, logs, delta, key_t, value_t
    )
    d_pair = dealt(jnp.stack([d_key_n, d_value_n])).astype(BF)
    d_pair = lax.psum_scatter(d_pair, ("row", "side"), scatter_dimension=0, tiled=True)[0]
    d_pair = d_pair.astype(F32).transpose(0, 1, 3, 2)
    d_query_raw, query_gain_part = query_back(d_query.reshape(QH, HD, mine) * scale)
    d_key_raw, key_gain_part = key_back(d_pair[0])
    d_projected = jnp.concatenate(
        [
            d_query_raw.reshape(cols, q_width, mine),
            d_key_raw.reshape(cols, k_width, mine),
            d_pair[1].reshape(cols, k_width, mine),
        ],
        axis=1,
    ).astype(BF)
    d_normed_one = dot(d_projected, w_project, ((0, 1), (0, 2)))
    grad_input = d_hidden + norm_back(states, inverse_one, gain_one, d_normed_one)
    norm_one_part = jnp.sum(d_normed_one * states * inverse_one, axis=0)
    grad_input = from_members(grad_input)

    grad_project = lax.dot_general(
        d_projected, normed_one, (((2,), (0,)), ((), ())), preferred_element_type=F32
    )
    grad_project = grad_project.astype(BF).transpose(0, 2, 1)
    grad_out = grad_out.reshape(cols, q_width, D)
    norm_one_part = jnp.roll(norm_one_part.reshape(rows, width), row_index, 0).reshape(D)
    norm_two_part = jnp.roll(norm_two_part.reshape(rows, width), row_index, 0).reshape(D)
    small = jnp.concatenate([norm_one_part, norm_two_part, query_gain_part, key_gain_part])
    if rows == 2 and cols == 4 and lax.axis_size("dp") == 4:
        padded = jnp.pad(small, (0, SMALL * 128 - small.shape[0])).reshape(SMALL, 128)
        grad_down, grad_gate_up, grad_out, grad_project, small = reduce_all(
            4,
            [(grad_down, 1, 128), (grad_gate_up, 0, 64), (grad_out, 1, 160), (grad_project, 0, 512)],
            padded,
        )
        small = small.reshape(-1)[: 2 * D + 2 * HD]
    else:
        small = lax.psum(small, ("dp", "row", "group", "side"))
        col_axes = ("group", "side")
        grad_project = lax.psum_scatter(grad_project, col_axes, scatter_dimension=0, tiled=True)
        grad_out = lax.psum_scatter(grad_out, col_axes, scatter_dimension=0, tiled=True)
        grad_down = sum_planes(scatter_rows(grad_down, 1), 2)
        grad_gate_up = sum_planes(scatter_rows(grad_gate_up, 0), 4)
        grad_out = sum_planes(scatter_rows(grad_out[0], 1), 1)
        grad_project = sum_planes(scatter_rows(grad_project[0], 0), 2)
    grad_norm1 = lax.dynamic_slice_in_dim(small, row_index * width, width, 0)
    grad_norm2 = lax.dynamic_slice_in_dim(small, D + row_index * width, width, 0)
    grad_project = grad_project.astype(F32)
    return (
        block_out,
        grad_input,
        grad_norm1,
        grad_project[:, :q_width],
        grad_project[:, q_width : q_width + k_width],
        grad_project[:, q_width + k_width :],
        small[2 * D : 2 * D + HD],
        small[2 * D + HD :],
        grad_out.astype(F32),
        grad_norm2,
        grad_gate_up[:, :ff].astype(F32),
        grad_gate_up[:, ff:].astype(F32),
        grad_down.astype(F32),
    )


def solution(mesh):
    dp, row, col = mesh.shape["dp"], mesh.shape["row"], mesh.shape["col"]

    def call(*args):
        side = GROUP * dp * col // args[0].shape[0]
        fine = Mesh(
            mesh.devices.reshape(dp, row, col // side, side), ("dp", "row", "group", "side")
        )
        col_axes = ("group", "side")
        token_spec = P(("dp", "group", "side"), "row")
        wide = P("row", col_axes)
        tall = P(col_axes, "row")
        return jax.shard_map(
            body,
            mesh=fine,
            in_specs=(
                token_spec,
                P("row"),
                wide,
                wide,
                wide,
                P(),
                P(),
                tall,
                P("row"),
                wide,
                wide,
                tall,
                token_spec,
                P("dp"),
                P(),
            ),
            out_specs=(
                token_spec,
                token_spec,
                P("row"),
                wide,
                wide,
                wide,
                P(),
                P(),
                tall,
                P("row"),
                wide,
                wide,
                tall,
            ),
            check_vma=False,
        )(*args)

    return call
```

```python
import functools
import math

import jax
import jax.numpy as jnp
from jax import lax
from jax.experimental import pallas as pl
from jax.experimental.pallas import tpu as pltpu
from jax.sharding import Mesh
from jax.sharding import PartitionSpec as P

D = 2048
QH = 20
KVH = 5
HD = 64
PROMPT = 1024
CONT = 128
NCONT = 8
GROUP = PROMPT + NCONT * CONT
REP = QH // KVH
KEYS = 256

EPSILON = 1e-06
BF = jnp.bfloat16
F32 = jnp.float32


def dot(left, right, dims=((1,), (0,))):
    return lax.dot_general(left, right, (dims, ((), ())), preferred_element_type=F32)


def rms(values):
    return lax.rsqrt(jnp.mean(values * values, axis=1, keepdims=True) + EPSILON)


def norm_back(states, inverse, gain, d_normed):
    mean = jnp.mean(states * gain * d_normed, axis=1, keepdims=True)
    return inverse * gain * d_normed - states * inverse**3 * mean


def prepare(raw, gain, cosine, sine):
    values = raw * lax.rsqrt(jnp.mean(raw * raw, axis=1, keepdims=True) + EPSILON)
    values = values * gain[None, :, None]
    half = HD // 2
    first, second = values[:, :half], values[:, half:]
    return jnp.concatenate(
        [first * cosine - second * sine, second * cosine + first * sine], axis=1
    )


def allowed(first_query, first_key, span, rows):
    key = first_key + lax.broadcasted_iota(jnp.int32, (KEYS, rows), 0)
    query = first_query + lax.broadcasted_iota(jnp.int32, (KEYS, rows), 1) % span
    return (key <= query) & ((key < PROMPT) | (key // CONT == query // CONT))


def side_by_side(ref, index, span):
    return jnp.concatenate(
        [ref[0, head, :, index * span : (index + 1) * span] for head in range(REP)], axis=1
    )


def tiles_of(first_query):
    last = first_query // KEYS
    return jnp.minimum(last, PROMPT // KEYS), last


def attend_kernel(chunks, span, first_ref, query_ref, key_ref, value_ref, out_ref, log_ref):
    rows = REP * span
    for index in range(chunks):
        query = side_by_side(query_ref, index, span)
        first_query = first_ref[index]
        full, last = tiles_of(first_query)

        def tile(where, accum, masked):
            first_key = pl.multiple_of(where * KEYS, KEYS)
            scores = dot(key_ref[0, pl.ds(first_key, KEYS), :], query)
            expo = jnp.exp(scores)
            if masked:
                expo = jnp.where(allowed(first_query, first_key, span, rows), expo, 0.0)
            return accum + dot(value_ref[0, :, pl.ds(first_key, KEYS)], expo.astype(BF))

        accum = tile(last, jnp.zeros((value_ref.shape[1], rows), F32), True)
        accum = lax.fori_loop(0, full, lambda where, total: tile(where, total, False), accum)
        total = accum[HD : HD + 1]
        mixed = accum[:HD] / total
        logs = jnp.log(total)
        for head in range(REP):
            cut = slice(head * span, (head + 1) * span)
            out_ref[0, head, :, index * span : (index + 1) * span] = mixed[:, cut]
            log_ref[0, head : head + 1, index * span : (index + 1) * span] = logs[:, cut]


def attend_back_kernel(
    chunks,
    span,
    first_ref,
    query_ref,
    d_out_ref,
    log_ref,
    delta_ref,
    key_t_ref,
    value_t_ref,
    d_query_ref,
    d_key_ref,
    d_value_ref,
    key_ref,
    value_ref,
):
    rows = REP * span
    key_ref[...] = key_t_ref[0].T
    value_ref[...] = value_t_ref[0].T
    d_key_ref[...] = jnp.zeros_like(d_key_ref)
    d_value_ref[...] = jnp.zeros_like(d_value_ref)
    for index in range(chunks):
        query = side_by_side(query_ref, index, span)
        d_out = side_by_side(d_out_ref, index, span)
        query_t = query.T
        d_out_t = d_out.T
        cut = slice(index * span, (index + 1) * span)
        logs = jnp.concatenate([log_ref[0, h : h + 1, cut] for h in range(REP)], axis=1)
        delta = jnp.concatenate([delta_ref[0, h : h + 1, cut] for h in range(REP)], axis=1)
        first_query = first_ref[index]
        full, last = tiles_of(first_query)

        def tile(where, accum, masked):
            first_key = pl.multiple_of(where * KEYS, KEYS)
            here = pl.ds(first_key, KEYS)
            probs = jnp.exp(dot(key_ref[here, :], query) - logs)
            if masked:
                probs = jnp.where(allowed(first_query, first_key, span, rows), probs, 0.0)
            d_probs = dot(value_ref[here, :], d_out)
            d_scores = (probs * (d_probs - delta)).astype(BF)
            d_value_ref[0, here, :] += dot(probs.astype(BF), d_out_t)
            d_key_ref[0, here, :] += dot(d_scores, query_t)
            return accum + dot(key_t_ref[0, :, here], d_scores)

        accum = tile(last, jnp.zeros((HD, rows), F32), True)
        accum = lax.fori_loop(0, full, lambda where, total: tile(where, total, False), accum)
        for head in range(REP):
            part = accum[:, head * span : (head + 1) * span]
            d_query_ref[0, head, :, cut] = part


def per_head(shape):
    return pl.BlockSpec((1,) + shape, lambda head, first: (head,) + (0,) * len(shape))


def attend(first, query, key, value_t):
    tokens = query.shape[-1]
    chunks = first.shape[0]
    return pl.pallas_call(
        functools.partial(attend_kernel, chunks, tokens // chunks),
        out_shape=(
            jax.ShapeDtypeStruct((KVH, REP, HD, tokens), F32),
            jax.ShapeDtypeStruct((KVH, REP, tokens), F32),
        ),
        grid_spec=pltpu.PrefetchScalarGridSpec(
            num_scalar_prefetch=1,
            grid=(KVH,),
            in_specs=[
                per_head((REP, HD, tokens)),
                per_head((GROUP, HD)),
                per_head((value_t.shape[1], GROUP)),
            ],
            out_specs=[per_head((REP, HD, tokens)), per_head((REP, tokens))],
        ),
        compiler_params=pltpu.CompilerParams(vmem_limit_bytes=32 * 1024 * 1024),
        name="attend",
    )(first, query, key, value_t)


def attend_back(first, query, d_out, logs, delta, key_t, value_t):
    tokens = query.shape[-1]
    chunks = first.shape[0]
    return pl.pallas_call(
        functools.partial(attend_back_kernel, chunks, tokens // chunks),
        out_shape=(
            jax.ShapeDtypeStruct((KVH, REP, HD, tokens), F32),
            jax.ShapeDtypeStruct((KVH, GROUP, HD), F32),
            jax.ShapeDtypeStruct((KVH, GROUP, HD), F32),
        ),
        grid_spec=pltpu.PrefetchScalarGridSpec(
            num_scalar_prefetch=1,
            grid=(KVH,),
            in_specs=[
                per_head((REP, HD, tokens)),
                per_head((REP, HD, tokens)),
                per_head((REP, tokens)),
                per_head((REP, tokens)),
                per_head((HD, GROUP)),
                per_head((HD, GROUP)),
            ],
            out_specs=[
                per_head((REP, HD, tokens)),
                per_head((GROUP, HD)),
                per_head((GROUP, HD)),
            ],
            scratch_shapes=[pltpu.VMEM((GROUP, HD), BF), pltpu.VMEM((GROUP, HD), BF)],
        ),
        compiler_params=pltpu.CompilerParams(vmem_limit_bytes=32 * 1024 * 1024),
        name="attend_back",
    )(first, query, d_out, logs, delta, key_t, value_t)


AHEAD = 4
SLOTS = AHEAD + 2
FAR_LAG, WIDE_LAG, LAG = 1, 2, 4
SMALL = 40


class Part:
    def __init__(self, axis, rows, cols, count, base, col):
        self.axis, self.rows, self.cols = axis, rows, cols
        self.count, self.base, self.col = count, base, col

    def cut(self, ref, index, half, lead=()):
        first = pl.ds(index * self.rows, self.rows)
        if self.axis == 0:
            first = pl.ds((half * self.count + index) * self.rows, self.rows)
            return ref.at[(*lead, first, slice(None))]
        return ref.at[(*lead, first, pl.ds(half * self.cols, self.cols))]


def reduce_kernel(parts, planes, *refs):
    count = len(parts)
    refs = list(refs)

    def take(number):
        taken = refs[:number]
        del refs[:number]
        return taken

    grads = take(count)
    (small_ref, mine_ref) = take(2)
    outs = take(count)
    (small_out, dealt_ref) = take(2)
    near, far, wide, own = take(count), take(count), take(count), take(count)
    col_parts = [j for j in range(count) if parts[j].col]
    mate_in = dict(zip(col_parts, take(len(col_parts))))
    far_in = dict(zip(col_parts, take(len(col_parts))))
    own_sem, out_sem, row_send, row_recv, in_send, far_recv, mid_send, wide_recv = take(8)
    col_own, col_send, col_recv, x_send, x_recv, small_local, small_send, small_recv = take(8)
    small_in, small_sum, deal_send, deal_recv, deal_local = take(5)
    plane, row = lax.axis_index("dp"), lax.axis_index("row")
    group, side = lax.axis_index("group"), lax.axis_index("side")
    other_row, mate, far_dev = {"row": 1 - row}, {"side": 1 - side}, {"group": 1 - group}
    cross = {"row": 1 - row, "side": 1 - side}
    at_end = (plane == 0) | (plane == planes - 1)
    low = plane < planes // 2
    end_next = {"dp": jnp.where(low, 1, planes - 2)}
    mid_outer = {"dp": jnp.where(low, 0, planes - 1)}
    mid_other = {"dp": jnp.where(low, planes // 2, planes // 2 - 1)}

    def remote(source, target, send, recv, where):
        return pltpu.make_async_remote_copy(
            source, target, send, recv, device_id=where, device_id_type=pl.DeviceIdType.MESH
        )

    barrier = pltpu.get_barrier_semaphore()

    def greet(where):
        pl.semaphore_signal(barrier, 1, device_id=where, device_id_type=pl.DeviceIdType.MESH)

    for where in (other_row, mate, far_dev, cross):
        greet(where)

    @pl.when(at_end)
    def _():
        greet(end_next)
        pl.semaphore_wait(barrier, 5)

    @pl.when(jnp.logical_not(at_end))
    def _():
        greet(mid_outer)
        greet(mid_other)
        pl.semaphore_wait(barrier, 6)

    def col_slot(j, half, index):
        before = sum(2 * parts[i].count for i in col_parts if i < j)
        return before + half * parts[j].count + index

    def col_own_copy(j, half, index, target):
        return pltpu.make_async_copy(
            parts[j].cut(grads[j], index, half, (2 * target + side,)),
            own[j].at[target, half, index],
            col_own.at[target, col_slot(j, half, index)],
        )

    def col_copy(j, half, index, target):
        slot = col_slot(j, half, index)
        return remote(
            parts[j].cut(grads[j], index, half, (2 * target + 1 - side,)),
            mate_in[j].at[target, half, index],
            col_send.at[target, slot],
            col_recv.at[target, slot],
            mate,
        )

    def x_copy(j, half, index):
        slot = col_slot(j, half, index)
        return remote(
            mate_in[j].at[1 - group, half, index],
            far_in[j].at[half, index],
            x_send.at[slot],
            x_recv.at[slot],
            far_dev,
        )

    def take_col(j, half, index):
        for target in range(2):
            col_own_copy(j, half, index, target).wait()
            col_copy(j, half, index, target).wait_recv()
            mate_in[j][target, half, index] = mate_in[j][target, half, index] + own[j][target, half, index]
        x_copy(j, half, index).start()

    def take_x(j, half, index):
        x_copy(j, half, index).wait_recv()
        far_in[j][half, index] = far_in[j][half, index] + mate_in[j][group, half, index]

    def row_copy(j, index):
        slot = parts[j].base + index
        source = far_in[j].at[1, index] if parts[j].col else parts[j].cut(grads[j], index, 1)
        return remote(source, near[j].at[index], row_send.at[slot], row_recv.at[slot], other_row)

    def in_copy(j, index):
        slot = parts[j].base + index
        return remote(near[j].at[index], far[j].at[index], in_send.at[slot], far_recv.at[slot], end_next)

    def mid_copy(j, index):
        slot = parts[j].base + index
        return remote(far[j].at[index], wide[j].at[index], mid_send.at[slot], wide_recv.at[slot], mid_other)

    def back_copy(j, index):
        slot = parts[j].base + index
        return remote(wide[j].at[index], far[j].at[index], in_send.at[slot], far_recv.at[slot], mid_outer)

    def out_copy(j, index, source):
        slot = parts[j].base + index
        return pltpu.make_async_copy(source[j].at[index], parts[j].cut(outs[j], index, 0), out_sem.at[slot])

    def own_copy(j, index):
        slot = parts[j].base + index
        return pltpu.make_async_copy(
            parts[j].cut(grads[j], index, 0), own[j].at[index % SLOTS], own_sem.at[slot]
        )

    def each(step, action):
        for j, part in enumerate(parts):
            index = step - part.base

            @pl.when((index >= 0) & (index < part.count))
            def _(j=j, index=index):
                action(j, index)

    def send_row(j, index):
        if not parts[j].col:
            own_copy(j, index).start()
        row_copy(j, index).start()

    def take_row(j, index):
        row_copy(j, index).wait_recv()
        if parts[j].col:
            mine = far_in[j][0, index]
        else:
            own_copy(j, index).wait()
            mine = own[j][index % SLOTS]
        near[j][index] = near[j][index] + mine

        @pl.when(at_end)
        def _():
            in_copy(j, index).start()

    def take_far(j, index):
        back_copy(j, index).wait_recv()
        far[j][index] = far[j][index] + near[j][index]
        mid_copy(j, index).start()

    def take_wide(j, index):
        mid_copy(j, index).wait_recv()
        wide[j][index] = wide[j][index] + far[j][index]
        back_copy(j, index).start()
        out_copy(j, index, wide).start()

    def take_back(j, index):
        in_copy(j, index).wait_recv()
        out_copy(j, index, far).start()

    def finish_end(j, index):
        row_copy(j, index).wait_send()
        in_copy(j, index).wait_send()
        out_copy(j, index, far).wait()

    def finish_mid(j, index):
        row_copy(j, index).wait_send()
        mid_copy(j, index).wait_send()
        back_copy(j, index).wait_send()
        out_copy(j, index, wide).wait()

    def small_copy(stage, source, where):
        return remote(small_sum.at[source], small_in.at[stage], small_send.at[stage], small_recv.at[stage], where)

    plane_hops = [small_copy(0, 0, mate), small_copy(1, 1, far_dev), small_copy(2, 2, other_row)]
    small_end = small_copy(3, 3, end_next)
    small_mid = small_copy(4, 4, mid_other)
    small_back = small_copy(3, 5, mid_outer)
    small_load = pltpu.make_async_copy(small_ref, small_sum.at[0], small_local.at[0])
    small_store = pltpu.make_async_copy(small_sum.at[5], small_out, small_local.at[1])

    span, width = mine_ref.shape[0] // 4, mine_ref.shape[1] // 2
    member = 2 * row + side
    dealt = []
    for index, (to_row, to_side, where) in enumerate(
        [(1 - row, side, other_row), (1 - row, 1 - side, cross), (row, 1 - side, mate), (row, side, None)]
    ):
        for high in range(2):
            piece = 7 - member if high else member
            first = pl.multiple_of(to_side * 2 * span + high * span, span)
            source = mine_ref.at[pl.ds(first, span), pl.ds((0 if index >= 2 else 1) * width, width)]
            target = dealt_ref.at[pl.ds(pl.multiple_of(piece * span, span), span), :]
            if where is None:
                dealt.append(pltpu.make_async_copy(source, target, deal_local.at[high]))
            else:
                dealt.append(remote(source, target, deal_send.at[index, high], deal_recv.at[index, high], where))

    total = sum(part.count for part in parts)
    small_load.start()
    for copy in dealt[4:]:
        copy.start()
    for j in col_parts:
        for half in (1, 0):
            for index in range(parts[j].count):
                for target in range(2):
                    col_own_copy(j, half, index, target).start()
                    col_copy(j, half, index, target).start()

    @pl.loop(0, AHEAD)
    def _(step):
        each(step, send_row)

    pieces = [(j, half, index) for j in col_parts for half in (1, 0) for index in range(parts[j].count)]

    @pl.loop(0, total + LAG)
    def _(step):
        each(step + AHEAD, send_row)
        each(step, take_row)

        @pl.when(at_end)
        def _():
            each(step - LAG, take_back)

        @pl.when(jnp.logical_not(at_end))
        def _():
            each(step - FAR_LAG, take_far)
            each(step - WIDE_LAG, take_wide)

        @pl.when(step == total - AHEAD)
        def _():
            for copy in dealt[:4]:
                copy.start()

        for place, piece in enumerate(pieces):
            @pl.when(step == place + 1)
            def _(piece=piece):
                take_col(*piece)

            @pl.when(step == place + 5)
            def _(piece=piece):
                take_x(*piece)

        @pl.when(step == 0)
        def _():
            small_load.wait()
            plane_hops[0].start()

        for hop in range(3):
            @pl.when(step == hop + 1)
            def _(hop=hop):
                plane_hops[hop].wait_recv()
                small_sum[hop + 1] = small_sum[hop] + small_in[hop]
                if hop < 2:
                    plane_hops[hop + 1].start()

        @pl.when(at_end & (step == 3))
        def _():
            small_end.start()

        @pl.when(at_end & (step == 10))
        def _():
            small_end.wait_recv()
            small_sum[5] = small_in[3]
            small_store.start()

        @pl.when(jnp.logical_not(at_end) & (step == 5))
        def _():
            small_back.wait_recv()
            small_sum[4] = small_sum[3] + small_in[3]
            small_mid.start()

        @pl.when(jnp.logical_not(at_end) & (step == 7))
        def _():
            small_mid.wait_recv()
            small_sum[5] = small_sum[4] + small_in[4]
            small_back.start()
            small_store.start()

    for copy in plane_hops:
        copy.wait_send()
    small_store.wait()
    for copy in dealt:
        copy.wait()
    for j, half, index in pieces:
        for target in range(2):
            col_copy(j, half, index, target).wait_send()
        x_copy(j, half, index).wait_send()

    @pl.when(at_end)
    def _():
        small_end.wait_send()

        @pl.loop(0, total)
        def _(step):
            each(step, finish_end)

    @pl.when(jnp.logical_not(at_end))
    def _():
        small_mid.wait_send()
        small_back.wait_send()

        @pl.loop(0, total)
        def _(step):
            each(step, finish_mid)


def reduce_all(planes, grads, small, mine):
    parts, base = [], 0
    for grad, axis, rows in grads:
        height, width = grad.shape[-2:]
        height, width = (height // 2, width) if axis == 0 else (height, width // 2)
        parts.append(Part(axis, rows, width, height // rows, base, grad.ndim == 3))
        base += height // rows
    shapes = [(part.count, part.rows, part.cols) for part in parts]
    col_shapes = [(2, *shape) for part, shape in zip(parts, shapes) if part.col]
    pieces = sum(shape[1] * 2 for shape in col_shapes)
    own_shapes = [
        (2, 2, *shape) if part.col else (SLOTS, *shape[1:]) for part, shape in zip(parts, shapes)
    ]
    anywhere = pl.BlockSpec(memory_space=pl.ANY)
    dma = pltpu.SemaphoreType.DMA
    return pl.pallas_call(
        functools.partial(reduce_kernel, parts, planes),
        out_shape=[jax.ShapeDtypeStruct((n * r, c), BF) for n, r, c in shapes]
        + [
            jax.ShapeDtypeStruct(small.shape, F32),
            jax.ShapeDtypeStruct((2 * mine.shape[0], mine.shape[1] // 2), BF),
        ],
        in_specs=[anywhere] * (len(parts) + 2),
        out_specs=[anywhere] * (len(parts) + 2),
        scratch_shapes=[pltpu.VMEM(shape, BF) for _ in range(3) for shape in shapes]
        + [pltpu.VMEM(shape, BF) for shape in own_shapes]
        + [pltpu.VMEM((2, *shape), BF) for shape in col_shapes]
        + [pltpu.VMEM(shape, BF) for shape in col_shapes]
        + [dma((base,)) for _ in range(8)]
        + [dma((2, pieces)), dma((2, pieces)), dma((2, pieces)), dma((pieces,)), dma((pieces,))]
        + [dma((2,)), dma((5,)), dma((5,))]
        + [pltpu.VMEM((5, *small.shape), F32), pltpu.VMEM((6, *small.shape), F32)]
        + [dma((3, 2)), dma((3, 2)), dma((2,))],
        compiler_params=pltpu.CompilerParams(
            collective_id=0, has_side_effects=True, vmem_limit_bytes=60 * 1024 * 1024
        ),
        name="reduce_grads",
    )(*[grad for grad, _, _ in grads], small, mine)


TILE = 256
STEPS = 8


def spread_kernel(forward, fast, *refs):
    refs = list(refs)

    def take(number):
        taken = refs[:number]
        del refs[:number]
        return taken

    (mine_ref,) = take(1)
    weights = take(5 if forward and fast else 6)
    if not forward:
        gate_ref, up_ref = take(2)
    dealt_in = take(1) if fast else None
    if forward:
        all_ref, gate_ref, up_ref, act_ref, out_ref = take(5)
        if fast:
            (down_out,) = take(1)
    else:
        all_ref, d_gate_up_ref, out_ref = take(3)
    dealt_out = take(1) if fast else None
    block, w_gate, w_up, w_down, kept, to_mate, from_mate, far_part, to_far, from_mate_far, far_sum, from_far = take(12)
    (
        weight_sem, block_sem, out_sem, mate_send, mate_recv, x_send, x_recv, pass_send, pass_recv,
        sum_send, sum_recv, part_send, part_recv, back_send, back_recv,
    ) = take(15)
    deal_send, deal_recv, deal_local, row_send, row_recv, plane_send, plane_recv = take(7)
    stage = refs
    tokens, depth = mine_ref.shape
    quarter = tokens // 4
    width = w_gate.shape[1]
    half = depth // 2
    row = lax.axis_index("row")
    group, side = lax.axis_index("group"), lax.axis_index("side")
    mate, far = {"side": 1 - side}, {"group": 1 - group}
    other_row, cross = {"row": 1 - row}, {"row": 1 - row, "side": 1 - side}
    parity = lax.axis_index("dp") % 2
    next_plane = {"dp": lax.axis_index("dp") + 1 - 2 * parity}

    def remote(source, target, send, recv, where):
        return pltpu.make_async_remote_copy(
            source, target, send, recv, device_id=where, device_id_type=pl.DeviceIdType.MESH
        )

    barrier = pltpu.get_barrier_semaphore()
    greeted = [mate, far]
    if fast:
        greeted += [other_row, cross] + ([next_plane] if forward else [])
    for where in greeted:
        pl.semaphore_signal(barrier, 1, device_id=where, device_id_type=pl.DeviceIdType.MESH)

    dealt_own, dealt_sent, down_chunks = [], [], []
    if fast:
        span = tokens // 4
        member = 2 * row + side
        for index, (to_row, to_side, where) in enumerate(
            [(1 - row, side, other_row), (1 - row, 1 - side, cross), (row, 1 - side, mate), (row, side, None)]
        ):
            slot = 0 if index >= 2 else 1
            there = 2 * to_row + to_side
            for high in range(2):
                piece = 7 - there if high else there
                if not forward:
                    piece = 7 - member if high else member
                whole = pl.ds(pl.multiple_of(piece * span, span), span), slice(None)
                of_side = side if forward else to_side
                first = pl.multiple_of(of_side * 2 * span + high * span, span)
                part = pl.ds(first, span), pl.ds(slot * half, half)
                source = dealt_in[0].at[whole] if forward else dealt_in[0].at[part]
                target = dealt_out[0].at[part] if forward else dealt_out[0].at[whole]
                if where is None:
                    dealt_own.append(pltpu.make_async_copy(source, target, deal_local.at[high]))
                else:
                    sems = deal_send.at[index, high], deal_recv.at[index, high]
                    dealt_sent.append(remote(source, target, *sems, where))
        if forward:
            rows = width // 8
            for index in range(4):
                here = pl.ds(pl.multiple_of((4 * parity + index) * rows, 16), rows)
                place = w_down.at[here, pl.ds(half, half)]
                down_chunks.append(
                    (
                        remote(weights[4].at[here, :], place, row_send.at[index], row_recv.at[index], other_row),
                        remote(place, place, plane_send.at[index], plane_recv.at[index], next_plane),
                    )
                )

    loads = []
    for index, (source, target) in enumerate(
        [
            (weights[0], w_gate.at[pl.ds(0, half), :]),
            (weights[1], w_gate.at[pl.ds(half, half), :]),
            (weights[2], w_up.at[pl.ds(0, half), :]),
            (weights[3], w_up.at[pl.ds(half, half), :]),
            (weights[4], w_down.at[:, pl.ds(0, half)]),
        ]
        + ([] if forward and fast else [(weights[5], w_down.at[:, pl.ds(half, half)])])
    ):
        loads.append(pltpu.make_async_copy(source, target, weight_sem.at[index]))
    order = loads if forward else loads[4:] + loads[:4]
    mine_copies = [
        pltpu.make_async_copy(
            mine_ref.at[pl.ds(i * 2 * quarter, 2 * quarter), :], block.at[i], block_sem.at[i]
        )
        for i in range(2)
    ]
    for copy in mine_copies:
        copy.start()
    for copy in order:
        copy.start()
    pl.semaphore_wait(barrier, len(greeted))
    for over_row, over_planes in down_chunks:
        over_row.start()

    def piece(index):
        return mine_ref.at[pl.ds(index * quarter, quarter), :]

    def mate_copy(index):
        return remote(
            piece(index),
            block.at[2 + index // 2, pl.ds(index % 2 * quarter, quarter), :],
            mate_send.at[index],
            mate_recv.at[index],
            mate,
        )

    def x_copy(index):
        return remote(
            piece(index), block.at[4 + index, pl.ds(0, quarter), :], x_send.at[index], x_recv.at[index], far
        )

    def pass_copy(index):
        return remote(
            block.at[4 + index, pl.ds(0, quarter), :],
            block.at[4 + index, pl.ds(quarter, quarter), :],
            pass_send.at[index],
            pass_recv.at[index],
            mate,
        )

    def sum_copy(index):
        return remote(to_mate.at[index], from_mate.at[index], sum_send.at[index], sum_recv.at[index], mate)

    def part_copy(index):
        return remote(to_far.at[index], from_mate_far.at[index], part_send.at[index], part_recv.at[index], mate)

    def back_copy(index):
        return remote(far_sum.at[index], from_far.at[index], back_send.at[index], back_recv.at[index], far)

    x_copy(0).start()
    for index in range(4):
        mate_copy(index).start()
    x_copy(1).start()
    for copy in dealt_sent + dealt_own:
        copy.start()
    for copy in mine_copies:
        copy.wait()

    def emit(step, where, part):
        @pl.when(step < 2)
        def _():
            kept[jnp.minimum(step, 1), :, where] = part

        @pl.when((step >= 2) & (step < 4))
        def _():
            to_mate[jnp.clip(step - 2, 0, 1), :, where] = part.astype(BF)

        @pl.when(step >= 4)
        def _():
            far_part[jnp.maximum(step - 4, 0), :, where] = part[:quarter]
            to_far[jnp.maximum(step - 4, 0), :, where] = part[quarter:].astype(BF)

    def all_copy(step):
        return pltpu.make_async_copy(block.at[step], all_ref.at[step], out_sem.at[0, step])

    if forward:
        stage_gate, stage_up, stage_act = stage

        def saves(step):
            slot = step % 2
            return [
                pltpu.make_async_copy(stage_gate.at[slot], gate_ref.at[step], out_sem.at[1, step]),
                pltpu.make_async_copy(stage_up.at[slot], up_ref.at[step], out_sem.at[2, step]),
                pltpu.make_async_copy(stage_act.at[step], act_ref.at[step], out_sem.at[3, step]),
            ]

        def fetches(step):
            return []

        def first_loads():
            for copy in loads[:4]:
                copy.wait()

        def second_loads():
            for copy in loads[4:]:
                copy.wait()

        def first_half(step):
            slot = step % 2

            @pl.loop(0, width // TILE)
            def _(tile):
                where = pl.ds(pl.multiple_of(tile * TILE, TILE), TILE)
                gate = dot(block[step], w_gate[:, where])
                up = dot(block[step], w_up[:, where])
                stage_gate[slot, :, where] = gate.astype(BF)
                stage_up[slot, :, where] = up.astype(BF)
                stage_act[step, :, where] = (gate * up / (1.0 + jnp.exp(-gate))).astype(BF)

        def second_half(step, first=0, last=depth // TILE):
            @pl.loop(first, last)
            def _(tile):
                where = pl.ds(pl.multiple_of(tile * TILE, TILE), TILE)
                emit(step, where, dot(stage_act[step], w_down[:, where]))

    else:
        stage_gate, stage_up, stage_d, fetch_sem = stage

        def saves(step):
            return [
                pltpu.make_async_copy(stage_d.at[step % 2], d_gate_up_ref.at[step], out_sem.at[1, step])
            ]

        def fetches(step):
            slot = step % 2
            return [
                pltpu.make_async_copy(gate_ref.at[step], stage_gate.at[slot], fetch_sem.at[0, step]),
                pltpu.make_async_copy(up_ref.at[step], stage_up.at[slot], fetch_sem.at[1, step]),
            ]

        def first_loads():
            for copy in loads[4:]:
                copy.wait()

        def second_loads():
            for copy in loads[:4]:
                copy.wait()

        def first_half(step):
            slot = step % 2

            @pl.loop(0, width // TILE)
            def _(tile):
                first = pl.multiple_of(tile * TILE, TILE)
                where = pl.ds(first, TILE)
                d_act = dot(block[step], w_down[where, :], ((1,), (1,)))
                gate = stage_gate[slot, :, where].astype(F32)
                up = stage_up[slot, :, where].astype(F32)
                sig = 1.0 / (1.0 + jnp.exp(-gate))
                d_gate = d_act * up * sig * (1.0 + gate * (1.0 - sig))
                stage_d[slot, :, where] = d_gate.astype(BF)
                stage_d[slot, :, pl.ds(pl.multiple_of(width + first, TILE), TILE)] = (d_act * gate * sig).astype(BF)

        def second_half(step):
            slot = step % 2

            @pl.loop(0, depth // TILE)
            def _(tile):
                where = pl.ds(pl.multiple_of(tile * TILE, TILE), TILE)
                part = dot(stage_d[slot, :, :width], w_gate[where, :], ((1,), (1,)))
                part += dot(stage_d[slot, :, width:], w_up[where, :], ((1,), (1,)))
                emit(step, where, part)

    def finish_far(index):
        part_copy(index).wait_recv()
        total = far_part[index] + from_mate_far[index].astype(F32)
        far_sum[index] = total.astype(BF)
        back_copy(index).start()

    if forward and fast:
        down_saved = pltpu.make_async_copy(w_down.at[:, pl.ds(half, half)], down_out, weight_sem.at[5])
    for copy in fetches(0):
        copy.start()

    @pl.loop(0, STEPS)
    def _(step):
        @pl.when((step == 2) | (step == 3))
        def _():
            index = jnp.clip(2 * (step - 2), 0, 2)
            mate_copy(index).wait_recv()
            mate_copy(index + 1).wait_recv()

        @pl.when(step >= 4)
        def _():
            index = jnp.maximum(step - 4, 0)
            x_copy(index).wait_recv()
            pass_copy(index).start()
            pass_copy(index).wait_recv()

        all_copy(step).start()
        for copy in fetches(step):
            copy.wait()

        if not forward:
            @pl.when(step < STEPS - 1)
            def _():
                for copy in fetches(jnp.minimum(step + 1, STEPS - 1)):
                    copy.start()

        @pl.when(step == 0)
        def _():
            first_loads()

        @pl.when(step >= 2)
        def _():
            for copy in saves(jnp.maximum(step - 2, 0)):
                copy.wait()

        first_half(step)

        @pl.when(step == 0)
        def _():
            second_loads()

        if forward and fast:
            @pl.when(step < 4)
            def _():
                second_half(step, 0, half // TILE)

            for index in range(4):
                @pl.when(step == min(index + 1, 3))
                def _(index=index):
                    down_chunks[index][0].wait_recv()
                    down_chunks[index][1].start()

            @pl.when(step == 3)
            def _():
                for _, over_planes in down_chunks:
                    over_planes.wait_recv()
                down_saved.start()

                @pl.loop(0, 4)
                def _(early):
                    second_half(early, half // TILE)

                sum_copy(0).start()

            @pl.when(step >= 4)
            def _():
                second_half(step)
        else:
            second_half(step)
        for copy in saves(step):
            copy.start()

        @pl.when((step == 1) | (step == 3))
        def _():
            x_copy(2 + step // 2).start()

        @pl.when((step == 3) if forward and fast else ((step >= 2) & (step < 4)))
        def _():
            sum_copy(jnp.clip(step - 2, 0, 1)).start()

        @pl.when(step >= 4)
        def _():
            part_copy(jnp.maximum(step - 4, 0)).start()

        @pl.when(step >= 5)
        def _():
            finish_far(jnp.maximum(step - 5, 0))

    finish_far(3)
    for index in range(2):
        sum_copy(index).wait_recv()
        kept[index] = kept[index] + from_mate[index].astype(F32)
    results = []
    for index in range(4):
        back_copy(index).wait_recv()
        rows = pl.ds(index % 2 * quarter, quarter)
        kept[index // 2, rows, :] = kept[index // 2, rows, :] + from_far[index].astype(F32)
        if index % 2:
            copy = pltpu.make_async_copy(kept.at[index // 2], out_ref.at[index // 2], block_sem.at[index // 2])
            copy.start()
            results.append(copy)
    for copy in results + dealt_own:
        copy.wait()
    for copy in dealt_sent:
        copy.wait()
    for over_row, over_planes in down_chunks:
        over_row.wait_send()
        over_planes.wait_send()
    if forward and fast:
        down_saved.wait()

    @pl.loop(0, STEPS)
    def _(step):
        all_copy(step).wait()

        @pl.when(step >= STEPS - 2)
        def _():
            for copy in saves(step):
                copy.wait()

        @pl.when(step < 4)
        def _():
            index = jnp.minimum(step, 3)
            mate_copy(index).wait_send()
            x_copy(index).wait_send()
            pass_copy(index).wait_send()
            part_copy(index).wait_send()
            back_copy(index).wait_send()

        @pl.when(step < 2)
        def _():
            sum_copy(jnp.minimum(step, 1)).wait_send()


def spread(forward, mine, weights, kept=(), dealt=None):
    tokens, depth = mine.shape
    quarter, double = tokens // 4, tokens // 2
    width = weights[0].shape[1]
    anywhere = pl.BlockSpec(memory_space=pl.ANY)
    wide = jax.ShapeDtypeStruct((STEPS, double, width), BF)
    whole = jax.ShapeDtypeStruct((STEPS, double, depth), BF)
    out = jax.ShapeDtypeStruct((2, double, depth), F32)
    if forward:
        outs = [whole, wide, wide, wide, out]
        if dealt is not None:
            outs.append(jax.ShapeDtypeStruct((width, depth // 2), BF))
            outs.append(jax.ShapeDtypeStruct((tokens, depth), BF))
        stage = [
            pltpu.VMEM((2, double, width), BF),
            pltpu.VMEM((2, double, width), BF),
            pltpu.VMEM((STEPS, double, width), BF),
        ]
    else:
        outs = [whole, jax.ShapeDtypeStruct((STEPS, double, 2 * width), BF), out]
        if dealt is not None:
            outs.append(jax.ShapeDtypeStruct((2 * tokens, depth // 2), BF))
        stage = [
            pltpu.VMEM((2, double, width), BF),
            pltpu.VMEM((2, double, width), BF),
            pltpu.VMEM((2, double, 2 * width), BF),
            pltpu.SemaphoreType.DMA((2, STEPS)),
        ]
    inputs = [mine, *weights, *kept] + ([] if dealt is None else [dealt])
    return pl.pallas_call(
        functools.partial(spread_kernel, forward, dealt is not None),
        out_shape=outs,
        in_specs=[anywhere] * len(inputs),
        out_specs=[anywhere] * len(outs),
        scratch_shapes=[
            pltpu.VMEM((STEPS, double, depth), BF),
            pltpu.VMEM((depth, width), BF),
            pltpu.VMEM((depth, width), BF),
            pltpu.VMEM((width, depth), BF),
            pltpu.VMEM((2, double, depth), F32),
            pltpu.VMEM((2, double, depth), BF),
            pltpu.VMEM((2, double, depth), BF),
            pltpu.VMEM((4, quarter, depth), F32),
            pltpu.VMEM((4, quarter, depth), BF),
            pltpu.VMEM((4, quarter, depth), BF),
            pltpu.VMEM((4, quarter, depth), BF),
            pltpu.VMEM((4, quarter, depth), BF),
            pltpu.SemaphoreType.DMA((6,)),
            pltpu.SemaphoreType.DMA((2,)),
            pltpu.SemaphoreType.DMA((4, STEPS)),
        ]
        + [pltpu.SemaphoreType.DMA((4,)) for _ in range(6)]
        + [pltpu.SemaphoreType.DMA((2,)) for _ in range(2)]
        + [pltpu.SemaphoreType.DMA((4,)) for _ in range(4)]
        + [pltpu.SemaphoreType.DMA((3, 2)), pltpu.SemaphoreType.DMA((3, 2)), pltpu.SemaphoreType.DMA((2,))]
        + [pltpu.SemaphoreType.DMA((4,)) for _ in range(4)]
        + stage,
        compiler_params=pltpu.CompilerParams(
            collective_id=1 if forward else 2,
            has_side_effects=True,
            vmem_limit_bytes=60 * 1024 * 1024,
        ),
        name="feed_forward" if forward else "feed_forward_back",
    )(*inputs)


def front_kernel(*refs):
    refs = list(refs)

    def take(number):
        taken = refs[:number]
        del refs[:number]
        return taken

    tokens_ref, w_project_ref, w_out_ref, gains_ref, gate_ref, up_ref = take(6)
    cos_ref, sin_ref, query_gain_ref, key_gain_ref = take(4)
    (
        states_out, normed_out, raw_out, query_out, key_out, pair_out, mixed_out, logs_out, hidden_out, normed_two_out,
        w_project_out, w_out_out, gate_out, up_out, gains_out,
    ) = take(15)
    states, normed, w_project, raw, key_raw, query, pair_own, pair, key_n, mixed_t, logs, mixed = take(12)
    w_out, hidden, gains = take(3)
    token_send, token_recv, token_local = take(3)
    project_send, project_recv, out_send, out_recv, gain_send, gain_recv = take(6)
    pair_send, pair_recv, row_send, row_recv, plane_send, plane_recv, local, store = take(8)

    plane, row = lax.axis_index("dp"), lax.axis_index("row")
    group, side = lax.axis_index("group"), lax.axis_index("side")
    other_row, mate, far = {"row": 1 - row}, {"side": 1 - side}, {"group": 1 - group}
    cross = {"row": 1 - row, "side": 1 - side}
    parity = plane % 2
    next_plane = {"dp": plane + 1 - 2 * parity}
    shard, width = tokens_ref.shape
    mine, depth = states.shape
    pieces = 8
    span = shard // pieces
    member = 2 * row + side
    kv_rows = key_raw.shape[0]

    def remote(source, target, send, recv, where):
        return pltpu.make_async_remote_copy(
            source, target, send, recv, device_id=where, device_id_type=pl.DeviceIdType.MESH
        )

    barrier = pltpu.get_barrier_semaphore()
    for where in (other_row, mate, far, cross, next_plane):
        pl.semaphore_signal(barrier, 1, device_id=where, device_id_type=pl.DeviceIdType.MESH)

    def token_copies(to_row, to_side, index, where):
        target_member = 2 * to_row + to_side
        slot = 1 if to_row is not row else 0
        copies = []
        for high in range(2):
            piece = pieces - 1 - target_member if high else target_member
            source = tokens_ref.at[pl.ds(pl.multiple_of(piece * span, span), span), :]
            first = pl.multiple_of(side * 2 * span + high * span, span)
            target = states.at[pl.ds(first, span), pl.ds(slot * width, width)]
            if where is None:
                copies.append(pltpu.make_async_copy(source, target, token_local.at[high]))
            else:
                sems = token_send.at[index, high], token_recv.at[index, high]
                copies.append(remote(source, target, *sems, where))
        return copies

    own_tokens = token_copies(row, side, 0, None)
    other = 1 - row
    sent_tokens = token_copies(other, side, 0, other_row)
    sent_tokens += token_copies(other, 1 - side, 1, cross)
    sent_tokens += token_copies(row, 1 - side, 2, mate)

    me, far_col = 2 * group + side, 2 * (1 - group) + side

    class Spread:
        def __init__(self, source, place, send, recv):
            self.copies = []

            def add(origin, target, where):
                index = len(self.copies)
                self.copies.append(remote(origin, target, send.at[index], recv.at[index], where))
                return self.copies[-1]

            here, there = parity, 1 - parity
            rows = source.shape[0] // 2
            first_half = source.at[pl.ds(pl.multiple_of(here * rows, 16), rows), :]
            self.to_row = add(first_half, place(me, 1, here), other_row)
            self.to_plane = add(place(me, 1, here), place(me, 1, here), next_plane)
            self.to_far = [add(source, place(me, 0, None), far)]
            self.to_far += [add(place(me, 1, half), place(me, 1, half), far) for half in (here, there)]
            self.to_mate = [add(source, place(me, 0, None), mate)]
            self.to_mate += [add(place(me, 1, half), place(me, 1, half), mate) for half in (here, there)]
            self.to_mate += [add(place(far_col, 0, None), place(far_col, 0, None), mate)]
            self.to_mate += [
                add(place(far_col, 1, half), place(far_col, 1, half), mate) for half in (here, there)
            ]

        def first(self):
            self.to_row.start()
            self.to_far[0].start()
            self.to_mate[0].start()

        def row_in(self):
            self.to_row.wait_recv()
            for copy in (self.to_plane, self.to_far[1], self.to_mate[1]):
                copy.start()

        def plane_in(self):
            self.to_plane.wait_recv()
            self.to_far[2].start()
            self.to_mate[2].start()

        def far_in(self, index):
            self.to_far[index].wait_recv()
            self.to_mate[3 + index].start()

        def mate_in(self, first, last):
            for copy in self.to_mate[first:last]:
                copy.wait_recv()

        def sent(self):
            for copy in self.copies:
                copy.wait_send()

    q_width = w_out_ref.shape[0]

    def project_place(col, slot, half):
        if half is None:
            return w_project.at[col, slot]
        return w_project.at[col, slot, pl.ds(pl.multiple_of(half * (width // 2), 16), width // 2), :]

    def out_place(col, slot, half):
        first, rows = col * q_width, q_width
        if half is not None:
            rows = q_width // 2
            first = first + half * rows
        return w_out.at[pl.ds(pl.multiple_of(first, 16), rows), pl.ds(slot * width, width)]

    project = Spread(w_project_ref, project_place, project_send, project_recv)
    output = Spread(w_out_ref, out_place, out_send, out_recv)
    own_project = pltpu.make_async_copy(w_project_ref, w_project.at[me, 0], local.at[0])
    own_output = pltpu.make_async_copy(w_out_ref, out_place(me, 0, None), local.at[1])
    own_gains = pltpu.make_async_copy(gains_ref, gains.at[0], local.at[2])
    sent_gains = remote(gains_ref, gains.at[1], gain_send.at[0], gain_recv.at[0], other_row)

    chunks = []
    for index, (source, target) in enumerate([(gate_ref, gate_out), (up_ref, up_out)]):
        rows = source.shape[0] // 4
        for part in range(2):
            here = pl.ds(pl.multiple_of((2 * parity + part) * rows, 64), rows)
            slot = 2 * index + part
            over_row = remote(source.at[here, :], target.at[here, :], row_send.at[slot], row_recv.at[slot], other_row)
            over_planes = remote(
                target.at[here, :], target.at[here, :], plane_send.at[slot], plane_recv.at[slot], next_plane
            )
            chunks.append((over_row, over_planes))

    def pass_on(index):
        chunks[index][0].wait_recv()
        chunks[index][1].start()

    own_copies = [own_gains, *own_tokens, own_project, own_output]
    for copy in own_copies:
        copy.start()
    pl.semaphore_wait(barrier, 5)
    sent_gains.start()
    project.first()
    for copy in sent_tokens:
        copy.start()
    output.first()
    chunks[0][0].start()
    for copy in own_copies:
        copy.wait()
    sent_gains.wait_recv()
    project.row_in()
    for copy in sent_tokens:
        copy.wait_recv()

    stores = []

    def save(source, target):
        copy = pltpu.make_async_copy(source, target, store.at[len(stores)])
        copy.start()
        stores.append(copy)
        return copy

    block = mine // 4

    @pl.loop(0, 4)
    def _(index):
        here = pl.ds(pl.multiple_of(index * block, block), block)
        values = states[here, :].astype(F32)
        inverse = lax.rsqrt(jnp.mean(values * values, axis=1, keepdims=True) + EPSILON)
        for slot in range(2):
            part = values[:, slot * width : (slot + 1) * width] * inverse
            normed[here, slot * width : (slot + 1) * width] = (part * gains[slot, 0:1, :]).astype(BF)

    save(states, states_out)
    normed_saved = save(normed, normed_out)
    save(gains, gains_out)

    def project_col(col):
        part = dot(normed[:, :width], w_project[col, 0]) + dot(normed[:, width:], w_project[col, 1])
        part = part.T
        heads = q_width // HD
        for head in range(heads):
            raw[col * heads + head] = part[head * HD : (head + 1) * HD]
        k_width = kv_rows // 4
        first = pl.multiple_of(col * k_width, 16)
        key_raw[pl.ds(first, k_width), :] = part[q_width : q_width + k_width].astype(BF)
        first = pl.multiple_of(kv_rows + col * k_width, 16)
        pair_own[pl.ds(first, k_width), :] = part[q_width + k_width :].astype(BF)

    project.plane_in()
    project.far_in(0)
    project_col(me)
    project.mate_in(0, 3)
    project_col(2 * group + 1 - side)
    project.far_in(1)
    project.far_in(2)
    project_col(far_col)
    project.mate_in(3, 6)
    project_col(2 * (1 - group) + 1 - side)
    save(raw, raw_out)
    save(key_raw, key_out)
    save(w_project, w_project_out)

    cosine, sine = cos_ref[...], sin_ref[...]

    def turned(values, gain):
        values = values * lax.rsqrt(jnp.mean(values * values, axis=0, keepdims=True) + EPSILON) * gain
        first, second = values[: HD // 2], values[HD // 2 :]
        return jnp.concatenate([first * cosine - second * sine, second * cosine + first * sine], axis=0)

    for head in range(kv_rows // HD):
        cut = slice(head * HD, (head + 1) * HD)
        pair_own[cut, :] = turned(key_raw[cut, :].astype(F32), key_gain_ref[...]).astype(BF)

    def places(who):
        starts = [who, pieces - 1 - who, pieces + who, 2 * pieces - 1 - who]
        return [pair.at[:, pl.ds(pl.multiple_of(start * span, span), span)] for start in starts]

    for index, place in enumerate(places(member)):
        place[...] = pair_own[:, index * span : (index + 1) * span]
    to_mate, to_row, passed = [], [], []
    for index, place in enumerate(places(member)):
        to_row.append(remote(place, place, pair_send.at[0, index], pair_recv.at[0, index], other_row))
        to_mate.append(remote(place, place, pair_send.at[1, index], pair_recv.at[1, index], mate))
    for index, place in enumerate(places(2 * (1 - row) + side)):
        passed.append(remote(place, place, pair_send.at[2, index], pair_recv.at[2, index], mate))
    for copy in to_row + to_mate:
        copy.start()
    chunks[1][0].start()
    output.row_in()
    output.far_in(0)

    @pl.loop(0, raw.shape[0])
    def _(head):
        values = turned(raw[head], query_gain_ref[...]).astype(BF)
        query[head] = values * BF(1.0 / math.sqrt(HD))

    for index in range(4):
        to_row[index].wait_recv()
        passed[index].start()
    chunks[2][0].start()
    output.plane_in()
    pass_on(0)
    for index in range(4):
        to_mate[index].wait_recv()
        passed[index].wait_recv()
    chunks[3][0].start()
    output.far_in(1)
    output.far_in(2)

    firsts = [member, pieces - 1 - member, pieces + member, 2 * pieces - 1 - member]
    rows = REP * span
    ones = jnp.ones((16, KEYS), BF)

    @pl.loop(0, kv_rows // HD)
    def _(head):
        key_n[...] = pair[pl.ds(pl.multiple_of(head * HD, HD), HD), :].T
        value_rows = pl.ds(pl.multiple_of(kv_rows + head * HD, HD), HD)
        for index in range(4):
            cut = slice(index * span, (index + 1) * span)
            query_here = jnp.concatenate([query[head * REP + rep, :, cut] for rep in range(REP)], axis=1)
            first_query = firsts[index] * span
            full, last = tiles_of(first_query)

            def tile(where, accum, masked):
                first_key = pl.multiple_of(where * KEYS, KEYS)
                expo = jnp.exp(dot(key_n[pl.ds(first_key, KEYS), :], query_here))
                if masked:
                    expo = jnp.where(allowed(first_query, first_key, span, rows), expo, 0.0)
                value = jnp.concatenate([pair[value_rows, pl.ds(first_key, KEYS)], ones], axis=0)
                return accum + dot(value, expo.astype(BF))

            accum = tile(last, jnp.zeros((HD + 16, rows), F32), True)
            accum = lax.fori_loop(0, full, lambda where, total: tile(where, total, False), accum)
            total = accum[HD : HD + 1]
            result = accum[:HD] / total
            log = jnp.log(total)
            for rep in range(REP):
                part = slice(rep * span, (rep + 1) * span)
                mixed_t[pl.ds(pl.multiple_of((head * REP + rep) * HD, HD), HD), cut] = result[:, part]
                logs[head, rep : rep + 1, cut] = log[:, part]

        for number, index in ((1, 1), (3, 2)):
            @pl.when(head == number)
            def _(index=index):
                pass_on(index)

    save(query, query_out)
    save(mixed_t, mixed_out)
    save(logs, logs_out)
    save(pair, pair_out)
    pass_on(3)
    output.mate_in(0, 6)
    save(w_out, w_out_out)

    @pl.loop(0, mixed_t.shape[0] // 128)
    def _(index):
        here = pl.ds(pl.multiple_of(index * 128, 128), 128)
        mixed[:, here] = mixed_t[here, :].astype(BF).T

    @pl.loop(0, depth // TILE)
    def _(index):
        here = pl.ds(pl.multiple_of(index * TILE, TILE), TILE)
        hidden[:, here] = states[:, here].astype(F32) + dot(mixed[...], w_out[:, here])

    normed_saved.wait()

    @pl.loop(0, 4)
    def _(index):
        here = pl.ds(pl.multiple_of(index * block, block), block)
        values = hidden[here, :]
        inverse = lax.rsqrt(jnp.mean(values * values, axis=1, keepdims=True) + EPSILON)
        for slot in range(2):
            part = values[:, slot * width : (slot + 1) * width] * inverse
            normed[here, slot * width : (slot + 1) * width] = (part * gains[slot, 1:2, :]).astype(BF)

    save(hidden, hidden_out)
    save(normed, normed_two_out)
    for copy in stores:
        if copy is not normed_saved:
            copy.wait()
    sent_gains.wait_send()
    for copy in sent_tokens + to_row + to_mate + passed:
        copy.wait_send()
    project.sent()
    output.sent()
    for over_row, over_planes in chunks:
        over_row.wait_send()
        over_planes.wait_recv()
        over_planes.wait_send()


def front(tokens, w_project, w_out, gains, w_gate, w_up, cosine, sine, query_gain, key_gain):
    shard, width = tokens.shape
    mine, depth = shard // 2, 2 * width
    q_width, columns = w_out.shape[0], w_project.shape[1]
    kv_rows = KVH * HD
    anywhere = pl.BlockSpec(memory_space=pl.ANY)
    inside = pl.BlockSpec(memory_space=pltpu.VMEM)
    dma = pltpu.SemaphoreType.DMA
    shape = jax.ShapeDtypeStruct
    return pl.pallas_call(
        front_kernel,
        out_shape=[
            shape((mine, depth), BF),
            shape((mine, depth), BF),
            shape((QH, HD, mine), F32),
            shape((QH, HD, mine), BF),
            shape((kv_rows, mine), BF),
            shape((2 * kv_rows, GROUP), BF),
            shape((QH * HD, mine), F32),
            shape((KVH, REP, mine), F32),
            shape((mine, depth), F32),
            shape((mine, depth), BF),
            shape((4, 2, width, columns), BF),
            shape((4 * q_width, depth), BF),
            shape(w_gate.shape, BF),
            shape(w_up.shape, BF),
            shape((2, 2, width), F32),
        ],
        in_specs=[anywhere] * 6 + [inside] * 4,
        out_specs=[anywhere] * 15,
        scratch_shapes=[
            pltpu.VMEM((mine, depth), BF),
            pltpu.VMEM((mine, depth), BF),
            pltpu.VMEM((4, 2, width, columns), BF),
            pltpu.VMEM((QH, HD, mine), F32),
            pltpu.VMEM((kv_rows, mine), BF),
            pltpu.VMEM((QH, HD, mine), BF),
            pltpu.VMEM((2 * kv_rows, mine), BF),
            pltpu.VMEM((2 * kv_rows, GROUP), BF),
            pltpu.VMEM((GROUP, HD), BF),
            pltpu.VMEM((QH * HD, mine), F32),
            pltpu.VMEM((KVH, REP, mine), F32),
            pltpu.VMEM((mine, QH * HD), BF),
            pltpu.VMEM((4 * q_width, depth), BF),
            pltpu.VMEM((mine, depth), F32),
            pltpu.VMEM((2, 2, width), F32),
            dma((3, 2)), dma((3, 2)), dma((2,)),
            dma((11,)), dma((11,)), dma((11,)), dma((11,)), dma((1,)), dma((1,)),
            dma((3, 4)), dma((3, 4)), dma((4,)), dma((4,)), dma((4,)), dma((4,)), dma((3,)), dma((13,)),
        ],
        compiler_params=pltpu.CompilerParams(
            collective_id=3, has_side_effects=True, vmem_limit_bytes=56 * 1024 * 1024
        ),
        name="front",
    )(tokens, w_project, w_out, gains, w_gate, w_up, cosine, sine, query_gain, key_gain)


def back_kernel(*refs):
    query, d_out, logs_ref, delta_ref, pair, raw, key_raw, cos_ref, sin_ref, query_gain, key_gain = refs[:11]
    d_project, query_gain_out, key_gain_out = refs[11:14]
    key_n, value_n, d_key, d_value, both_t, staged, come, gain_sum, send_sem, recv_sem = refs[14:]
    row, side = lax.axis_index("row"), lax.axis_index("side")
    others = [
        (2 * (1 - row) + side, {"row": 1 - row}),
        (2 * (1 - row) + 1 - side, {"row": 1 - row, "side": 1 - side}),
        (2 * row + 1 - side, {"side": 1 - side}),
    ]
    member = 2 * row + side
    pieces = 8
    span = query.shape[2] // 4
    rows = REP * span
    kv_rows = key_raw.shape[0]
    half = HD // 2

    barrier = pltpu.get_barrier_semaphore()
    for _, where in others:
        pl.semaphore_signal(barrier, 1, device_id=where, device_id_type=pl.DeviceIdType.MESH)
    pl.semaphore_wait(barrier, 3)

    def sent(index, head):
        return pltpu.make_async_remote_copy(
            staged.at[index, head],
            come.at[index, head],
            send_sem.at[index, head],
            recv_sem.at[index, head],
            device_id=others[index][1],
            device_id_type=pl.DeviceIdType.MESH,
        )

    def starts(who):
        return [who, pieces - 1 - who, pieces + who, 2 * pieces - 1 - who]

    def through_norm(values, gain, cosine, sine, d_turned):
        first, second = d_turned[:half], d_turned[half:]
        d_scaled = jnp.concatenate([first * cosine + second * sine, second * cosine - first * sine], axis=0)
        inverse = lax.rsqrt(jnp.mean(values * values, axis=0, keepdims=True) + EPSILON)
        d_normed = d_scaled * gain
        mean = jnp.mean(values * d_normed, axis=0, keepdims=True)
        return inverse * d_normed - values * inverse**3 * mean, d_scaled * values * inverse

    gain_sum[...] = jnp.zeros_like(gain_sum)
    scale = 1.0 / math.sqrt(HD)

    @pl.loop(0, KVH)
    def _(head):
        key_rows = pl.ds(pl.multiple_of(head * HD, HD), HD)
        value_rows = pl.ds(pl.multiple_of(kv_rows + head * HD, HD), HD)
        key_n[...] = pair[key_rows, :].T
        value_n[...] = pair[value_rows, :].T
        d_key[...] = jnp.zeros_like(d_key)
        d_value[...] = jnp.zeros_like(d_value)
        for index, start in enumerate(starts(member)):
            cut = slice(index * span, (index + 1) * span)

            def beside(ref):
                return jnp.concatenate([ref[head * REP + rep, :, cut] for rep in range(REP)], axis=1)

            query_here, d_out_here = beside(query), beside(d_out)
            query_t, d_out_t = query_here.T, d_out_here.T
            logs = jnp.concatenate([logs_ref[head, rep : rep + 1, cut] for rep in range(REP)], axis=1)
            delta = jnp.concatenate([delta_ref[head, rep : rep + 1, cut] for rep in range(REP)], axis=1)
            first_query = start * span
            full, last = tiles_of(first_query)

            def tile(where, accum, masked):
                first_key = pl.multiple_of(where * KEYS, KEYS)
                here = pl.ds(first_key, KEYS)
                probs = jnp.exp(dot(key_n[here, :], query_here) - logs)
                if masked:
                    probs = jnp.where(allowed(first_query, first_key, span, rows), probs, 0.0)
                d_probs = dot(value_n[here, :], d_out_here)
                d_scores = (probs * (d_probs - delta)).astype(BF)
                d_value[here, :] += dot(probs.astype(BF), d_out_t)
                d_key[here, :] += dot(d_scores, query_t)
                return accum + dot(pair[key_rows, here], d_scores)

            accum = tile(last, jnp.zeros((HD, rows), F32), True)
            accum = lax.fori_loop(0, full, lambda where, total: tile(where, total, False), accum)
            cosine = jnp.concatenate([cos_ref[:, cut]] * REP, axis=1)
            sine = jnp.concatenate([sin_ref[:, cut]] * REP, axis=1)
            d_raw, part = through_norm(beside(raw), query_gain[...], cosine, sine, accum * scale)
            gain_sum[0] += part
            for rep in range(REP):
                which = head * REP + rep
                place = pl.ds(pl.multiple_of(which % KVH * HD, HD), HD)
                d_project[which // KVH, place, cut] = d_raw[:, rep * span : (rep + 1) * span].astype(BF)
        both_t[:HD, :] = d_key[...].T.astype(BF)
        both_t[HD:, :] = d_value[...].T.astype(BF)
        for index, who in enumerate([who for who, _ in others] + [member]):
            for number, start in enumerate(starts(who)):
                part = both_t[:, pl.ds(pl.multiple_of(start * span, span), span)]
                staged[index, head, :, number * span : (number + 1) * span] = part
            if index < 3:
                sent(index, head).start()

    cosine, sine = cos_ref[...], sin_ref[...]
    width = kv_rows // 4
    for head in range(KVH):
        total = staged[3, head].astype(F32)
        for index in range(3):
            sent(index, head).wait_recv()
            total += come[index, head].astype(F32)
        values = key_raw[head * HD : (head + 1) * HD, :].astype(F32)
        d_raw, part = through_norm(values, key_gain[...], cosine, sine, total[:HD])
        gain_sum[1] += part
        for offset, result in ((0, d_raw.astype(BF)), (width, total[HD:].astype(BF))):
            first = head * HD
            while first < (head + 1) * HD:
                col, inside = first // width, first % width
                size = min(width - inside, (head + 1) * HD - first)
                place = d_project.shape[1] - 2 * width + offset + inside
                d_project[col, place : place + size, :] = result[first - head * HD : first - head * HD + size]
                first += size
    query_gain_out[...] = jnp.sum(gain_sum[0], axis=1, keepdims=True)
    key_gain_out[...] = jnp.sum(gain_sum[1], axis=1, keepdims=True)
    for head in range(KVH):
        for index in range(3):
            sent(index, head).wait_send()


def back(query, d_out, logs, delta, pair, raw, key_raw, cosine, sine, query_gain, key_gain):
    mine = query.shape[2]
    inside = pl.BlockSpec(memory_space=pltpu.VMEM)
    dma = pltpu.SemaphoreType.DMA
    shape = jax.ShapeDtypeStruct
    columns = (QH + 2 * KVH) * HD // 4
    return pl.pallas_call(
        back_kernel,
        out_shape=[shape((4, columns, mine), BF), shape((HD, 1), F32), shape((HD, 1), F32)],
        in_specs=[inside] * 11,
        out_specs=[inside] * 3,
        scratch_shapes=[
            pltpu.VMEM((GROUP, HD), BF),
            pltpu.VMEM((GROUP, HD), BF),
            pltpu.VMEM((GROUP, HD), F32),
            pltpu.VMEM((GROUP, HD), F32),
            pltpu.VMEM((2 * HD, GROUP), BF),
            pltpu.VMEM((4, KVH, 2 * HD, mine), BF),
            pltpu.VMEM((3, KVH, 2 * HD, mine), BF),
            pltpu.VMEM((2, HD, mine), F32),
            dma((3, KVH)),
            dma((3, KVH)),
        ],
        compiler_params=pltpu.CompilerParams(
            collective_id=4, has_side_effects=True, vmem_limit_bytes=48 * 1024 * 1024
        ),
        name="attend_back",
    )(query, d_out, logs, delta, pair, raw, key_raw, cosine, sine, query_gain, key_gain)


def body(
    tokens,
    norm1_gain,
    w_query,
    w_key,
    w_value,
    query_gain,
    key_gain,
    w_out,
    norm2_gain,
    w_gate,
    w_up,
    w_down,
    teacher,
    positions,
    token_count,
):
    rows = lax.axis_size("row")
    cores = lax.axis_size("side")
    cols = lax.axis_size("group") * cores
    row_index = lax.axis_index("row")
    group_index = lax.axis_index("group")
    members = rows * cores
    member = row_index * cores + lax.axis_index("side")
    shard, width = tokens.shape
    pieces = 2 * members
    span = shard // pieces
    mine = shard // members * cores
    q_width, k_width = w_query.shape[1], w_key.shape[1]
    ff = w_gate.shape[1]

    def from_row(block, ahead):
        pairs = [((r + ahead) % rows, r) for r in range(rows)]
        return lax.ppermute(block, "row", pairs)

    def gather_rows(block, axis):
        parts = [block] + [from_row(block, ahead) for ahead in range(1, rows)]
        return jnp.concatenate(parts, axis=axis)

    def scatter_rows(block, axis):
        size = block.shape[axis] // rows
        total = lax.slice_in_dim(block, 0, size, axis=axis).astype(F32)
        for ahead in range(1, rows):
            part = lax.slice_in_dim(block, ahead * size, (ahead + 1) * size, axis=axis)
            total = total + from_row(part, rows - ahead).astype(F32)
        return total.astype(BF)

    def sum_planes(block, cuts):
        planes = lax.axis_size("dp")
        plane = lax.axis_index("dp")
        half = planes // 2
        edge = jnp.minimum(plane, planes - 1 - plane)
        done = []
        for part in jnp.split(block, cuts, axis=0):
            for step in range(half - 1):
                pairs = [(step, step + 1), (planes - 1 - step, planes - 2 - step)]
                come = lax.ppermute(part, "dp", pairs)
                part = (part.astype(F32) + come.astype(F32)).astype(BF)
            come = lax.ppermute(part, "dp", [(half - 1, half), (half, half - 1)])
            part = (part.astype(F32) + come.astype(F32)).astype(BF)
            for step in reversed(range(half - 1)):
                pairs = [(step + 1, step), (planes - 2 - step, planes - 1 - step)]
                come = lax.ppermute(part, "dp", pairs)
                part = jnp.where(edge == step, come, part)
            done.append(part)
        return jnp.concatenate(done, axis=0)

    def to_members(block):
        parts = block.reshape(pieces, span, width)
        parts = jnp.stack([parts[:members], parts[members:][::-1]], axis=1)
        moved = lax.all_to_all(parts, ("row", "side"), 0, 0, tiled=True)
        moved = jnp.roll(moved.reshape(rows, cores, 2 * span, width), -row_index, 0)
        moved = moved.transpose(1, 2, 0, 3)
        return moved.reshape(mine, rows * width)

    def from_members(block):
        parts = block.reshape(cores, 2, span, rows, width).transpose(3, 0, 1, 2, 4)
        parts = jnp.roll(parts, row_index, 0).reshape(members, 2, span, width)
        moved = lax.all_to_all(parts, ("row", "side"), 0, 0, tiled=True)
        moved = jnp.concatenate([moved[:, 0], moved[:, 1][::-1]], axis=0)
        return moved.reshape(shard, width)

    def pick(values):
        part = lax.dynamic_slice_in_dim(values.reshape(-1, cores, pieces, span), group_index, 1, 0)[0]
        low = lax.dynamic_slice_in_dim(part, member, 1, 1)
        high = lax.dynamic_slice_in_dim(part, pieces - 1 - member, 1, 1)
        return jnp.concatenate([low, high], axis=1).reshape(-1)

    first_tokens = (
        jnp.array([0, 0, shard, shard], jnp.int32)
        + jnp.stack([member, pieces - 1 - member] * 2).astype(jnp.int32) * span
    )

    half = HD // 2
    freq = jnp.exp(jnp.arange(half, dtype=F32) * (-2.0 * math.log(10000.0) / HD))
    angle = freq[:, None] * pick(positions).astype(F32)[None, :]
    cosine, sine = jnp.cos(angle), jnp.sin(angle)
    def dealt(full):
        lead, entry = full.shape[:-2], full.shape[-1]
        parts = full.reshape(lead + (cores, pieces, span, entry))
        low = parts[..., :members, :, :]
        high = parts[..., members:, :, :][..., ::-1, :, :]
        both = jnp.stack([low, high], axis=-3)
        both = jnp.moveaxis(both, -4, 0)
        return both.reshape((members,) + lead + (mine, entry))

    w_project = jnp.concatenate([w_query, w_key, w_value], axis=1)
    scale = 1.0 / math.sqrt(HD)
    fast = rows == 2 and cols == 4 and lax.axis_size("dp") % 2 == 0 and mine == 4 * span
    if fast:
        (
            states, normed_one, query_raw, query_use, key_sent, pair, mixed_f, logs, hidden,
            normed_two, w_project, w_out_all, gate_other, up_other, gains,
        ) = front(
            tokens, w_project, w_out, jnp.stack([norm1_gain, norm2_gain]), w_gate, w_up,
            cosine, sine, query_gain[:, None], key_gain[:, None],
        )
        states = states.astype(F32)
        inverse_one, inverse_two = rms(states), rms(hidden)
        gain_one, gain_two = gains[:, 0].reshape(D), gains[:, 1].reshape(D)
        mixed_f = mixed_f.reshape(KVH, REP, HD, mine)
        mixed = mixed_f.reshape(QH * HD, mine).astype(BF)
        w_project = w_project.reshape(cols, D, -1)
        ffn_weights = [w_gate, gate_other, w_up, up_other, w_down]
    else:
        states = to_members(tokens).astype(F32)
        gain_one = gather_rows(norm1_gain, 0)
        gain_two = gather_rows(norm2_gain, 0)
        w_project = gather_rows(w_project, 0)
        w_project = lax.all_gather(w_project, ("group", "side"), axis=0)
        w_out_all = gather_rows(w_out, 1)
        w_out_all = lax.all_gather(w_out_all, ("group", "side"), axis=0, tiled=True)
        def halves(block, axis):
            if rows == 2:
                return [block, from_row(block, 1)]
            return jnp.split(gather_rows(block, axis), 2, axis=axis)

        ffn_weights = halves(w_gate, 0) + halves(w_up, 0) + halves(w_down, 1)
        inverse_one = rms(states)
        normed_one = (states * inverse_one * gain_one).astype(BF)
        projected = dot(w_project, normed_one, ((1,), (1,)))
        query_raw = projected[:, :q_width].reshape(QH, HD, mine)
        key_sent = projected[:, q_width : q_width + k_width].reshape(KVH, HD, mine).astype(BF)
        value_sent = projected[:, q_width + k_width :].reshape(KVH, HD, mine).astype(BF)
        query_rot, query_back = jax.vjp(
            lambda raw, gain: prepare(raw, gain, cosine, sine), query_raw, query_gain
        )
        key_rot, key_back = jax.vjp(
            lambda raw, gain: prepare(raw, gain, cosine, sine), key_sent.astype(F32), key_gain
        )
        query_use = (query_rot.astype(BF) * BF(scale)).reshape(KVH, REP, HD, mine)
        pair = jnp.stack([key_rot.astype(BF), value_sent])
        pair = lax.all_gather(pair, ("row", "side"), axis=0)

        def natural(stacked):
            lead = stacked.shape[1:-1]
            parts = stacked.reshape((members,) + lead + (cores, 2, span))
            low, high = parts[..., 0, :], parts[..., 1, :]
            both = jnp.concatenate([low, high[::-1]], axis=0)
            return jnp.moveaxis(both, 0, -2).reshape(lead + (GROUP,))

        pair = natural(pair)
        key_t, value_t = pair[0], pair[1]
        key_n = key_t.transpose(0, 2, 1)
        value_one = jnp.concatenate([value_t, jnp.ones((KVH, 16, GROUP), BF)], axis=1)
        mixed_f, logs = attend(first_tokens, query_use, key_n, value_one)
        mixed = mixed_f.reshape(QH * HD, mine).astype(BF)
        hidden = states + dot(mixed, w_out_all, ((0,), (0,)))

        inverse_two = rms(hidden)
        normed_two = (hidden * inverse_two * gain_two).astype(BF)

    if fast:
        normed_all, gate, up, activated, ffn_out, down_other, target = spread(
            True, normed_two, ffn_weights, dealt=teacher
        )
        ffn_weights.append(down_other)
    else:
        normed_all, gate, up, activated, ffn_out = spread(True, normed_two, ffn_weights)
        target = to_members(teacher)
    ffn_out = ffn_out.reshape(mine, D)
    result = hidden + ffn_out

    total_tokens = shard * cols * lax.axis_size("dp")
    loss_scale = total_tokens / token_count[0].astype(F32)
    d_result = loss_scale * (result - target.astype(F32))
    if fast:
        d_low, d_gate_up, d_normed, block_out = spread(
            False, d_result.astype(BF), ffn_weights, (gate, up), result.astype(BF)
        )
    else:
        d_low, d_gate_up, d_normed = spread(False, d_result.astype(BF), ffn_weights, (gate, up))
        block_out = from_members(result.astype(BF))
    d_normed = d_normed.reshape(mine, D)
    d_low, normed_all = d_low.reshape(-1, D), normed_all.reshape(-1, D)
    grad_down = dot(activated.reshape(-1, ff), d_low, ((0,), (0,))).astype(BF)
    grad_gate_up = dot(normed_all, d_gate_up.reshape(-1, 2 * ff), ((0,), (0,))).astype(BF)

    norm_two_part = jnp.sum(d_normed * hidden * inverse_two, axis=0)
    d_hidden = d_result + norm_back(hidden, inverse_two, gain_two, d_normed)
    d_hidden_low = d_hidden.astype(BF)
    grad_out = dot(mixed, d_hidden_low, ((1,), (0,))).astype(BF)
    d_mixed = dot(w_out_all, d_hidden_low, ((1,), (1,))).astype(BF)
    d_mixed = d_mixed.reshape(KVH, REP, HD, mine)
    delta = jnp.sum(d_mixed.astype(F32) * mixed_f, axis=2)
    if fast:
        d_projected, query_gain_part, key_gain_part = back(
            query_use, d_mixed.reshape(QH, HD, mine), logs, delta, pair, query_raw, key_sent,
            cosine, sine, query_gain[:, None], key_gain[:, None],
        )
        query_gain_part, key_gain_part = query_gain_part[:, 0], key_gain_part[:, 0]
    else:
        d_query, d_key_n, d_value_n = attend_back(
            first_tokens, query_use, d_mixed, logs, delta, key_t, value_t
        )
        d_pair = dealt(jnp.stack([d_key_n, d_value_n])).astype(BF)
        d_pair = lax.psum_scatter(d_pair, ("row", "side"), scatter_dimension=0, tiled=True)[0]
        d_pair = d_pair.astype(F32).transpose(0, 1, 3, 2)
        d_query_raw, query_gain_part = query_back(d_query.reshape(QH, HD, mine) * scale)
        d_key_raw, key_gain_part = key_back(d_pair[0])
        d_projected = jnp.concatenate(
            [
                d_query_raw.reshape(cols, q_width, mine),
                d_key_raw.reshape(cols, k_width, mine),
                d_pair[1].reshape(cols, k_width, mine),
            ],
            axis=1,
        ).astype(BF)
    d_normed_one = dot(d_projected, w_project, ((0, 1), (0, 2)))
    grad_input = d_hidden + norm_back(states, inverse_one, gain_one, d_normed_one)
    norm_one_part = jnp.sum(d_normed_one * states * inverse_one, axis=0)

    grad_project = lax.dot_general(
        d_projected, normed_one, (((2,), (0,)), ((), ())), preferred_element_type=F32
    )
    grad_project = grad_project.astype(BF)
    grad_out = grad_out.reshape(cols, q_width, D)
    norm_one_part = jnp.roll(norm_one_part.reshape(rows, width), row_index, 0).reshape(D)
    norm_two_part = jnp.roll(norm_two_part.reshape(rows, width), row_index, 0).reshape(D)
    small = jnp.concatenate([norm_one_part, norm_two_part, query_gain_part, key_gain_part])
    if fast and lax.axis_size("dp") == 4:
        padded = jnp.pad(small, (0, SMALL * 128 - small.shape[0])).reshape(SMALL, 128)
        grad_down, grad_gate_up, grad_out, grad_project, small, grad_input = reduce_all(
            4,
            [(grad_down, 1, 128), (grad_gate_up, 0, 64), (grad_out, 1, 160), (grad_project, 1, 240)],
            padded,
            grad_input.astype(BF),
        )
        grad_input = grad_input.astype(F32)
        small = small.reshape(-1)[: 2 * D + 2 * HD]
    else:
        grad_input = from_members(grad_input)
        small = lax.psum(small, ("dp", "row", "group", "side"))
        col_axes = ("group", "side")
        grad_project = lax.psum_scatter(grad_project, col_axes, scatter_dimension=0, tiled=True)
        grad_out = lax.psum_scatter(grad_out, col_axes, scatter_dimension=0, tiled=True)
        grad_down = sum_planes(scatter_rows(grad_down, 1), 2)
        grad_gate_up = sum_planes(scatter_rows(grad_gate_up, 0), 4)
        grad_out = sum_planes(scatter_rows(grad_out[0], 1), 1)
        grad_project = sum_planes(scatter_rows(grad_project[0], 1), 2)
    grad_norm1 = lax.dynamic_slice_in_dim(small, row_index * width, width, 0)
    grad_norm2 = lax.dynamic_slice_in_dim(small, D + row_index * width, width, 0)
    grad_project = grad_project.astype(F32).T
    return (
        block_out,
        grad_input,
        grad_norm1,
        grad_project[:, :q_width],
        grad_project[:, q_width : q_width + k_width],
        grad_project[:, q_width + k_width :],
        small[2 * D : 2 * D + HD],
        small[2 * D + HD :],
        grad_out.astype(F32),
        grad_norm2,
        grad_gate_up[:, :ff].astype(F32),
        grad_gate_up[:, ff:].astype(F32),
        grad_down.astype(F32),
    )


def solution(mesh):
    dp, row, col = mesh.shape["dp"], mesh.shape["row"], mesh.shape["col"]

    def call(*args):
        side = GROUP * dp * col // args[0].shape[0]
        fine = Mesh(
            mesh.devices.reshape(dp, row, col // side, side), ("dp", "row", "group", "side")
        )
        col_axes = ("group", "side")
        token_spec = P(("dp", "group", "side"), "row")
        wide = P("row", col_axes)
        tall = P(col_axes, "row")
        return jax.shard_map(
            body,
            mesh=fine,
            in_specs=(
                token_spec,
                P("row"),
                wide,
                wide,
                wide,
                P(),
                P(),
                tall,
                P("row"),
                wide,
                wide,
                tall,
                token_spec,
                P("dp"),
                P(),
            ),
            out_specs=(
                token_spec,
                token_spec,
                P("row"),
                wide,
                wide,
                wide,
                P(),
                P(),
                tall,
                P("row"),
                wide,
                wide,
                tall,
            ),
            check_vma=False,
        )(*args)

    return call
```

```python
import functools
import math

import jax
import jax.numpy as jnp
from jax import lax
from jax.experimental import pallas as pl
from jax.experimental.pallas import tpu as pltpu
from jax.sharding import Mesh
from jax.sharding import PartitionSpec as P

D = 2048
QH = 20
KVH = 5
HD = 64
PROMPT = 1024
CONT = 128
NCONT = 8
GROUP = PROMPT + NCONT * CONT
REP = QH // KVH
KEYS = 256

EPSILON = 1e-06
BF = jnp.bfloat16
F32 = jnp.float32


def dot(left, right, dims=((1,), (0,))):
    return lax.dot_general(left, right, (dims, ((), ())), preferred_element_type=F32)


def rms(values):
    return lax.rsqrt(jnp.mean(values * values, axis=1, keepdims=True) + EPSILON)


def norm_back(states, inverse, gain, d_normed):
    mean = jnp.mean(states * gain * d_normed, axis=1, keepdims=True)
    return inverse * gain * d_normed - states * inverse**3 * mean


def prepare(raw, gain, cosine, sine):
    values = raw * lax.rsqrt(jnp.mean(raw * raw, axis=1, keepdims=True) + EPSILON)
    values = values * gain[None, :, None]
    half = HD // 2
    first, second = values[:, :half], values[:, half:]
    return jnp.concatenate(
        [first * cosine - second * sine, second * cosine + first * sine], axis=1
    )


def allowed(first_query, first_key, span, rows):
    key = first_key + lax.broadcasted_iota(jnp.int32, (KEYS, rows), 0)
    query = first_query + lax.broadcasted_iota(jnp.int32, (KEYS, rows), 1) % span
    return (key <= query) & ((key < PROMPT) | (key // CONT == query // CONT))


def side_by_side(ref, index, span):
    return jnp.concatenate(
        [ref[0, head, :, index * span : (index + 1) * span] for head in range(REP)], axis=1
    )


def tiles_of(first_query):
    last = first_query // KEYS
    return jnp.minimum(last, PROMPT // KEYS), last


def attend_kernel(chunks, span, first_ref, query_ref, key_ref, value_ref, out_ref, log_ref):
    rows = REP * span
    for index in range(chunks):
        query = side_by_side(query_ref, index, span)
        first_query = first_ref[index]
        full, last = tiles_of(first_query)

        def tile(where, accum, masked):
            first_key = pl.multiple_of(where * KEYS, KEYS)
            scores = dot(key_ref[0, pl.ds(first_key, KEYS), :], query)
            expo = jnp.exp(scores)
            if masked:
                expo = jnp.where(allowed(first_query, first_key, span, rows), expo, 0.0)
            return accum + dot(value_ref[0, :, pl.ds(first_key, KEYS)], expo.astype(BF))

        accum = tile(last, jnp.zeros((value_ref.shape[1], rows), F32), True)
        accum = lax.fori_loop(0, full, lambda where, total: tile(where, total, False), accum)
        total = accum[HD : HD + 1]
        mixed = accum[:HD] / total
        logs = jnp.log(total)
        for head in range(REP):
            cut = slice(head * span, (head + 1) * span)
            out_ref[0, head, :, index * span : (index + 1) * span] = mixed[:, cut]
            log_ref[0, head : head + 1, index * span : (index + 1) * span] = logs[:, cut]


def attend_back_kernel(
    chunks,
    span,
    first_ref,
    query_ref,
    d_out_ref,
    log_ref,
    delta_ref,
    key_t_ref,
    value_t_ref,
    d_query_ref,
    d_key_ref,
    d_value_ref,
    key_ref,
    value_ref,
):
    rows = REP * span
    key_ref[...] = key_t_ref[0].T
    value_ref[...] = value_t_ref[0].T
    d_key_ref[...] = jnp.zeros_like(d_key_ref)
    d_value_ref[...] = jnp.zeros_like(d_value_ref)
    for index in range(chunks):
        query = side_by_side(query_ref, index, span)
        d_out = side_by_side(d_out_ref, index, span)
        query_t = query.T
        d_out_t = d_out.T
        cut = slice(index * span, (index + 1) * span)
        logs = jnp.concatenate([log_ref[0, h : h + 1, cut] for h in range(REP)], axis=1)
        delta = jnp.concatenate([delta_ref[0, h : h + 1, cut] for h in range(REP)], axis=1)
        first_query = first_ref[index]
        full, last = tiles_of(first_query)

        def tile(where, accum, masked):
            first_key = pl.multiple_of(where * KEYS, KEYS)
            here = pl.ds(first_key, KEYS)
            probs = jnp.exp(dot(key_ref[here, :], query) - logs)
            if masked:
                probs = jnp.where(allowed(first_query, first_key, span, rows), probs, 0.0)
            d_probs = dot(value_ref[here, :], d_out)
            d_scores = (probs * (d_probs - delta)).astype(BF)
            d_value_ref[0, here, :] += dot(probs.astype(BF), d_out_t)
            d_key_ref[0, here, :] += dot(d_scores, query_t)
            return accum + dot(key_t_ref[0, :, here], d_scores)

        accum = tile(last, jnp.zeros((HD, rows), F32), True)
        accum = lax.fori_loop(0, full, lambda where, total: tile(where, total, False), accum)
        for head in range(REP):
            part = accum[:, head * span : (head + 1) * span]
            d_query_ref[0, head, :, cut] = part


def per_head(shape):
    return pl.BlockSpec((1,) + shape, lambda head, first: (head,) + (0,) * len(shape))


def attend(first, query, key, value_t):
    tokens = query.shape[-1]
    chunks = first.shape[0]
    return pl.pallas_call(
        functools.partial(attend_kernel, chunks, tokens // chunks),
        out_shape=(
            jax.ShapeDtypeStruct((KVH, REP, HD, tokens), F32),
            jax.ShapeDtypeStruct((KVH, REP, tokens), F32),
        ),
        grid_spec=pltpu.PrefetchScalarGridSpec(
            num_scalar_prefetch=1,
            grid=(KVH,),
            in_specs=[
                per_head((REP, HD, tokens)),
                per_head((GROUP, HD)),
                per_head((value_t.shape[1], GROUP)),
            ],
            out_specs=[per_head((REP, HD, tokens)), per_head((REP, tokens))],
        ),
        compiler_params=pltpu.CompilerParams(vmem_limit_bytes=32 * 1024 * 1024),
        name="attend",
    )(first, query, key, value_t)


def attend_back(first, query, d_out, logs, delta, key_t, value_t):
    tokens = query.shape[-1]
    chunks = first.shape[0]
    return pl.pallas_call(
        functools.partial(attend_back_kernel, chunks, tokens // chunks),
        out_shape=(
            jax.ShapeDtypeStruct((KVH, REP, HD, tokens), F32),
            jax.ShapeDtypeStruct((KVH, GROUP, HD), F32),
            jax.ShapeDtypeStruct((KVH, GROUP, HD), F32),
        ),
        grid_spec=pltpu.PrefetchScalarGridSpec(
            num_scalar_prefetch=1,
            grid=(KVH,),
            in_specs=[
                per_head((REP, HD, tokens)),
                per_head((REP, HD, tokens)),
                per_head((REP, tokens)),
                per_head((REP, tokens)),
                per_head((HD, GROUP)),
                per_head((HD, GROUP)),
            ],
            out_specs=[
                per_head((REP, HD, tokens)),
                per_head((GROUP, HD)),
                per_head((GROUP, HD)),
            ],
            scratch_shapes=[pltpu.VMEM((GROUP, HD), BF), pltpu.VMEM((GROUP, HD), BF)],
        ),
        compiler_params=pltpu.CompilerParams(vmem_limit_bytes=32 * 1024 * 1024),
        name="attend_back",
    )(first, query, d_out, logs, delta, key_t, value_t)


AHEAD = 4
SLOTS = AHEAD + 2
FAR_LAG, WIDE_LAG, LAG = 1, 2, 4
SMALL = 40


class Part:
    def __init__(self, axis, rows, cols, count, base, col):
        self.axis, self.rows, self.cols = axis, rows, cols
        self.count, self.base, self.col = count, base, col

    def cut(self, ref, index, half, lead=()):
        first = pl.ds(index * self.rows, self.rows)
        if self.axis == 0:
            first = pl.ds((half * self.count + index) * self.rows, self.rows)
            return ref.at[(*lead, first, slice(None))]
        return ref.at[(*lead, first, pl.ds(half * self.cols, self.cols))]


def reduce_kernel(parts, planes, *refs):
    count = len(parts)
    refs = list(refs)

    def take(number):
        taken = refs[:number]
        del refs[:number]
        return taken

    col_parts = [j for j in range(count) if parts[j].col]
    normed_ref, d_gate_up_ref, act_ref, d_low_ref = take(4)
    grads = dict(zip(col_parts, take(len(col_parts))))
    (small_ref, mine_ref) = take(2)
    outs = take(count)
    (small_out, dealt_ref) = take(2)
    near, far, own = take(count), take(count), take(count)
    made = [j for j in range(count) if not parts[j].col]
    leaving = dict(zip(made, take(len(made))))
    mate_in = dict(zip(col_parts, take(len(col_parts))))
    far_in = dict(zip(col_parts, take(len(col_parts))))
    right, left, left_t, right_sem, left_sem, free_sem = take(6)
    out_sem, row_send, row_recv, in_send, far_recv, mid_send, wide_recv = take(7)
    col_own, col_send, col_recv, x_send, x_recv, small_local, small_send, small_recv = take(8)
    small_in, small_sum, deal_send, deal_recv, deal_local = take(5)
    plane, row = lax.axis_index("dp"), lax.axis_index("row")
    group, side = lax.axis_index("group"), lax.axis_index("side")
    other_row, mate, far_dev = {"row": 1 - row}, {"side": 1 - side}, {"group": 1 - group}
    cross = {"row": 1 - row, "side": 1 - side}
    at_end = (plane == 0) | (plane == planes - 1)
    low = plane < planes // 2
    end_next = {"dp": jnp.where(low, 1, planes - 2)}
    mid_outer = {"dp": jnp.where(low, 0, planes - 1)}
    mid_other = {"dp": jnp.where(low, planes // 2, planes // 2 - 1)}

    def remote(source, target, send, recv, where):
        return pltpu.make_async_remote_copy(
            source, target, send, recv, device_id=where, device_id_type=pl.DeviceIdType.MESH
        )

    barrier = pltpu.get_barrier_semaphore()

    def greet(where):
        pl.semaphore_signal(barrier, 1, device_id=where, device_id_type=pl.DeviceIdType.MESH)

    for where in (other_row, mate, far_dev, cross):
        greet(where)

    @pl.when(at_end)
    def _():
        greet(end_next)
        pl.semaphore_wait(barrier, 5)

    @pl.when(jnp.logical_not(at_end))
    def _():
        greet(mid_outer)
        greet(mid_other)
        pl.semaphore_wait(barrier, 6)

    def col_slot(j, half, index):
        before = sum(2 * parts[i].count for i in col_parts if i < j)
        return before + half * parts[j].count + index

    def col_own_copy(j, half, index, target):
        return pltpu.make_async_copy(
            parts[j].cut(grads[j], index, half, (2 * target + side,)),
            own[j].at[target, half, index],
            col_own.at[target, col_slot(j, half, index)],
        )

    def col_copy(j, half, index, target):
        slot = col_slot(j, half, index)
        return remote(
            parts[j].cut(grads[j], index, half, (2 * target + 1 - side,)),
            mate_in[j].at[target, half, index],
            col_send.at[target, slot],
            col_recv.at[target, slot],
            mate,
        )

    def x_copy(j, half, index):
        slot = col_slot(j, half, index)
        return remote(
            mate_in[j].at[1 - group, half, index],
            far_in[j].at[half, index],
            x_send.at[slot],
            x_recv.at[slot],
            far_dev,
        )

    def take_col(j, half, index):
        for target in range(2):
            col_own_copy(j, half, index, target).wait()
            col_copy(j, half, index, target).wait_recv()
            mate_in[j][target, half, index] = mate_in[j][target, half, index] + own[j][target, half, index]
        x_copy(j, half, index).start()

    def take_x(j, half, index):
        x_copy(j, half, index).wait_recv()
        far_in[j][half, index] = far_in[j][half, index] + mate_in[j][group, half, index]

    half_depth = normed_ref.shape[1] // 2
    gate_up, down = made
    units = parts[gate_up].count // 2

    def left_copies(unit, of_down):
        if of_down:
            source = act_ref.at[:, pl.ds(pl.multiple_of(unit * 256, 256), 256)]
            slot = (units + unit) % 2
            return [pltpu.make_async_copy(source, left.at[slot], left_sem.at[slot, 0])]
        slot = unit % 2
        copies = []
        for half in range(2):
            first = pl.multiple_of(half * half_depth + unit * 128, 128)
            target = left.at[slot, :, pl.ds(half * 128, 128)]
            copies.append(
                pltpu.make_async_copy(normed_ref.at[:, pl.ds(first, 128)], target, left_sem.at[slot, half])
            )
        return copies

    d_low_load = pltpu.make_async_copy(d_low_ref, right.at[:, pl.ds(0, d_low_ref.shape[1])], right_sem.at[1])
    d_gate_up_load = pltpu.make_async_copy(d_gate_up_ref, right, right_sem.at[0])

    def start_unit(j, unit):
        of_down = j == down
        part = parts[j]
        for copy in left_copies(unit, of_down):
            copy.wait()

        @pl.when(unit + 1 < part.count // 2)
        def _():
            for copy in left_copies(unit + 1, of_down):
                copy.start()

        if not of_down:
            @pl.when(unit + 1 == units)
            def _():
                for copy in left_copies(0, True):
                    copy.start()

        @pl.when(unit == 0)
        def _():
            (d_low_load if of_down else d_gate_up_load).wait()

        for chunk in range(2):
            index = 2 * unit + chunk

            @pl.when(index >= SLOTS)
            def _(index=index):
                row_copy(j, jnp.maximum(index - SLOTS, 0)).wait_send()

        slot = ((units + unit) if of_down else unit) % 2

        @pl.loop(0, left.shape[1] // 256)
        def _(block):
            here = pl.ds(pl.multiple_of(block * 256, 256), 256)
            left_t[:, here] = left[slot, here, :].T

    def tile(j, unit, number, targets):
        rows = parts[j].rows
        where = pl.ds(pl.multiple_of(number * 256, 256), 256)
        product = dot(left_t[...], right[:, where]).astype(BF)
        for place, (target, chunk, first_tile) in enumerate(targets):
            to = pl.ds(pl.multiple_of((number - first_tile) * 256, 256), 256)
            target[j][(2 * unit + chunk) % SLOTS, :, to] = product[place * rows : (place + 1) * rows]

    def make(j, unit, second):
        part = parts[j]
        if not second:
            start_unit(j, unit)
        if j == down:
            tiles = part.cols // 256
            first, target = (0, own) if second else (tiles, leaving)
            targets = [(target, 0, first), (target, 1, first)]
            pl.loop(first, first + tiles)(lambda number: tile(j, unit, number, targets))
        else:
            tiles = part.cols // 256
            targets = [(own, 0, 0), (own, 1, 0), (leaving, 0, 0), (leaving, 1, 0)]
            bounds = (tiles // 2, tiles) if second else (0, tiles // 2)
            pl.loop(*bounds)(lambda number: tile(j, unit, number, targets))
        if second and j != down:
            @pl.when(unit + 1 == units)
            def _():
                d_low_load.start()

        if second != (j == down):
            for chunk in range(2):
                row_copy(j, 2 * unit + chunk).start()

    def row_copy(j, index):
        slot = parts[j].base + index
        source = far_in[j].at[1, index] if parts[j].col else leaving[j].at[index % SLOTS]
        return remote(source, near[j].at[index], row_send.at[slot], row_recv.at[slot], other_row)

    def in_copy(j, index):
        slot = parts[j].base + index
        return remote(near[j].at[index], far[j].at[index], in_send.at[slot], far_recv.at[slot], end_next)

    def mid_copy(j, index):
        slot = parts[j].base + index
        return remote(far[j].at[index], near[j].at[index], mid_send.at[slot], wide_recv.at[slot], mid_other)

    def back_copy(j, index):
        slot = parts[j].base + index
        return remote(near[j].at[index], far[j].at[index], in_send.at[slot], far_recv.at[slot], mid_outer)

    def out_copy(j, index, source):
        slot = parts[j].base + index
        return pltpu.make_async_copy(source[j].at[index], parts[j].cut(outs[j], index, 0), out_sem.at[slot])

    def each(step, action):
        for j, part in enumerate(parts):
            index = step - part.base

            @pl.when((index >= 0) & (index < part.count))
            def _(j=j, index=index):
                action(j, index)

    def send_row(j, index):
        if parts[j].col:
            row_copy(j, index).start()
        else:
            @pl.when(index % 2 == 0)
            def _():
                make(j, index // 2, False)

            @pl.when(index % 2 == 1)
            def _():
                make(j, index // 2, True)

    def take_row(j, index):
        row_copy(j, index).wait_recv()
        mine = far_in[j][0, index] if parts[j].col else own[j][index % SLOTS]
        near[j][index] = near[j][index] + mine

        @pl.when(at_end)
        def _():
            in_copy(j, index).start()

    def take_far(j, index):
        back_copy(j, index).wait_recv()
        far[j][index] = far[j][index] + near[j][index]
        pl.semaphore_signal(free_sem, 1, device_id=mid_other, device_id_type=pl.DeviceIdType.MESH)
        pl.semaphore_wait(free_sem, 1)
        mid_copy(j, index).start()

    def take_wide(j, index):
        mid_copy(j, index).wait_recv()
        near[j][index] = near[j][index] + far[j][index]
        back_copy(j, index).start()
        out_copy(j, index, near).start()

    def take_back(j, index):
        in_copy(j, index).wait_recv()
        out_copy(j, index, far).start()

    def row_sent(j, index):
        @pl.when(jnp.logical_or(parts[j].col, index >= parts[j].count - SLOTS))
        def _():
            row_copy(j, index).wait_send()

    def finish_end(j, index):
        row_sent(j, index)
        in_copy(j, index).wait_send()
        out_copy(j, index, far).wait()

    def finish_mid(j, index):
        row_sent(j, index)
        mid_copy(j, index).wait_send()
        back_copy(j, index).wait_send()
        out_copy(j, index, near).wait()

    def small_copy(stage, source, where):
        return remote(small_sum.at[source], small_in.at[stage], small_send.at[stage], small_recv.at[stage], where)

    plane_hops = [small_copy(0, 0, mate), small_copy(1, 1, far_dev), small_copy(2, 2, other_row)]
    small_end = small_copy(3, 3, end_next)
    small_mid = small_copy(4, 4, mid_other)
    small_back = small_copy(3, 5, mid_outer)
    small_load = pltpu.make_async_copy(small_ref, small_sum.at[0], small_local.at[0])
    small_store = pltpu.make_async_copy(small_sum.at[5], small_out, small_local.at[1])

    span, width = mine_ref.shape[0] // 4, mine_ref.shape[1] // 2
    member = 2 * row + side
    dealt = []
    for index, (to_row, to_side, where) in enumerate(
        [(1 - row, side, other_row), (1 - row, 1 - side, cross), (row, 1 - side, mate), (row, side, None)]
    ):
        for high in range(2):
            piece = 7 - member if high else member
            first = pl.multiple_of(to_side * 2 * span + high * span, span)
            source = mine_ref.at[pl.ds(first, span), pl.ds((0 if index >= 2 else 1) * width, width)]
            target = dealt_ref.at[pl.ds(pl.multiple_of(piece * span, span), span), :]
            if where is None:
                dealt.append(pltpu.make_async_copy(source, target, deal_local.at[high]))
            else:
                dealt.append(remote(source, target, deal_send.at[index, high], deal_recv.at[index, high], where))

    total = sum(part.count for part in parts)
    for copy in left_copies(0, False):
        copy.start()
    d_gate_up_load.start()
    small_load.start()
    for copy in dealt[4:]:
        copy.start()
    for j in col_parts:
        for half in (1, 0):
            for index in range(parts[j].count):
                for target in range(2):
                    col_own_copy(j, half, index, target).start()
                    col_copy(j, half, index, target).start()

    @pl.loop(0, AHEAD)
    def _(step):
        each(step, send_row)

    pieces = [(j, half, index) for j in col_parts for half in (1, 0) for index in range(parts[j].count)]

    @pl.loop(0, total + LAG)
    def _(step):
        each(step + AHEAD, send_row)
        each(step, take_row)

        @pl.when(at_end)
        def _():
            each(step - LAG, take_back)

        @pl.when(jnp.logical_not(at_end))
        def _():
            each(step - FAR_LAG, take_far)
            each(step - WIDE_LAG, take_wide)

        @pl.when(step == total - AHEAD)
        def _():
            for copy in dealt[:4]:
                copy.start()

        for place, piece in enumerate(pieces):
            @pl.when(step == place + 1)
            def _(piece=piece):
                take_col(*piece)

            @pl.when(step == place + 5)
            def _(piece=piece):
                take_x(*piece)

        @pl.when(step == 0)
        def _():
            small_load.wait()
            plane_hops[0].start()

        for hop in range(3):
            @pl.when(step == hop + 1)
            def _(hop=hop):
                plane_hops[hop].wait_recv()
                small_sum[hop + 1] = small_sum[hop] + small_in[hop]
                if hop < 2:
                    plane_hops[hop + 1].start()

        @pl.when(at_end & (step == 3))
        def _():
            small_end.start()

        @pl.when(at_end & (step == 10))
        def _():
            small_end.wait_recv()
            small_sum[5] = small_in[3]
            small_store.start()

        @pl.when(jnp.logical_not(at_end) & (step == 5))
        def _():
            small_back.wait_recv()
            small_sum[4] = small_sum[3] + small_in[3]
            small_mid.start()

        @pl.when(jnp.logical_not(at_end) & (step == 7))
        def _():
            small_mid.wait_recv()
            small_sum[5] = small_sum[4] + small_in[4]
            small_back.start()
            small_store.start()

    for copy in plane_hops:
        copy.wait_send()
    small_store.wait()
    for copy in dealt:
        copy.wait()
    for j, half, index in pieces:
        for target in range(2):
            col_copy(j, half, index, target).wait_send()
        x_copy(j, half, index).wait_send()

    @pl.when(at_end)
    def _():
        small_end.wait_send()

        @pl.loop(0, total)
        def _(step):
            each(step, finish_end)

    @pl.when(jnp.logical_not(at_end))
    def _():
        small_mid.wait_send()
        small_back.wait_send()

        @pl.loop(0, total)
        def _(step):
            each(step, finish_mid)


def reduce_all(planes, normed, d_gate_up, act, d_low, grad_out, grad_project, small, mine):
    depth, width = normed.shape[1], act.shape[1]
    parts = [Part(0, 64, d_gate_up.shape[1], depth // 128, 0, False)]
    for rows, height, col in ((grad_out.shape[1] // 2, grad_out.shape[1], True),
                              (grad_project.shape[1] // 2, grad_project.shape[1], True), (128, width, False)):
        parts.append(Part(1, rows, depth // 2, height // rows, parts[-1].base + parts[-1].count, col))
    base = parts[-1].base + parts[-1].count
    shapes = [(part.count, part.rows, part.cols) for part in parts]
    col_shapes = [(2, *shape) for part, shape in zip(parts, shapes) if part.col]
    made_shapes = [(SLOTS, *shape[1:]) for part, shape in zip(parts, shapes) if not part.col]
    pieces = sum(shape[1] * 2 for shape in col_shapes)
    own_shapes = [
        (2, 2, *shape) if part.col else (SLOTS, *shape[1:]) for part, shape in zip(parts, shapes)
    ]
    anywhere = pl.BlockSpec(memory_space=pl.ANY)
    dma = pltpu.SemaphoreType.DMA
    tokens = normed.shape[0]
    inputs = (normed, d_gate_up, act, d_low, grad_out, grad_project, small, mine)
    return pl.pallas_call(
        functools.partial(reduce_kernel, parts, planes),
        out_shape=[jax.ShapeDtypeStruct((n * r, c), BF) for n, r, c in shapes]
        + [
            jax.ShapeDtypeStruct(small.shape, F32),
            jax.ShapeDtypeStruct((2 * mine.shape[0], mine.shape[1] // 2), BF),
        ],
        in_specs=[anywhere] * len(inputs),
        out_specs=[anywhere] * (len(parts) + 2),
        scratch_shapes=[pltpu.VMEM(shape, BF) for _ in range(2) for shape in shapes]
        + [pltpu.VMEM(shape, BF) for shape in own_shapes + made_shapes]
        + [pltpu.VMEM((2, *shape), BF) for shape in col_shapes]
        + [pltpu.VMEM(shape, BF) for shape in col_shapes]
        + [
            pltpu.VMEM((tokens, d_gate_up.shape[1]), BF),
            pltpu.VMEM((2, tokens, 256), BF),
            pltpu.VMEM((256, tokens), BF),
            dma((2,)),
            dma((2, 2)),
            pltpu.SemaphoreType.REGULAR,
        ]
        + [dma((base,)) for _ in range(7)]
        + [dma((2, pieces)), dma((2, pieces)), dma((2, pieces)), dma((pieces,)), dma((pieces,))]
        + [dma((2,)), dma((5,)), dma((5,))]
        + [pltpu.VMEM((5, *small.shape), F32), pltpu.VMEM((6, *small.shape), F32)]
        + [dma((3, 2)), dma((3, 2)), dma((2,))],
        compiler_params=pltpu.CompilerParams(
            collective_id=0, has_side_effects=True, vmem_limit_bytes=60 * 1024 * 1024
        ),
        name="reduce_grads",
    )(*inputs)


TILE = 256
STEPS = 8


def spread_kernel(forward, fast, *refs):
    refs = list(refs)

    def take(number):
        taken = refs[:number]
        del refs[:number]
        return taken

    (mine_ref,) = take(1)
    weights = take(5 if forward and fast else 6)
    if not forward:
        gate_ref, up_ref = take(2)
    dealt_in = take(1) if fast else None
    if forward:
        all_ref, gate_ref, up_ref, act_ref, out_ref = take(5)
        if fast:
            (down_out,) = take(1)
    else:
        all_ref, d_gate_up_ref, out_ref = take(3)
    dealt_out = take(1) if fast else None
    block, w_gate, w_up, w_down, kept, to_mate, from_mate, far_part, to_far, from_mate_far, far_sum, from_far = take(12)
    (
        weight_sem, block_sem, out_sem, mate_send, mate_recv, x_send, x_recv, pass_send, pass_recv,
        sum_send, sum_recv, part_send, part_recv, back_send, back_recv,
    ) = take(15)
    deal_send, deal_recv, deal_local, row_send, row_recv, plane_send, plane_recv = take(7)
    stage = refs
    tokens, depth = mine_ref.shape
    quarter = tokens // 4
    width = w_gate.shape[1]
    half = depth // 2
    row = lax.axis_index("row")
    group, side = lax.axis_index("group"), lax.axis_index("side")
    mate, far = {"side": 1 - side}, {"group": 1 - group}
    other_row, cross = {"row": 1 - row}, {"row": 1 - row, "side": 1 - side}
    parity = lax.axis_index("dp") % 2
    next_plane = {"dp": lax.axis_index("dp") + 1 - 2 * parity}

    def remote(source, target, send, recv, where):
        return pltpu.make_async_remote_copy(
            source, target, send, recv, device_id=where, device_id_type=pl.DeviceIdType.MESH
        )

    barrier = pltpu.get_barrier_semaphore()
    greeted = [mate, far]
    if fast:
        greeted += [other_row, cross] + ([next_plane] if forward else [])
    for where in greeted:
        pl.semaphore_signal(barrier, 1, device_id=where, device_id_type=pl.DeviceIdType.MESH)

    dealt_own, dealt_sent, down_chunks = [], [], []
    if fast:
        span = tokens // 4
        member = 2 * row + side
        for index, (to_row, to_side, where) in enumerate(
            [(1 - row, side, other_row), (1 - row, 1 - side, cross), (row, 1 - side, mate), (row, side, None)]
        ):
            slot = 0 if index >= 2 else 1
            there = 2 * to_row + to_side
            for high in range(2):
                piece = 7 - there if high else there
                if not forward:
                    piece = 7 - member if high else member
                whole = pl.ds(pl.multiple_of(piece * span, span), span), slice(None)
                of_side = side if forward else to_side
                first = pl.multiple_of(of_side * 2 * span + high * span, span)
                part = pl.ds(first, span), pl.ds(slot * half, half)
                source = dealt_in[0].at[whole] if forward else dealt_in[0].at[part]
                target = dealt_out[0].at[part] if forward else dealt_out[0].at[whole]
                if where is None:
                    dealt_own.append(pltpu.make_async_copy(source, target, deal_local.at[high]))
                else:
                    sems = deal_send.at[index, high], deal_recv.at[index, high]
                    dealt_sent.append(remote(source, target, *sems, where))
        if forward:
            rows = width // 8
            for index in range(4):
                here = pl.ds(pl.multiple_of((4 * parity + index) * rows, 16), rows)
                place = w_down.at[here, pl.ds(half, half)]
                down_chunks.append(
                    (
                        remote(weights[4].at[here, :], place, row_send.at[index], row_recv.at[index], other_row),
                        remote(place, place, plane_send.at[index], plane_recv.at[index], next_plane),
                    )
                )

    loads = []
    for index, (source, target) in enumerate(
        [
            (weights[0], w_gate.at[pl.ds(0, half), :]),
            (weights[1], w_gate.at[pl.ds(half, half), :]),
            (weights[2], w_up.at[pl.ds(0, half), :]),
            (weights[3], w_up.at[pl.ds(half, half), :]),
            (weights[4], w_down.at[:, pl.ds(0, half)]),
        ]
        + ([] if forward and fast else [(weights[5], w_down.at[:, pl.ds(half, half)])])
    ):
        loads.append(pltpu.make_async_copy(source, target, weight_sem.at[index]))
    order = loads if forward else loads[4:] + loads[:4]
    mine_copies = [
        pltpu.make_async_copy(
            mine_ref.at[pl.ds(i * 2 * quarter, 2 * quarter), :], block.at[i], block_sem.at[i]
        )
        for i in range(2)
    ]
    for copy in mine_copies:
        copy.start()
    for copy in order:
        copy.start()
    pl.semaphore_wait(barrier, len(greeted))
    for over_row, over_planes in down_chunks:
        over_row.start()

    def piece(index):
        return mine_ref.at[pl.ds(index * quarter, quarter), :]

    def mate_copy(index):
        return remote(
            piece(index),
            block.at[2 + index // 2, pl.ds(index % 2 * quarter, quarter), :],
            mate_send.at[index],
            mate_recv.at[index],
            mate,
        )

    def x_copy(index):
        return remote(
            piece(index), block.at[4 + index, pl.ds(0, quarter), :], x_send.at[index], x_recv.at[index], far
        )

    def pass_copy(index):
        return remote(
            block.at[4 + index, pl.ds(0, quarter), :],
            block.at[4 + index, pl.ds(quarter, quarter), :],
            pass_send.at[index],
            pass_recv.at[index],
            mate,
        )

    def sum_copy(index):
        return remote(to_mate.at[index], from_mate.at[index], sum_send.at[index], sum_recv.at[index], mate)

    def part_copy(index):
        return remote(to_far.at[index], from_mate_far.at[index], part_send.at[index], part_recv.at[index], mate)

    def back_copy(index):
        return remote(far_sum.at[index], from_far.at[index], back_send.at[index], back_recv.at[index], far)

    x_copy(0).start()
    for index in range(4):
        mate_copy(index).start()
    x_copy(1).start()
    for copy in dealt_sent + dealt_own:
        copy.start()
    for copy in mine_copies:
        copy.wait()

    def emit(step, where, part):
        @pl.when(step < 2)
        def _():
            kept[jnp.minimum(step, 1), :, where] = part

        @pl.when((step >= 2) & (step < 4))
        def _():
            to_mate[jnp.clip(step - 2, 0, 1), :, where] = part.astype(BF)

        @pl.when(step >= 4)
        def _():
            far_part[jnp.maximum(step - 4, 0), :, where] = part[:quarter]
            to_far[jnp.maximum(step - 4, 0), :, where] = part[quarter:].astype(BF)

    def all_copy(step):
        return pltpu.make_async_copy(block.at[step], all_ref.at[step], out_sem.at[0, step])

    if forward:
        stage_gate, stage_up, stage_act = stage

        def saves(step):
            slot = step % 2
            return [
                pltpu.make_async_copy(stage_gate.at[slot], gate_ref.at[step], out_sem.at[1, step]),
                pltpu.make_async_copy(stage_up.at[slot], up_ref.at[step], out_sem.at[2, step]),
                pltpu.make_async_copy(stage_act.at[step], act_ref.at[step], out_sem.at[3, step]),
            ]

        def fetches(step):
            return []

        def first_loads():
            for copy in loads[:4]:
                copy.wait()

        def second_loads():
            for copy in loads[4:]:
                copy.wait()

        def first_half(step):
            slot = step % 2

            @pl.loop(0, width // TILE)
            def _(tile):
                where = pl.ds(pl.multiple_of(tile * TILE, TILE), TILE)
                gate = dot(block[step], w_gate[:, where])
                up = dot(block[step], w_up[:, where])
                stage_gate[slot, :, where] = gate.astype(BF)
                stage_up[slot, :, where] = up.astype(BF)
                stage_act[step, :, where] = (gate * up / (1.0 + jnp.exp(-gate))).astype(BF)

        def second_half(step, first=0, last=depth // TILE):
            @pl.loop(first, last)
            def _(tile):
                where = pl.ds(pl.multiple_of(tile * TILE, TILE), TILE)
                emit(step, where, dot(stage_act[step], w_down[:, where]))

    else:
        stage_gate, stage_up, stage_d, fetch_sem = stage

        def saves(step):
            return [
                pltpu.make_async_copy(stage_d.at[step % 2], d_gate_up_ref.at[step], out_sem.at[1, step])
            ]

        def fetches(step):
            slot = step % 2
            return [
                pltpu.make_async_copy(gate_ref.at[step], stage_gate.at[slot], fetch_sem.at[0, step]),
                pltpu.make_async_copy(up_ref.at[step], stage_up.at[slot], fetch_sem.at[1, step]),
            ]

        def first_loads():
            for copy in loads[4:]:
                copy.wait()

        def second_loads():
            for copy in loads[:4]:
                copy.wait()

        def first_half(step):
            slot = step % 2

            @pl.loop(0, width // TILE)
            def _(tile):
                first = pl.multiple_of(tile * TILE, TILE)
                where = pl.ds(first, TILE)
                d_act = dot(block[step], w_down[where, :], ((1,), (1,)))
                gate = stage_gate[slot, :, where].astype(F32)
                up = stage_up[slot, :, where].astype(F32)
                sig = 1.0 / (1.0 + jnp.exp(-gate))
                d_gate = d_act * up * sig * (1.0 + gate * (1.0 - sig))
                stage_d[slot, :, where] = d_gate.astype(BF)
                stage_d[slot, :, pl.ds(pl.multiple_of(width + first, TILE), TILE)] = (d_act * gate * sig).astype(BF)

        def second_half(step):
            slot = step % 2

            @pl.loop(0, depth // TILE)
            def _(tile):
                where = pl.ds(pl.multiple_of(tile * TILE, TILE), TILE)
                part = dot(stage_d[slot, :, :width], w_gate[where, :], ((1,), (1,)))
                part += dot(stage_d[slot, :, width:], w_up[where, :], ((1,), (1,)))
                emit(step, where, part)

    def finish_far(index):
        part_copy(index).wait_recv()
        total = far_part[index] + from_mate_far[index].astype(F32)
        far_sum[index] = total.astype(BF)
        back_copy(index).start()

    split = forward and fast
    if split:
        down_saved = pltpu.make_async_copy(w_down.at[:, pl.ds(half, half)], down_out, weight_sem.at[5])
    for copy in fetches(0):
        copy.start()

    @pl.loop(0, STEPS)
    def _(step):
        @pl.when((step == 2) | (step == 3))
        def _():
            index = jnp.clip(2 * (step - 2), 0, 2)
            mate_copy(index).wait_recv()
            mate_copy(index + 1).wait_recv()

        @pl.when(step >= 4)
        def _():
            index = jnp.maximum(step - 4, 0)
            x_copy(index).wait_recv()
            pass_copy(index).start()
            pass_copy(index).wait_recv()

        all_copy(step).start()
        for copy in fetches(step):
            copy.wait()

        if not forward:
            @pl.when(step < STEPS - 1)
            def _():
                for copy in fetches(jnp.minimum(step + 1, STEPS - 1)):
                    copy.start()

        @pl.when(step == 0)
        def _():
            first_loads()

        @pl.when(step >= 2)
        def _():
            for copy in saves(jnp.maximum(step - 2, 0)):
                copy.wait()

        first_half(step)

        @pl.when(step == 0)
        def _():
            second_loads()

        if split:
            @pl.when(step < 6)
            def _():
                second_half(step, 0, half // TILE)

            for index in range(4):
                @pl.when(step == index + 1)
                def _(index=index):
                    down_chunks[index][0].wait_recv()
                    down_chunks[index][1].start()

            @pl.when(step == 5)
            def _():
                for _, over_planes in down_chunks:
                    over_planes.wait_recv()
                down_saved.start()
                pl.loop(4, 6)(lambda early: second_half(early, half // TILE))
                part_copy(0).start()
                part_copy(1).start()

            @pl.when(step >= 6)
            def _():
                second_half(step)
                part_copy(jnp.maximum(step - 4, 0)).start()

            @pl.when(step == 6)
            def _():
                finish_far(0)
                finish_far(1)

            @pl.when(step == 7)
            def _():
                finish_far(2)
        else:
            second_half(step)
        for copy in saves(step):
            copy.start()

        @pl.when((step == 1) | (step == 3))
        def _():
            x_copy(2 + step // 2).start()

        if not split:
            @pl.when((step >= 2) & (step < 4))
            def _():
                sum_copy(jnp.clip(step - 2, 0, 1)).start()

            @pl.when(step >= 4)
            def _():
                part_copy(jnp.maximum(step - 4, 0)).start()

            @pl.when(step >= 5)
            def _():
                finish_far(jnp.maximum(step - 5, 0))

    if split:
        pl.loop(2, 4)(lambda early: second_half(early, half // TILE))
        sum_copy(0).start()
        sum_copy(1).start()
    finish_far(3)
    if split:
        pl.loop(0, 2)(lambda early: second_half(early, half // TILE))
    for index in range(2):
        sum_copy(index).wait_recv()
        kept[index] = kept[index] + from_mate[index].astype(F32)
    results = []
    for index in range(4):
        back_copy(index).wait_recv()
        rows = pl.ds(index % 2 * quarter, quarter)
        kept[index // 2, rows, :] = kept[index // 2, rows, :] + from_far[index].astype(F32)
        if index % 2:
            copy = pltpu.make_async_copy(kept.at[index // 2], out_ref.at[index // 2], block_sem.at[index // 2])
            copy.start()
            results.append(copy)
    for copy in results + dealt_own:
        copy.wait()
    for copy in dealt_sent:
        copy.wait()
    for over_row, over_planes in down_chunks:
        over_row.wait_send()
        over_planes.wait_send()
    if forward and fast:
        down_saved.wait()

    @pl.loop(0, STEPS)
    def _(step):
        all_copy(step).wait()

        @pl.when(step >= STEPS - 2)
        def _():
            for copy in saves(step):
                copy.wait()

        @pl.when(step < 4)
        def _():
            index = jnp.minimum(step, 3)
            mate_copy(index).wait_send()
            x_copy(index).wait_send()
            pass_copy(index).wait_send()
            part_copy(index).wait_send()
            back_copy(index).wait_send()

        @pl.when(step < 2)
        def _():
            sum_copy(jnp.minimum(step, 1)).wait_send()


def spread(forward, mine, weights, kept=(), dealt=None):
    tokens, depth = mine.shape
    quarter, double = tokens // 4, tokens // 2
    width = weights[0].shape[1]
    anywhere = pl.BlockSpec(memory_space=pl.ANY)
    wide = jax.ShapeDtypeStruct((STEPS, double, width), BF)
    whole = jax.ShapeDtypeStruct((STEPS, double, depth), BF)
    out = jax.ShapeDtypeStruct((2, double, depth), F32)
    if forward:
        outs = [whole, wide, wide, wide, out]
        if dealt is not None:
            outs.append(jax.ShapeDtypeStruct((width, depth // 2), BF))
            outs.append(jax.ShapeDtypeStruct((tokens, depth), BF))
        stage = [
            pltpu.VMEM((2, double, width), BF),
            pltpu.VMEM((2, double, width), BF),
            pltpu.VMEM((STEPS, double, width), BF),
        ]
    else:
        outs = [whole, jax.ShapeDtypeStruct((STEPS, double, 2 * width), BF), out]
        if dealt is not None:
            outs.append(jax.ShapeDtypeStruct((2 * tokens, depth // 2), BF))
        stage = [
            pltpu.VMEM((2, double, width), BF),
            pltpu.VMEM((2, double, width), BF),
            pltpu.VMEM((2, double, 2 * width), BF),
            pltpu.SemaphoreType.DMA((2, STEPS)),
        ]
    inputs = [mine, *weights, *kept] + ([] if dealt is None else [dealt])
    return pl.pallas_call(
        functools.partial(spread_kernel, forward, dealt is not None),
        out_shape=outs,
        in_specs=[anywhere] * len(inputs),
        out_specs=[anywhere] * len(outs),
        scratch_shapes=[
            pltpu.VMEM((STEPS, double, depth), BF),
            pltpu.VMEM((depth, width), BF),
            pltpu.VMEM((depth, width), BF),
            pltpu.VMEM((width, depth), BF),
            pltpu.VMEM((2, double, depth), F32),
            pltpu.VMEM((2, double, depth), BF),
            pltpu.VMEM((2, double, depth), BF),
            pltpu.VMEM((4, quarter, depth), F32),
            pltpu.VMEM((4, quarter, depth), BF),
            pltpu.VMEM((4, quarter, depth), BF),
            pltpu.VMEM((4, quarter, depth), BF),
            pltpu.VMEM((4, quarter, depth), BF),
            pltpu.SemaphoreType.DMA((6,)),
            pltpu.SemaphoreType.DMA((2,)),
            pltpu.SemaphoreType.DMA((4, STEPS)),
        ]
        + [pltpu.SemaphoreType.DMA((4,)) for _ in range(6)]
        + [pltpu.SemaphoreType.DMA((2,)) for _ in range(2)]
        + [pltpu.SemaphoreType.DMA((4,)) for _ in range(4)]
        + [pltpu.SemaphoreType.DMA((3, 2)), pltpu.SemaphoreType.DMA((3, 2)), pltpu.SemaphoreType.DMA((2,))]
        + [pltpu.SemaphoreType.DMA((4,)) for _ in range(4)]
        + stage,
        compiler_params=pltpu.CompilerParams(
            collective_id=1 if forward else 2,
            has_side_effects=True,
            vmem_limit_bytes=60 * 1024 * 1024,
        ),
        name="feed_forward" if forward else "feed_forward_back",
    )(*inputs)


def front_kernel(*refs):
    refs = list(refs)

    def take(number):
        taken = refs[:number]
        del refs[:number]
        return taken

    tokens_ref, w_project_ref, w_out_ref, gains_ref, gate_ref, up_ref = take(6)
    cos_ref, sin_ref, query_gain_ref, key_gain_ref = take(4)
    (
        states_out, normed_out, raw_out, query_out, key_out, pair_out, mixed_out, logs_out, hidden_out, normed_two_out,
        w_project_out, w_out_out, gate_out, up_out, gains_out,
    ) = take(15)
    states, normed, w_project, raw, key_raw, query, pair_own, pair, key_n, mixed_t, logs, mixed = take(12)
    w_out, hidden, gains = take(3)
    token_send, token_recv, token_local = take(3)
    project_send, project_recv, out_send, out_recv, gain_send, gain_recv = take(6)
    pair_send, pair_recv, row_send, row_recv, plane_send, plane_recv, local, store = take(8)

    plane, row = lax.axis_index("dp"), lax.axis_index("row")
    group, side = lax.axis_index("group"), lax.axis_index("side")
    other_row, mate, far = {"row": 1 - row}, {"side": 1 - side}, {"group": 1 - group}
    cross = {"row": 1 - row, "side": 1 - side}
    parity = plane % 2
    next_plane = {"dp": plane + 1 - 2 * parity}
    shard, width = tokens_ref.shape
    mine, depth = states.shape
    pieces = 8
    span = shard // pieces
    member = 2 * row + side
    kv_rows = key_raw.shape[0]

    def remote(source, target, send, recv, where):
        return pltpu.make_async_remote_copy(
            source, target, send, recv, device_id=where, device_id_type=pl.DeviceIdType.MESH
        )

    barrier = pltpu.get_barrier_semaphore()
    for where in (other_row, mate, far, cross, next_plane):
        pl.semaphore_signal(barrier, 1, device_id=where, device_id_type=pl.DeviceIdType.MESH)

    def token_copies(to_row, to_side, index, where):
        target_member = 2 * to_row + to_side
        slot = 1 if to_row is not row else 0
        copies = []
        for high in range(2):
            piece = pieces - 1 - target_member if high else target_member
            source = tokens_ref.at[pl.ds(pl.multiple_of(piece * span, span), span), :]
            first = pl.multiple_of(side * 2 * span + high * span, span)
            target = states.at[pl.ds(first, span), pl.ds(slot * width, width)]
            if where is None:
                copies.append(pltpu.make_async_copy(source, target, token_local.at[high]))
            else:
                sems = token_send.at[index, high], token_recv.at[index, high]
                copies.append(remote(source, target, *sems, where))
        return copies

    own_tokens = token_copies(row, side, 0, None)
    other = 1 - row
    sent_tokens = token_copies(other, side, 0, other_row)
    sent_tokens += token_copies(other, 1 - side, 1, cross)
    sent_tokens += token_copies(row, 1 - side, 2, mate)

    me, far_col = 2 * group + side, 2 * (1 - group) + side

    class Spread:
        def __init__(self, source, place, send, recv):
            self.copies = []

            def add(origin, target, where):
                index = len(self.copies)
                self.copies.append(remote(origin, target, send.at[index], recv.at[index], where))
                return self.copies[-1]

            here, there = parity, 1 - parity
            rows = source.shape[0] // 2
            first_half = source.at[pl.ds(pl.multiple_of(here * rows, 16), rows), :]
            self.to_row = add(first_half, place(me, 1, here), other_row)
            self.to_plane = add(place(me, 1, here), place(me, 1, here), next_plane)
            self.to_far = [add(source, place(me, 0, None), far)]
            self.to_far += [add(place(me, 1, half), place(me, 1, half), far) for half in (here, there)]
            self.to_mate = [add(source, place(me, 0, None), mate)]
            self.to_mate += [add(place(me, 1, half), place(me, 1, half), mate) for half in (here, there)]
            self.to_mate += [add(place(far_col, 0, None), place(far_col, 0, None), mate)]
            self.to_mate += [
                add(place(far_col, 1, half), place(far_col, 1, half), mate) for half in (here, there)
            ]

        def first(self):
            self.to_row.start()
            self.to_far[0].start()
            self.to_mate[0].start()

        def row_in(self):
            self.to_row.wait_recv()
            for copy in (self.to_plane, self.to_far[1], self.to_mate[1]):
                copy.start()

        def plane_in(self):
            self.to_plane.wait_recv()
            self.to_far[2].start()
            self.to_mate[2].start()

        def far_in(self, index):
            self.to_far[index].wait_recv()
            self.to_mate[3 + index].start()

        def mate_in(self, first, last):
            for copy in self.to_mate[first:last]:
                copy.wait_recv()

        def sent(self):
            for copy in self.copies:
                copy.wait_send()

    q_width = w_out_ref.shape[0]

    def project_place(col, slot, half):
        if half is None:
            return w_project.at[col, slot]
        return w_project.at[col, slot, pl.ds(pl.multiple_of(half * (width // 2), 16), width // 2), :]

    def out_place(col, slot, half):
        first, rows = col * q_width, q_width
        if half is not None:
            rows = q_width // 2
            first = first + half * rows
        return w_out.at[pl.ds(pl.multiple_of(first, 16), rows), pl.ds(slot * width, width)]

    project = Spread(w_project_ref, project_place, project_send, project_recv)
    output = Spread(w_out_ref, out_place, out_send, out_recv)
    own_project = pltpu.make_async_copy(w_project_ref, w_project.at[me, 0], local.at[0])
    own_output = pltpu.make_async_copy(w_out_ref, out_place(me, 0, None), local.at[1])
    own_gains = pltpu.make_async_copy(gains_ref, gains.at[0], local.at[2])
    sent_gains = remote(gains_ref, gains.at[1], gain_send.at[0], gain_recv.at[0], other_row)

    chunks = []
    for index, (source, target) in enumerate([(gate_ref, gate_out), (up_ref, up_out)]):
        rows = source.shape[0] // 4
        for part in range(2):
            here = pl.ds(pl.multiple_of((2 * parity + part) * rows, 64), rows)
            slot = 2 * index + part
            over_row = remote(source.at[here, :], target.at[here, :], row_send.at[slot], row_recv.at[slot], other_row)
            over_planes = remote(
                target.at[here, :], target.at[here, :], plane_send.at[slot], plane_recv.at[slot], next_plane
            )
            chunks.append((over_row, over_planes))

    def pass_on(index):
        chunks[index][0].wait_recv()
        chunks[index][1].start()

    own_copies = [own_gains, *own_tokens, own_project, own_output]
    for copy in own_copies:
        copy.start()
    pl.semaphore_wait(barrier, 5)
    sent_gains.start()
    project.first()
    for copy in sent_tokens:
        copy.start()
    chunks[0][0].start()
    for copy in own_copies:
        copy.wait()
    sent_gains.wait_recv()
    project.row_in()
    for copy in sent_tokens:
        copy.wait_recv()

    stores = []

    def save(source, target):
        copy = pltpu.make_async_copy(source, target, store.at[len(stores)])
        copy.start()
        stores.append(copy)
        return copy

    block = mine // 4

    @pl.loop(0, 4)
    def _(index):
        here = pl.ds(pl.multiple_of(index * block, block), block)
        values = states[here, :].astype(F32)
        inverse = lax.rsqrt(jnp.mean(values * values, axis=1, keepdims=True) + EPSILON)
        for slot in range(2):
            part = values[:, slot * width : (slot + 1) * width] * inverse
            normed[here, slot * width : (slot + 1) * width] = (part * gains[slot, 0:1, :]).astype(BF)

    save(states, states_out)
    normed_saved = save(normed, normed_out)
    save(gains, gains_out)

    def project_col(col):
        part = dot(normed[:, :width], w_project[col, 0]) + dot(normed[:, width:], w_project[col, 1])
        part = part.T
        heads = q_width // HD
        for head in range(heads):
            raw[col * heads + head] = part[head * HD : (head + 1) * HD]
        k_width = kv_rows // 4
        first = pl.multiple_of(col * k_width, 16)
        key_raw[pl.ds(first, k_width), :] = part[q_width : q_width + k_width].astype(BF)
        first = pl.multiple_of(kv_rows + col * k_width, 16)
        pair_own[pl.ds(first, k_width), :] = part[q_width + k_width :].astype(BF)

    project.plane_in()
    project.far_in(0)
    output.to_row.start()
    project_col(me)
    project.mate_in(0, 3)
    project_col(2 * group + 1 - side)
    project.far_in(1)
    project.far_in(2)
    project_col(far_col)
    project.mate_in(3, 6)
    project_col(2 * (1 - group) + 1 - side)
    save(raw, raw_out)
    save(key_raw, key_out)
    save(w_project, w_project_out)

    cosine, sine = cos_ref[...], sin_ref[...]

    def turned(values, gain):
        values = values * lax.rsqrt(jnp.mean(values * values, axis=0, keepdims=True) + EPSILON) * gain
        first, second = values[: HD // 2], values[HD // 2 :]
        return jnp.concatenate([first * cosine - second * sine, second * cosine + first * sine], axis=0)

    for head in range(kv_rows // HD):
        cut = slice(head * HD, (head + 1) * HD)
        pair_own[cut, :] = turned(key_raw[cut, :].astype(F32), key_gain_ref[...]).astype(BF)

    def places(who):
        starts = [who, pieces - 1 - who, pieces + who, 2 * pieces - 1 - who]
        return [pair.at[:, pl.ds(pl.multiple_of(start * span, span), span)] for start in starts]

    for index, place in enumerate(places(member)):
        place[...] = pair_own[:, index * span : (index + 1) * span]
    to_mate, to_row, passed = [], [], []
    for index, place in enumerate(places(member)):
        to_row.append(remote(place, place, pair_send.at[0, index], pair_recv.at[0, index], other_row))
        to_mate.append(remote(place, place, pair_send.at[1, index], pair_recv.at[1, index], mate))
    for index, place in enumerate(places(2 * (1 - row) + side)):
        passed.append(remote(place, place, pair_send.at[2, index], pair_recv.at[2, index], mate))
    for copy in to_row + to_mate:
        copy.start()
    output.to_far[0].start()
    output.to_mate[0].start()
    chunks[1][0].start()

    @pl.loop(0, raw.shape[0])
    def _(head):
        values = turned(raw[head], query_gain_ref[...]).astype(BF)
        query[head] = values * BF(1.0 / math.sqrt(HD))

    for index in range(4):
        to_row[index].wait_recv()
        passed[index].start()
    output.row_in()
    chunks[2][0].start()
    pass_on(0)
    for index in range(4):
        to_mate[index].wait_recv()
        passed[index].wait_recv()
    chunks[3][0].start()
    output.plane_in()
    output.far_in(0)

    firsts = [member, pieces - 1 - member, pieces + member, 2 * pieces - 1 - member]
    rows = REP * span
    ones = jnp.ones((16, KEYS), BF)

    @pl.loop(0, kv_rows // HD)
    def _(head):
        key_n[...] = pair[pl.ds(pl.multiple_of(head * HD, HD), HD), :].T
        value_rows = pl.ds(pl.multiple_of(kv_rows + head * HD, HD), HD)
        for index in range(4):
            cut = slice(index * span, (index + 1) * span)
            query_here = jnp.concatenate([query[head * REP + rep, :, cut] for rep in range(REP)], axis=1)
            first_query = firsts[index] * span
            full, last = tiles_of(first_query)

            def tile(where, accum, masked):
                first_key = pl.multiple_of(where * KEYS, KEYS)
                expo = jnp.exp(dot(key_n[pl.ds(first_key, KEYS), :], query_here))
                if masked:
                    expo = jnp.where(allowed(first_query, first_key, span, rows), expo, 0.0)
                value = jnp.concatenate([pair[value_rows, pl.ds(first_key, KEYS)], ones], axis=0)
                return accum + dot(value, expo.astype(BF))

            accum = tile(last, jnp.zeros((HD + 16, rows), F32), True)
            accum = lax.fori_loop(0, full, lambda where, total: tile(where, total, False), accum)
            total = accum[HD : HD + 1]
            result = accum[:HD] / total
            log = jnp.log(total)
            for rep in range(REP):
                part = slice(rep * span, (rep + 1) * span)
                mixed_t[pl.ds(pl.multiple_of((head * REP + rep) * HD, HD), HD), cut] = result[:, part]
                logs[head, rep : rep + 1, cut] = log[:, part]

        @pl.when(head == 2)
        def _():
            output.far_in(1)
            output.far_in(2)

        for number, index in ((1, 1), (3, 2)):
            @pl.when(head == number)
            def _(index=index):
                pass_on(index)

    save(query, query_out)
    save(mixed_t, mixed_out)
    save(logs, logs_out)
    save(pair, pair_out)
    pass_on(3)
    output.mate_in(0, 6)
    save(w_out, w_out_out)

    @pl.loop(0, mixed_t.shape[0] // 128)
    def _(index):
        here = pl.ds(pl.multiple_of(index * 128, 128), 128)
        mixed[:, here] = mixed_t[here, :].astype(BF).T

    @pl.loop(0, depth // TILE)
    def _(index):
        here = pl.ds(pl.multiple_of(index * TILE, TILE), TILE)
        hidden[:, here] = states[:, here].astype(F32) + dot(mixed[...], w_out[:, here])

    normed_saved.wait()

    @pl.loop(0, 4)
    def _(index):
        here = pl.ds(pl.multiple_of(index * block, block), block)
        values = hidden[here, :]
        inverse = lax.rsqrt(jnp.mean(values * values, axis=1, keepdims=True) + EPSILON)
        for slot in range(2):
            part = values[:, slot * width : (slot + 1) * width] * inverse
            normed[here, slot * width : (slot + 1) * width] = (part * gains[slot, 1:2, :]).astype(BF)

    save(hidden, hidden_out)
    save(normed, normed_two_out)
    for copy in stores:
        if copy is not normed_saved:
            copy.wait()
    sent_gains.wait_send()
    for copy in sent_tokens + to_row + to_mate + passed:
        copy.wait_send()
    project.sent()
    output.sent()
    for over_row, over_planes in chunks:
        over_row.wait_send()
        over_planes.wait_recv()
        over_planes.wait_send()


def front(tokens, w_project, w_out, gains, w_gate, w_up, cosine, sine, query_gain, key_gain):
    shard, width = tokens.shape
    mine, depth = shard // 2, 2 * width
    q_width, columns = w_out.shape[0], w_project.shape[1]
    kv_rows = KVH * HD
    anywhere = pl.BlockSpec(memory_space=pl.ANY)
    inside = pl.BlockSpec(memory_space=pltpu.VMEM)
    dma = pltpu.SemaphoreType.DMA
    shape = jax.ShapeDtypeStruct
    return pl.pallas_call(
        front_kernel,
        out_shape=[
            shape((mine, depth), BF),
            shape((mine, depth), BF),
            shape((QH, HD, mine), F32),
            shape((QH, HD, mine), BF),
            shape((kv_rows, mine), BF),
            shape((2 * kv_rows, GROUP), BF),
            shape((QH * HD, mine), F32),
            shape((KVH, REP, mine), F32),
            shape((mine, depth), F32),
            shape((mine, depth), BF),
            shape((4, 2, width, columns), BF),
            shape((4 * q_width, depth), BF),
            shape(w_gate.shape, BF),
            shape(w_up.shape, BF),
            shape((2, 2, width), F32),
        ],
        in_specs=[anywhere] * 6 + [inside] * 4,
        out_specs=[anywhere] * 15,
        scratch_shapes=[
            pltpu.VMEM((mine, depth), BF),
            pltpu.VMEM((mine, depth), BF),
            pltpu.VMEM((4, 2, width, columns), BF),
            pltpu.VMEM((QH, HD, mine), F32),
            pltpu.VMEM((kv_rows, mine), BF),
            pltpu.VMEM((QH, HD, mine), BF),
            pltpu.VMEM((2 * kv_rows, mine), BF),
            pltpu.VMEM((2 * kv_rows, GROUP), BF),
            pltpu.VMEM((GROUP, HD), BF),
            pltpu.VMEM((QH * HD, mine), F32),
            pltpu.VMEM((KVH, REP, mine), F32),
            pltpu.VMEM((mine, QH * HD), BF),
            pltpu.VMEM((4 * q_width, depth), BF),
            pltpu.VMEM((mine, depth), F32),
            pltpu.VMEM((2, 2, width), F32),
            dma((3, 2)), dma((3, 2)), dma((2,)),
            dma((11,)), dma((11,)), dma((11,)), dma((11,)), dma((1,)), dma((1,)),
            dma((3, 4)), dma((3, 4)), dma((4,)), dma((4,)), dma((4,)), dma((4,)), dma((3,)), dma((13,)),
        ],
        compiler_params=pltpu.CompilerParams(
            collective_id=3, has_side_effects=True, vmem_limit_bytes=56 * 1024 * 1024
        ),
        name="front",
    )(tokens, w_project, w_out, gains, w_gate, w_up, cosine, sine, query_gain, key_gain)


def back_kernel(*refs):
    query, d_out, logs_ref, delta_ref, pair, raw, key_raw, cos_ref, sin_ref, query_gain, key_gain = refs[:11]
    d_project, query_gain_out, key_gain_out = refs[11:14]
    key_n, value_n, d_key, d_value, both_t, staged, come, gain_sum, send_sem, recv_sem = refs[14:]
    row, side = lax.axis_index("row"), lax.axis_index("side")
    others = [
        (2 * (1 - row) + side, {"row": 1 - row}),
        (2 * (1 - row) + 1 - side, {"row": 1 - row, "side": 1 - side}),
        (2 * row + 1 - side, {"side": 1 - side}),
    ]
    member = 2 * row + side
    pieces = 8
    span = query.shape[2] // 4
    rows = REP * span
    kv_rows = key_raw.shape[0]
    half = HD // 2

    barrier = pltpu.get_barrier_semaphore()
    for _, where in others:
        pl.semaphore_signal(barrier, 1, device_id=where, device_id_type=pl.DeviceIdType.MESH)
    pl.semaphore_wait(barrier, 3)

    def sent(index, head):
        return pltpu.make_async_remote_copy(
            staged.at[index, head],
            come.at[index, head],
            send_sem.at[index, head],
            recv_sem.at[index, head],
            device_id=others[index][1],
            device_id_type=pl.DeviceIdType.MESH,
        )

    def starts(who):
        return [who, pieces - 1 - who, pieces + who, 2 * pieces - 1 - who]

    def through_norm(values, gain, cosine, sine, d_turned):
        first, second = d_turned[:half], d_turned[half:]
        d_scaled = jnp.concatenate([first * cosine + second * sine, second * cosine - first * sine], axis=0)
        inverse = lax.rsqrt(jnp.mean(values * values, axis=0, keepdims=True) + EPSILON)
        d_normed = d_scaled * gain
        mean = jnp.mean(values * d_normed, axis=0, keepdims=True)
        return inverse * d_normed - values * inverse**3 * mean, d_scaled * values * inverse

    gain_sum[...] = jnp.zeros_like(gain_sum)
    scale = 1.0 / math.sqrt(HD)

    @pl.loop(0, KVH)
    def _(head):
        key_rows = pl.ds(pl.multiple_of(head * HD, HD), HD)
        value_rows = pl.ds(pl.multiple_of(kv_rows + head * HD, HD), HD)
        key_n[...] = pair[key_rows, :].T
        value_n[...] = pair[value_rows, :].T
        d_key[...] = jnp.zeros_like(d_key)
        d_value[...] = jnp.zeros_like(d_value)
        for index, start in enumerate(starts(member)):
            cut = slice(index * span, (index + 1) * span)

            def beside(ref):
                return jnp.concatenate([ref[head * REP + rep, :, cut] for rep in range(REP)], axis=1)

            query_here, d_out_here = beside(query), beside(d_out)
            query_t, d_out_t = query_here.T, d_out_here.T
            logs = jnp.concatenate([logs_ref[head, rep : rep + 1, cut] for rep in range(REP)], axis=1)
            delta = jnp.concatenate([delta_ref[head, rep : rep + 1, cut] for rep in range(REP)], axis=1)
            first_query = start * span
            full, last = tiles_of(first_query)

            def tile(where, accum, masked):
                first_key = pl.multiple_of(where * KEYS, KEYS)
                here = pl.ds(first_key, KEYS)
                probs = jnp.exp(dot(key_n[here, :], query_here) - logs)
                if masked:
                    probs = jnp.where(allowed(first_query, first_key, span, rows), probs, 0.0)
                d_probs = dot(value_n[here, :], d_out_here)
                d_scores = (probs * (d_probs - delta)).astype(BF)
                d_value[here, :] += dot(probs.astype(BF), d_out_t)
                d_key[here, :] += dot(d_scores, query_t)
                return accum + dot(pair[key_rows, here], d_scores)

            accum = tile(last, jnp.zeros((HD, rows), F32), True)
            accum = lax.fori_loop(0, full, lambda where, total: tile(where, total, False), accum)
            cosine = jnp.concatenate([cos_ref[:, cut]] * REP, axis=1)
            sine = jnp.concatenate([sin_ref[:, cut]] * REP, axis=1)
            d_raw, part = through_norm(beside(raw), query_gain[...], cosine, sine, accum * scale)
            gain_sum[0] += part
            for rep in range(REP):
                which = head * REP + rep
                place = pl.ds(pl.multiple_of(which % KVH * HD, HD), HD)
                d_project[which // KVH, place, cut] = d_raw[:, rep * span : (rep + 1) * span].astype(BF)
        both_t[:HD, :] = d_key[...].T.astype(BF)
        both_t[HD:, :] = d_value[...].T.astype(BF)
        for index, who in enumerate([who for who, _ in others] + [member]):
            for number, start in enumerate(starts(who)):
                part = both_t[:, pl.ds(pl.multiple_of(start * span, span), span)]
                staged[index, head, :, number * span : (number + 1) * span] = part
            if index < 3:
                sent(index, head).start()

    cosine, sine = cos_ref[...], sin_ref[...]
    width = kv_rows // 4
    for head in range(KVH):
        total = staged[3, head].astype(F32)
        for index in range(3):
            sent(index, head).wait_recv()
            total += come[index, head].astype(F32)
        values = key_raw[head * HD : (head + 1) * HD, :].astype(F32)
        d_raw, part = through_norm(values, key_gain[...], cosine, sine, total[:HD])
        gain_sum[1] += part
        for offset, result in ((0, d_raw.astype(BF)), (width, total[HD:].astype(BF))):
            first = head * HD
            while first < (head + 1) * HD:
                col, inside = first // width, first % width
                size = min(width - inside, (head + 1) * HD - first)
                place = d_project.shape[1] - 2 * width + offset + inside
                d_project[col, place : place + size, :] = result[first - head * HD : first - head * HD + size]
                first += size
    query_gain_out[...] = jnp.sum(gain_sum[0], axis=1, keepdims=True)
    key_gain_out[...] = jnp.sum(gain_sum[1], axis=1, keepdims=True)
    for head in range(KVH):
        for index in range(3):
            sent(index, head).wait_send()


def back(query, d_out, logs, delta, pair, raw, key_raw, cosine, sine, query_gain, key_gain):
    mine = query.shape[2]
    inside = pl.BlockSpec(memory_space=pltpu.VMEM)
    dma = pltpu.SemaphoreType.DMA
    shape = jax.ShapeDtypeStruct
    columns = (QH + 2 * KVH) * HD // 4
    return pl.pallas_call(
        back_kernel,
        out_shape=[shape((4, columns, mine), BF), shape((HD, 1), F32), shape((HD, 1), F32)],
        in_specs=[inside] * 11,
        out_specs=[inside] * 3,
        scratch_shapes=[
            pltpu.VMEM((GROUP, HD), BF),
            pltpu.VMEM((GROUP, HD), BF),
            pltpu.VMEM((GROUP, HD), F32),
            pltpu.VMEM((GROUP, HD), F32),
            pltpu.VMEM((2 * HD, GROUP), BF),
            pltpu.VMEM((4, KVH, 2 * HD, mine), BF),
            pltpu.VMEM((3, KVH, 2 * HD, mine), BF),
            pltpu.VMEM((2, HD, mine), F32),
            dma((3, KVH)),
            dma((3, KVH)),
        ],
        compiler_params=pltpu.CompilerParams(
            collective_id=4, has_side_effects=True, vmem_limit_bytes=48 * 1024 * 1024
        ),
        name="attend_back",
    )(query, d_out, logs, delta, pair, raw, key_raw, cosine, sine, query_gain, key_gain)


def body(
    tokens,
    norm1_gain,
    w_query,
    w_key,
    w_value,
    query_gain,
    key_gain,
    w_out,
    norm2_gain,
    w_gate,
    w_up,
    w_down,
    teacher,
    positions,
    token_count,
):
    rows = lax.axis_size("row")
    cores = lax.axis_size("side")
    cols = lax.axis_size("group") * cores
    row_index = lax.axis_index("row")
    group_index = lax.axis_index("group")
    members = rows * cores
    member = row_index * cores + lax.axis_index("side")
    shard, width = tokens.shape
    pieces = 2 * members
    span = shard // pieces
    mine = shard // members * cores
    q_width, k_width = w_query.shape[1], w_key.shape[1]
    ff = w_gate.shape[1]

    def from_row(block, ahead):
        pairs = [((r + ahead) % rows, r) for r in range(rows)]
        return lax.ppermute(block, "row", pairs)

    def gather_rows(block, axis):
        parts = [block] + [from_row(block, ahead) for ahead in range(1, rows)]
        return jnp.concatenate(parts, axis=axis)

    def scatter_rows(block, axis):
        size = block.shape[axis] // rows
        total = lax.slice_in_dim(block, 0, size, axis=axis).astype(F32)
        for ahead in range(1, rows):
            part = lax.slice_in_dim(block, ahead * size, (ahead + 1) * size, axis=axis)
            total = total + from_row(part, rows - ahead).astype(F32)
        return total.astype(BF)

    def sum_planes(block, cuts):
        planes = lax.axis_size("dp")
        plane = lax.axis_index("dp")
        half = planes // 2
        edge = jnp.minimum(plane, planes - 1 - plane)
        done = []
        for part in jnp.split(block, cuts, axis=0):
            for step in range(half - 1):
                pairs = [(step, step + 1), (planes - 1 - step, planes - 2 - step)]
                come = lax.ppermute(part, "dp", pairs)
                part = (part.astype(F32) + come.astype(F32)).astype(BF)
            come = lax.ppermute(part, "dp", [(half - 1, half), (half, half - 1)])
            part = (part.astype(F32) + come.astype(F32)).astype(BF)
            for step in reversed(range(half - 1)):
                pairs = [(step + 1, step), (planes - 2 - step, planes - 1 - step)]
                come = lax.ppermute(part, "dp", pairs)
                part = jnp.where(edge == step, come, part)
            done.append(part)
        return jnp.concatenate(done, axis=0)

    def to_members(block):
        parts = block.reshape(pieces, span, width)
        parts = jnp.stack([parts[:members], parts[members:][::-1]], axis=1)
        moved = lax.all_to_all(parts, ("row", "side"), 0, 0, tiled=True)
        moved = jnp.roll(moved.reshape(rows, cores, 2 * span, width), -row_index, 0)
        moved = moved.transpose(1, 2, 0, 3)
        return moved.reshape(mine, rows * width)

    def from_members(block):
        parts = block.reshape(cores, 2, span, rows, width).transpose(3, 0, 1, 2, 4)
        parts = jnp.roll(parts, row_index, 0).reshape(members, 2, span, width)
        moved = lax.all_to_all(parts, ("row", "side"), 0, 0, tiled=True)
        moved = jnp.concatenate([moved[:, 0], moved[:, 1][::-1]], axis=0)
        return moved.reshape(shard, width)

    def pick(values):
        part = lax.dynamic_slice_in_dim(values.reshape(-1, cores, pieces, span), group_index, 1, 0)[0]
        low = lax.dynamic_slice_in_dim(part, member, 1, 1)
        high = lax.dynamic_slice_in_dim(part, pieces - 1 - member, 1, 1)
        return jnp.concatenate([low, high], axis=1).reshape(-1)

    first_tokens = (
        jnp.array([0, 0, shard, shard], jnp.int32)
        + jnp.stack([member, pieces - 1 - member] * 2).astype(jnp.int32) * span
    )

    half = HD // 2
    freq = jnp.exp(jnp.arange(half, dtype=F32) * (-2.0 * math.log(10000.0) / HD))
    angle = freq[:, None] * pick(positions).astype(F32)[None, :]
    cosine, sine = jnp.cos(angle), jnp.sin(angle)
    def dealt(full):
        lead, entry = full.shape[:-2], full.shape[-1]
        parts = full.reshape(lead + (cores, pieces, span, entry))
        low = parts[..., :members, :, :]
        high = parts[..., members:, :, :][..., ::-1, :, :]
        both = jnp.stack([low, high], axis=-3)
        both = jnp.moveaxis(both, -4, 0)
        return both.reshape((members,) + lead + (mine, entry))

    w_project = jnp.concatenate([w_query, w_key, w_value], axis=1)
    scale = 1.0 / math.sqrt(HD)
    fast = rows == 2 and cols == 4 and lax.axis_size("dp") % 2 == 0 and mine == 4 * span
    if fast:
        (
            states, normed_one, query_raw, query_use, key_sent, pair, mixed_f, logs, hidden,
            normed_two, w_project, w_out_all, gate_other, up_other, gains,
        ) = front(
            tokens, w_project, w_out, jnp.stack([norm1_gain, norm2_gain]), w_gate, w_up,
            cosine, sine, query_gain[:, None], key_gain[:, None],
        )
        states = states.astype(F32)
        inverse_one, inverse_two = rms(states), rms(hidden)
        gain_one, gain_two = gains[:, 0].reshape(D), gains[:, 1].reshape(D)
        mixed_f = mixed_f.reshape(KVH, REP, HD, mine)
        mixed = mixed_f.reshape(QH * HD, mine).astype(BF)
        w_project = w_project.reshape(cols, D, -1)
        ffn_weights = [w_gate, gate_other, w_up, up_other, w_down]
    else:
        states = to_members(tokens).astype(F32)
        gain_one = gather_rows(norm1_gain, 0)
        gain_two = gather_rows(norm2_gain, 0)
        w_project = gather_rows(w_project, 0)
        w_project = lax.all_gather(w_project, ("group", "side"), axis=0)
        w_out_all = gather_rows(w_out, 1)
        w_out_all = lax.all_gather(w_out_all, ("group", "side"), axis=0, tiled=True)
        def halves(block, axis):
            if rows == 2:
                return [block, from_row(block, 1)]
            return jnp.split(gather_rows(block, axis), 2, axis=axis)

        ffn_weights = halves(w_gate, 0) + halves(w_up, 0) + halves(w_down, 1)
        inverse_one = rms(states)
        normed_one = (states * inverse_one * gain_one).astype(BF)
        projected = dot(w_project, normed_one, ((1,), (1,)))
        query_raw = projected[:, :q_width].reshape(QH, HD, mine)
        key_sent = projected[:, q_width : q_width + k_width].reshape(KVH, HD, mine).astype(BF)
        value_sent = projected[:, q_width + k_width :].reshape(KVH, HD, mine).astype(BF)
        query_rot, query_back = jax.vjp(
            lambda raw, gain: prepare(raw, gain, cosine, sine), query_raw, query_gain
        )
        key_rot, key_back = jax.vjp(
            lambda raw, gain: prepare(raw, gain, cosine, sine), key_sent.astype(F32), key_gain
        )
        query_use = (query_rot.astype(BF) * BF(scale)).reshape(KVH, REP, HD, mine)
        pair = jnp.stack([key_rot.astype(BF), value_sent])
        pair = lax.all_gather(pair, ("row", "side"), axis=0)

        def natural(stacked):
            lead = stacked.shape[1:-1]
            parts = stacked.reshape((members,) + lead + (cores, 2, span))
            low, high = parts[..., 0, :], parts[..., 1, :]
            both = jnp.concatenate([low, high[::-1]], axis=0)
            return jnp.moveaxis(both, 0, -2).reshape(lead + (GROUP,))

        pair = natural(pair)
        key_t, value_t = pair[0], pair[1]
        key_n = key_t.transpose(0, 2, 1)
        value_one = jnp.concatenate([value_t, jnp.ones((KVH, 16, GROUP), BF)], axis=1)
        mixed_f, logs = attend(first_tokens, query_use, key_n, value_one)
        mixed = mixed_f.reshape(QH * HD, mine).astype(BF)
        hidden = states + dot(mixed, w_out_all, ((0,), (0,)))

        inverse_two = rms(hidden)
        normed_two = (hidden * inverse_two * gain_two).astype(BF)

    if fast:
        normed_all, gate, up, activated, ffn_out, down_other, target = spread(
            True, normed_two, ffn_weights, dealt=teacher
        )
        ffn_weights.append(down_other)
    else:
        normed_all, gate, up, activated, ffn_out = spread(True, normed_two, ffn_weights)
        target = to_members(teacher)
    ffn_out = ffn_out.reshape(mine, D)
    result = hidden + ffn_out

    total_tokens = shard * cols * lax.axis_size("dp")
    loss_scale = total_tokens / token_count[0].astype(F32)
    d_result = loss_scale * (result - target.astype(F32))
    if fast:
        d_low, d_gate_up, d_normed, block_out = spread(
            False, d_result.astype(BF), ffn_weights, (gate, up), result.astype(BF)
        )
    else:
        d_low, d_gate_up, d_normed = spread(False, d_result.astype(BF), ffn_weights, (gate, up))
        block_out = from_members(result.astype(BF))
    d_normed = d_normed.reshape(mine, D)
    d_low, normed_all = d_low.reshape(-1, D), normed_all.reshape(-1, D)
    activated, d_gate_up = activated.reshape(-1, ff), d_gate_up.reshape(-1, 2 * ff)

    norm_two_part = jnp.sum(d_normed * hidden * inverse_two, axis=0)
    d_hidden = d_result + norm_back(hidden, inverse_two, gain_two, d_normed)
    d_hidden_low = d_hidden.astype(BF)
    grad_out = dot(mixed, d_hidden_low, ((1,), (0,))).astype(BF)
    d_mixed = dot(w_out_all, d_hidden_low, ((1,), (1,))).astype(BF)
    d_mixed = d_mixed.reshape(KVH, REP, HD, mine)
    delta = jnp.sum(d_mixed.astype(F32) * mixed_f, axis=2)
    if fast:
        d_projected, query_gain_part, key_gain_part = back(
            query_use, d_mixed.reshape(QH, HD, mine), logs, delta, pair, query_raw, key_sent,
            cosine, sine, query_gain[:, None], key_gain[:, None],
        )
        query_gain_part, key_gain_part = query_gain_part[:, 0], key_gain_part[:, 0]
    else:
        d_query, d_key_n, d_value_n = attend_back(
            first_tokens, query_use, d_mixed, logs, delta, key_t, value_t
        )
        d_pair = dealt(jnp.stack([d_key_n, d_value_n])).astype(BF)
        d_pair = lax.psum_scatter(d_pair, ("row", "side"), scatter_dimension=0, tiled=True)[0]
        d_pair = d_pair.astype(F32).transpose(0, 1, 3, 2)
        d_query_raw, query_gain_part = query_back(d_query.reshape(QH, HD, mine) * scale)
        d_key_raw, key_gain_part = key_back(d_pair[0])
        d_projected = jnp.concatenate(
            [
                d_query_raw.reshape(cols, q_width, mine),
                d_key_raw.reshape(cols, k_width, mine),
                d_pair[1].reshape(cols, k_width, mine),
            ],
            axis=1,
        ).astype(BF)
    d_normed_one = dot(d_projected, w_project, ((0, 1), (0, 2)))
    grad_input = d_hidden + norm_back(states, inverse_one, gain_one, d_normed_one)
    norm_one_part = jnp.sum(d_normed_one * states * inverse_one, axis=0)

    grad_project = lax.dot_general(
        d_projected, normed_one, (((2,), (0,)), ((), ())), preferred_element_type=F32
    )
    grad_project = grad_project.astype(BF)
    grad_out = grad_out.reshape(cols, q_width, D)
    norm_one_part = jnp.roll(norm_one_part.reshape(rows, width), row_index, 0).reshape(D)
    norm_two_part = jnp.roll(norm_two_part.reshape(rows, width), row_index, 0).reshape(D)
    small = jnp.concatenate([norm_one_part, norm_two_part, query_gain_part, key_gain_part])
    if fast and lax.axis_size("dp") == 4:
        padded = jnp.pad(small, (0, SMALL * 128 - small.shape[0])).reshape(SMALL, 128)
        grad_gate_up, grad_out, grad_project, grad_down, small, grad_input = reduce_all(
            4, normed_all, d_gate_up, activated, d_low, grad_out, grad_project, padded, grad_input.astype(BF)
        )
        grad_input = grad_input.astype(F32)
        small = small.reshape(-1)[: 2 * D + 2 * HD]
    else:
        grad_input = from_members(grad_input)
        small = lax.psum(small, ("dp", "row", "group", "side"))
        col_axes = ("group", "side")
        grad_project = lax.psum_scatter(grad_project, col_axes, scatter_dimension=0, tiled=True)
        grad_out = lax.psum_scatter(grad_out, col_axes, scatter_dimension=0, tiled=True)
        grad_down = dot(activated, d_low, ((0,), (0,))).astype(BF)
        grad_gate_up = dot(normed_all, d_gate_up, ((0,), (0,))).astype(BF)
        grad_down = sum_planes(scatter_rows(grad_down, 1), 2)
        grad_gate_up = sum_planes(scatter_rows(grad_gate_up, 0), 4)
        grad_out = sum_planes(scatter_rows(grad_out[0], 1), 1)
        grad_project = sum_planes(scatter_rows(grad_project[0], 1), 2)
    grad_norm1 = lax.dynamic_slice_in_dim(small, row_index * width, width, 0)
    grad_norm2 = lax.dynamic_slice_in_dim(small, D + row_index * width, width, 0)
    grad_project = grad_project.astype(F32).T
    return (
        block_out,
        grad_input,
        grad_norm1,
        grad_project[:, :q_width],
        grad_project[:, q_width : q_width + k_width],
        grad_project[:, q_width + k_width :],
        small[2 * D : 2 * D + HD],
        small[2 * D + HD :],
        grad_out.astype(F32),
        grad_norm2,
        grad_gate_up[:, :ff].astype(F32),
        grad_gate_up[:, ff:].astype(F32),
        grad_down.astype(F32),
    )


def solution(mesh):
    dp, row, col = mesh.shape["dp"], mesh.shape["row"], mesh.shape["col"]

    def call(*args):
        side = GROUP * dp * col // args[0].shape[0]
        fine = Mesh(
            mesh.devices.reshape(dp, row, col // side, side), ("dp", "row", "group", "side")
        )
        col_axes = ("group", "side")
        token_spec = P(("dp", "group", "side"), "row")
        wide = P("row", col_axes)
        tall = P(col_axes, "row")
        return jax.shard_map(
            body,
            mesh=fine,
            in_specs=(
                token_spec,
                P("row"),
                wide,
                wide,
                wide,
                P(),
                P(),
                tall,
                P("row"),
                wide,
                wide,
                tall,
                token_spec,
                P("dp"),
                P(),
            ),
            out_specs=(
                token_spec,
                token_spec,
                P("row"),
                wide,
                wide,
                wide,
                P(),
                P(),
                tall,
                P("row"),
                wide,
                wide,
                tall,
            ),
            check_vma=False,
        )(*args)

    return call
```

```python
import functools
import math

import jax
import jax.numpy as jnp
from jax import lax
from jax.experimental import pallas as pl
from jax.experimental.pallas import tpu as pltpu
from jax.sharding import Mesh
from jax.sharding import PartitionSpec as P

D = 2048
QH = 20
KVH = 5
HD = 64
PROMPT = 1024
CONT = 128
NCONT = 8
GROUP = PROMPT + NCONT * CONT
REP = QH // KVH
KEYS = 256

EPSILON = 1e-06
BF = jnp.bfloat16
F32 = jnp.float32


def dot(left, right, dims=((1,), (0,))):
    return lax.dot_general(left, right, (dims, ((), ())), preferred_element_type=F32)


def rms(values):
    return lax.rsqrt(jnp.mean(values * values, axis=1, keepdims=True) + EPSILON)


def norm_back(states, inverse, gain, d_normed):
    mean = jnp.mean(states * gain * d_normed, axis=1, keepdims=True)
    return inverse * gain * d_normed - states * inverse**3 * mean


def prepare(raw, gain, cosine, sine):
    values = raw * lax.rsqrt(jnp.mean(raw * raw, axis=1, keepdims=True) + EPSILON)
    values = values * gain[None, :, None]
    half = HD // 2
    first, second = values[:, :half], values[:, half:]
    return jnp.concatenate(
        [first * cosine - second * sine, second * cosine + first * sine], axis=1
    )


def allowed(first_query, first_key, span, rows):
    key = first_key + lax.broadcasted_iota(jnp.int32, (KEYS, rows), 0)
    query = first_query + lax.broadcasted_iota(jnp.int32, (KEYS, rows), 1) % span
    return (key <= query) & ((key < PROMPT) | (key // CONT == query // CONT))


def side_by_side(ref, index, span):
    return jnp.concatenate(
        [ref[0, head, :, index * span : (index + 1) * span] for head in range(REP)], axis=1
    )


def tiles_of(first_query):
    last = first_query // KEYS
    return jnp.minimum(last, PROMPT // KEYS), last


def attend_kernel(chunks, span, first_ref, query_ref, key_ref, value_ref, out_ref, log_ref):
    rows = REP * span
    for index in range(chunks):
        query = side_by_side(query_ref, index, span)
        first_query = first_ref[index]
        full, last = tiles_of(first_query)

        def tile(where, accum, masked):
            first_key = pl.multiple_of(where * KEYS, KEYS)
            scores = dot(key_ref[0, pl.ds(first_key, KEYS), :], query)
            expo = jnp.exp(scores)
            if masked:
                expo = jnp.where(allowed(first_query, first_key, span, rows), expo, 0.0)
            return accum + dot(value_ref[0, :, pl.ds(first_key, KEYS)], expo.astype(BF))

        accum = tile(last, jnp.zeros((value_ref.shape[1], rows), F32), True)
        accum = lax.fori_loop(0, full, lambda where, total: tile(where, total, False), accum)
        total = accum[HD : HD + 1]
        mixed = accum[:HD] / total
        logs = jnp.log(total)
        for head in range(REP):
            cut = slice(head * span, (head + 1) * span)
            out_ref[0, head, :, index * span : (index + 1) * span] = mixed[:, cut]
            log_ref[0, head : head + 1, index * span : (index + 1) * span] = logs[:, cut]


def attend_back_kernel(
    chunks,
    span,
    first_ref,
    query_ref,
    d_out_ref,
    log_ref,
    delta_ref,
    key_t_ref,
    value_t_ref,
    d_query_ref,
    d_key_ref,
    d_value_ref,
    key_ref,
    value_ref,
):
    rows = REP * span
    key_ref[...] = key_t_ref[0].T
    value_ref[...] = value_t_ref[0].T
    d_key_ref[...] = jnp.zeros_like(d_key_ref)
    d_value_ref[...] = jnp.zeros_like(d_value_ref)
    for index in range(chunks):
        query = side_by_side(query_ref, index, span)
        d_out = side_by_side(d_out_ref, index, span)
        query_t = query.T
        d_out_t = d_out.T
        cut = slice(index * span, (index + 1) * span)
        logs = jnp.concatenate([log_ref[0, h : h + 1, cut] for h in range(REP)], axis=1)
        delta = jnp.concatenate([delta_ref[0, h : h + 1, cut] for h in range(REP)], axis=1)
        first_query = first_ref[index]
        full, last = tiles_of(first_query)

        def tile(where, accum, masked):
            first_key = pl.multiple_of(where * KEYS, KEYS)
            here = pl.ds(first_key, KEYS)
            probs = jnp.exp(dot(key_ref[here, :], query) - logs)
            if masked:
                probs = jnp.where(allowed(first_query, first_key, span, rows), probs, 0.0)
            d_probs = dot(value_ref[here, :], d_out)
            d_scores = (probs * (d_probs - delta)).astype(BF)
            d_value_ref[0, here, :] += dot(probs.astype(BF), d_out_t)
            d_key_ref[0, here, :] += dot(d_scores, query_t)
            return accum + dot(key_t_ref[0, :, here], d_scores)

        accum = tile(last, jnp.zeros((HD, rows), F32), True)
        accum = lax.fori_loop(0, full, lambda where, total: tile(where, total, False), accum)
        for head in range(REP):
            part = accum[:, head * span : (head + 1) * span]
            d_query_ref[0, head, :, cut] = part


def per_head(shape):
    return pl.BlockSpec((1,) + shape, lambda head, first: (head,) + (0,) * len(shape))


def attend(first, query, key, value_t):
    tokens = query.shape[-1]
    chunks = first.shape[0]
    return pl.pallas_call(
        functools.partial(attend_kernel, chunks, tokens // chunks),
        out_shape=(
            jax.ShapeDtypeStruct((KVH, REP, HD, tokens), F32),
            jax.ShapeDtypeStruct((KVH, REP, tokens), F32),
        ),
        grid_spec=pltpu.PrefetchScalarGridSpec(
            num_scalar_prefetch=1,
            grid=(KVH,),
            in_specs=[
                per_head((REP, HD, tokens)),
                per_head((GROUP, HD)),
                per_head((value_t.shape[1], GROUP)),
            ],
            out_specs=[per_head((REP, HD, tokens)), per_head((REP, tokens))],
        ),
        compiler_params=pltpu.CompilerParams(vmem_limit_bytes=32 * 1024 * 1024),
        name="attend",
    )(first, query, key, value_t)


def attend_back(first, query, d_out, logs, delta, key_t, value_t):
    tokens = query.shape[-1]
    chunks = first.shape[0]
    return pl.pallas_call(
        functools.partial(attend_back_kernel, chunks, tokens // chunks),
        out_shape=(
            jax.ShapeDtypeStruct((KVH, REP, HD, tokens), F32),
            jax.ShapeDtypeStruct((KVH, GROUP, HD), F32),
            jax.ShapeDtypeStruct((KVH, GROUP, HD), F32),
        ),
        grid_spec=pltpu.PrefetchScalarGridSpec(
            num_scalar_prefetch=1,
            grid=(KVH,),
            in_specs=[
                per_head((REP, HD, tokens)),
                per_head((REP, HD, tokens)),
                per_head((REP, tokens)),
                per_head((REP, tokens)),
                per_head((HD, GROUP)),
                per_head((HD, GROUP)),
            ],
            out_specs=[
                per_head((REP, HD, tokens)),
                per_head((GROUP, HD)),
                per_head((GROUP, HD)),
            ],
            scratch_shapes=[pltpu.VMEM((GROUP, HD), BF), pltpu.VMEM((GROUP, HD), BF)],
        ),
        compiler_params=pltpu.CompilerParams(vmem_limit_bytes=32 * 1024 * 1024),
        name="attend_back",
    )(first, query, d_out, logs, delta, key_t, value_t)


AHEAD = 4
SLOTS = AHEAD + 2
FAR_LAG, WIDE_LAG, LAG = 1, 2, 4
SMALL = 40


class Part:
    def __init__(self, axis, rows, cols, count, base, col):
        self.axis, self.rows, self.cols = axis, rows, cols
        self.count, self.base, self.col = count, base, col

    def cut(self, ref, index, half, lead=()):
        first = pl.ds(index * self.rows, self.rows)
        if self.axis == 0:
            first = pl.ds((half * self.count + index) * self.rows, self.rows)
            return ref.at[(*lead, first, slice(None))]
        return ref.at[(*lead, first, pl.ds(half * self.cols, self.cols))]


def reduce_kernel(parts, planes, *refs):
    count = len(parts)
    refs = list(refs)

    def take(number):
        taken = refs[:number]
        del refs[:number]
        return taken

    col_parts = [j for j in range(count) if parts[j].col]
    normed_ref, d_gate_up_ref, act_ref, d_low_ref = take(4)
    grads = dict(zip(col_parts, take(len(col_parts))))
    (small_ref, mine_ref) = take(2)
    outs = take(count)
    (small_out, dealt_ref) = take(2)
    near, far, own = take(count), take(count), take(count)
    made = [j for j in range(count) if not parts[j].col]
    leaving = dict(zip(made, take(len(made))))
    mate_in = dict(zip(col_parts, take(len(col_parts))))
    far_in = dict(zip(col_parts, take(len(col_parts))))
    right, left, left_t, right_sem, left_sem, free_sem = take(6)
    out_sem, row_send, row_recv, in_send, far_recv, mid_send, wide_recv = take(7)
    col_own, col_send, col_recv, x_send, x_recv, small_local, small_send, small_recv = take(8)
    small_in, small_sum, deal_send, deal_recv, deal_local = take(5)
    plane, row = lax.axis_index("dp"), lax.axis_index("row")
    group, side = lax.axis_index("group"), lax.axis_index("side")
    other_row, mate, far_dev = {"row": 1 - row}, {"side": 1 - side}, {"group": 1 - group}
    cross = {"row": 1 - row, "side": 1 - side}
    at_end = (plane == 0) | (plane == planes - 1)
    low = plane < planes // 2
    end_next = {"dp": jnp.where(low, 1, planes - 2)}
    mid_outer = {"dp": jnp.where(low, 0, planes - 1)}
    mid_other = {"dp": jnp.where(low, planes // 2, planes // 2 - 1)}

    def remote(source, target, send, recv, where):
        return pltpu.make_async_remote_copy(
            source, target, send, recv, device_id=where, device_id_type=pl.DeviceIdType.MESH
        )

    barrier = pltpu.get_barrier_semaphore()

    def greet(where):
        pl.semaphore_signal(barrier, 1, device_id=where, device_id_type=pl.DeviceIdType.MESH)

    for where in (other_row, mate, far_dev, cross):
        greet(where)

    @pl.when(at_end)
    def _():
        greet(end_next)
        pl.semaphore_wait(barrier, 5)

    @pl.when(jnp.logical_not(at_end))
    def _():
        greet(mid_outer)
        greet(mid_other)
        pl.semaphore_wait(barrier, 6)

    def col_slot(j, half, index):
        before = sum(2 * parts[i].count for i in col_parts if i < j)
        return before + half * parts[j].count + index

    def col_own_copy(j, half, index, target):
        return pltpu.make_async_copy(
            parts[j].cut(grads[j], index, half, (2 * target + side,)),
            own[j].at[target, half, index],
            col_own.at[target, col_slot(j, half, index)],
        )

    def col_copy(j, half, index, target):
        slot = col_slot(j, half, index)
        return remote(
            parts[j].cut(grads[j], index, half, (2 * target + 1 - side,)),
            mate_in[j].at[target, half, index],
            col_send.at[target, slot],
            col_recv.at[target, slot],
            mate,
        )

    def x_copy(j, half, index):
        slot = col_slot(j, half, index)
        return remote(
            mate_in[j].at[1 - group, half, index],
            far_in[j].at[half, index],
            x_send.at[slot],
            x_recv.at[slot],
            far_dev,
        )

    def take_col(j, half, index):
        for target in range(2):
            col_own_copy(j, half, index, target).wait()
            col_copy(j, half, index, target).wait_recv()
            mate_in[j][target, half, index] = mate_in[j][target, half, index] + own[j][target, half, index]
        x_copy(j, half, index).start()

    def take_x(j, half, index):
        x_copy(j, half, index).wait_recv()
        far_in[j][half, index] = far_in[j][half, index] + mate_in[j][group, half, index]

    half_depth = normed_ref.shape[1] // 2
    gate_up, down = made
    units = parts[gate_up].count // 2

    def left_copies(unit, of_down):
        if of_down:
            source = act_ref.at[:, pl.ds(pl.multiple_of(unit * 256, 256), 256)]
            slot = (units + unit) % 2
            return [pltpu.make_async_copy(source, left.at[slot], left_sem.at[slot, 0])]
        slot = unit % 2
        copies = []
        for half in range(2):
            first = pl.multiple_of(half * half_depth + unit * 128, 128)
            target = left.at[slot, :, pl.ds(half * 128, 128)]
            copies.append(
                pltpu.make_async_copy(normed_ref.at[:, pl.ds(first, 128)], target, left_sem.at[slot, half])
            )
        return copies

    d_low_load = pltpu.make_async_copy(d_low_ref, right.at[:, pl.ds(0, d_low_ref.shape[1])], right_sem.at[1])
    d_gate_up_load = pltpu.make_async_copy(d_gate_up_ref, right, right_sem.at[0])

    def start_unit(j, unit):
        of_down = j == down
        part = parts[j]
        for copy in left_copies(unit, of_down):
            copy.wait()

        @pl.when(unit + 1 < part.count // 2)
        def _():
            for copy in left_copies(unit + 1, of_down):
                copy.start()

        if not of_down:
            @pl.when(unit + 1 == units)
            def _():
                for copy in left_copies(0, True):
                    copy.start()

        @pl.when(unit == 0)
        def _():
            (d_low_load if of_down else d_gate_up_load).wait()

        for chunk in range(2):
            index = 2 * unit + chunk

            @pl.when(index >= SLOTS)
            def _(index=index):
                row_copy(j, jnp.maximum(index - SLOTS, 0)).wait_send()

        slot = ((units + unit) if of_down else unit) % 2

        @pl.loop(0, left.shape[1] // 256)
        def _(block):
            here = pl.ds(pl.multiple_of(block * 256, 256), 256)
            left_t[:, here] = left[slot, here, :].T

    def tile(j, unit, number, targets):
        rows = parts[j].rows
        where = pl.ds(pl.multiple_of(number * 256, 256), 256)
        product = dot(left_t[...], right[:, where]).astype(BF)
        for place, (target, chunk, first_tile) in enumerate(targets):
            to = pl.ds(pl.multiple_of((number - first_tile) * 256, 256), 256)
            target[j][(2 * unit + chunk) % SLOTS, :, to] = product[place * rows : (place + 1) * rows]

    def make(j, unit, second):
        part = parts[j]
        if not second:
            start_unit(j, unit)
        if j == down:
            tiles = part.cols // 256
            first, target = (0, own) if second else (tiles, leaving)
            targets = [(target, 0, first), (target, 1, first)]
            pl.loop(first, first + tiles)(lambda number: tile(j, unit, number, targets))
        else:
            tiles = part.cols // 256
            targets = [(own, 0, 0), (own, 1, 0), (leaving, 0, 0), (leaving, 1, 0)]
            bounds = (tiles // 2, tiles) if second else (0, tiles // 2)
            pl.loop(*bounds)(lambda number: tile(j, unit, number, targets))
        if second and j != down:
            @pl.when(unit + 1 == units)
            def _():
                d_low_load.start()

        if second != (j == down):
            for chunk in range(2):
                row_copy(j, 2 * unit + chunk).start()

    def row_copy(j, index):
        slot = parts[j].base + index
        source = far_in[j].at[1, index] if parts[j].col else leaving[j].at[index % SLOTS]
        return remote(source, near[j].at[index], row_send.at[slot], row_recv.at[slot], other_row)

    def in_copy(j, index):
        slot = parts[j].base + index
        return remote(near[j].at[index], far[j].at[index], in_send.at[slot], far_recv.at[slot], end_next)

    def mid_copy(j, index):
        slot = parts[j].base + index
        return remote(far[j].at[index], near[j].at[index], mid_send.at[slot], wide_recv.at[slot], mid_other)

    def back_copy(j, index):
        slot = parts[j].base + index
        return remote(near[j].at[index], far[j].at[index], in_send.at[slot], far_recv.at[slot], mid_outer)

    def out_copy(j, index, source):
        slot = parts[j].base + index
        return pltpu.make_async_copy(source[j].at[index], parts[j].cut(outs[j], index, 0), out_sem.at[slot])

    def each(step, action):
        for j, part in enumerate(parts):
            index = step - part.base

            @pl.when((index >= 0) & (index < part.count))
            def _(j=j, index=index):
                action(j, index)

    def send_row(j, index):
        if parts[j].col:
            row_copy(j, index).start()
        else:
            @pl.when(index % 2 == 0)
            def _():
                make(j, index // 2, False)

            @pl.when(index % 2 == 1)
            def _():
                make(j, index // 2, True)

    def take_row(j, index):
        row_copy(j, index).wait_recv()
        mine = far_in[j][0, index] if parts[j].col else own[j][index % SLOTS]
        near[j][index] = near[j][index] + mine

        @pl.when(at_end)
        def _():
            in_copy(j, index).start()

    def take_far(j, index):
        back_copy(j, index).wait_recv()
        far[j][index] = far[j][index] + near[j][index]
        pl.semaphore_signal(free_sem, 1, device_id=mid_other, device_id_type=pl.DeviceIdType.MESH)
        pl.semaphore_wait(free_sem, 1)
        mid_copy(j, index).start()

    def take_wide(j, index):
        mid_copy(j, index).wait_recv()
        near[j][index] = near[j][index] + far[j][index]
        back_copy(j, index).start()
        out_copy(j, index, near).start()

    def take_back(j, index):
        in_copy(j, index).wait_recv()
        out_copy(j, index, far).start()

    def row_sent(j, index):
        @pl.when(jnp.logical_or(parts[j].col, index >= parts[j].count - SLOTS))
        def _():
            row_copy(j, index).wait_send()

    def finish_end(j, index):
        row_sent(j, index)
        in_copy(j, index).wait_send()
        out_copy(j, index, far).wait()

    def finish_mid(j, index):
        row_sent(j, index)
        mid_copy(j, index).wait_send()
        back_copy(j, index).wait_send()
        out_copy(j, index, near).wait()

    def small_copy(stage, source, where):
        return remote(small_sum.at[source], small_in.at[stage], small_send.at[stage], small_recv.at[stage], where)

    plane_hops = [small_copy(0, 0, mate), small_copy(1, 1, far_dev), small_copy(2, 2, other_row)]
    small_end = small_copy(3, 3, end_next)
    small_mid = small_copy(4, 4, mid_other)
    small_back = small_copy(3, 5, mid_outer)
    small_load = pltpu.make_async_copy(small_ref, small_sum.at[0], small_local.at[0])
    small_store = pltpu.make_async_copy(small_sum.at[5], small_out, small_local.at[1])

    span, width = mine_ref.shape[0] // 4, mine_ref.shape[1] // 2
    member = 2 * row + side
    dealt = []
    for index, (to_row, to_side, where) in enumerate(
        [(1 - row, side, other_row), (1 - row, 1 - side, cross), (row, 1 - side, mate), (row, side, None)]
    ):
        for high in range(2):
            piece = 7 - member if high else member
            first = pl.multiple_of(to_side * 2 * span + high * span, span)
            source = mine_ref.at[pl.ds(first, span), pl.ds((0 if index >= 2 else 1) * width, width)]
            target = dealt_ref.at[pl.ds(pl.multiple_of(piece * span, span), span), :]
            if where is None:
                dealt.append(pltpu.make_async_copy(source, target, deal_local.at[high]))
            else:
                dealt.append(remote(source, target, deal_send.at[index, high], deal_recv.at[index, high], where))

    total = sum(part.count for part in parts)
    for copy in left_copies(0, False):
        copy.start()
    d_gate_up_load.start()
    small_load.start()
    for copy in dealt[4:]:
        copy.start()
    for j in col_parts:
        for half in (1, 0):
            for index in range(parts[j].count):
                for target in range(2):
                    col_own_copy(j, half, index, target).start()
                    col_copy(j, half, index, target).start()

    @pl.loop(0, AHEAD)
    def _(step):
        each(step, send_row)

    pieces = [(j, half, index) for j in col_parts for half in (1, 0) for index in range(parts[j].count)]

    @pl.loop(0, total + LAG)
    def _(step):
        each(step + AHEAD, send_row)
        each(step, take_row)

        @pl.when(at_end)
        def _():
            each(step - LAG, take_back)

        @pl.when(jnp.logical_not(at_end))
        def _():
            each(step - FAR_LAG, take_far)
            each(step - WIDE_LAG, take_wide)

        @pl.when(step == total - AHEAD)
        def _():
            for copy in dealt[:4]:
                copy.start()

        for place, piece in enumerate(pieces):
            @pl.when(step == place + 1)
            def _(piece=piece):
                take_col(*piece)

            @pl.when(step == place + 5)
            def _(piece=piece):
                take_x(*piece)

        @pl.when(step == 0)
        def _():
            small_load.wait()
            plane_hops[0].start()

        for hop in range(3):
            @pl.when(step == hop + 1)
            def _(hop=hop):
                plane_hops[hop].wait_recv()
                small_sum[hop + 1] = small_sum[hop] + small_in[hop]
                if hop < 2:
                    plane_hops[hop + 1].start()

        @pl.when(at_end & (step == 3))
        def _():
            small_end.start()

        @pl.when(at_end & (step == 10))
        def _():
            small_end.wait_recv()
            small_sum[5] = small_in[3]
            small_store.start()

        @pl.when(jnp.logical_not(at_end) & (step == 5))
        def _():
            small_back.wait_recv()
            small_sum[4] = small_sum[3] + small_in[3]
            small_mid.start()

        @pl.when(jnp.logical_not(at_end) & (step == 7))
        def _():
            small_mid.wait_recv()
            small_sum[5] = small_sum[4] + small_in[4]
            small_back.start()
            small_store.start()

    for copy in plane_hops:
        copy.wait_send()
    small_store.wait()
    for copy in dealt:
        copy.wait()
    for j, half, index in pieces:
        for target in range(2):
            col_copy(j, half, index, target).wait_send()
        x_copy(j, half, index).wait_send()

    @pl.when(at_end)
    def _():
        small_end.wait_send()

        @pl.loop(0, total)
        def _(step):
            each(step, finish_end)

    @pl.when(jnp.logical_not(at_end))
    def _():
        small_mid.wait_send()
        small_back.wait_send()

        @pl.loop(0, total)
        def _(step):
            each(step, finish_mid)


def reduce_all(planes, normed, d_gate_up, act, d_low, grad_out, grad_project, small, mine):
    depth, width = normed.shape[1], act.shape[1]
    parts = [Part(0, 64, d_gate_up.shape[1], depth // 128, 0, False)]
    for rows, height, col in ((grad_out.shape[1] // 2, grad_out.shape[1], True),
                              (grad_project.shape[1] // 2, grad_project.shape[1], True), (128, width, False)):
        parts.append(Part(1, rows, depth // 2, height // rows, parts[-1].base + parts[-1].count, col))
    base = parts[-1].base + parts[-1].count
    shapes = [(part.count, part.rows, part.cols) for part in parts]
    col_shapes = [(2, *shape) for part, shape in zip(parts, shapes) if part.col]
    made_shapes = [(SLOTS, *shape[1:]) for part, shape in zip(parts, shapes) if not part.col]
    pieces = sum(shape[1] * 2 for shape in col_shapes)
    own_shapes = [
        (2, 2, *shape) if part.col else (SLOTS, *shape[1:]) for part, shape in zip(parts, shapes)
    ]
    anywhere = pl.BlockSpec(memory_space=pl.ANY)
    dma = pltpu.SemaphoreType.DMA
    tokens = normed.shape[0]
    inputs = (normed, d_gate_up, act, d_low, grad_out, grad_project, small, mine)
    return pl.pallas_call(
        functools.partial(reduce_kernel, parts, planes),
        out_shape=[jax.ShapeDtypeStruct((n * r, c), BF) for n, r, c in shapes]
        + [
            jax.ShapeDtypeStruct(small.shape, F32),
            jax.ShapeDtypeStruct((2 * mine.shape[0], mine.shape[1] // 2), BF),
        ],
        in_specs=[anywhere] * len(inputs),
        out_specs=[anywhere] * (len(parts) + 2),
        scratch_shapes=[pltpu.VMEM(shape, BF) for _ in range(2) for shape in shapes]
        + [pltpu.VMEM(shape, BF) for shape in own_shapes + made_shapes]
        + [pltpu.VMEM((2, *shape), BF) for shape in col_shapes]
        + [pltpu.VMEM(shape, BF) for shape in col_shapes]
        + [
            pltpu.VMEM((tokens, d_gate_up.shape[1]), BF),
            pltpu.VMEM((2, tokens, 256), BF),
            pltpu.VMEM((256, tokens), BF),
            dma((2,)),
            dma((2, 2)),
            pltpu.SemaphoreType.REGULAR,
        ]
        + [dma((base,)) for _ in range(7)]
        + [dma((2, pieces)), dma((2, pieces)), dma((2, pieces)), dma((pieces,)), dma((pieces,))]
        + [dma((2,)), dma((5,)), dma((5,))]
        + [pltpu.VMEM((5, *small.shape), F32), pltpu.VMEM((6, *small.shape), F32)]
        + [dma((3, 2)), dma((3, 2)), dma((2,))],
        compiler_params=pltpu.CompilerParams(
            collective_id=0, has_side_effects=True, vmem_limit_bytes=60 * 1024 * 1024
        ),
        name="reduce_grads",
    )(*inputs)


TILE = 256
STEPS = 8


def spread_kernel(forward, *refs):
    if forward:
        mine_ref, *weights = refs[:7]
        all_ref, gate_ref, up_ref, act_ref, out_ref = refs[7:12]
        rest = refs[12:]
    else:
        mine_ref, *weights = refs[:7]
        gate_ref, up_ref = refs[7:9]
        all_ref, d_gate_up_ref, out_ref = refs[9:12]
        rest = refs[12:]
    block, w_gate, w_up, w_down, kept, to_mate, from_mate, far_part, to_far, from_mate_far, far_sum, from_far = rest[:12]
    (
        weight_sem, block_sem, out_sem, mate_send, mate_recv, x_send, x_recv, pass_send, pass_recv,
        sum_send, sum_recv, part_send, part_recv, back_send, back_recv,
    ) = rest[12:27]
    stage = rest[27:]
    tokens, depth = mine_ref.shape
    quarter = tokens // 4
    width = w_gate.shape[1]
    group, side = lax.axis_index("group"), lax.axis_index("side")
    mate, far = {"side": 1 - side}, {"group": 1 - group}

    def remote(source, target, send, recv, where):
        return pltpu.make_async_remote_copy(
            source, target, send, recv, device_id=where, device_id_type=pl.DeviceIdType.MESH
        )

    barrier = pltpu.get_barrier_semaphore()
    for where in (mate, far):
        pl.semaphore_signal(barrier, 1, device_id=where, device_id_type=pl.DeviceIdType.MESH)

    half = depth // 2
    loads = []
    for index, (source, target) in enumerate(
        [
            (weights[0], w_gate.at[pl.ds(0, half), :]),
            (weights[1], w_gate.at[pl.ds(half, half), :]),
            (weights[2], w_up.at[pl.ds(0, half), :]),
            (weights[3], w_up.at[pl.ds(half, half), :]),
            (weights[4], w_down.at[:, pl.ds(0, half)]),
            (weights[5], w_down.at[:, pl.ds(half, half)]),
        ]
    ):
        loads.append(pltpu.make_async_copy(source, target, weight_sem.at[index]))
    order = loads if forward else loads[4:] + loads[:4]
    mine_copies = [
        pltpu.make_async_copy(
            mine_ref.at[pl.ds(i * 2 * quarter, 2 * quarter), :], block.at[i], block_sem.at[i]
        )
        for i in range(2)
    ]
    for copy in mine_copies:
        copy.start()
    for copy in order:
        copy.start()
    pl.semaphore_wait(barrier, 2)

    def piece(index):
        return mine_ref.at[pl.ds(index * quarter, quarter), :]

    def mate_copy(index):
        return remote(
            piece(index),
            block.at[2 + index // 2, pl.ds(index % 2 * quarter, quarter), :],
            mate_send.at[index],
            mate_recv.at[index],
            mate,
        )

    def x_copy(index):
        return remote(
            piece(index), block.at[4 + index, pl.ds(0, quarter), :], x_send.at[index], x_recv.at[index], far
        )

    def pass_copy(index):
        return remote(
            block.at[4 + index, pl.ds(0, quarter), :],
            block.at[4 + index, pl.ds(quarter, quarter), :],
            pass_send.at[index],
            pass_recv.at[index],
            mate,
        )

    def sum_copy(index):
        return remote(to_mate.at[index], from_mate.at[index], sum_send.at[index], sum_recv.at[index], mate)

    def part_copy(index):
        return remote(to_far.at[index], from_mate_far.at[index], part_send.at[index], part_recv.at[index], mate)

    def back_copy(index):
        return remote(far_sum.at[index], from_far.at[index], back_send.at[index], back_recv.at[index], far)

    x_copy(0).start()
    for index in range(4):
        mate_copy(index).start()
    x_copy(1).start()
    for copy in mine_copies:
        copy.wait()

    def emit(step, where, part):
        @pl.when(step < 2)
        def _():
            kept[jnp.minimum(step, 1), :, where] = part

        @pl.when((step >= 2) & (step < 4))
        def _():
            to_mate[jnp.clip(step - 2, 0, 1), :, where] = part.astype(BF)

        @pl.when(step >= 4)
        def _():
            far_part[jnp.maximum(step - 4, 0), :, where] = part[:quarter]
            to_far[jnp.maximum(step - 4, 0), :, where] = part[quarter:].astype(BF)

    def all_copy(step):
        return pltpu.make_async_copy(block.at[step], all_ref.at[step], out_sem.at[0, step])

    if forward:
        stage_gate, stage_up, stage_act = stage

        def saves(step):
            slot = step % 2
            return [
                pltpu.make_async_copy(stage_gate.at[slot], gate_ref.at[step], out_sem.at[1, step]),
                pltpu.make_async_copy(stage_up.at[slot], up_ref.at[step], out_sem.at[2, step]),
                pltpu.make_async_copy(stage_act.at[slot], act_ref.at[step], out_sem.at[3, step]),
            ]

        def fetches(step):
            return []

        def first_loads():
            for copy in loads[:4]:
                copy.wait()

        def second_loads():
            for copy in loads[4:]:
                copy.wait()

        def first_half(step):
            slot = step % 2

            @pl.loop(0, width // TILE)
            def _(tile):
                where = pl.ds(pl.multiple_of(tile * TILE, TILE), TILE)
                gate = dot(block[step], w_gate[:, where])
                up = dot(block[step], w_up[:, where])
                stage_gate[slot, :, where] = gate.astype(BF)
                stage_up[slot, :, where] = up.astype(BF)
                stage_act[slot, :, where] = (gate * up / (1.0 + jnp.exp(-gate))).astype(BF)

        def second_half(step):
            slot = step % 2

            @pl.loop(0, depth // TILE)
            def _(tile):
                where = pl.ds(pl.multiple_of(tile * TILE, TILE), TILE)
                emit(step, where, dot(stage_act[slot], w_down[:, where]))

    else:
        stage_gate, stage_up, stage_d, fetch_sem = stage

        def saves(step):
            return [
                pltpu.make_async_copy(stage_d.at[step % 2], d_gate_up_ref.at[step], out_sem.at[1, step])
            ]

        def fetches(step):
            slot = step % 2
            return [
                pltpu.make_async_copy(gate_ref.at[step], stage_gate.at[slot], fetch_sem.at[0, step]),
                pltpu.make_async_copy(up_ref.at[step], stage_up.at[slot], fetch_sem.at[1, step]),
            ]

        def first_loads():
            for copy in loads[4:]:
                copy.wait()

        def second_loads():
            for copy in loads[:4]:
                copy.wait()

        def first_half(step):
            slot = step % 2

            @pl.loop(0, width // TILE)
            def _(tile):
                first = pl.multiple_of(tile * TILE, TILE)
                where = pl.ds(first, TILE)
                d_act = dot(block[step], w_down[where, :], ((1,), (1,)))
                gate = stage_gate[slot, :, where].astype(F32)
                up = stage_up[slot, :, where].astype(F32)
                sig = 1.0 / (1.0 + jnp.exp(-gate))
                d_gate = d_act * up * sig * (1.0 + gate * (1.0 - sig))
                stage_d[slot, :, where] = d_gate.astype(BF)
                stage_d[slot, :, pl.ds(pl.multiple_of(width + first, TILE), TILE)] = (d_act * gate * sig).astype(BF)

        def second_half(step):
            slot = step % 2

            @pl.loop(0, depth // TILE)
            def _(tile):
                where = pl.ds(pl.multiple_of(tile * TILE, TILE), TILE)
                part = dot(stage_d[slot, :, :width], w_gate[where, :], ((1,), (1,)))
                part += dot(stage_d[slot, :, width:], w_up[where, :], ((1,), (1,)))
                emit(step, where, part)

    def finish_far(index):
        part_copy(index).wait_recv()
        total = far_part[index] + from_mate_far[index].astype(F32)
        far_sum[index] = total.astype(BF)
        back_copy(index).start()

    for copy in fetches(0):
        copy.start()

    @pl.loop(0, STEPS)
    def _(step):
        @pl.when((step == 2) | (step == 3))
        def _():
            index = jnp.clip(2 * (step - 2), 0, 2)
            mate_copy(index).wait_recv()
            mate_copy(index + 1).wait_recv()

        @pl.when(step >= 4)
        def _():
            index = jnp.maximum(step - 4, 0)
            x_copy(index).wait_recv()
            pass_copy(index).start()
            pass_copy(index).wait_recv()

        all_copy(step).start()
        for copy in fetches(step):
            copy.wait()

        if not forward:
            @pl.when(step < STEPS - 1)
            def _():
                for copy in fetches(jnp.minimum(step + 1, STEPS - 1)):
                    copy.start()

        @pl.when(step == 0)
        def _():
            first_loads()

        @pl.when(step >= 2)
        def _():
            for copy in saves(jnp.maximum(step - 2, 0)):
                copy.wait()

        first_half(step)

        @pl.when(step == 0)
        def _():
            second_loads()

        second_half(step)
        for copy in saves(step):
            copy.start()

        @pl.when((step == 1) | (step == 3))
        def _():
            x_copy(2 + step // 2).start()

        @pl.when((step >= 2) & (step < 4))
        def _():
            sum_copy(jnp.clip(step - 2, 0, 1)).start()

        @pl.when(step >= 4)
        def _():
            part_copy(jnp.maximum(step - 4, 0)).start()

        @pl.when(step >= 5)
        def _():
            finish_far(jnp.maximum(step - 5, 0))

    finish_far(3)
    for index in range(2):
        sum_copy(index).wait_recv()
        kept[index] = kept[index] + from_mate[index].astype(F32)
    results = []
    for index in range(4):
        back_copy(index).wait_recv()
        rows = pl.ds(index % 2 * quarter, quarter)
        kept[index // 2, rows, :] = kept[index // 2, rows, :] + from_far[index].astype(F32)
        if index % 2:
            copy = pltpu.make_async_copy(kept.at[index // 2], out_ref.at[index // 2], block_sem.at[index // 2])
            copy.start()
            results.append(copy)
    for copy in results:
        copy.wait()

    @pl.loop(0, STEPS)
    def _(step):
        all_copy(step).wait()

        @pl.when(step >= STEPS - 2)
        def _():
            for copy in saves(step):
                copy.wait()

        @pl.when(step < 4)
        def _():
            index = jnp.minimum(step, 3)
            mate_copy(index).wait_send()
            x_copy(index).wait_send()
            pass_copy(index).wait_send()
            part_copy(index).wait_send()
            back_copy(index).wait_send()

        @pl.when(step < 2)
        def _():
            sum_copy(jnp.minimum(step, 1)).wait_send()


def spread(forward, mine, weights, *kept):
    tokens, depth = mine.shape
    quarter, double = tokens // 4, tokens // 2
    width = weights[0].shape[1]
    anywhere = pl.BlockSpec(memory_space=pl.ANY)
    wide = jax.ShapeDtypeStruct((STEPS, double, width), BF)
    whole = jax.ShapeDtypeStruct((STEPS, double, depth), BF)
    out = jax.ShapeDtypeStruct((2, double, depth), F32)
    if forward:
        outs = [whole, wide, wide, wide, out]
        stage = [pltpu.VMEM((2, double, width), BF) for _ in range(3)]
    else:
        outs = [whole, jax.ShapeDtypeStruct((STEPS, double, 2 * width), BF), out]
        stage = [
            pltpu.VMEM((2, double, width), BF),
            pltpu.VMEM((2, double, width), BF),
            pltpu.VMEM((2, double, 2 * width), BF),
            pltpu.SemaphoreType.DMA((2, STEPS)),
        ]
    result = pl.pallas_call(
        functools.partial(spread_kernel, forward),
        out_shape=outs,
        in_specs=[anywhere] * (7 + len(kept)),
        out_specs=[anywhere] * len(outs),
        scratch_shapes=[
            pltpu.VMEM((STEPS, double, depth), BF),
            pltpu.VMEM((depth, width), BF),
            pltpu.VMEM((depth, width), BF),
            pltpu.VMEM((width, depth), BF),
            pltpu.VMEM((2, double, depth), F32),
            pltpu.VMEM((2, double, depth), BF),
            pltpu.VMEM((2, double, depth), BF),
            pltpu.VMEM((4, quarter, depth), F32),
            pltpu.VMEM((4, quarter, depth), BF),
            pltpu.VMEM((4, quarter, depth), BF),
            pltpu.VMEM((4, quarter, depth), BF),
            pltpu.VMEM((4, quarter, depth), BF),
            pltpu.SemaphoreType.DMA((6,)),
            pltpu.SemaphoreType.DMA((2,)),
            pltpu.SemaphoreType.DMA((4, STEPS)),
        ]
        + [pltpu.SemaphoreType.DMA((4,)) for _ in range(6)]
        + [pltpu.SemaphoreType.DMA((2,)) for _ in range(2)]
        + [pltpu.SemaphoreType.DMA((4,)) for _ in range(4)]
        + stage,
        compiler_params=pltpu.CompilerParams(
            collective_id=5 if forward else 2,
            has_side_effects=True,
            vmem_limit_bytes=60 * 1024 * 1024,
        ),
        name="spread" if forward else "spread_back",
    )(mine, *weights, *kept)
    return result


def feed_kernel(*refs):
    refs = list(refs)

    def take(number):
        taken = refs[:number]
        del refs[:number]
        return taken

    mine_ref, *weights = take(6)
    teacher_ref, hidden_ref, scale_ref = take(3)
    all_ref, gate_ref, up_ref, act_ref, target_ref = take(5)
    all_low_ref, d_gate_up_ref, d_result_ref, out_ref, block_out_ref = take(5)
    block, w_gate, w_up, w_down, kept, to_mate, from_mate, far_part, to_far, from_mate_far, far_sum, from_far = take(12)
    stage_gate, stage_up, stage_act = take(3)
    weight_sem, block_sem, out_sem, fetch_sem, result_sem = take(5)
    mate_send, mate_recv, x_send, x_recv, pass_send, pass_recv, sum_send, sum_recv = take(8)
    part_send, part_recv, back_send, back_recv = take(4)
    deal_send, deal_recv, deal_local, row_send, row_recv, plane_send, plane_recv = take(7)
    tokens, depth = mine_ref.shape
    quarter = tokens // 4
    width = w_gate.shape[1]
    half = depth // 2
    row = lax.axis_index("row")
    group, side = lax.axis_index("group"), lax.axis_index("side")
    mate, far = {"side": 1 - side}, {"group": 1 - group}
    other_row, cross = {"row": 1 - row}, {"row": 1 - row, "side": 1 - side}
    parity = lax.axis_index("dp") % 2
    next_plane = {"dp": lax.axis_index("dp") + 1 - 2 * parity}
    member = 2 * row + side

    def remote(source, target, send, recv, where):
        return pltpu.make_async_remote_copy(
            source, target, send, recv, device_id=where, device_id_type=pl.DeviceIdType.MESH
        )

    def local(source, target, sem):
        return pltpu.make_async_copy(source, target, sem)

    barrier = pltpu.get_barrier_semaphore()
    greeted = [mate, far, other_row, cross, next_plane]
    for where in greeted:
        pl.semaphore_signal(barrier, 1, device_id=where, device_id_type=pl.DeviceIdType.MESH)

    mine_copies = [
        local(mine_ref.at[pl.ds(i * 2 * quarter, 2 * quarter), :], block.at[i], block_sem.at[i]) for i in range(2)
    ]
    loads = [
        local(weights[0], w_gate.at[pl.ds(0, half), :], weight_sem.at[0]),
        local(weights[1], w_gate.at[pl.ds(half, half), :], weight_sem.at[1]),
        local(weights[2], w_up.at[pl.ds(0, half), :], weight_sem.at[2]),
        local(weights[3], w_up.at[pl.ds(half, half), :], weight_sem.at[3]),
        local(weights[4], w_down.at[:, pl.ds(0, half)], weight_sem.at[4]),
    ]
    for copy in mine_copies + loads:
        copy.start()

    down_chunks = []
    rows = width // 8
    for index in range(4):
        here = pl.ds(pl.multiple_of((4 * parity + index) * rows, 16), rows)
        place = w_down.at[here, pl.ds(half, half)]
        down_chunks.append(
            (
                remote(weights[4].at[here, :], place, row_send.at[index], row_recv.at[index], other_row),
                remote(place, place, plane_send.at[index], plane_recv.at[index], next_plane),
            )
        )

    def deals(outward):
        sent, own = [], []
        for index, (to_row, to_side, where) in enumerate(
            [(1 - row, side, other_row), (1 - row, 1 - side, cross), (row, 1 - side, mate), (row, side, None)]
        ):
            slot = 0 if index >= 2 else 1
            there = 2 * to_row + to_side if outward == 0 else member
            for high in range(2):
                piece = 7 - there if high else there
                whole = pl.ds(pl.multiple_of(piece * quarter, quarter), quarter), slice(None)
                columns = pl.ds(slot * half, half)
                if outward == 0:
                    first = pl.multiple_of(side * 2 * quarter + high * quarter, quarter)
                    source, target = teacher_ref.at[whole], target_ref.at[pl.ds(first, quarter), columns]
                else:
                    source = to_mate.at[to_side, pl.ds(high * quarter, quarter), columns]
                    target = block_out_ref.at[whole]
                if where is None:
                    own.append(local(source, target, deal_local.at[outward, high]))
                else:
                    sems = deal_send.at[outward, index, high], deal_recv.at[outward, index, high]
                    sent.append(remote(source, target, *sems, where))
        return sent, own

    teacher_sent, teacher_own = deals(0)
    result_sent, result_own = deals(1)

    def piece(phase, index):
        if phase == 0:
            return mine_ref.at[pl.ds(index * quarter, quarter), :]
        return block.at[index // 2, pl.ds(index % 2 * quarter, quarter), :]

    def mate_copy(phase, index):
        target = block.at[2 + index // 2, pl.ds(index % 2 * quarter, quarter), :]
        return remote(piece(phase, index), target, mate_send.at[phase, index], mate_recv.at[phase, index], mate)

    def x_copy(phase, index):
        target = block.at[4 + index, pl.ds(0, quarter), :]
        return remote(piece(phase, index), target, x_send.at[phase, index], x_recv.at[phase, index], far)

    def pass_copy(phase, index):
        return remote(
            block.at[4 + index, pl.ds(0, quarter), :],
            block.at[4 + index, pl.ds(quarter, quarter), :],
            pass_send.at[phase, index],
            pass_recv.at[phase, index],
            mate,
        )

    def sum_copy(phase, index):
        return remote(
            to_mate.at[index], from_mate.at[index], sum_send.at[phase, index], sum_recv.at[phase, index], mate
        )

    def part_copy(phase, index):
        return remote(
            to_far.at[index], from_mate_far.at[index], part_send.at[phase, index], part_recv.at[phase, index], mate
        )

    def back_copy(phase, index):
        return remote(
            far_sum.at[index], from_far.at[index], back_send.at[phase, index], back_recv.at[phase, index], far
        )

    def all_copy(phase, step):
        return local(block.at[step], (all_ref, all_low_ref)[phase].at[step], out_sem.at[4 * phase, step])

    def saves(step):
        return [
            local(stage_gate.at[step % 2], gate_ref.at[step], out_sem.at[1, step]),
            local(stage_up.at[step % 2], up_ref.at[step], out_sem.at[2, step]),
            local(stage_act.at[step], act_ref.at[step], out_sem.at[3, step]),
        ]

    def back_saves(step):
        slot = 2 * (step % 2)
        return [
            local(stage_act.at[slot + i], d_gate_up_ref.at[step, :, pl.ds(i * width, width)], out_sem.at[5 + i, step])
            for i in range(2)
        ]

    def fetches(step):
        return [
            local(gate_ref.at[step], stage_gate.at[step % 2], fetch_sem.at[0, step]),
            local(up_ref.at[step], stage_up.at[step % 2], fetch_sem.at[1, step]),
        ]

    def emit(step, where, part):
        @pl.when(step < 2)
        def _():
            kept[jnp.minimum(step, 1), :, where] = part

        @pl.when((step >= 2) & (step < 4))
        def _():
            to_mate[jnp.clip(step - 2, 0, 1), :, where] = part.astype(BF)

        @pl.when(step >= 4)
        def _():
            far_part[jnp.maximum(step - 4, 0), :, where] = part[:quarter]
            to_far[jnp.maximum(step - 4, 0), :, where] = part[quarter:].astype(BF)

    def tiles(first, last, action):
        @pl.loop(first, last)
        def _(tile):
            action(pl.ds(pl.multiple_of(tile * TILE, TILE), TILE), pl.multiple_of(tile * TILE, TILE))

    def multiply_in(step):
        slot = step % 2

        def action(where, first):
            gate = dot(block[step], w_gate[:, where])
            up = dot(block[step], w_up[:, where])
            stage_gate[slot, :, where] = gate.astype(BF)
            stage_up[slot, :, where] = up.astype(BF)
            stage_act[step, :, where] = (gate * up / (1.0 + jnp.exp(-gate))).astype(BF)

        tiles(0, width // TILE, action)

    def multiply_out(step, first=0, last=depth // TILE):
        tiles(first, last, lambda where, _: emit(step, where, dot(stage_act[step], w_down[:, where])))

    def multiply_back_in(step):
        slot = step % 2

        def action(where, first):
            d_act = dot(block[step], w_down[where, :], ((1,), (1,)))
            gate = stage_gate[slot, :, where].astype(F32)
            up = stage_up[slot, :, where].astype(F32)
            sig = 1.0 / (1.0 + jnp.exp(-gate))
            d_gate = d_act * up * sig * (1.0 + gate * (1.0 - sig))
            stage_act[2 * slot, :, where] = d_gate.astype(BF)
            stage_act[2 * slot + 1, :, where] = (d_act * gate * sig).astype(BF)

        tiles(0, width // TILE, action)

    def multiply_back_out(step):
        slot = 2 * (step % 2)

        def action(where, first):
            part = dot(stage_act[slot], w_gate[where, :], ((1,), (1,)))
            part += dot(stage_act[slot + 1], w_up[where, :], ((1,), (1,)))
            emit(step, where, part)

        tiles(0, depth // TILE, action)

    def finish_far(phase, index):
        part_copy(phase, index).wait_recv()
        total = far_part[index] + from_mate_far[index].astype(F32)
        far_sum[index] = total.astype(BF)
        if phase == 0:
            all_copy(0, 4 + index).wait()
            pass_copy(0, index).wait_send()
        back_copy(phase, index).start()

    def arrive(phase, step):
        @pl.when((step == 2) | (step == 3))
        def _():
            index = jnp.clip(2 * (step - 2), 0, 2)
            mate_copy(phase, index).wait_recv()
            mate_copy(phase, index + 1).wait_recv()

        @pl.when(step >= 4)
        def _():
            index = jnp.maximum(step - 4, 0)
            x_copy(phase, index).wait_recv()
            pass_copy(phase, index).start()
            pass_copy(phase, index).wait_recv()

        all_copy(phase, step).start()

    pl.semaphore_wait(barrier, len(greeted))
    for over_row, _ in down_chunks:
        over_row.start()
    x_copy(0, 0).start()
    for index in range(4):
        mate_copy(0, index).start()
    x_copy(0, 1).start()
    for copy in teacher_sent + teacher_own:
        copy.start()
    for copy in mine_copies:
        copy.wait()

    @pl.loop(0, STEPS)
    def _(step):
        @pl.when(step == 7)
        def _():
            finish_far(0, 2)

        arrive(0, step)

        @pl.when(step == 0)
        def _():
            for copy in loads:
                copy.wait()

        @pl.when(step >= 2)
        def _():
            for copy in saves(jnp.maximum(step - 2, 0)):
                copy.wait()

        multiply_in(step)

        @pl.when(step < 6)
        def _():
            multiply_out(step, 0, half // TILE)

        for index in range(4):
            @pl.when(step == index + 1)
            def _(index=index):
                down_chunks[index][0].wait_recv()
                down_chunks[index][1].start()

        @pl.when(step == 5)
        def _():
            for _, over_planes in down_chunks:
                over_planes.wait_recv()
            pl.loop(4, 6)(lambda early: multiply_out(early, half // TILE))
            part_copy(0, 0).start()
            part_copy(0, 1).start()
            pl.loop(2, 4)(lambda early: multiply_out(early, half // TILE))
            for index in range(2):
                all_copy(0, 2 + index).wait()
                sum_copy(0, index).start()
            finish_far(0, 0)
            finish_far(0, 1)
            pl.loop(0, 2)(lambda early: multiply_out(early, half // TILE))

        @pl.when(step >= 6)
        def _():
            multiply_out(step)
            part_copy(0, jnp.maximum(step - 4, 0)).start()

        for copy in saves(step):
            copy.start()

        @pl.when((step == 1) | (step == 3))
        def _():
            x_copy(0, 2 + step // 2).start()

    for copy in teacher_own:
        copy.wait()
    for copy in teacher_sent:
        copy.wait_recv()
    result_loads = []
    for index in range(4):
        if index == 3:
            finish_far(0, 3)
        part_copy(0, index).wait_send()
        here = pl.ds(index * quarter, quarter)
        result_loads.append(
            [
                local(target_ref.at[here, :], to_far.at[index], result_sem.at[0, index]),
                local(hidden_ref.at[here, :], far_part.at[index], result_sem.at[1, index]),
            ]
        )
        for copy in result_loads[-1]:
            copy.start()
    for index in range(2):
        all_copy(0, index).wait()
        sum_copy(0, index).wait()
    for step in (STEPS - 2, STEPS - 1):
        for copy in saves(step):
            copy.wait()
    for copy in fetches(0):
        copy.start()
    scale = scale_ref[0]
    d_result_saves = []
    for index in range(4):
        back_copy(0, index).wait_recv()
        for copy in result_loads[index]:
            copy.wait()
        here = pl.ds(index % 2 * quarter, quarter)

        def action(where, first):
            total = kept[index // 2, here, where] + from_mate[index // 2, here, where].astype(F32)
            total = total + from_far[index, :, where].astype(F32)
            result = far_part[index, :, where] + total
            d_result = scale * (result - to_far[index, :, where].astype(F32))
            to_mate[index // 2, here, where] = result.astype(BF)
            kept[index // 2, here, where] = d_result
            block[index // 2, here, where] = d_result.astype(BF)

        tiles(0, depth // TILE, action)
        x_copy(1, index).start()
        mate_copy(1, index).start()
        if index % 2:
            copy = local(kept.at[index // 2], d_result_ref.at[index // 2], block_sem.at[index // 2])
            copy.start()
            d_result_saves.append(copy)
    for copy in result_sent + result_own:
        copy.start()
    for index in range(4):
        mate_copy(0, index).wait_send()
        x_copy(0, index).wait_send()
        back_copy(0, index).wait_send()

    @pl.loop(0, STEPS)
    def _(step):
        @pl.when(step >= 5)
        def _():
            finish_far(1, jnp.maximum(step - 5, 0))

        arrive(1, step)
        for copy in fetches(step):
            copy.wait()

        @pl.when(step < STEPS - 1)
        def _():
            for copy in fetches(jnp.minimum(step + 1, STEPS - 1)):
                copy.start()

        @pl.when(step >= 2)
        def _():
            for copy in back_saves(jnp.maximum(step - 2, 0)):
                copy.wait()

        multiply_back_in(step)

        @pl.when(step == 0)
        def _():
            for copy in d_result_saves:
                copy.wait()

        @pl.when(step == 2)
        def _():
            for copy in result_own:
                copy.wait()
            for copy in result_sent:
                copy.wait_send()

        multiply_back_out(step)
        for copy in back_saves(step):
            copy.start()

        @pl.when((step >= 2) & (step < 4))
        def _():
            sum_copy(1, jnp.clip(step - 2, 0, 1)).start()

        @pl.when(step >= 4)
        def _():
            part_copy(1, jnp.maximum(step - 4, 0)).start()

    finish_far(1, 3)
    for index in range(2):
        sum_copy(1, index).wait_recv()
        kept[index] = kept[index] + from_mate[index].astype(F32)
    results = []
    for index in range(4):
        back_copy(1, index).wait_recv()
        here = pl.ds(index % 2 * quarter, quarter)
        kept[index // 2, here, :] = kept[index // 2, here, :] + from_far[index].astype(F32)
        if index % 2:
            results.append(local(kept.at[index // 2], out_ref.at[index // 2], block_sem.at[index // 2]))
            results[-1].start()
    for copy in results:
        copy.wait()
    for copy in result_sent:
        copy.wait_recv()
    for copy in teacher_sent:
        copy.wait_send()
    for over_row, over_planes in down_chunks:
        over_row.wait_send()
        over_planes.wait_send()

    @pl.loop(0, STEPS)
    def _(step):
        all_copy(1, step).wait()

        @pl.when(step >= STEPS - 2)
        def _():
            for copy in back_saves(step):
                copy.wait()

        @pl.when(step < 4)
        def _():
            index = jnp.minimum(step, 3)
            for copy in (mate_copy, x_copy, pass_copy, part_copy, back_copy):
                copy(1, index).wait_send()

        @pl.when(step < 2)
        def _():
            sum_copy(1, jnp.minimum(step, 1)).wait_send()


def feed(mine, weights, teacher, hidden, scale):
    tokens, depth = mine.shape
    quarter, double = tokens // 4, tokens // 2
    width = weights[0].shape[1]
    anywhere = pl.BlockSpec(memory_space=pl.ANY)
    shape = jax.ShapeDtypeStruct
    wide, whole = shape((STEPS, double, width), BF), shape((STEPS, double, depth), BF)
    own = shape((2, double, depth), F32)
    outs = [
        whole, wide, wide, wide, shape((tokens, depth), BF),
        whole, shape((STEPS, double, 2 * width), BF), own, own, shape((2 * tokens, depth // 2), BF),
    ]
    dma = pltpu.SemaphoreType.DMA
    return pl.pallas_call(
        feed_kernel,
        out_shape=outs,
        in_specs=[anywhere] * 8 + [pl.BlockSpec(memory_space=pltpu.SMEM)],
        out_specs=[anywhere] * len(outs),
        scratch_shapes=[
            pltpu.VMEM((STEPS, double, depth), BF),
            pltpu.VMEM((depth, width), BF),
            pltpu.VMEM((depth, width), BF),
            pltpu.VMEM((width, depth), BF),
            pltpu.VMEM((2, double, depth), F32),
            pltpu.VMEM((2, double, depth), BF),
            pltpu.VMEM((2, double, depth), BF),
            pltpu.VMEM((4, quarter, depth), F32),
            pltpu.VMEM((4, quarter, depth), BF),
            pltpu.VMEM((4, quarter, depth), BF),
            pltpu.VMEM((4, quarter, depth), BF),
            pltpu.VMEM((4, quarter, depth), BF),
            pltpu.VMEM((2, double, width), BF),
            pltpu.VMEM((2, double, width), BF),
            pltpu.VMEM((STEPS, double, width), BF),
            dma((5,)), dma((2,)), dma((7, STEPS)), dma((2, STEPS)), dma((2, 4)),
            dma((2, 4)), dma((2, 4)), dma((2, 4)), dma((2, 4)), dma((2, 4)), dma((2, 4)), dma((2, 2)), dma((2, 2)),
            dma((2, 4)), dma((2, 4)), dma((2, 4)), dma((2, 4)),
            dma((2, 3, 2)), dma((2, 3, 2)), dma((2, 2)), dma((4,)), dma((4,)), dma((4,)), dma((4,)),
        ],
        compiler_params=pltpu.CompilerParams(
            collective_id=1, has_side_effects=True, vmem_limit_bytes=60 * 1024 * 1024
        ),
        name="feed_forward",
    )(mine, *weights, teacher, hidden, scale)


def front_kernel(*refs):
    refs = list(refs)

    def take(number):
        taken = refs[:number]
        del refs[:number]
        return taken

    tokens_ref, w_project_ref, w_out_ref, gains_ref, gate_ref, up_ref = take(6)
    cos_ref, sin_ref, query_gain_ref, key_gain_ref = take(4)
    (
        states_out, normed_out, raw_out, query_out, key_out, pair_out, mixed_out, logs_out, hidden_out, normed_two_out,
        w_project_out, w_out_out, gate_out, up_out, gains_out,
    ) = take(15)
    states, normed, w_project, raw, key_raw, query, pair_own, pair, key_n, mixed_t, logs, mixed = take(12)
    w_out, hidden, gains = take(3)
    token_send, token_recv, token_local = take(3)
    project_send, project_recv, out_send, out_recv, gain_send, gain_recv = take(6)
    pair_send, pair_recv, row_send, row_recv, plane_send, plane_recv, local, store = take(8)

    plane, row = lax.axis_index("dp"), lax.axis_index("row")
    group, side = lax.axis_index("group"), lax.axis_index("side")
    other_row, mate, far = {"row": 1 - row}, {"side": 1 - side}, {"group": 1 - group}
    cross = {"row": 1 - row, "side": 1 - side}
    parity = plane % 2
    next_plane = {"dp": plane + 1 - 2 * parity}
    shard, width = tokens_ref.shape
    mine, depth = states.shape
    pieces = 8
    span = shard // pieces
    member = 2 * row + side
    kv_rows = key_raw.shape[0]

    def remote(source, target, send, recv, where):
        return pltpu.make_async_remote_copy(
            source, target, send, recv, device_id=where, device_id_type=pl.DeviceIdType.MESH
        )

    barrier = pltpu.get_barrier_semaphore()
    for where in (other_row, mate, far, cross, next_plane):
        pl.semaphore_signal(barrier, 1, device_id=where, device_id_type=pl.DeviceIdType.MESH)

    def token_copies(to_row, to_side, index, where):
        target_member = 2 * to_row + to_side
        slot = 1 if to_row is not row else 0
        copies = []
        for high in range(2):
            piece = pieces - 1 - target_member if high else target_member
            source = tokens_ref.at[pl.ds(pl.multiple_of(piece * span, span), span), :]
            first = pl.multiple_of(side * 2 * span + high * span, span)
            target = states.at[pl.ds(first, span), pl.ds(slot * width, width)]
            if where is None:
                copies.append(pltpu.make_async_copy(source, target, token_local.at[high]))
            else:
                sems = token_send.at[index, high], token_recv.at[index, high]
                copies.append(remote(source, target, *sems, where))
        return copies

    own_tokens = token_copies(row, side, 0, None)
    other = 1 - row
    sent_tokens = token_copies(other, side, 0, other_row)
    sent_tokens += token_copies(other, 1 - side, 1, cross)
    sent_tokens += token_copies(row, 1 - side, 2, mate)

    me, far_col = 2 * group + side, 2 * (1 - group) + side

    class Spread:
        def __init__(self, source, place, send, recv):
            self.copies = []

            def add(origin, target, where):
                index = len(self.copies)
                self.copies.append(remote(origin, target, send.at[index], recv.at[index], where))
                return self.copies[-1]

            here, there = parity, 1 - parity
            rows = source.shape[0] // 2
            first_half = source.at[pl.ds(pl.multiple_of(here * rows, 16), rows), :]
            self.to_row = add(first_half, place(me, 1, here), other_row)
            self.to_plane = add(place(me, 1, here), place(me, 1, here), next_plane)
            self.to_far = [add(source, place(me, 0, None), far)]
            self.to_far += [add(place(me, 1, half), place(me, 1, half), far) for half in (here, there)]
            self.to_mate = [add(source, place(me, 0, None), mate)]
            self.to_mate += [add(place(me, 1, half), place(me, 1, half), mate) for half in (here, there)]
            self.to_mate += [add(place(far_col, 0, None), place(far_col, 0, None), mate)]
            self.to_mate += [
                add(place(far_col, 1, half), place(far_col, 1, half), mate) for half in (here, there)
            ]

        def first(self):
            self.to_row.start()
            self.to_far[0].start()
            self.to_mate[0].start()

        def row_in(self):
            self.to_row.wait_recv()
            for copy in (self.to_plane, self.to_far[1], self.to_mate[1]):
                copy.start()

        def plane_in(self):
            self.to_plane.wait_recv()
            self.to_far[2].start()
            self.to_mate[2].start()

        def far_in(self, index):
            self.to_far[index].wait_recv()
            self.to_mate[3 + index].start()

        def mate_in(self, first, last):
            for copy in self.to_mate[first:last]:
                copy.wait_recv()

        def sent(self):
            for copy in self.copies:
                copy.wait_send()

    q_width = w_out_ref.shape[0]

    def project_place(col, slot, half):
        if half is None:
            return w_project.at[col, slot]
        return w_project.at[col, slot, pl.ds(pl.multiple_of(half * (width // 2), 16), width // 2), :]

    def out_place(col, slot, half):
        first, rows = col * q_width, q_width
        if half is not None:
            rows = q_width // 2
            first = first + half * rows
        return w_out.at[pl.ds(pl.multiple_of(first, 16), rows), pl.ds(slot * width, width)]

    project = Spread(w_project_ref, project_place, project_send, project_recv)
    output = Spread(w_out_ref, out_place, out_send, out_recv)
    own_project = pltpu.make_async_copy(w_project_ref, w_project.at[me, 0], local.at[0])
    own_output = pltpu.make_async_copy(w_out_ref, out_place(me, 0, None), local.at[1])
    own_gains = pltpu.make_async_copy(gains_ref, gains.at[0], local.at[2])
    sent_gains = remote(gains_ref, gains.at[1], gain_send.at[0], gain_recv.at[0], other_row)

    chunks = []
    for index, (source, target) in enumerate([(gate_ref, gate_out), (up_ref, up_out)]):
        rows = source.shape[0] // 4
        for part in range(2):
            here = pl.ds(pl.multiple_of((2 * parity + part) * rows, 64), rows)
            slot = 2 * index + part
            over_row = remote(source.at[here, :], target.at[here, :], row_send.at[slot], row_recv.at[slot], other_row)
            over_planes = remote(
                target.at[here, :], target.at[here, :], plane_send.at[slot], plane_recv.at[slot], next_plane
            )
            chunks.append((over_row, over_planes))

    def pass_on(index):
        chunks[index][0].wait_recv()
        chunks[index][1].start()

    own_copies = [own_gains, *own_tokens, own_project, own_output]
    for copy in own_copies:
        copy.start()
    pl.semaphore_wait(barrier, 5)
    sent_gains.start()
    project.first()
    for copy in sent_tokens:
        copy.start()
    chunks[0][0].start()
    for copy in own_copies:
        copy.wait()
    sent_gains.wait_recv()
    project.row_in()
    for copy in sent_tokens:
        copy.wait_recv()

    stores = []

    def save(source, target):
        copy = pltpu.make_async_copy(source, target, store.at[len(stores)])
        copy.start()
        stores.append(copy)
        return copy

    block = mine // 4

    @pl.loop(0, 4)
    def _(index):
        here = pl.ds(pl.multiple_of(index * block, block), block)
        values = states[here, :].astype(F32)
        inverse = lax.rsqrt(jnp.mean(values * values, axis=1, keepdims=True) + EPSILON)
        for slot in range(2):
            part = values[:, slot * width : (slot + 1) * width] * inverse
            normed[here, slot * width : (slot + 1) * width] = (part * gains[slot, 0:1, :]).astype(BF)

    save(states, states_out)
    normed_saved = save(normed, normed_out)
    save(gains, gains_out)

    def project_col(col):
        part = dot(normed[:, :width], w_project[col, 0]) + dot(normed[:, width:], w_project[col, 1])
        part = part.T
        heads = q_width // HD
        for head in range(heads):
            raw[col * heads + head] = part[head * HD : (head + 1) * HD]
        k_width = kv_rows // 4
        first = pl.multiple_of(col * k_width, 16)
        key_raw[pl.ds(first, k_width), :] = part[q_width : q_width + k_width].astype(BF)
        first = pl.multiple_of(kv_rows + col * k_width, 16)
        pair_own[pl.ds(first, k_width), :] = part[q_width + k_width :].astype(BF)

    project.plane_in()
    project.far_in(0)
    output.to_row.start()
    project_col(me)
    project.mate_in(0, 3)
    project_col(2 * group + 1 - side)
    project.far_in(1)
    project.far_in(2)
    project_col(far_col)
    project.mate_in(3, 6)
    project_col(2 * (1 - group) + 1 - side)
    save(raw, raw_out)
    save(key_raw, key_out)
    save(w_project, w_project_out)

    cosine, sine = cos_ref[...], sin_ref[...]

    def turned(values, gain):
        values = values * lax.rsqrt(jnp.mean(values * values, axis=0, keepdims=True) + EPSILON) * gain
        first, second = values[: HD // 2], values[HD // 2 :]
        return jnp.concatenate([first * cosine - second * sine, second * cosine + first * sine], axis=0)

    for head in range(kv_rows // HD):
        cut = slice(head * HD, (head + 1) * HD)
        pair_own[cut, :] = turned(key_raw[cut, :].astype(F32), key_gain_ref[...]).astype(BF)

    def places(who):
        starts = [who, pieces - 1 - who, pieces + who, 2 * pieces - 1 - who]
        return [pair.at[:, pl.ds(pl.multiple_of(start * span, span), span)] for start in starts]

    for index, place in enumerate(places(member)):
        place[...] = pair_own[:, index * span : (index + 1) * span]
    to_mate, to_row, passed = [], [], []
    for index, place in enumerate(places(member)):
        to_row.append(remote(place, place, pair_send.at[0, index], pair_recv.at[0, index], other_row))
        to_mate.append(remote(place, place, pair_send.at[1, index], pair_recv.at[1, index], mate))
    for index, place in enumerate(places(2 * (1 - row) + side)):
        passed.append(remote(place, place, pair_send.at[2, index], pair_recv.at[2, index], mate))
    for copy in to_row + to_mate:
        copy.start()
    output.to_far[0].start()
    output.to_mate[0].start()
    chunks[1][0].start()

    @pl.loop(0, raw.shape[0])
    def _(head):
        values = turned(raw[head], query_gain_ref[...]).astype(BF)
        query[head] = values * BF(1.0 / math.sqrt(HD))

    for index in range(4):
        to_row[index].wait_recv()
        passed[index].start()
    output.row_in()
    chunks[2][0].start()
    pass_on(0)
    for index in range(4):
        to_mate[index].wait_recv()
        passed[index].wait_recv()
    chunks[3][0].start()
    output.plane_in()
    output.far_in(0)

    firsts = [member, pieces - 1 - member, pieces + member, 2 * pieces - 1 - member]
    rows = REP * span
    ones = jnp.ones((16, KEYS), BF)

    @pl.loop(0, kv_rows // HD)
    def _(head):
        key_n[...] = pair[pl.ds(pl.multiple_of(head * HD, HD), HD), :].T
        value_rows = pl.ds(pl.multiple_of(kv_rows + head * HD, HD), HD)
        for index in range(4):
            cut = slice(index * span, (index + 1) * span)
            query_here = jnp.concatenate([query[head * REP + rep, :, cut] for rep in range(REP)], axis=1)
            first_query = firsts[index] * span
            full, last = tiles_of(first_query)

            def tile(where, accum, masked):
                first_key = pl.multiple_of(where * KEYS, KEYS)
                expo = jnp.exp(dot(key_n[pl.ds(first_key, KEYS), :], query_here))
                if masked:
                    expo = jnp.where(allowed(first_query, first_key, span, rows), expo, 0.0)
                value = jnp.concatenate([pair[value_rows, pl.ds(first_key, KEYS)], ones], axis=0)
                return accum + dot(value, expo.astype(BF))

            accum = tile(last, jnp.zeros((HD + 16, rows), F32), True)
            accum = lax.fori_loop(0, full, lambda where, total: tile(where, total, False), accum)
            total = accum[HD : HD + 1]
            result = accum[:HD] / total
            log = jnp.log(total)
            for rep in range(REP):
                part = slice(rep * span, (rep + 1) * span)
                mixed_t[pl.ds(pl.multiple_of((head * REP + rep) * HD, HD), HD), cut] = result[:, part]
                logs[head, rep : rep + 1, cut] = log[:, part]

        @pl.when(head == 2)
        def _():
            output.far_in(1)
            output.far_in(2)

        for number, index in ((1, 1), (3, 2)):
            @pl.when(head == number)
            def _(index=index):
                pass_on(index)

    save(query, query_out)
    save(mixed_t, mixed_out)
    save(logs, logs_out)
    save(pair, pair_out)
    pass_on(3)
    output.mate_in(0, 6)
    save(w_out, w_out_out)

    @pl.loop(0, mixed_t.shape[0] // 128)
    def _(index):
        here = pl.ds(pl.multiple_of(index * 128, 128), 128)
        mixed[:, here] = mixed_t[here, :].astype(BF).T

    @pl.loop(0, depth // TILE)
    def _(index):
        here = pl.ds(pl.multiple_of(index * TILE, TILE), TILE)
        hidden[:, here] = states[:, here].astype(F32) + dot(mixed[...], w_out[:, here])

    normed_saved.wait()

    @pl.loop(0, 4)
    def _(index):
        here = pl.ds(pl.multiple_of(index * block, block), block)
        values = hidden[here, :]
        inverse = lax.rsqrt(jnp.mean(values * values, axis=1, keepdims=True) + EPSILON)
        for slot in range(2):
            part = values[:, slot * width : (slot + 1) * width] * inverse
            normed[here, slot * width : (slot + 1) * width] = (part * gains[slot, 1:2, :]).astype(BF)

    save(hidden, hidden_out)
    save(normed, normed_two_out)
    for copy in stores:
        if copy is not normed_saved:
            copy.wait()
    sent_gains.wait_send()
    for copy in sent_tokens + to_row + to_mate + passed:
        copy.wait_send()
    project.sent()
    output.sent()
    for over_row, over_planes in chunks:
        over_row.wait_send()
        over_planes.wait_recv()
        over_planes.wait_send()


def front(tokens, w_project, w_out, gains, w_gate, w_up, cosine, sine, query_gain, key_gain):
    shard, width = tokens.shape
    mine, depth = shard // 2, 2 * width
    q_width, columns = w_out.shape[0], w_project.shape[1]
    kv_rows = KVH * HD
    anywhere = pl.BlockSpec(memory_space=pl.ANY)
    inside = pl.BlockSpec(memory_space=pltpu.VMEM)
    dma = pltpu.SemaphoreType.DMA
    shape = jax.ShapeDtypeStruct
    return pl.pallas_call(
        front_kernel,
        out_shape=[
            shape((mine, depth), BF),
            shape((mine, depth), BF),
            shape((QH, HD, mine), F32),
            shape((QH, HD, mine), BF),
            shape((kv_rows, mine), BF),
            shape((2 * kv_rows, GROUP), BF),
            shape((QH * HD, mine), F32),
            shape((KVH, REP, mine), F32),
            shape((mine, depth), F32),
            shape((mine, depth), BF),
            shape((4, 2, width, columns), BF),
            shape((4 * q_width, depth), BF),
            shape(w_gate.shape, BF),
            shape(w_up.shape, BF),
            shape((2, 2, width), F32),
        ],
        in_specs=[anywhere] * 6 + [inside] * 4,
        out_specs=[anywhere] * 15,
        scratch_shapes=[
            pltpu.VMEM((mine, depth), BF),
            pltpu.VMEM((mine, depth), BF),
            pltpu.VMEM((4, 2, width, columns), BF),
            pltpu.VMEM((QH, HD, mine), F32),
            pltpu.VMEM((kv_rows, mine), BF),
            pltpu.VMEM((QH, HD, mine), BF),
            pltpu.VMEM((2 * kv_rows, mine), BF),
            pltpu.VMEM((2 * kv_rows, GROUP), BF),
            pltpu.VMEM((GROUP, HD), BF),
            pltpu.VMEM((QH * HD, mine), F32),
            pltpu.VMEM((KVH, REP, mine), F32),
            pltpu.VMEM((mine, QH * HD), BF),
            pltpu.VMEM((4 * q_width, depth), BF),
            pltpu.VMEM((mine, depth), F32),
            pltpu.VMEM((2, 2, width), F32),
            dma((3, 2)), dma((3, 2)), dma((2,)),
            dma((11,)), dma((11,)), dma((11,)), dma((11,)), dma((1,)), dma((1,)),
            dma((3, 4)), dma((3, 4)), dma((4,)), dma((4,)), dma((4,)), dma((4,)), dma((3,)), dma((13,)),
        ],
        compiler_params=pltpu.CompilerParams(
            collective_id=3, has_side_effects=True, vmem_limit_bytes=56 * 1024 * 1024
        ),
        name="front",
    )(tokens, w_project, w_out, gains, w_gate, w_up, cosine, sine, query_gain, key_gain)


def back_kernel(*refs):
    query, d_out, logs_ref, delta_ref, pair, raw, key_raw, cos_ref, sin_ref, query_gain, key_gain = refs[:11]
    d_project, query_gain_out, key_gain_out = refs[11:14]
    key_n, value_n, d_key, d_value, both_t, staged, come, gain_sum, send_sem, recv_sem = refs[14:]
    row, side = lax.axis_index("row"), lax.axis_index("side")
    others = [
        (2 * (1 - row) + side, {"row": 1 - row}),
        (2 * (1 - row) + 1 - side, {"row": 1 - row, "side": 1 - side}),
        (2 * row + 1 - side, {"side": 1 - side}),
    ]
    member = 2 * row + side
    pieces = 8
    span = query.shape[2] // 4
    rows = REP * span
    kv_rows = key_raw.shape[0]
    half = HD // 2

    barrier = pltpu.get_barrier_semaphore()
    for _, where in others:
        pl.semaphore_signal(barrier, 1, device_id=where, device_id_type=pl.DeviceIdType.MESH)
    pl.semaphore_wait(barrier, 3)

    def sent(index, head):
        return pltpu.make_async_remote_copy(
            staged.at[index, head],
            come.at[index, head],
            send_sem.at[index, head],
            recv_sem.at[index, head],
            device_id=others[index][1],
            device_id_type=pl.DeviceIdType.MESH,
        )

    def starts(who):
        return [who, pieces - 1 - who, pieces + who, 2 * pieces - 1 - who]

    def through_norm(values, gain, cosine, sine, d_turned):
        first, second = d_turned[:half], d_turned[half:]
        d_scaled = jnp.concatenate([first * cosine + second * sine, second * cosine - first * sine], axis=0)
        inverse = lax.rsqrt(jnp.mean(values * values, axis=0, keepdims=True) + EPSILON)
        d_normed = d_scaled * gain
        mean = jnp.mean(values * d_normed, axis=0, keepdims=True)
        return inverse * d_normed - values * inverse**3 * mean, d_scaled * values * inverse

    gain_sum[...] = jnp.zeros_like(gain_sum)
    scale = 1.0 / math.sqrt(HD)

    @pl.loop(0, KVH)
    def _(head):
        key_rows = pl.ds(pl.multiple_of(head * HD, HD), HD)
        value_rows = pl.ds(pl.multiple_of(kv_rows + head * HD, HD), HD)
        key_n[...] = pair[key_rows, :].T
        value_n[...] = pair[value_rows, :].T
        d_key[...] = jnp.zeros_like(d_key)
        d_value[...] = jnp.zeros_like(d_value)
        for index, start in enumerate(starts(member)):
            cut = slice(index * span, (index + 1) * span)

            def beside(ref):
                return jnp.concatenate([ref[head * REP + rep, :, cut] for rep in range(REP)], axis=1)

            query_here, d_out_here = beside(query), beside(d_out)
            query_t, d_out_t = query_here.T, d_out_here.T
            logs = jnp.concatenate([logs_ref[head, rep : rep + 1, cut] for rep in range(REP)], axis=1)
            delta = jnp.concatenate([delta_ref[head, rep : rep + 1, cut] for rep in range(REP)], axis=1)
            first_query = start * span
            full, last = tiles_of(first_query)

            def tile(where, accum, masked):
                first_key = pl.multiple_of(where * KEYS, KEYS)
                here = pl.ds(first_key, KEYS)
                probs = jnp.exp(dot(key_n[here, :], query_here) - logs)
                if masked:
                    probs = jnp.where(allowed(first_query, first_key, span, rows), probs, 0.0)
                d_probs = dot(value_n[here, :], d_out_here)
                d_scores = (probs * (d_probs - delta)).astype(BF)
                d_value[here, :] += dot(probs.astype(BF), d_out_t)
                d_key[here, :] += dot(d_scores, query_t)
                return accum + dot(pair[key_rows, here], d_scores)

            accum = tile(last, jnp.zeros((HD, rows), F32), True)
            accum = lax.fori_loop(0, full, lambda where, total: tile(where, total, False), accum)
            cosine = jnp.concatenate([cos_ref[:, cut]] * REP, axis=1)
            sine = jnp.concatenate([sin_ref[:, cut]] * REP, axis=1)
            d_raw, part = through_norm(beside(raw), query_gain[...], cosine, sine, accum * scale)
            gain_sum[0] += part
            for rep in range(REP):
                which = head * REP + rep
                place = pl.ds(pl.multiple_of(which % KVH * HD, HD), HD)
                d_project[which // KVH, place, cut] = d_raw[:, rep * span : (rep + 1) * span].astype(BF)
        both_t[:HD, :] = d_key[...].T.astype(BF)
        both_t[HD:, :] = d_value[...].T.astype(BF)
        for index, who in enumerate([who for who, _ in others] + [member]):
            for number, start in enumerate(starts(who)):
                part = both_t[:, pl.ds(pl.multiple_of(start * span, span), span)]
                staged[index, head, :, number * span : (number + 1) * span] = part
            if index < 3:
                sent(index, head).start()

    cosine, sine = cos_ref[...], sin_ref[...]
    width = kv_rows // 4
    for head in range(KVH):
        total = staged[3, head].astype(F32)
        for index in range(3):
            sent(index, head).wait_recv()
            total += come[index, head].astype(F32)
        values = key_raw[head * HD : (head + 1) * HD, :].astype(F32)
        d_raw, part = through_norm(values, key_gain[...], cosine, sine, total[:HD])
        gain_sum[1] += part
        for offset, result in ((0, d_raw.astype(BF)), (width, total[HD:].astype(BF))):
            first = head * HD
            while first < (head + 1) * HD:
                col, inside = first // width, first % width
                size = min(width - inside, (head + 1) * HD - first)
                place = d_project.shape[1] - 2 * width + offset + inside
                d_project[col, place : place + size, :] = result[first - head * HD : first - head * HD + size]
                first += size
    query_gain_out[...] = jnp.sum(gain_sum[0], axis=1, keepdims=True)
    key_gain_out[...] = jnp.sum(gain_sum[1], axis=1, keepdims=True)
    for head in range(KVH):
        for index in range(3):
            sent(index, head).wait_send()


def back(query, d_out, logs, delta, pair, raw, key_raw, cosine, sine, query_gain, key_gain):
    mine = query.shape[2]
    inside = pl.BlockSpec(memory_space=pltpu.VMEM)
    dma = pltpu.SemaphoreType.DMA
    shape = jax.ShapeDtypeStruct
    columns = (QH + 2 * KVH) * HD // 4
    return pl.pallas_call(
        back_kernel,
        out_shape=[shape((4, columns, mine), BF), shape((HD, 1), F32), shape((HD, 1), F32)],
        in_specs=[inside] * 11,
        out_specs=[inside] * 3,
        scratch_shapes=[
            pltpu.VMEM((GROUP, HD), BF),
            pltpu.VMEM((GROUP, HD), BF),
            pltpu.VMEM((GROUP, HD), F32),
            pltpu.VMEM((GROUP, HD), F32),
            pltpu.VMEM((2 * HD, GROUP), BF),
            pltpu.VMEM((4, KVH, 2 * HD, mine), BF),
            pltpu.VMEM((3, KVH, 2 * HD, mine), BF),
            pltpu.VMEM((2, HD, mine), F32),
            dma((3, KVH)),
            dma((3, KVH)),
        ],
        compiler_params=pltpu.CompilerParams(
            collective_id=4, has_side_effects=True, vmem_limit_bytes=48 * 1024 * 1024
        ),
        name="attend_back",
    )(query, d_out, logs, delta, pair, raw, key_raw, cosine, sine, query_gain, key_gain)


def body(
    tokens,
    norm1_gain,
    w_query,
    w_key,
    w_value,
    query_gain,
    key_gain,
    w_out,
    norm2_gain,
    w_gate,
    w_up,
    w_down,
    teacher,
    positions,
    token_count,
):
    rows = lax.axis_size("row")
    cores = lax.axis_size("side")
    cols = lax.axis_size("group") * cores
    row_index = lax.axis_index("row")
    group_index = lax.axis_index("group")
    members = rows * cores
    member = row_index * cores + lax.axis_index("side")
    shard, width = tokens.shape
    pieces = 2 * members
    span = shard // pieces
    mine = shard // members * cores
    q_width, k_width = w_query.shape[1], w_key.shape[1]
    ff = w_gate.shape[1]

    def from_row(block, ahead):
        pairs = [((r + ahead) % rows, r) for r in range(rows)]
        return lax.ppermute(block, "row", pairs)

    def gather_rows(block, axis):
        parts = [block] + [from_row(block, ahead) for ahead in range(1, rows)]
        return jnp.concatenate(parts, axis=axis)

    def scatter_rows(block, axis):
        size = block.shape[axis] // rows
        total = lax.slice_in_dim(block, 0, size, axis=axis).astype(F32)
        for ahead in range(1, rows):
            part = lax.slice_in_dim(block, ahead * size, (ahead + 1) * size, axis=axis)
            total = total + from_row(part, rows - ahead).astype(F32)
        return total.astype(BF)

    def sum_planes(block, cuts):
        planes = lax.axis_size("dp")
        plane = lax.axis_index("dp")
        half = planes // 2
        edge = jnp.minimum(plane, planes - 1 - plane)
        done = []
        for part in jnp.split(block, cuts, axis=0):
            for step in range(half - 1):
                pairs = [(step, step + 1), (planes - 1 - step, planes - 2 - step)]
                come = lax.ppermute(part, "dp", pairs)
                part = (part.astype(F32) + come.astype(F32)).astype(BF)
            come = lax.ppermute(part, "dp", [(half - 1, half), (half, half - 1)])
            part = (part.astype(F32) + come.astype(F32)).astype(BF)
            for step in reversed(range(half - 1)):
                pairs = [(step + 1, step), (planes - 2 - step, planes - 1 - step)]
                come = lax.ppermute(part, "dp", pairs)
                part = jnp.where(edge == step, come, part)
            done.append(part)
        return jnp.concatenate(done, axis=0)

    def to_members(block):
        parts = block.reshape(pieces, span, width)
        parts = jnp.stack([parts[:members], parts[members:][::-1]], axis=1)
        moved = lax.all_to_all(parts, ("row", "side"), 0, 0, tiled=True)
        moved = jnp.roll(moved.reshape(rows, cores, 2 * span, width), -row_index, 0)
        moved = moved.transpose(1, 2, 0, 3)
        return moved.reshape(mine, rows * width)

    def from_members(block):
        parts = block.reshape(cores, 2, span, rows, width).transpose(3, 0, 1, 2, 4)
        parts = jnp.roll(parts, row_index, 0).reshape(members, 2, span, width)
        moved = lax.all_to_all(parts, ("row", "side"), 0, 0, tiled=True)
        moved = jnp.concatenate([moved[:, 0], moved[:, 1][::-1]], axis=0)
        return moved.reshape(shard, width)

    def pick(values):
        part = lax.dynamic_slice_in_dim(values.reshape(-1, cores, pieces, span), group_index, 1, 0)[0]
        low = lax.dynamic_slice_in_dim(part, member, 1, 1)
        high = lax.dynamic_slice_in_dim(part, pieces - 1 - member, 1, 1)
        return jnp.concatenate([low, high], axis=1).reshape(-1)

    first_tokens = (
        jnp.array([0, 0, shard, shard], jnp.int32)
        + jnp.stack([member, pieces - 1 - member] * 2).astype(jnp.int32) * span
    )

    half = HD // 2
    freq = jnp.exp(jnp.arange(half, dtype=F32) * (-2.0 * math.log(10000.0) / HD))
    angle = freq[:, None] * pick(positions).astype(F32)[None, :]
    cosine, sine = jnp.cos(angle), jnp.sin(angle)
    def dealt(full):
        lead, entry = full.shape[:-2], full.shape[-1]
        parts = full.reshape(lead + (cores, pieces, span, entry))
        low = parts[..., :members, :, :]
        high = parts[..., members:, :, :][..., ::-1, :, :]
        both = jnp.stack([low, high], axis=-3)
        both = jnp.moveaxis(both, -4, 0)
        return both.reshape((members,) + lead + (mine, entry))

    w_project = jnp.concatenate([w_query, w_key, w_value], axis=1)
    scale = 1.0 / math.sqrt(HD)
    fast = rows == 2 and cols == 4 and lax.axis_size("dp") % 2 == 0 and mine == 4 * span
    if fast:
        (
            states, normed_one, query_raw, query_use, key_sent, pair, mixed_f, logs, hidden,
            normed_two, w_project, w_out_all, gate_other, up_other, gains,
        ) = front(
            tokens, w_project, w_out, jnp.stack([norm1_gain, norm2_gain]), w_gate, w_up,
            cosine, sine, query_gain[:, None], key_gain[:, None],
        )
        states = states.astype(F32)
        inverse_one, inverse_two = rms(states), rms(hidden)
        gain_one, gain_two = gains[:, 0].reshape(D), gains[:, 1].reshape(D)
        mixed_f = mixed_f.reshape(KVH, REP, HD, mine)
        mixed = mixed_f.reshape(QH * HD, mine).astype(BF)
        w_project = w_project.reshape(cols, D, -1)
        ffn_weights = [w_gate, gate_other, w_up, up_other, w_down]
    else:
        states = to_members(tokens).astype(F32)
        gain_one = gather_rows(norm1_gain, 0)
        gain_two = gather_rows(norm2_gain, 0)
        w_project = gather_rows(w_project, 0)
        w_project = lax.all_gather(w_project, ("group", "side"), axis=0)
        w_out_all = gather_rows(w_out, 1)
        w_out_all = lax.all_gather(w_out_all, ("group", "side"), axis=0, tiled=True)
        def halves(block, axis):
            if rows == 2:
                return [block, from_row(block, 1)]
            return jnp.split(gather_rows(block, axis), 2, axis=axis)

        ffn_weights = halves(w_gate, 0) + halves(w_up, 0) + halves(w_down, 1)
        inverse_one = rms(states)
        normed_one = (states * inverse_one * gain_one).astype(BF)
        projected = dot(w_project, normed_one, ((1,), (1,)))
        query_raw = projected[:, :q_width].reshape(QH, HD, mine)
        key_sent = projected[:, q_width : q_width + k_width].reshape(KVH, HD, mine).astype(BF)
        value_sent = projected[:, q_width + k_width :].reshape(KVH, HD, mine).astype(BF)
        query_rot, query_back = jax.vjp(
            lambda raw, gain: prepare(raw, gain, cosine, sine), query_raw, query_gain
        )
        key_rot, key_back = jax.vjp(
            lambda raw, gain: prepare(raw, gain, cosine, sine), key_sent.astype(F32), key_gain
        )
        query_use = (query_rot.astype(BF) * BF(scale)).reshape(KVH, REP, HD, mine)
        pair = jnp.stack([key_rot.astype(BF), value_sent])
        pair = lax.all_gather(pair, ("row", "side"), axis=0)

        def natural(stacked):
            lead = stacked.shape[1:-1]
            parts = stacked.reshape((members,) + lead + (cores, 2, span))
            low, high = parts[..., 0, :], parts[..., 1, :]
            both = jnp.concatenate([low, high[::-1]], axis=0)
            return jnp.moveaxis(both, 0, -2).reshape(lead + (GROUP,))

        pair = natural(pair)
        key_t, value_t = pair[0], pair[1]
        key_n = key_t.transpose(0, 2, 1)
        value_one = jnp.concatenate([value_t, jnp.ones((KVH, 16, GROUP), BF)], axis=1)
        mixed_f, logs = attend(first_tokens, query_use, key_n, value_one)
        mixed = mixed_f.reshape(QH * HD, mine).astype(BF)
        hidden = states + dot(mixed, w_out_all, ((0,), (0,)))

        inverse_two = rms(hidden)
        normed_two = (hidden * inverse_two * gain_two).astype(BF)

    total_tokens = shard * cols * lax.axis_size("dp")
    loss_scale = total_tokens / token_count[0].astype(F32)
    if fast:
        normed_all, _, _, activated, _, d_low, d_gate_up, d_result, d_normed, block_out = feed(
            normed_two, ffn_weights, teacher, hidden, loss_scale[None]
        )
        d_result = d_result.reshape(mine, D)
    else:
        normed_all, gate, up, activated, ffn_out = spread(True, normed_two, ffn_weights)
        result = hidden + ffn_out.reshape(mine, D)
        d_result = loss_scale * (result - to_members(teacher).astype(F32))
        d_low, d_gate_up, d_normed = spread(False, d_result.astype(BF), ffn_weights, gate, up)
        block_out = from_members(result.astype(BF))
    d_normed = d_normed.reshape(mine, D)
    d_low, normed_all = d_low.reshape(-1, D), normed_all.reshape(-1, D)
    activated, d_gate_up = activated.reshape(-1, ff), d_gate_up.reshape(-1, 2 * ff)

    norm_two_part = jnp.sum(d_normed * hidden * inverse_two, axis=0)
    d_hidden = d_result + norm_back(hidden, inverse_two, gain_two, d_normed)
    d_hidden_low = d_hidden.astype(BF)
    grad_out = dot(mixed, d_hidden_low, ((1,), (0,))).astype(BF)
    d_mixed = dot(w_out_all, d_hidden_low, ((1,), (1,))).astype(BF)
    d_mixed = d_mixed.reshape(KVH, REP, HD, mine)
    delta = jnp.sum(d_mixed.astype(F32) * mixed_f, axis=2)
    if fast:
        d_projected, query_gain_part, key_gain_part = back(
            query_use, d_mixed.reshape(QH, HD, mine), logs, delta, pair, query_raw, key_sent,
            cosine, sine, query_gain[:, None], key_gain[:, None],
        )
        query_gain_part, key_gain_part = query_gain_part[:, 0], key_gain_part[:, 0]
    else:
        d_query, d_key_n, d_value_n = attend_back(
            first_tokens, query_use, d_mixed, logs, delta, key_t, value_t
        )
        d_pair = dealt(jnp.stack([d_key_n, d_value_n])).astype(BF)
        d_pair = lax.psum_scatter(d_pair, ("row", "side"), scatter_dimension=0, tiled=True)[0]
        d_pair = d_pair.astype(F32).transpose(0, 1, 3, 2)
        d_query_raw, query_gain_part = query_back(d_query.reshape(QH, HD, mine) * scale)
        d_key_raw, key_gain_part = key_back(d_pair[0])
        d_projected = jnp.concatenate(
            [
                d_query_raw.reshape(cols, q_width, mine),
                d_key_raw.reshape(cols, k_width, mine),
                d_pair[1].reshape(cols, k_width, mine),
            ],
            axis=1,
        ).astype(BF)
    d_normed_one = dot(d_projected, w_project, ((0, 1), (0, 2)))
    grad_input = d_hidden + norm_back(states, inverse_one, gain_one, d_normed_one)
    norm_one_part = jnp.sum(d_normed_one * states * inverse_one, axis=0)

    grad_project = lax.dot_general(
        d_projected, normed_one, (((2,), (0,)), ((), ())), preferred_element_type=F32
    )
    grad_project = grad_project.astype(BF)
    grad_out = grad_out.reshape(cols, q_width, D)
    norm_one_part = jnp.roll(norm_one_part.reshape(rows, width), row_index, 0).reshape(D)
    norm_two_part = jnp.roll(norm_two_part.reshape(rows, width), row_index, 0).reshape(D)
    small = jnp.concatenate([norm_one_part, norm_two_part, query_gain_part, key_gain_part])
    if fast and lax.axis_size("dp") == 4:
        padded = jnp.pad(small, (0, SMALL * 128 - small.shape[0])).reshape(SMALL, 128)
        grad_gate_up, grad_out, grad_project, grad_down, small, grad_input = reduce_all(
            4, normed_all, d_gate_up, activated, d_low, grad_out, grad_project, padded, grad_input.astype(BF)
        )
        grad_input = grad_input.astype(F32)
        small = small.reshape(-1)[: 2 * D + 2 * HD]
    else:
        grad_input = from_members(grad_input)
        small = lax.psum(small, ("dp", "row", "group", "side"))
        col_axes = ("group", "side")
        grad_project = lax.psum_scatter(grad_project, col_axes, scatter_dimension=0, tiled=True)
        grad_out = lax.psum_scatter(grad_out, col_axes, scatter_dimension=0, tiled=True)
        grad_down = dot(activated, d_low, ((0,), (0,))).astype(BF)
        grad_gate_up = dot(normed_all, d_gate_up, ((0,), (0,))).astype(BF)
        grad_down = sum_planes(scatter_rows(grad_down, 1), 2)
        grad_gate_up = sum_planes(scatter_rows(grad_gate_up, 0), 4)
        grad_out = sum_planes(scatter_rows(grad_out[0], 1), 1)
        grad_project = sum_planes(scatter_rows(grad_project[0], 1), 2)
    grad_norm1 = lax.dynamic_slice_in_dim(small, row_index * width, width, 0)
    grad_norm2 = lax.dynamic_slice_in_dim(small, D + row_index * width, width, 0)
    grad_project = grad_project.astype(F32).T
    return (
        block_out,
        grad_input,
        grad_norm1,
        grad_project[:, :q_width],
        grad_project[:, q_width : q_width + k_width],
        grad_project[:, q_width + k_width :],
        small[2 * D : 2 * D + HD],
        small[2 * D + HD :],
        grad_out.astype(F32),
        grad_norm2,
        grad_gate_up[:, :ff].astype(F32),
        grad_gate_up[:, ff:].astype(F32),
        grad_down.astype(F32),
    )


def solution(mesh):
    dp, row, col = mesh.shape["dp"], mesh.shape["row"], mesh.shape["col"]

    def call(*args):
        side = GROUP * dp * col // args[0].shape[0]
        fine = Mesh(
            mesh.devices.reshape(dp, row, col // side, side), ("dp", "row", "group", "side")
        )
        col_axes = ("group", "side")
        token_spec = P(("dp", "group", "side"), "row")
        wide = P("row", col_axes)
        tall = P(col_axes, "row")
        return jax.shard_map(
            body,
            mesh=fine,
            in_specs=(
                token_spec,
                P("row"),
                wide,
                wide,
                wide,
                P(),
                P(),
                tall,
                P("row"),
                wide,
                wide,
                tall,
                token_spec,
                P("dp"),
                P(),
            ),
            out_specs=(
                token_spec,
                token_spec,
                P("row"),
                wide,
                wide,
                wide,
                P(),
                P(),
                tall,
                P("row"),
                wide,
                wide,
                tall,
            ),
            check_vma=False,
        )(*args)

    return call
```

```python
import functools
import math

import jax
import jax.numpy as jnp
from jax import lax
from jax.experimental import pallas as pl
from jax.experimental.pallas import tpu as pltpu
from jax.sharding import Mesh
from jax.sharding import PartitionSpec as P

D = 2048
QH = 20
KVH = 5
HD = 64
PROMPT = 1024
CONT = 128
NCONT = 8
GROUP = PROMPT + NCONT * CONT
REP = QH // KVH
KEYS = 256

EPSILON = 1e-06
BF = jnp.bfloat16
F32 = jnp.float32


def dot(left, right, dims=((1,), (0,))):
    return lax.dot_general(left, right, (dims, ((), ())), preferred_element_type=F32)


def rms(values):
    return lax.rsqrt(jnp.mean(values * values, axis=1, keepdims=True) + EPSILON)


def norm_back(states, inverse, gain, d_normed):
    mean = jnp.mean(states * gain * d_normed, axis=1, keepdims=True)
    return inverse * gain * d_normed - states * inverse**3 * mean


def prepare(raw, gain, cosine, sine):
    values = raw * lax.rsqrt(jnp.mean(raw * raw, axis=1, keepdims=True) + EPSILON)
    values = values * gain[None, :, None]
    half = HD // 2
    first, second = values[:, :half], values[:, half:]
    return jnp.concatenate(
        [first * cosine - second * sine, second * cosine + first * sine], axis=1
    )


def allowed(first_query, first_key, span, rows):
    key = first_key + lax.broadcasted_iota(jnp.int32, (KEYS, rows), 0)
    query = first_query + lax.broadcasted_iota(jnp.int32, (KEYS, rows), 1) % span
    return (key <= query) & ((key < PROMPT) | (key // CONT == query // CONT))


def side_by_side(ref, index, span):
    return jnp.concatenate(
        [ref[0, head, :, index * span : (index + 1) * span] for head in range(REP)], axis=1
    )


def tiles_of(first_query):
    last = first_query // KEYS
    return jnp.minimum(last, PROMPT // KEYS), last


def attend_kernel(chunks, span, first_ref, query_ref, key_ref, value_ref, out_ref, log_ref):
    rows = REP * span
    for index in range(chunks):
        query = side_by_side(query_ref, index, span)
        first_query = first_ref[index]
        full, last = tiles_of(first_query)

        def tile(where, accum, masked):
            first_key = pl.multiple_of(where * KEYS, KEYS)
            scores = dot(key_ref[0, pl.ds(first_key, KEYS), :], query)
            expo = jnp.exp(scores)
            if masked:
                expo = jnp.where(allowed(first_query, first_key, span, rows), expo, 0.0)
            return accum + dot(value_ref[0, :, pl.ds(first_key, KEYS)], expo.astype(BF))

        accum = tile(last, jnp.zeros((value_ref.shape[1], rows), F32), True)
        accum = lax.fori_loop(0, full, lambda where, total: tile(where, total, False), accum)
        total = accum[HD : HD + 1]
        mixed = accum[:HD] / total
        logs = jnp.log(total)
        for head in range(REP):
            cut = slice(head * span, (head + 1) * span)
            out_ref[0, head, :, index * span : (index + 1) * span] = mixed[:, cut]
            log_ref[0, head : head + 1, index * span : (index + 1) * span] = logs[:, cut]


def attend_back_kernel(
    chunks,
    span,
    first_ref,
    query_ref,
    d_out_ref,
    log_ref,
    delta_ref,
    key_t_ref,
    value_t_ref,
    d_query_ref,
    d_key_ref,
    d_value_ref,
    key_ref,
    value_ref,
):
    rows = REP * span
    key_ref[...] = key_t_ref[0].T
    value_ref[...] = value_t_ref[0].T
    d_key_ref[...] = jnp.zeros_like(d_key_ref)
    d_value_ref[...] = jnp.zeros_like(d_value_ref)
    for index in range(chunks):
        query = side_by_side(query_ref, index, span)
        d_out = side_by_side(d_out_ref, index, span)
        query_t = query.T
        d_out_t = d_out.T
        cut = slice(index * span, (index + 1) * span)
        logs = jnp.concatenate([log_ref[0, h : h + 1, cut] for h in range(REP)], axis=1)
        delta = jnp.concatenate([delta_ref[0, h : h + 1, cut] for h in range(REP)], axis=1)
        first_query = first_ref[index]
        full, last = tiles_of(first_query)

        def tile(where, accum, masked):
            first_key = pl.multiple_of(where * KEYS, KEYS)
            here = pl.ds(first_key, KEYS)
            probs = jnp.exp(dot(key_ref[here, :], query) - logs)
            if masked:
                probs = jnp.where(allowed(first_query, first_key, span, rows), probs, 0.0)
            d_probs = dot(value_ref[here, :], d_out)
            d_scores = (probs * (d_probs - delta)).astype(BF)
            d_value_ref[0, here, :] += dot(probs.astype(BF), d_out_t)
            d_key_ref[0, here, :] += dot(d_scores, query_t)
            return accum + dot(key_t_ref[0, :, here], d_scores)

        accum = tile(last, jnp.zeros((HD, rows), F32), True)
        accum = lax.fori_loop(0, full, lambda where, total: tile(where, total, False), accum)
        for head in range(REP):
            part = accum[:, head * span : (head + 1) * span]
            d_query_ref[0, head, :, cut] = part


def per_head(shape):
    return pl.BlockSpec((1,) + shape, lambda head, first: (head,) + (0,) * len(shape))


def attend(first, query, key, value_t):
    tokens = query.shape[-1]
    chunks = first.shape[0]
    return pl.pallas_call(
        functools.partial(attend_kernel, chunks, tokens // chunks),
        out_shape=(
            jax.ShapeDtypeStruct((KVH, REP, HD, tokens), F32),
            jax.ShapeDtypeStruct((KVH, REP, tokens), F32),
        ),
        grid_spec=pltpu.PrefetchScalarGridSpec(
            num_scalar_prefetch=1,
            grid=(KVH,),
            in_specs=[
                per_head((REP, HD, tokens)),
                per_head((GROUP, HD)),
                per_head((value_t.shape[1], GROUP)),
            ],
            out_specs=[per_head((REP, HD, tokens)), per_head((REP, tokens))],
        ),
        compiler_params=pltpu.CompilerParams(vmem_limit_bytes=32 * 1024 * 1024),
        name="attend",
    )(first, query, key, value_t)


def attend_back(first, query, d_out, logs, delta, key_t, value_t):
    tokens = query.shape[-1]
    chunks = first.shape[0]
    return pl.pallas_call(
        functools.partial(attend_back_kernel, chunks, tokens // chunks),
        out_shape=(
            jax.ShapeDtypeStruct((KVH, REP, HD, tokens), F32),
            jax.ShapeDtypeStruct((KVH, GROUP, HD), F32),
            jax.ShapeDtypeStruct((KVH, GROUP, HD), F32),
        ),
        grid_spec=pltpu.PrefetchScalarGridSpec(
            num_scalar_prefetch=1,
            grid=(KVH,),
            in_specs=[
                per_head((REP, HD, tokens)),
                per_head((REP, HD, tokens)),
                per_head((REP, tokens)),
                per_head((REP, tokens)),
                per_head((HD, GROUP)),
                per_head((HD, GROUP)),
            ],
            out_specs=[
                per_head((REP, HD, tokens)),
                per_head((GROUP, HD)),
                per_head((GROUP, HD)),
            ],
            scratch_shapes=[pltpu.VMEM((GROUP, HD), BF), pltpu.VMEM((GROUP, HD), BF)],
        ),
        compiler_params=pltpu.CompilerParams(vmem_limit_bytes=32 * 1024 * 1024),
        name="attend_back",
    )(first, query, d_out, logs, delta, key_t, value_t)


AHEAD = 4
SLOTS = AHEAD + 2
FAR_LAG, WIDE_LAG, LAG = 1, 2, 4
SMALL = 40


class Part:
    def __init__(self, axis, rows, cols, count, base, col):
        self.axis, self.rows, self.cols = axis, rows, cols
        self.count, self.base, self.col = count, base, col

    def cut(self, ref, index, half, lead=()):
        first = pl.ds(index * self.rows, self.rows)
        if self.axis == 0:
            first = pl.ds((half * self.count + index) * self.rows, self.rows)
            return ref.at[(*lead, first, slice(None))]
        return ref.at[(*lead, first, pl.ds(half * self.cols, self.cols))]


def reduce_kernel(parts, planes, *refs):
    count = len(parts)
    refs = list(refs)

    def take(number):
        taken = refs[:number]
        del refs[:number]
        return taken

    col_parts = [j for j in range(count) if parts[j].col]
    normed_ref, d_gate_up_ref, act_ref, d_low_ref = take(4)
    grads = dict(zip(col_parts, take(len(col_parts))))
    (small_ref, mine_ref) = take(2)
    outs = take(count)
    (small_out, dealt_ref) = take(2)
    near, far, own = take(count), take(count), take(count)
    made = [j for j in range(count) if not parts[j].col]
    leaving = dict(zip(made, take(len(made))))
    mate_in = dict(zip(col_parts, take(len(col_parts))))
    far_in = dict(zip(col_parts, take(len(col_parts))))
    right, left, left_t, right_sem, left_sem, free_sem = take(6)
    out_sem, row_send, row_recv, in_send, far_recv, mid_send, wide_recv = take(7)
    col_own, col_send, col_recv, x_send, x_recv, small_local, small_send, small_recv = take(8)
    small_in, small_sum, deal_send, deal_recv, deal_local = take(5)
    plane, row = lax.axis_index("dp"), lax.axis_index("row")
    group, side = lax.axis_index("group"), lax.axis_index("side")
    other_row, mate, far_dev = {"row": 1 - row}, {"side": 1 - side}, {"group": 1 - group}
    cross = {"row": 1 - row, "side": 1 - side}
    at_end = (plane == 0) | (plane == planes - 1)
    low = plane < planes // 2
    end_next = {"dp": jnp.where(low, 1, planes - 2)}
    mid_outer = {"dp": jnp.where(low, 0, planes - 1)}
    mid_other = {"dp": jnp.where(low, planes // 2, planes // 2 - 1)}

    def remote(source, target, send, recv, where):
        return pltpu.make_async_remote_copy(
            source, target, send, recv, device_id=where, device_id_type=pl.DeviceIdType.MESH
        )

    barrier = pltpu.get_barrier_semaphore()

    def greet(where):
        pl.semaphore_signal(barrier, 1, device_id=where, device_id_type=pl.DeviceIdType.MESH)

    for where in (other_row, mate, far_dev, cross):
        greet(where)

    @pl.when(at_end)
    def _():
        greet(end_next)
        pl.semaphore_wait(barrier, 5)

    @pl.when(jnp.logical_not(at_end))
    def _():
        greet(mid_outer)
        greet(mid_other)
        pl.semaphore_wait(barrier, 6)

    def col_slot(j, half, index):
        before = sum(2 * parts[i].count for i in col_parts if i < j)
        return before + half * parts[j].count + index

    def col_own_copy(j, half, index, target):
        return pltpu.make_async_copy(
            parts[j].cut(grads[j], index, half, (2 * target + side,)),
            own[j].at[target, half, index],
            col_own.at[target, col_slot(j, half, index)],
        )

    def col_copy(j, half, index, target):
        slot = col_slot(j, half, index)
        return remote(
            parts[j].cut(grads[j], index, half, (2 * target + 1 - side,)),
            mate_in[j].at[target, half, index],
            col_send.at[target, slot],
            col_recv.at[target, slot],
            mate,
        )

    def x_copy(j, half, index):
        slot = col_slot(j, half, index)
        return remote(
            mate_in[j].at[1 - group, half, index],
            far_in[j].at[half, index],
            x_send.at[slot],
            x_recv.at[slot],
            far_dev,
        )

    def take_col(j, half, index):
        for target in range(2):
            col_own_copy(j, half, index, target).wait()
            col_copy(j, half, index, target).wait_recv()
            mate_in[j][target, half, index] = mate_in[j][target, half, index] + own[j][target, half, index]
        x_copy(j, half, index).start()

    def take_x(j, half, index):
        x_copy(j, half, index).wait_recv()
        far_in[j][half, index] = far_in[j][half, index] + mate_in[j][group, half, index]

    half_depth = normed_ref.shape[1] // 2
    gate_up, down = made
    units = parts[gate_up].count // 2

    def left_copies(unit, of_down):
        if of_down:
            source = act_ref.at[:, pl.ds(pl.multiple_of(unit * 256, 256), 256)]
            slot = (units + unit) % 2
            return [pltpu.make_async_copy(source, left.at[slot], left_sem.at[slot, 0])]
        slot = unit % 2
        copies = []
        for half in range(2):
            first = pl.multiple_of(half * half_depth + unit * 128, 128)
            target = left.at[slot, :, pl.ds(half * 128, 128)]
            copies.append(
                pltpu.make_async_copy(normed_ref.at[:, pl.ds(first, 128)], target, left_sem.at[slot, half])
            )
        return copies

    d_low_load = pltpu.make_async_copy(d_low_ref, right.at[:, pl.ds(0, d_low_ref.shape[1])], right_sem.at[1])
    d_gate_up_load = pltpu.make_async_copy(d_gate_up_ref, right, right_sem.at[0])

    def start_unit(j, unit):
        of_down = j == down
        part = parts[j]
        for copy in left_copies(unit, of_down):
            copy.wait()

        @pl.when(unit + 1 < part.count // 2)
        def _():
            for copy in left_copies(unit + 1, of_down):
                copy.start()

        if not of_down:
            @pl.when(unit + 1 == units)
            def _():
                for copy in left_copies(0, True):
                    copy.start()

        @pl.when(unit == 0)
        def _():
            (d_low_load if of_down else d_gate_up_load).wait()

        for chunk in range(2):
            index = 2 * unit + chunk

            @pl.when(index >= SLOTS)
            def _(index=index):
                row_copy(j, jnp.maximum(index - SLOTS, 0)).wait_send()

        slot = ((units + unit) if of_down else unit) % 2

        @pl.loop(0, left.shape[1] // 256)
        def _(block):
            here = pl.ds(pl.multiple_of(block * 256, 256), 256)
            left_t[:, here] = left[slot, here, :].T

    def tile(j, unit, number, targets):
        rows = parts[j].rows
        where = pl.ds(pl.multiple_of(number * 256, 256), 256)
        product = dot(left_t[...], right[:, where]).astype(BF)
        for place, (target, chunk, first_tile) in enumerate(targets):
            to = pl.ds(pl.multiple_of((number - first_tile) * 256, 256), 256)
            target[j][(2 * unit + chunk) % SLOTS, :, to] = product[place * rows : (place + 1) * rows]

    def make(j, unit, second):
        part = parts[j]
        if not second:
            start_unit(j, unit)
        if j == down:
            tiles = part.cols // 256
            first, target = (0, own) if second else (tiles, leaving)
            targets = [(target, 0, first), (target, 1, first)]
            pl.loop(first, first + tiles)(lambda number: tile(j, unit, number, targets))
        else:
            tiles = part.cols // 256
            targets = [(own, 0, 0), (own, 1, 0), (leaving, 0, 0), (leaving, 1, 0)]
            bounds = (tiles // 2, tiles) if second else (0, tiles // 2)
            pl.loop(*bounds)(lambda number: tile(j, unit, number, targets))
        if second and j != down:
            @pl.when(unit + 1 == units)
            def _():
                d_low_load.start()

        if second != (j == down):
            for chunk in range(2):
                row_copy(j, 2 * unit + chunk).start()

    def row_copy(j, index):
        slot = parts[j].base + index
        source = far_in[j].at[1, index] if parts[j].col else leaving[j].at[index % SLOTS]
        return remote(source, near[j].at[index], row_send.at[slot], row_recv.at[slot], other_row)

    def in_copy(j, index):
        slot = parts[j].base + index
        return remote(near[j].at[index], far[j].at[index], in_send.at[slot], far_recv.at[slot], end_next)

    def mid_copy(j, index):
        slot = parts[j].base + index
        return remote(far[j].at[index], near[j].at[index], mid_send.at[slot], wide_recv.at[slot], mid_other)

    def back_copy(j, index):
        slot = parts[j].base + index
        return remote(near[j].at[index], far[j].at[index], in_send.at[slot], far_recv.at[slot], mid_outer)

    def out_copy(j, index, source):
        slot = parts[j].base + index
        return pltpu.make_async_copy(source[j].at[index], parts[j].cut(outs[j], index, 0), out_sem.at[slot])

    def each(step, action):
        for j, part in enumerate(parts):
            index = step - part.base

            @pl.when((index >= 0) & (index < part.count))
            def _(j=j, index=index):
                action(j, index)

    def send_row(j, index):
        if parts[j].col:
            row_copy(j, index).start()
        else:
            @pl.when(index % 2 == 0)
            def _():
                make(j, index // 2, False)

            @pl.when(index % 2 == 1)
            def _():
                make(j, index // 2, True)

    def take_row(j, index):
        row_copy(j, index).wait_recv()
        mine = far_in[j][0, index] if parts[j].col else own[j][index % SLOTS]
        near[j][index] = near[j][index] + mine

        @pl.when(at_end)
        def _():
            in_copy(j, index).start()

    def take_far(j, index):
        back_copy(j, index).wait_recv()
        far[j][index] = far[j][index] + near[j][index]
        pl.semaphore_signal(free_sem, 1, device_id=mid_other, device_id_type=pl.DeviceIdType.MESH)
        pl.semaphore_wait(free_sem, 1)
        mid_copy(j, index).start()

    def take_wide(j, index):
        mid_copy(j, index).wait_recv()
        near[j][index] = near[j][index] + far[j][index]
        back_copy(j, index).start()
        out_copy(j, index, near).start()

    def take_back(j, index):
        in_copy(j, index).wait_recv()
        out_copy(j, index, far).start()

    def row_sent(j, index):
        @pl.when(jnp.logical_or(parts[j].col, index >= parts[j].count - SLOTS))
        def _():
            row_copy(j, index).wait_send()

    def finish_end(j, index):
        row_sent(j, index)
        in_copy(j, index).wait_send()
        out_copy(j, index, far).wait()

    def finish_mid(j, index):
        row_sent(j, index)
        mid_copy(j, index).wait_send()
        back_copy(j, index).wait_send()
        out_copy(j, index, near).wait()

    def small_copy(stage, source, where):
        return remote(small_sum.at[source], small_in.at[stage], small_send.at[stage], small_recv.at[stage], where)

    plane_hops = [small_copy(0, 0, mate), small_copy(1, 1, far_dev), small_copy(2, 2, other_row)]
    small_end = small_copy(3, 3, end_next)
    small_mid = small_copy(4, 4, mid_other)
    small_back = small_copy(3, 5, mid_outer)
    small_load = pltpu.make_async_copy(small_ref, small_sum.at[0], small_local.at[0])
    small_store = pltpu.make_async_copy(small_sum.at[5], small_out, small_local.at[1])

    span, width = mine_ref.shape[0] // 4, mine_ref.shape[1] // 2
    member = 2 * row + side
    dealt = []
    for index, (to_row, to_side, where) in enumerate(
        [(1 - row, side, other_row), (1 - row, 1 - side, cross), (row, 1 - side, mate), (row, side, None)]
    ):
        for high in range(2):
            piece = 7 - member if high else member
            first = pl.multiple_of(to_side * 2 * span + high * span, span)
            source = mine_ref.at[pl.ds(first, span), pl.ds((0 if index >= 2 else 1) * width, width)]
            target = dealt_ref.at[pl.ds(pl.multiple_of(piece * span, span), span), :]
            if where is None:
                dealt.append(pltpu.make_async_copy(source, target, deal_local.at[high]))
            else:
                dealt.append(remote(source, target, deal_send.at[index, high], deal_recv.at[index, high], where))

    total = sum(part.count for part in parts)
    for copy in left_copies(0, False):
        copy.start()
    d_gate_up_load.start()
    small_load.start()
    for copy in dealt[4:]:
        copy.start()
    for j in col_parts:
        for half in (1, 0):
            for index in range(parts[j].count):
                for target in range(2):
                    col_own_copy(j, half, index, target).start()
                    col_copy(j, half, index, target).start()

    @pl.loop(0, AHEAD)
    def _(step):
        each(step, send_row)

    pieces = [(j, half, index) for j in col_parts for half in (1, 0) for index in range(parts[j].count)]

    @pl.loop(0, total + LAG)
    def _(step):
        each(step + AHEAD, send_row)
        each(step, take_row)

        @pl.when(at_end)
        def _():
            each(step - LAG, take_back)

        @pl.when(jnp.logical_not(at_end))
        def _():
            each(step - FAR_LAG, take_far)
            each(step - WIDE_LAG, take_wide)

        @pl.when(step == total - AHEAD)
        def _():
            for copy in dealt[:4]:
                copy.start()

        for place, piece in enumerate(pieces):
            @pl.when(step == place + 1)
            def _(piece=piece):
                take_col(*piece)

            @pl.when(step == place + 5)
            def _(piece=piece):
                take_x(*piece)

        @pl.when(step == 0)
        def _():
            small_load.wait()
            plane_hops[0].start()

        for hop in range(3):
            @pl.when(step == hop + 1)
            def _(hop=hop):
                plane_hops[hop].wait_recv()
                small_sum[hop + 1] = small_sum[hop] + small_in[hop]
                if hop < 2:
                    plane_hops[hop + 1].start()

        @pl.when(at_end & (step == 3))
        def _():
            small_end.start()

        @pl.when(at_end & (step == 10))
        def _():
            small_end.wait_recv()
            small_sum[5] = small_in[3]
            small_store.start()

        @pl.when(jnp.logical_not(at_end) & (step == 5))
        def _():
            small_back.wait_recv()
            small_sum[4] = small_sum[3] + small_in[3]
            small_mid.start()

        @pl.when(jnp.logical_not(at_end) & (step == 7))
        def _():
            small_mid.wait_recv()
            small_sum[5] = small_sum[4] + small_in[4]
            small_back.start()
            small_store.start()

    for copy in plane_hops:
        copy.wait_send()
    small_store.wait()
    for copy in dealt:
        copy.wait()
    for j, half, index in pieces:
        for target in range(2):
            col_copy(j, half, index, target).wait_send()
        x_copy(j, half, index).wait_send()

    @pl.when(at_end)
    def _():
        small_end.wait_send()

        @pl.loop(0, total)
        def _(step):
            each(step, finish_end)

    @pl.when(jnp.logical_not(at_end))
    def _():
        small_mid.wait_send()
        small_back.wait_send()

        @pl.loop(0, total)
        def _(step):
            each(step, finish_mid)


def reduce_all(planes, normed, d_gate_up, act, d_low, grad_out, grad_project, small, mine):
    depth, width = normed.shape[1], act.shape[1]
    parts = [Part(0, 64, d_gate_up.shape[1], depth // 128, 0, False)]
    for rows, height, col in ((grad_out.shape[1] // 2, grad_out.shape[1], True),
                              (grad_project.shape[1] // 2, grad_project.shape[1], True), (128, width, False)):
        parts.append(Part(1, rows, depth // 2, height // rows, parts[-1].base + parts[-1].count, col))
    base = parts[-1].base + parts[-1].count
    shapes = [(part.count, part.rows, part.cols) for part in parts]
    col_shapes = [(2, *shape) for part, shape in zip(parts, shapes) if part.col]
    made_shapes = [(SLOTS, *shape[1:]) for part, shape in zip(parts, shapes) if not part.col]
    pieces = sum(shape[1] * 2 for shape in col_shapes)
    own_shapes = [
        (2, 2, *shape) if part.col else (SLOTS, *shape[1:]) for part, shape in zip(parts, shapes)
    ]
    anywhere = pl.BlockSpec(memory_space=pl.ANY)
    dma = pltpu.SemaphoreType.DMA
    tokens = normed.shape[0]
    inputs = (normed, d_gate_up, act, d_low, grad_out, grad_project, small, mine)
    return pl.pallas_call(
        functools.partial(reduce_kernel, parts, planes),
        out_shape=[jax.ShapeDtypeStruct((n * r, c), BF) for n, r, c in shapes]
        + [
            jax.ShapeDtypeStruct(small.shape, F32),
            jax.ShapeDtypeStruct((2 * mine.shape[0], mine.shape[1] // 2), BF),
        ],
        in_specs=[anywhere] * len(inputs),
        out_specs=[anywhere] * (len(parts) + 2),
        scratch_shapes=[pltpu.VMEM(shape, BF) for _ in range(2) for shape in shapes]
        + [pltpu.VMEM(shape, BF) for shape in own_shapes + made_shapes]
        + [pltpu.VMEM((2, *shape), BF) for shape in col_shapes]
        + [pltpu.VMEM(shape, BF) for shape in col_shapes]
        + [
            pltpu.VMEM((tokens, d_gate_up.shape[1]), BF),
            pltpu.VMEM((2, tokens, 256), BF),
            pltpu.VMEM((256, tokens), BF),
            dma((2,)),
            dma((2, 2)),
            pltpu.SemaphoreType.REGULAR,
        ]
        + [dma((base,)) for _ in range(7)]
        + [dma((2, pieces)), dma((2, pieces)), dma((2, pieces)), dma((pieces,)), dma((pieces,))]
        + [dma((2,)), dma((5,)), dma((5,))]
        + [pltpu.VMEM((5, *small.shape), F32), pltpu.VMEM((6, *small.shape), F32)]
        + [dma((3, 2)), dma((3, 2)), dma((2,))],
        compiler_params=pltpu.CompilerParams(
            collective_id=0, has_side_effects=True, vmem_limit_bytes=60 * 1024 * 1024
        ),
        name="reduce_grads",
    )(*inputs)


TILE = 256
STEPS = 8


def spread_kernel(forward, *refs):
    if forward:
        mine_ref, *weights = refs[:7]
        all_ref, gate_ref, up_ref, act_ref, out_ref = refs[7:12]
        rest = refs[12:]
    else:
        mine_ref, *weights = refs[:7]
        gate_ref, up_ref = refs[7:9]
        all_ref, d_gate_up_ref, out_ref = refs[9:12]
        rest = refs[12:]
    block, w_gate, w_up, w_down, kept, to_mate, from_mate, far_part, to_far, from_mate_far, far_sum, from_far = rest[:12]
    (
        weight_sem, block_sem, out_sem, mate_send, mate_recv, x_send, x_recv, pass_send, pass_recv,
        sum_send, sum_recv, part_send, part_recv, back_send, back_recv,
    ) = rest[12:27]
    stage = rest[27:]
    tokens, depth = mine_ref.shape
    quarter = tokens // 4
    width = w_gate.shape[1]
    group, side = lax.axis_index("group"), lax.axis_index("side")
    mate, far = {"side": 1 - side}, {"group": 1 - group}

    def remote(source, target, send, recv, where):
        return pltpu.make_async_remote_copy(
            source, target, send, recv, device_id=where, device_id_type=pl.DeviceIdType.MESH
        )

    barrier = pltpu.get_barrier_semaphore()
    for where in (mate, far):
        pl.semaphore_signal(barrier, 1, device_id=where, device_id_type=pl.DeviceIdType.MESH)

    half = depth // 2
    loads = []
    for index, (source, target) in enumerate(
        [
            (weights[0], w_gate.at[pl.ds(0, half), :]),
            (weights[1], w_gate.at[pl.ds(half, half), :]),
            (weights[2], w_up.at[pl.ds(0, half), :]),
            (weights[3], w_up.at[pl.ds(half, half), :]),
            (weights[4], w_down.at[:, pl.ds(0, half)]),
            (weights[5], w_down.at[:, pl.ds(half, half)]),
        ]
    ):
        loads.append(pltpu.make_async_copy(source, target, weight_sem.at[index]))
    order = loads if forward else loads[4:] + loads[:4]
    mine_copies = [
        pltpu.make_async_copy(
            mine_ref.at[pl.ds(i * 2 * quarter, 2 * quarter), :], block.at[i], block_sem.at[i]
        )
        for i in range(2)
    ]
    for copy in mine_copies:
        copy.start()
    for copy in order:
        copy.start()
    pl.semaphore_wait(barrier, 2)

    def piece(index):
        return mine_ref.at[pl.ds(index * quarter, quarter), :]

    def mate_copy(index):
        return remote(
            piece(index),
            block.at[2 + index // 2, pl.ds(index % 2 * quarter, quarter), :],
            mate_send.at[index],
            mate_recv.at[index],
            mate,
        )

    def x_copy(index):
        return remote(
            piece(index), block.at[4 + index, pl.ds(0, quarter), :], x_send.at[index], x_recv.at[index], far
        )

    def pass_copy(index):
        return remote(
            block.at[4 + index, pl.ds(0, quarter), :],
            block.at[4 + index, pl.ds(quarter, quarter), :],
            pass_send.at[index],
            pass_recv.at[index],
            mate,
        )

    def sum_copy(index):
        return remote(to_mate.at[index], from_mate.at[index], sum_send.at[index], sum_recv.at[index], mate)

    def part_copy(index):
        return remote(to_far.at[index], from_mate_far.at[index], part_send.at[index], part_recv.at[index], mate)

    def back_copy(index):
        return remote(far_sum.at[index], from_far.at[index], back_send.at[index], back_recv.at[index], far)

    x_copy(0).start()
    for index in range(4):
        mate_copy(index).start()
    x_copy(1).start()
    for copy in mine_copies:
        copy.wait()

    def emit(step, where, part):
        @pl.when(step < 2)
        def _():
            kept[jnp.minimum(step, 1), :, where] = part

        @pl.when((step >= 2) & (step < 4))
        def _():
            to_mate[jnp.clip(step - 2, 0, 1), :, where] = part.astype(BF)

        @pl.when(step >= 4)
        def _():
            far_part[jnp.maximum(step - 4, 0), :, where] = part[:quarter]
            to_far[jnp.maximum(step - 4, 0), :, where] = part[quarter:].astype(BF)

    def all_copy(step):
        return pltpu.make_async_copy(block.at[step], all_ref.at[step], out_sem.at[0, step])

    if forward:
        stage_gate, stage_up, stage_act = stage

        def saves(step):
            slot = step % 2
            return [
                pltpu.make_async_copy(stage_gate.at[slot], gate_ref.at[step], out_sem.at[1, step]),
                pltpu.make_async_copy(stage_up.at[slot], up_ref.at[step], out_sem.at[2, step]),
                pltpu.make_async_copy(stage_act.at[slot], act_ref.at[step], out_sem.at[3, step]),
            ]

        def fetches(step):
            return []

        def first_loads():
            for copy in loads[:4]:
                copy.wait()

        def second_loads():
            for copy in loads[4:]:
                copy.wait()

        def first_half(step):
            slot = step % 2

            @pl.loop(0, width // TILE)
            def _(tile):
                where = pl.ds(pl.multiple_of(tile * TILE, TILE), TILE)
                gate = dot(block[step], w_gate[:, where])
                up = dot(block[step], w_up[:, where])
                stage_gate[slot, :, where] = gate.astype(BF)
                stage_up[slot, :, where] = up.astype(BF)
                stage_act[slot, :, where] = (gate * up / (1.0 + jnp.exp(-gate))).astype(BF)

        def second_half(step):
            slot = step % 2

            @pl.loop(0, depth // TILE)
            def _(tile):
                where = pl.ds(pl.multiple_of(tile * TILE, TILE), TILE)
                emit(step, where, dot(stage_act[slot], w_down[:, where]))

    else:
        stage_gate, stage_up, stage_d, fetch_sem = stage

        def saves(step):
            return [
                pltpu.make_async_copy(stage_d.at[step % 2], d_gate_up_ref.at[step], out_sem.at[1, step])
            ]

        def fetches(step):
            slot = step % 2
            return [
                pltpu.make_async_copy(gate_ref.at[step], stage_gate.at[slot], fetch_sem.at[0, step]),
                pltpu.make_async_copy(up_ref.at[step], stage_up.at[slot], fetch_sem.at[1, step]),
            ]

        def first_loads():
            for copy in loads[4:]:
                copy.wait()

        def second_loads():
            for copy in loads[:4]:
                copy.wait()

        def first_half(step):
            slot = step % 2

            @pl.loop(0, width // TILE)
            def _(tile):
                first = pl.multiple_of(tile * TILE, TILE)
                where = pl.ds(first, TILE)
                d_act = dot(block[step], w_down[where, :], ((1,), (1,)))
                gate = stage_gate[slot, :, where].astype(F32)
                up = stage_up[slot, :, where].astype(F32)
                sig = 1.0 / (1.0 + jnp.exp(-gate))
                d_gate = d_act * up * sig * (1.0 + gate * (1.0 - sig))
                stage_d[slot, :, where] = d_gate.astype(BF)
                stage_d[slot, :, pl.ds(pl.multiple_of(width + first, TILE), TILE)] = (d_act * gate * sig).astype(BF)

        def second_half(step):
            slot = step % 2

            @pl.loop(0, depth // TILE)
            def _(tile):
                where = pl.ds(pl.multiple_of(tile * TILE, TILE), TILE)
                part = dot(stage_d[slot, :, :width], w_gate[where, :], ((1,), (1,)))
                part += dot(stage_d[slot, :, width:], w_up[where, :], ((1,), (1,)))
                emit(step, where, part)

    def finish_far(index):
        part_copy(index).wait_recv()
        total = far_part[index] + from_mate_far[index].astype(F32)
        far_sum[index] = total.astype(BF)
        back_copy(index).start()

    for copy in fetches(0):
        copy.start()

    @pl.loop(0, STEPS)
    def _(step):
        @pl.when((step == 2) | (step == 3))
        def _():
            index = jnp.clip(2 * (step - 2), 0, 2)
            mate_copy(index).wait_recv()
            mate_copy(index + 1).wait_recv()

        @pl.when(step >= 4)
        def _():
            index = jnp.maximum(step - 4, 0)
            x_copy(index).wait_recv()
            pass_copy(index).start()
            pass_copy(index).wait_recv()

        all_copy(step).start()
        for copy in fetches(step):
            copy.wait()

        if not forward:
            @pl.when(step < STEPS - 1)
            def _():
                for copy in fetches(jnp.minimum(step + 1, STEPS - 1)):
                    copy.start()

        @pl.when(step == 0)
        def _():
            first_loads()

        @pl.when(step >= 2)
        def _():
            for copy in saves(jnp.maximum(step - 2, 0)):
                copy.wait()

        first_half(step)

        @pl.when(step == 0)
        def _():
            second_loads()

        second_half(step)
        for copy in saves(step):
            copy.start()

        @pl.when((step == 1) | (step == 3))
        def _():
            x_copy(2 + step // 2).start()

        @pl.when((step >= 2) & (step < 4))
        def _():
            sum_copy(jnp.clip(step - 2, 0, 1)).start()

        @pl.when(step >= 4)
        def _():
            part_copy(jnp.maximum(step - 4, 0)).start()

        @pl.when(step >= 5)
        def _():
            finish_far(jnp.maximum(step - 5, 0))

    finish_far(3)
    for index in range(2):
        sum_copy(index).wait_recv()
        kept[index] = kept[index] + from_mate[index].astype(F32)
    results = []
    for index in range(4):
        back_copy(index).wait_recv()
        rows = pl.ds(index % 2 * quarter, quarter)
        kept[index // 2, rows, :] = kept[index // 2, rows, :] + from_far[index].astype(F32)
        if index % 2:
            copy = pltpu.make_async_copy(kept.at[index // 2], out_ref.at[index // 2], block_sem.at[index // 2])
            copy.start()
            results.append(copy)
    for copy in results:
        copy.wait()

    @pl.loop(0, STEPS)
    def _(step):
        all_copy(step).wait()

        @pl.when(step >= STEPS - 2)
        def _():
            for copy in saves(step):
                copy.wait()

        @pl.when(step < 4)
        def _():
            index = jnp.minimum(step, 3)
            mate_copy(index).wait_send()
            x_copy(index).wait_send()
            pass_copy(index).wait_send()
            part_copy(index).wait_send()
            back_copy(index).wait_send()

        @pl.when(step < 2)
        def _():
            sum_copy(jnp.minimum(step, 1)).wait_send()


def spread(forward, mine, weights, *kept):
    tokens, depth = mine.shape
    quarter, double = tokens // 4, tokens // 2
    width = weights[0].shape[1]
    anywhere = pl.BlockSpec(memory_space=pl.ANY)
    wide = jax.ShapeDtypeStruct((STEPS, double, width), BF)
    whole = jax.ShapeDtypeStruct((STEPS, double, depth), BF)
    out = jax.ShapeDtypeStruct((2, double, depth), F32)
    if forward:
        outs = [whole, wide, wide, wide, out]
        stage = [pltpu.VMEM((2, double, width), BF) for _ in range(3)]
    else:
        outs = [whole, jax.ShapeDtypeStruct((STEPS, double, 2 * width), BF), out]
        stage = [
            pltpu.VMEM((2, double, width), BF),
            pltpu.VMEM((2, double, width), BF),
            pltpu.VMEM((2, double, 2 * width), BF),
            pltpu.SemaphoreType.DMA((2, STEPS)),
        ]
    result = pl.pallas_call(
        functools.partial(spread_kernel, forward),
        out_shape=outs,
        in_specs=[anywhere] * (7 + len(kept)),
        out_specs=[anywhere] * len(outs),
        scratch_shapes=[
            pltpu.VMEM((STEPS, double, depth), BF),
            pltpu.VMEM((depth, width), BF),
            pltpu.VMEM((depth, width), BF),
            pltpu.VMEM((width, depth), BF),
            pltpu.VMEM((2, double, depth), F32),
            pltpu.VMEM((2, double, depth), BF),
            pltpu.VMEM((2, double, depth), BF),
            pltpu.VMEM((4, quarter, depth), F32),
            pltpu.VMEM((4, quarter, depth), BF),
            pltpu.VMEM((4, quarter, depth), BF),
            pltpu.VMEM((4, quarter, depth), BF),
            pltpu.VMEM((4, quarter, depth), BF),
            pltpu.SemaphoreType.DMA((6,)),
            pltpu.SemaphoreType.DMA((2,)),
            pltpu.SemaphoreType.DMA((4, STEPS)),
        ]
        + [pltpu.SemaphoreType.DMA((4,)) for _ in range(6)]
        + [pltpu.SemaphoreType.DMA((2,)) for _ in range(2)]
        + [pltpu.SemaphoreType.DMA((4,)) for _ in range(4)]
        + stage,
        compiler_params=pltpu.CompilerParams(
            collective_id=5 if forward else 2,
            has_side_effects=True,
            vmem_limit_bytes=60 * 1024 * 1024,
        ),
        name="spread" if forward else "spread_back",
    )(mine, *weights, *kept)
    return result


def feed_kernel(*refs):
    refs = list(refs)

    def take(number):
        taken = refs[:number]
        del refs[:number]
        return taken

    mine_ref, *weights = take(6)
    teacher_ref, hidden_ref, scale_ref = take(3)
    all_ref, gate_ref, up_ref, act_ref, target_ref = take(5)
    all_low_ref, d_gate_up_ref, d_result_ref, out_ref, block_out_ref = take(5)
    block, w_gate, w_up, w_down, kept, to_mate, from_mate, far_part, to_far, from_mate_far, far_sum, from_far = take(12)
    stage_gate, stage_up, stage_act = take(3)
    weight_sem, block_sem, out_sem, fetch_sem, result_sem = take(5)
    mate_send, mate_recv, x_send, x_recv, pass_send, pass_recv, sum_send, sum_recv = take(8)
    part_send, part_recv, back_send, back_recv = take(4)
    deal_send, deal_recv, deal_local, row_send, row_recv, plane_send, plane_recv = take(7)
    tokens, depth = mine_ref.shape
    quarter = tokens // 4
    width = w_gate.shape[1]
    half = depth // 2
    row = lax.axis_index("row")
    group, side = lax.axis_index("group"), lax.axis_index("side")
    mate, far = {"side": 1 - side}, {"group": 1 - group}
    other_row, cross = {"row": 1 - row}, {"row": 1 - row, "side": 1 - side}
    parity = lax.axis_index("dp") % 2
    next_plane = {"dp": lax.axis_index("dp") + 1 - 2 * parity}
    member = 2 * row + side

    def remote(source, target, send, recv, where):
        return pltpu.make_async_remote_copy(
            source, target, send, recv, device_id=where, device_id_type=pl.DeviceIdType.MESH
        )

    def local(source, target, sem):
        return pltpu.make_async_copy(source, target, sem)

    barrier = pltpu.get_barrier_semaphore()
    greeted = [mate, far, other_row, cross, next_plane]
    for where in greeted:
        pl.semaphore_signal(barrier, 1, device_id=where, device_id_type=pl.DeviceIdType.MESH)

    mine_copies = [
        local(mine_ref.at[pl.ds(i * 2 * quarter, 2 * quarter), :], block.at[i], block_sem.at[i]) for i in range(2)
    ]
    loads = [
        local(weights[0], w_gate.at[pl.ds(0, half), :], weight_sem.at[0]),
        local(weights[1], w_gate.at[pl.ds(half, half), :], weight_sem.at[1]),
        local(weights[2], w_up.at[pl.ds(0, half), :], weight_sem.at[2]),
        local(weights[3], w_up.at[pl.ds(half, half), :], weight_sem.at[3]),
        local(weights[4], w_down.at[:, pl.ds(0, half)], weight_sem.at[4]),
    ]
    for copy in mine_copies + loads:
        copy.start()

    down_chunks = []
    rows = width // 8
    for index in range(4):
        here = pl.ds(pl.multiple_of((4 * parity + index) * rows, 16), rows)
        place = w_down.at[here, pl.ds(half, half)]
        down_chunks.append(
            (
                remote(weights[4].at[here, :], place, row_send.at[index], row_recv.at[index], other_row),
                remote(place, place, plane_send.at[index], plane_recv.at[index], next_plane),
            )
        )

    def deals(outward):
        sent, own = [], []
        for index, (to_row, to_side, where) in enumerate(
            [(1 - row, side, other_row), (1 - row, 1 - side, cross), (row, 1 - side, mate), (row, side, None)]
        ):
            slot = 0 if index >= 2 else 1
            there = 2 * to_row + to_side if outward == 0 else member
            for high in range(2):
                piece = 7 - there if high else there
                whole = pl.ds(pl.multiple_of(piece * quarter, quarter), quarter), slice(None)
                columns = pl.ds(slot * half, half)
                if outward == 0:
                    first = pl.multiple_of(side * 2 * quarter + high * quarter, quarter)
                    source, target = teacher_ref.at[whole], target_ref.at[pl.ds(first, quarter), columns]
                else:
                    source = to_mate.at[to_side, pl.ds(high * quarter, quarter), columns]
                    target = block_out_ref.at[whole]
                if where is None:
                    own.append(local(source, target, deal_local.at[outward, high]))
                else:
                    sems = deal_send.at[outward, index, high], deal_recv.at[outward, index, high]
                    sent.append(remote(source, target, *sems, where))
        return sent, own

    teacher_sent, teacher_own = deals(0)
    result_sent, result_own = deals(1)

    def piece(phase, index):
        if phase == 0:
            return mine_ref.at[pl.ds(index * quarter, quarter), :]
        return block.at[index // 2, pl.ds(index % 2 * quarter, quarter), :]

    def mate_copy(phase, index):
        target = block.at[2 + index // 2, pl.ds(index % 2 * quarter, quarter), :]
        return remote(piece(phase, index), target, mate_send.at[phase, index], mate_recv.at[phase, index], mate)

    def x_copy(phase, index):
        target = block.at[4 + index, pl.ds(0, quarter), :]
        return remote(piece(phase, index), target, x_send.at[phase, index], x_recv.at[phase, index], far)

    def pass_copy(phase, index):
        return remote(
            block.at[4 + index, pl.ds(0, quarter), :],
            block.at[4 + index, pl.ds(quarter, quarter), :],
            pass_send.at[phase, index],
            pass_recv.at[phase, index],
            mate,
        )

    def sum_copy(phase, index):
        return remote(
            to_mate.at[index], from_mate.at[index], sum_send.at[phase, index], sum_recv.at[phase, index], mate
        )

    def part_copy(phase, index):
        return remote(
            to_far.at[index], from_mate_far.at[index], part_send.at[phase, index], part_recv.at[phase, index], mate
        )

    def back_copy(phase, index):
        return remote(
            far_sum.at[index], from_far.at[index], back_send.at[phase, index], back_recv.at[phase, index], far
        )

    def all_copy(phase, step):
        return local(block.at[step], (all_ref, all_low_ref)[phase].at[step], out_sem.at[4 * phase, step])

    def saves(step):
        return [
            local(stage_gate.at[step % 2], gate_ref.at[step], out_sem.at[1, step]),
            local(stage_up.at[step % 2], up_ref.at[step], out_sem.at[2, step]),
            local(stage_act.at[step], act_ref.at[step], out_sem.at[3, step]),
        ]

    def back_saves(step):
        slot = 2 * (step % 2)
        return [
            local(stage_act.at[slot + i], d_gate_up_ref.at[step, :, pl.ds(i * width, width)], out_sem.at[5 + i, step])
            for i in range(2)
        ]

    def fetches(step):
        return [
            local(gate_ref.at[step], stage_gate.at[step % 2], fetch_sem.at[0, step]),
            local(up_ref.at[step], stage_up.at[step % 2], fetch_sem.at[1, step]),
        ]

    def emit(step, where, part):
        @pl.when(step < 2)
        def _():
            kept[jnp.minimum(step, 1), :, where] = part

        @pl.when((step >= 2) & (step < 4))
        def _():
            to_mate[jnp.clip(step - 2, 0, 1), :, where] = part.astype(BF)

        @pl.when(step >= 4)
        def _():
            far_part[jnp.maximum(step - 4, 0), :, where] = part[:quarter]
            to_far[jnp.maximum(step - 4, 0), :, where] = part[quarter:].astype(BF)

    def tiles(first, last, action):
        @pl.loop(first, last)
        def _(tile):
            action(pl.ds(pl.multiple_of(tile * TILE, TILE), TILE), pl.multiple_of(tile * TILE, TILE))

    def multiply_in(step):
        slot = step % 2

        def action(where, first):
            gate = dot(block[step], w_gate[:, where])
            up = dot(block[step], w_up[:, where])
            stage_gate[slot, :, where] = gate.astype(BF)
            stage_up[slot, :, where] = up.astype(BF)
            stage_act[step, :, where] = (gate * up / (1.0 + jnp.exp(-gate))).astype(BF)

        tiles(0, width // TILE, action)

    def multiply_out(step, first=0, last=depth // TILE):
        tiles(first, last, lambda where, _: emit(step, where, dot(stage_act[step], w_down[:, where])))

    def multiply_back_in(step):
        slot = step % 2

        def action(where, first):
            d_act = dot(block[step], w_down[where, :], ((1,), (1,)))
            gate = stage_gate[slot, :, where].astype(F32)
            up = stage_up[slot, :, where].astype(F32)
            sig = 1.0 / (1.0 + jnp.exp(-gate))
            d_gate = d_act * up * sig * (1.0 + gate * (1.0 - sig))
            stage_act[2 * slot, :, where] = d_gate.astype(BF)
            stage_act[2 * slot + 1, :, where] = (d_act * gate * sig).astype(BF)

        tiles(0, width // TILE, action)

    def multiply_back_out(step):
        slot = 2 * (step % 2)

        def action(where, first):
            part = dot(stage_act[slot], w_gate[where, :], ((1,), (1,)))
            part += dot(stage_act[slot + 1], w_up[where, :], ((1,), (1,)))
            emit(step, where, part)

        tiles(0, depth // TILE, action)

    def finish_far(phase, index):
        part_copy(phase, index).wait_recv()
        total = far_part[index] + from_mate_far[index].astype(F32)
        far_sum[index] = total.astype(BF)
        if phase == 0:
            all_copy(0, 4 + index).wait()
            pass_copy(0, index).wait_send()
        back_copy(phase, index).start()

    def arrive(phase, step):
        @pl.when((step == 2) | (step == 3))
        def _():
            index = jnp.clip(2 * (step - 2), 0, 2)
            mate_copy(phase, index).wait_recv()
            mate_copy(phase, index + 1).wait_recv()

        @pl.when(step >= 4)
        def _():
            index = jnp.maximum(step - 4, 0)
            x_copy(phase, index).wait_recv()
            pass_copy(phase, index).start()
            pass_copy(phase, index).wait_recv()

        all_copy(phase, step).start()

    pl.semaphore_wait(barrier, len(greeted))
    for over_row, _ in down_chunks:
        over_row.start()
    x_copy(0, 0).start()
    for index in range(4):
        mate_copy(0, index).start()
    x_copy(0, 1).start()
    for copy in teacher_sent + teacher_own:
        copy.start()
    for copy in mine_copies:
        copy.wait()

    @pl.loop(0, STEPS)
    def _(step):
        @pl.when(step == 7)
        def _():
            finish_far(0, 2)

        arrive(0, step)

        @pl.when(step == 0)
        def _():
            for copy in loads:
                copy.wait()

        @pl.when(step >= 2)
        def _():
            for copy in saves(jnp.maximum(step - 2, 0)):
                copy.wait()

        multiply_in(step)

        @pl.when(step < 6)
        def _():
            multiply_out(step, 0, half // TILE)

        for index in range(4):
            @pl.when(step == index + 1)
            def _(index=index):
                down_chunks[index][0].wait_recv()
                down_chunks[index][1].start()

        @pl.when(step == 5)
        def _():
            for _, over_planes in down_chunks:
                over_planes.wait_recv()
            pl.loop(4, 6)(lambda early: multiply_out(early, half // TILE))
            part_copy(0, 0).start()
            part_copy(0, 1).start()
            pl.loop(2, 4)(lambda early: multiply_out(early, half // TILE))
            for index in range(2):
                all_copy(0, 2 + index).wait()
                sum_copy(0, index).start()
            finish_far(0, 0)
            finish_far(0, 1)
            pl.loop(0, 2)(lambda early: multiply_out(early, half // TILE))

        @pl.when(step >= 6)
        def _():
            multiply_out(step)
            part_copy(0, jnp.maximum(step - 4, 0)).start()

        for copy in saves(step):
            copy.start()

        @pl.when((step == 1) | (step == 3))
        def _():
            x_copy(0, 2 + step // 2).start()

    for copy in teacher_own:
        copy.wait()
    for copy in teacher_sent:
        copy.wait_recv()
    result_loads = []
    for index in range(4):
        if index == 3:
            finish_far(0, 3)
        part_copy(0, index).wait_send()
        here = pl.ds(index * quarter, quarter)
        result_loads.append(
            [
                local(target_ref.at[here, :], to_far.at[index], result_sem.at[0, index]),
                local(hidden_ref.at[here, :], far_part.at[index], result_sem.at[1, index]),
            ]
        )
        for copy in result_loads[-1]:
            copy.start()
    for index in range(2):
        all_copy(0, index).wait()
        sum_copy(0, index).wait()
    for step in (STEPS - 2, STEPS - 1):
        for copy in saves(step):
            copy.wait()
    for copy in fetches(0):
        copy.start()
    scale = scale_ref[0]
    d_result_saves = []
    for index in range(4):
        back_copy(0, index).wait_recv()
        for copy in result_loads[index]:
            copy.wait()
        here = pl.ds(index % 2 * quarter, quarter)

        def action(where, first):
            total = kept[index // 2, here, where] + from_mate[index // 2, here, where].astype(F32)
            total = total + from_far[index, :, where].astype(F32)
            result = far_part[index, :, where] + total
            d_result = scale * (result - to_far[index, :, where].astype(F32))
            to_mate[index // 2, here, where] = result.astype(BF)
            kept[index // 2, here, where] = d_result
            block[index // 2, here, where] = d_result.astype(BF)

        tiles(0, depth // TILE, action)
        x_copy(1, index).start()
        mate_copy(1, index).start()
        if index % 2:
            copy = local(kept.at[index // 2], d_result_ref.at[index // 2], block_sem.at[index // 2])
            copy.start()
            d_result_saves.append(copy)
    for copy in result_sent + result_own:
        copy.start()
    for index in range(4):
        mate_copy(0, index).wait_send()
        x_copy(0, index).wait_send()
        back_copy(0, index).wait_send()

    @pl.loop(0, STEPS)
    def _(step):
        @pl.when(step >= 5)
        def _():
            finish_far(1, jnp.maximum(step - 5, 0))

        arrive(1, step)
        for copy in fetches(step):
            copy.wait()

        @pl.when(step < STEPS - 1)
        def _():
            for copy in fetches(jnp.minimum(step + 1, STEPS - 1)):
                copy.start()

        @pl.when(step >= 2)
        def _():
            for copy in back_saves(jnp.maximum(step - 2, 0)):
                copy.wait()

        multiply_back_in(step)

        @pl.when(step == 0)
        def _():
            for copy in d_result_saves:
                copy.wait()

        @pl.when(step == 2)
        def _():
            for copy in result_own:
                copy.wait()
            for copy in result_sent:
                copy.wait_send()

        multiply_back_out(step)
        for copy in back_saves(step):
            copy.start()

        @pl.when((step >= 2) & (step < 4))
        def _():
            sum_copy(1, jnp.clip(step - 2, 0, 1)).start()

        @pl.when(step >= 4)
        def _():
            part_copy(1, jnp.maximum(step - 4, 0)).start()

    finish_far(1, 3)
    for index in range(2):
        sum_copy(1, index).wait_recv()
        kept[index] = kept[index] + from_mate[index].astype(F32)
    results = []
    for index in range(4):
        back_copy(1, index).wait_recv()
        here = pl.ds(index % 2 * quarter, quarter)
        kept[index // 2, here, :] = kept[index // 2, here, :] + from_far[index].astype(F32)
        if index % 2:
            results.append(local(kept.at[index // 2], out_ref.at[index // 2], block_sem.at[index // 2]))
            results[-1].start()
    for copy in results:
        copy.wait()
    for copy in result_sent:
        copy.wait_recv()
    for copy in teacher_sent:
        copy.wait_send()
    for over_row, over_planes in down_chunks:
        over_row.wait_send()
        over_planes.wait_send()

    @pl.loop(0, STEPS)
    def _(step):
        all_copy(1, step).wait()

        @pl.when(step >= STEPS - 2)
        def _():
            for copy in back_saves(step):
                copy.wait()

        @pl.when(step < 4)
        def _():
            index = jnp.minimum(step, 3)
            for copy in (mate_copy, x_copy, pass_copy, part_copy, back_copy):
                copy(1, index).wait_send()

        @pl.when(step < 2)
        def _():
            sum_copy(1, jnp.minimum(step, 1)).wait_send()


def feed(mine, weights, teacher, hidden, scale):
    tokens, depth = mine.shape
    quarter, double = tokens // 4, tokens // 2
    width = weights[0].shape[1]
    anywhere = pl.BlockSpec(memory_space=pl.ANY)
    shape = jax.ShapeDtypeStruct
    wide, whole = shape((STEPS, double, width), BF), shape((STEPS, double, depth), BF)
    own = shape((2, double, depth), F32)
    outs = [
        whole, wide, wide, wide, shape((tokens, depth), BF),
        whole, shape((STEPS, double, 2 * width), BF), own, own, shape((2 * tokens, depth // 2), BF),
    ]
    dma = pltpu.SemaphoreType.DMA
    return pl.pallas_call(
        feed_kernel,
        out_shape=outs,
        in_specs=[anywhere] * 8 + [pl.BlockSpec(memory_space=pltpu.SMEM)],
        out_specs=[anywhere] * len(outs),
        scratch_shapes=[
            pltpu.VMEM((STEPS, double, depth), BF),
            pltpu.VMEM((depth, width), BF),
            pltpu.VMEM((depth, width), BF),
            pltpu.VMEM((width, depth), BF),
            pltpu.VMEM((2, double, depth), F32),
            pltpu.VMEM((2, double, depth), BF),
            pltpu.VMEM((2, double, depth), BF),
            pltpu.VMEM((4, quarter, depth), F32),
            pltpu.VMEM((4, quarter, depth), BF),
            pltpu.VMEM((4, quarter, depth), BF),
            pltpu.VMEM((4, quarter, depth), BF),
            pltpu.VMEM((4, quarter, depth), BF),
            pltpu.VMEM((2, double, width), BF),
            pltpu.VMEM((2, double, width), BF),
            pltpu.VMEM((STEPS, double, width), BF),
            dma((5,)), dma((2,)), dma((7, STEPS)), dma((2, STEPS)), dma((2, 4)),
            dma((2, 4)), dma((2, 4)), dma((2, 4)), dma((2, 4)), dma((2, 4)), dma((2, 4)), dma((2, 2)), dma((2, 2)),
            dma((2, 4)), dma((2, 4)), dma((2, 4)), dma((2, 4)),
            dma((2, 3, 2)), dma((2, 3, 2)), dma((2, 2)), dma((4,)), dma((4,)), dma((4,)), dma((4,)),
        ],
        compiler_params=pltpu.CompilerParams(
            collective_id=1, has_side_effects=True, vmem_limit_bytes=60 * 1024 * 1024
        ),
        name="feed_forward",
    )(mine, *weights, teacher, hidden, scale)


def front_kernel(*refs):
    refs = list(refs)

    def take(number):
        taken = refs[:number]
        del refs[:number]
        return taken

    tokens_ref, w_project_ref, w_out_ref, gains_ref, gate_ref, up_ref = take(6)
    cos_ref, sin_ref, query_gain_ref, key_gain_ref = take(4)
    (
        states_out, normed_out, raw_out, query_out, key_out, pair_out, mixed_out, logs_out, hidden_out, normed_two_out,
        w_project_out, w_out_out, gate_out, up_out, gains_out,
    ) = take(15)
    states, normed, w_project, raw, key_raw, query, pair_own, pair, key_n, mixed_t, logs, mixed = take(12)
    w_out, hidden, gains = take(3)
    token_send, token_recv, token_local = take(3)
    project_send, project_recv, out_send, out_recv, gain_send, gain_recv = take(6)
    pair_send, pair_recv, row_send, row_recv, plane_send, plane_recv, local, store = take(8)

    plane, row = lax.axis_index("dp"), lax.axis_index("row")
    group, side = lax.axis_index("group"), lax.axis_index("side")
    other_row, mate, far = {"row": 1 - row}, {"side": 1 - side}, {"group": 1 - group}
    cross = {"row": 1 - row, "side": 1 - side}
    parity = plane % 2
    next_plane = {"dp": plane + 1 - 2 * parity}
    shard, width = tokens_ref.shape
    mine, depth = states.shape
    pieces = 8
    span = shard // pieces
    member = 2 * row + side
    kv_rows = key_raw.shape[0]

    def remote(source, target, send, recv, where):
        return pltpu.make_async_remote_copy(
            source, target, send, recv, device_id=where, device_id_type=pl.DeviceIdType.MESH
        )

    barrier = pltpu.get_barrier_semaphore()
    for where in (other_row, mate, far, cross, next_plane):
        pl.semaphore_signal(barrier, 1, device_id=where, device_id_type=pl.DeviceIdType.MESH)

    def token_copies(to_row, to_side, index, where):
        target_member = 2 * to_row + to_side
        slot = 1 if to_row is not row else 0
        copies = []
        for high in range(2):
            piece = pieces - 1 - target_member if high else target_member
            source = tokens_ref.at[pl.ds(pl.multiple_of(piece * span, span), span), :]
            first = pl.multiple_of(side * 2 * span + high * span, span)
            target = states.at[pl.ds(first, span), pl.ds(slot * width, width)]
            if where is None:
                copies.append(pltpu.make_async_copy(source, target, token_local.at[high]))
            else:
                sems = token_send.at[index, high], token_recv.at[index, high]
                copies.append(remote(source, target, *sems, where))
        return copies

    own_tokens = token_copies(row, side, 0, None)
    other = 1 - row
    sent_tokens = token_copies(other, side, 0, other_row)
    sent_tokens += token_copies(other, 1 - side, 1, cross)
    sent_tokens += token_copies(row, 1 - side, 2, mate)

    me, far_col = 2 * group + side, 2 * (1 - group) + side

    class Spread:
        def __init__(self, source, place, send, recv):
            self.copies = []

            def add(origin, target, where):
                index = len(self.copies)
                self.copies.append(remote(origin, target, send.at[index], recv.at[index], where))
                return self.copies[-1]

            here, there = parity, 1 - parity
            rows = source.shape[0] // 2
            first_half = source.at[pl.ds(pl.multiple_of(here * rows, 16), rows), :]
            self.to_row = add(first_half, place(me, 1, here), other_row)
            self.to_plane = add(place(me, 1, here), place(me, 1, here), next_plane)
            self.to_far = [add(source, place(me, 0, None), far)]
            self.to_far += [add(place(me, 1, half), place(me, 1, half), far) for half in (here, there)]
            self.to_mate = [add(source, place(me, 0, None), mate)]
            self.to_mate += [add(place(me, 1, half), place(me, 1, half), mate) for half in (here, there)]
            self.to_mate += [add(place(far_col, 0, None), place(far_col, 0, None), mate)]
            self.to_mate += [
                add(place(far_col, 1, half), place(far_col, 1, half), mate) for half in (here, there)
            ]

        def first(self):
            self.to_row.start()
            self.to_far[0].start()
            self.to_mate[0].start()

        def row_in(self):
            self.to_row.wait_recv()
            for copy in (self.to_plane, self.to_far[1], self.to_mate[1]):
                copy.start()

        def plane_in(self):
            self.to_plane.wait_recv()
            self.to_far[2].start()
            self.to_mate[2].start()

        def far_in(self, index):
            self.to_far[index].wait_recv()
            self.to_mate[3 + index].start()

        def mate_in(self, first, last):
            for copy in self.to_mate[first:last]:
                copy.wait_recv()

        def sent(self):
            for copy in self.copies:
                copy.wait_send()

    q_width = w_out_ref.shape[0]

    def project_place(col, slot, half):
        if half is None:
            return w_project.at[col, slot]
        return w_project.at[col, slot, pl.ds(pl.multiple_of(half * (width // 2), 16), width // 2), :]

    def out_place(col, slot, half):
        first, rows = col * q_width, q_width
        if half is not None:
            rows = q_width // 2
            first = first + half * rows
        return w_out.at[pl.ds(pl.multiple_of(first, 16), rows), pl.ds(slot * width, width)]

    project = Spread(w_project_ref, project_place, project_send, project_recv)
    output = Spread(w_out_ref, out_place, out_send, out_recv)
    own_project = pltpu.make_async_copy(w_project_ref, w_project.at[me, 0], local.at[0])
    own_output = pltpu.make_async_copy(w_out_ref, out_place(me, 0, None), local.at[1])
    own_gains = pltpu.make_async_copy(gains_ref, gains.at[0], local.at[2])
    sent_gains = remote(gains_ref, gains.at[1], gain_send.at[0], gain_recv.at[0], other_row)

    chunks = []
    for index, (source, target) in enumerate([(gate_ref, gate_out), (up_ref, up_out)]):
        rows = source.shape[0] // 4
        for part in range(2):
            here = pl.ds(pl.multiple_of((2 * parity + part) * rows, 64), rows)
            slot = 2 * index + part
            over_row = remote(source.at[here, :], target.at[here, :], row_send.at[slot], row_recv.at[slot], other_row)
            over_planes = remote(
                target.at[here, :], target.at[here, :], plane_send.at[slot], plane_recv.at[slot], next_plane
            )
            chunks.append((over_row, over_planes))

    def pass_on(index):
        chunks[index][0].wait_recv()
        chunks[index][1].start()

    own_copies = [own_gains, *own_tokens, own_project, own_output]
    for copy in own_copies:
        copy.start()
    pl.semaphore_wait(barrier, 5)
    sent_gains.start()
    project.first()
    for copy in sent_tokens:
        copy.start()
    chunks[0][0].start()
    for copy in own_copies:
        copy.wait()
    sent_gains.wait_recv()
    project.row_in()
    for copy in sent_tokens:
        copy.wait_recv()

    stores = []

    def save(source, target):
        copy = pltpu.make_async_copy(source, target, store.at[len(stores)])
        copy.start()
        stores.append(copy)
        return copy

    block = mine // 4

    @pl.loop(0, 4)
    def _(index):
        here = pl.ds(pl.multiple_of(index * block, block), block)
        values = states[here, :].astype(F32)
        inverse = lax.rsqrt(jnp.mean(values * values, axis=1, keepdims=True) + EPSILON)
        for slot in range(2):
            part = values[:, slot * width : (slot + 1) * width] * inverse
            normed[here, slot * width : (slot + 1) * width] = (part * gains[slot, 0:1, :]).astype(BF)

    save(states, states_out)
    normed_saved = save(normed, normed_out)
    save(gains, gains_out)

    def project_col(col):
        part = dot(normed[:, :width], w_project[col, 0]) + dot(normed[:, width:], w_project[col, 1])
        part = part.T
        heads = q_width // HD
        for head in range(heads):
            raw[col * heads + head] = part[head * HD : (head + 1) * HD]
        k_width = kv_rows // 4
        first = pl.multiple_of(col * k_width, 16)
        key_raw[pl.ds(first, k_width), :] = part[q_width : q_width + k_width].astype(BF)
        first = pl.multiple_of(kv_rows + col * k_width, 16)
        pair_own[pl.ds(first, k_width), :] = part[q_width + k_width :].astype(BF)

    project.plane_in()
    project.far_in(0)
    output.to_row.start()
    project_col(me)
    project.mate_in(0, 3)
    project_col(2 * group + 1 - side)
    project.far_in(1)
    project.far_in(2)
    project_col(far_col)
    project.mate_in(3, 6)
    project_col(2 * (1 - group) + 1 - side)
    save(raw, raw_out)
    save(key_raw, key_out)
    save(w_project, w_project_out)

    cosine, sine = cos_ref[...], sin_ref[...]

    def turned(values, gain):
        values = values * lax.rsqrt(jnp.mean(values * values, axis=0, keepdims=True) + EPSILON) * gain
        first, second = values[: HD // 2], values[HD // 2 :]
        return jnp.concatenate([first * cosine - second * sine, second * cosine + first * sine], axis=0)

    for head in range(kv_rows // HD):
        cut = slice(head * HD, (head + 1) * HD)
        pair_own[cut, :] = turned(key_raw[cut, :].astype(F32), key_gain_ref[...]).astype(BF)

    def places(who):
        starts = [who, pieces - 1 - who, pieces + who, 2 * pieces - 1 - who]
        return [pair.at[:, pl.ds(pl.multiple_of(start * span, span), span)] for start in starts]

    for index, place in enumerate(places(member)):
        place[...] = pair_own[:, index * span : (index + 1) * span]
    to_mate, to_row, passed = [], [], []
    for index, place in enumerate(places(member)):
        to_row.append(remote(place, place, pair_send.at[0, index], pair_recv.at[0, index], other_row))
        to_mate.append(remote(place, place, pair_send.at[1, index], pair_recv.at[1, index], mate))
    for index, place in enumerate(places(2 * (1 - row) + side)):
        passed.append(remote(place, place, pair_send.at[2, index], pair_recv.at[2, index], mate))
    for copy in to_row + to_mate:
        copy.start()
    output.to_far[0].start()
    output.to_mate[0].start()
    chunks[1][0].start()

    @pl.loop(0, raw.shape[0])
    def _(head):
        values = turned(raw[head], query_gain_ref[...]).astype(BF)
        query[head] = values * BF(1.0 / math.sqrt(HD))

    for index in range(4):
        to_row[index].wait_recv()
        passed[index].start()
    output.row_in()
    chunks[2][0].start()
    pass_on(0)
    for index in range(4):
        to_mate[index].wait_recv()
        passed[index].wait_recv()
    chunks[3][0].start()
    output.plane_in()
    output.far_in(0)

    firsts = [member, pieces - 1 - member, pieces + member, 2 * pieces - 1 - member]
    rows = REP * span
    ones = jnp.ones((16, KEYS), BF)

    @pl.loop(0, kv_rows // HD)
    def _(head):
        key_n[...] = pair[pl.ds(pl.multiple_of(head * HD, HD), HD), :].T
        value_rows = pl.ds(pl.multiple_of(kv_rows + head * HD, HD), HD)
        for index in range(4):
            cut = slice(index * span, (index + 1) * span)
            query_here = jnp.concatenate([query[head * REP + rep, :, cut] for rep in range(REP)], axis=1)
            first_query = firsts[index] * span
            full, last = tiles_of(first_query)

            def tile(where, accum, masked):
                first_key = pl.multiple_of(where * KEYS, KEYS)
                expo = jnp.exp(dot(key_n[pl.ds(first_key, KEYS), :], query_here))
                if masked:
                    expo = jnp.where(allowed(first_query, first_key, span, rows), expo, 0.0)
                value = jnp.concatenate([pair[value_rows, pl.ds(first_key, KEYS)], ones], axis=0)
                return accum + dot(value, expo.astype(BF))

            accum = tile(last, jnp.zeros((HD + 16, rows), F32), True)
            least = (0, PROMPT // KEYS // 2, PROMPT // KEYS, PROMPT // KEYS)[index]
            for where in range(least):
                accum = tile(where, accum, False)
            if index < 2:
                accum = lax.fori_loop(least, full, lambda where, total: tile(where, total, False), accum)
            total = accum[HD : HD + 1]
            result = accum[:HD] / total
            log = jnp.log(total)
            for rep in range(REP):
                part = slice(rep * span, (rep + 1) * span)
                mixed_t[pl.ds(pl.multiple_of((head * REP + rep) * HD, HD), HD), cut] = result[:, part]
                logs[head, rep : rep + 1, cut] = log[:, part]

        @pl.when(head == 2)
        def _():
            output.far_in(1)
            output.far_in(2)

        for number, index in ((1, 1), (3, 2)):
            @pl.when(head == number)
            def _(index=index):
                pass_on(index)

    save(query, query_out)
    save(mixed_t, mixed_out)
    save(logs, logs_out)
    save(pair, pair_out)
    pass_on(3)
    output.mate_in(0, 6)
    save(w_out, w_out_out)

    @pl.loop(0, mixed_t.shape[0] // 128)
    def _(index):
        here = pl.ds(pl.multiple_of(index * 128, 128), 128)
        mixed[:, here] = mixed_t[here, :].astype(BF).T

    @pl.loop(0, depth // TILE)
    def _(index):
        here = pl.ds(pl.multiple_of(index * TILE, TILE), TILE)
        hidden[:, here] = states[:, here].astype(F32) + dot(mixed[...], w_out[:, here])

    normed_saved.wait()

    @pl.loop(0, 4)
    def _(index):
        here = pl.ds(pl.multiple_of(index * block, block), block)
        values = hidden[here, :]
        inverse = lax.rsqrt(jnp.mean(values * values, axis=1, keepdims=True) + EPSILON)
        for slot in range(2):
            part = values[:, slot * width : (slot + 1) * width] * inverse
            normed[here, slot * width : (slot + 1) * width] = (part * gains[slot, 1:2, :]).astype(BF)

    save(hidden, hidden_out)
    save(normed, normed_two_out)
    for copy in stores:
        if copy is not normed_saved:
            copy.wait()
    sent_gains.wait_send()
    for copy in sent_tokens + to_row + to_mate + passed:
        copy.wait_send()
    project.sent()
    output.sent()
    for over_row, over_planes in chunks:
        over_row.wait_send()
        over_planes.wait_recv()
        over_planes.wait_send()


def front(tokens, w_project, w_out, gains, w_gate, w_up, cosine, sine, query_gain, key_gain):
    shard, width = tokens.shape
    mine, depth = shard // 2, 2 * width
    q_width, columns = w_out.shape[0], w_project.shape[1]
    kv_rows = KVH * HD
    anywhere = pl.BlockSpec(memory_space=pl.ANY)
    inside = pl.BlockSpec(memory_space=pltpu.VMEM)
    dma = pltpu.SemaphoreType.DMA
    shape = jax.ShapeDtypeStruct
    return pl.pallas_call(
        front_kernel,
        out_shape=[
            shape((mine, depth), BF),
            shape((mine, depth), BF),
            shape((QH, HD, mine), F32),
            shape((QH, HD, mine), BF),
            shape((kv_rows, mine), BF),
            shape((2 * kv_rows, GROUP), BF),
            shape((QH * HD, mine), F32),
            shape((KVH, REP, mine), F32),
            shape((mine, depth), F32),
            shape((mine, depth), BF),
            shape((4, 2, width, columns), BF),
            shape((4 * q_width, depth), BF),
            shape(w_gate.shape, BF),
            shape(w_up.shape, BF),
            shape((2, 2, width), F32),
        ],
        in_specs=[anywhere] * 6 + [inside] * 4,
        out_specs=[anywhere] * 15,
        scratch_shapes=[
            pltpu.VMEM((mine, depth), BF),
            pltpu.VMEM((mine, depth), BF),
            pltpu.VMEM((4, 2, width, columns), BF),
            pltpu.VMEM((QH, HD, mine), F32),
            pltpu.VMEM((kv_rows, mine), BF),
            pltpu.VMEM((QH, HD, mine), BF),
            pltpu.VMEM((2 * kv_rows, mine), BF),
            pltpu.VMEM((2 * kv_rows, GROUP), BF),
            pltpu.VMEM((GROUP, HD), BF),
            pltpu.VMEM((QH * HD, mine), F32),
            pltpu.VMEM((KVH, REP, mine), F32),
            pltpu.VMEM((mine, QH * HD), BF),
            pltpu.VMEM((4 * q_width, depth), BF),
            pltpu.VMEM((mine, depth), F32),
            pltpu.VMEM((2, 2, width), F32),
            dma((3, 2)), dma((3, 2)), dma((2,)),
            dma((11,)), dma((11,)), dma((11,)), dma((11,)), dma((1,)), dma((1,)),
            dma((3, 4)), dma((3, 4)), dma((4,)), dma((4,)), dma((4,)), dma((4,)), dma((3,)), dma((13,)),
        ],
        compiler_params=pltpu.CompilerParams(
            collective_id=3, has_side_effects=True, vmem_limit_bytes=56 * 1024 * 1024
        ),
        name="front",
    )(tokens, w_project, w_out, gains, w_gate, w_up, cosine, sine, query_gain, key_gain)


def back_kernel(*refs):
    query, d_out, logs_ref, delta_ref, pair, raw, key_raw, cos_ref, sin_ref, query_gain, key_gain = refs[:11]
    d_project, query_gain_out, key_gain_out = refs[11:14]
    key_n, value_n, d_key, d_value, both_t, staged, come, gain_sum, send_sem, recv_sem = refs[14:]
    row, side = lax.axis_index("row"), lax.axis_index("side")
    others = [
        (2 * (1 - row) + side, {"row": 1 - row}),
        (2 * (1 - row) + 1 - side, {"row": 1 - row, "side": 1 - side}),
        (2 * row + 1 - side, {"side": 1 - side}),
    ]
    member = 2 * row + side
    pieces = 8
    span = query.shape[2] // 4
    rows = REP * span
    kv_rows = key_raw.shape[0]
    half = HD // 2

    barrier = pltpu.get_barrier_semaphore()
    for _, where in others:
        pl.semaphore_signal(barrier, 1, device_id=where, device_id_type=pl.DeviceIdType.MESH)
    pl.semaphore_wait(barrier, 3)

    def sent(index, head):
        return pltpu.make_async_remote_copy(
            staged.at[index, head],
            come.at[index, head],
            send_sem.at[index, head],
            recv_sem.at[index, head],
            device_id=others[index][1],
            device_id_type=pl.DeviceIdType.MESH,
        )

    def starts(who):
        return [who, pieces - 1 - who, pieces + who, 2 * pieces - 1 - who]

    def through_norm(values, gain, cosine, sine, d_turned):
        first, second = d_turned[:half], d_turned[half:]
        d_scaled = jnp.concatenate([first * cosine + second * sine, second * cosine - first * sine], axis=0)
        inverse = lax.rsqrt(jnp.mean(values * values, axis=0, keepdims=True) + EPSILON)
        d_normed = d_scaled * gain
        mean = jnp.mean(values * d_normed, axis=0, keepdims=True)
        return inverse * d_normed - values * inverse**3 * mean, d_scaled * values * inverse

    gain_sum[...] = jnp.zeros_like(gain_sum)
    scale = 1.0 / math.sqrt(HD)

    @pl.loop(0, KVH)
    def _(head):
        key_rows = pl.ds(pl.multiple_of(head * HD, HD), HD)
        value_rows = pl.ds(pl.multiple_of(kv_rows + head * HD, HD), HD)
        key_n[...] = pair[key_rows, :].T
        value_n[...] = pair[value_rows, :].T
        d_key[...] = jnp.zeros_like(d_key)
        d_value[...] = jnp.zeros_like(d_value)
        for index, start in enumerate(starts(member)):
            cut = slice(index * span, (index + 1) * span)

            def beside(ref):
                return jnp.concatenate([ref[head * REP + rep, :, cut] for rep in range(REP)], axis=1)

            query_here, d_out_here = beside(query), beside(d_out)
            query_t, d_out_t = query_here.T, d_out_here.T
            logs = jnp.concatenate([logs_ref[head, rep : rep + 1, cut] for rep in range(REP)], axis=1)
            delta = jnp.concatenate([delta_ref[head, rep : rep + 1, cut] for rep in range(REP)], axis=1)
            first_query = start * span
            full, last = tiles_of(first_query)

            def tile(where, accum, masked):
                first_key = pl.multiple_of(where * KEYS, KEYS)
                here = pl.ds(first_key, KEYS)
                probs = jnp.exp(dot(key_n[here, :], query_here) - logs)
                if masked:
                    probs = jnp.where(allowed(first_query, first_key, span, rows), probs, 0.0)
                d_probs = dot(value_n[here, :], d_out_here)
                d_scores = (probs * (d_probs - delta)).astype(BF)
                d_value[here, :] += dot(probs.astype(BF), d_out_t)
                d_key[here, :] += dot(d_scores, query_t)
                return accum + dot(pair[key_rows, here], d_scores)

            accum = tile(last, jnp.zeros((HD, rows), F32), True)
            least = (0, PROMPT // KEYS // 2, PROMPT // KEYS, PROMPT // KEYS)[index]
            for where in range(least):
                accum = tile(where, accum, False)
            if index < 2:
                accum = lax.fori_loop(least, full, lambda where, total: tile(where, total, False), accum)
            cosine = jnp.concatenate([cos_ref[:, cut]] * REP, axis=1)
            sine = jnp.concatenate([sin_ref[:, cut]] * REP, axis=1)
            d_raw, part = through_norm(beside(raw), query_gain[...], cosine, sine, accum * scale)
            gain_sum[0] += part
            for rep in range(REP):
                which = head * REP + rep
                place = pl.ds(pl.multiple_of(which % KVH * HD, HD), HD)
                d_project[which // KVH, place, cut] = d_raw[:, rep * span : (rep + 1) * span].astype(BF)
        both_t[:HD, :] = d_key[...].T.astype(BF)
        both_t[HD:, :] = d_value[...].T.astype(BF)
        for index, who in enumerate([who for who, _ in others] + [member]):
            for number, start in enumerate(starts(who)):
                part = both_t[:, pl.ds(pl.multiple_of(start * span, span), span)]
                staged[index, head, :, number * span : (number + 1) * span] = part
            if index < 3:
                sent(index, head).start()

    cosine, sine = cos_ref[...], sin_ref[...]
    width = kv_rows // 4
    for head in range(KVH):
        total = staged[3, head].astype(F32)
        for index in range(3):
            sent(index, head).wait_recv()
            total += come[index, head].astype(F32)
        values = key_raw[head * HD : (head + 1) * HD, :].astype(F32)
        d_raw, part = through_norm(values, key_gain[...], cosine, sine, total[:HD])
        gain_sum[1] += part
        for offset, result in ((0, d_raw.astype(BF)), (width, total[HD:].astype(BF))):
            first = head * HD
            while first < (head + 1) * HD:
                col, inside = first // width, first % width
                size = min(width - inside, (head + 1) * HD - first)
                place = d_project.shape[1] - 2 * width + offset + inside
                d_project[col, place : place + size, :] = result[first - head * HD : first - head * HD + size]
                first += size
    query_gain_out[...] = jnp.sum(gain_sum[0], axis=1, keepdims=True)
    key_gain_out[...] = jnp.sum(gain_sum[1], axis=1, keepdims=True)
    for head in range(KVH):
        for index in range(3):
            sent(index, head).wait_send()


def back(query, d_out, logs, delta, pair, raw, key_raw, cosine, sine, query_gain, key_gain):
    mine = query.shape[2]
    inside = pl.BlockSpec(memory_space=pltpu.VMEM)
    dma = pltpu.SemaphoreType.DMA
    shape = jax.ShapeDtypeStruct
    columns = (QH + 2 * KVH) * HD // 4
    return pl.pallas_call(
        back_kernel,
        out_shape=[shape((4, columns, mine), BF), shape((HD, 1), F32), shape((HD, 1), F32)],
        in_specs=[inside] * 11,
        out_specs=[inside] * 3,
        scratch_shapes=[
            pltpu.VMEM((GROUP, HD), BF),
            pltpu.VMEM((GROUP, HD), BF),
            pltpu.VMEM((GROUP, HD), F32),
            pltpu.VMEM((GROUP, HD), F32),
            pltpu.VMEM((2 * HD, GROUP), BF),
            pltpu.VMEM((4, KVH, 2 * HD, mine), BF),
            pltpu.VMEM((3, KVH, 2 * HD, mine), BF),
            pltpu.VMEM((2, HD, mine), F32),
            dma((3, KVH)),
            dma((3, KVH)),
        ],
        compiler_params=pltpu.CompilerParams(
            collective_id=4, has_side_effects=True, vmem_limit_bytes=48 * 1024 * 1024
        ),
        name="attend_back",
    )(query, d_out, logs, delta, pair, raw, key_raw, cosine, sine, query_gain, key_gain)


def body(
    tokens,
    norm1_gain,
    w_query,
    w_key,
    w_value,
    query_gain,
    key_gain,
    w_out,
    norm2_gain,
    w_gate,
    w_up,
    w_down,
    teacher,
    positions,
    token_count,
):
    rows = lax.axis_size("row")
    cores = lax.axis_size("side")
    cols = lax.axis_size("group") * cores
    row_index = lax.axis_index("row")
    group_index = lax.axis_index("group")
    members = rows * cores
    member = row_index * cores + lax.axis_index("side")
    shard, width = tokens.shape
    pieces = 2 * members
    span = shard // pieces
    mine = shard // members * cores
    q_width, k_width = w_query.shape[1], w_key.shape[1]
    ff = w_gate.shape[1]

    def from_row(block, ahead):
        pairs = [((r + ahead) % rows, r) for r in range(rows)]
        return lax.ppermute(block, "row", pairs)

    def gather_rows(block, axis):
        parts = [block] + [from_row(block, ahead) for ahead in range(1, rows)]
        return jnp.concatenate(parts, axis=axis)

    def scatter_rows(block, axis):
        size = block.shape[axis] // rows
        total = lax.slice_in_dim(block, 0, size, axis=axis).astype(F32)
        for ahead in range(1, rows):
            part = lax.slice_in_dim(block, ahead * size, (ahead + 1) * size, axis=axis)
            total = total + from_row(part, rows - ahead).astype(F32)
        return total.astype(BF)

    def sum_planes(block, cuts):
        planes = lax.axis_size("dp")
        plane = lax.axis_index("dp")
        half = planes // 2
        edge = jnp.minimum(plane, planes - 1 - plane)
        done = []
        for part in jnp.split(block, cuts, axis=0):
            for step in range(half - 1):
                pairs = [(step, step + 1), (planes - 1 - step, planes - 2 - step)]
                come = lax.ppermute(part, "dp", pairs)
                part = (part.astype(F32) + come.astype(F32)).astype(BF)
            come = lax.ppermute(part, "dp", [(half - 1, half), (half, half - 1)])
            part = (part.astype(F32) + come.astype(F32)).astype(BF)
            for step in reversed(range(half - 1)):
                pairs = [(step + 1, step), (planes - 2 - step, planes - 1 - step)]
                come = lax.ppermute(part, "dp", pairs)
                part = jnp.where(edge == step, come, part)
            done.append(part)
        return jnp.concatenate(done, axis=0)

    def to_members(block):
        parts = block.reshape(pieces, span, width)
        parts = jnp.stack([parts[:members], parts[members:][::-1]], axis=1)
        moved = lax.all_to_all(parts, ("row", "side"), 0, 0, tiled=True)
        moved = jnp.roll(moved.reshape(rows, cores, 2 * span, width), -row_index, 0)
        moved = moved.transpose(1, 2, 0, 3)
        return moved.reshape(mine, rows * width)

    def from_members(block):
        parts = block.reshape(cores, 2, span, rows, width).transpose(3, 0, 1, 2, 4)
        parts = jnp.roll(parts, row_index, 0).reshape(members, 2, span, width)
        moved = lax.all_to_all(parts, ("row", "side"), 0, 0, tiled=True)
        moved = jnp.concatenate([moved[:, 0], moved[:, 1][::-1]], axis=0)
        return moved.reshape(shard, width)

    def pick(values):
        part = lax.dynamic_slice_in_dim(values.reshape(-1, cores, pieces, span), group_index, 1, 0)[0]
        low = lax.dynamic_slice_in_dim(part, member, 1, 1)
        high = lax.dynamic_slice_in_dim(part, pieces - 1 - member, 1, 1)
        return jnp.concatenate([low, high], axis=1).reshape(-1)

    first_tokens = (
        jnp.array([0, 0, shard, shard], jnp.int32)
        + jnp.stack([member, pieces - 1 - member] * 2).astype(jnp.int32) * span
    )

    half = HD // 2
    freq = jnp.exp(jnp.arange(half, dtype=F32) * (-2.0 * math.log(10000.0) / HD))
    angle = freq[:, None] * pick(positions).astype(F32)[None, :]
    cosine, sine = jnp.cos(angle), jnp.sin(angle)
    def dealt(full):
        lead, entry = full.shape[:-2], full.shape[-1]
        parts = full.reshape(lead + (cores, pieces, span, entry))
        low = parts[..., :members, :, :]
        high = parts[..., members:, :, :][..., ::-1, :, :]
        both = jnp.stack([low, high], axis=-3)
        both = jnp.moveaxis(both, -4, 0)
        return both.reshape((members,) + lead + (mine, entry))

    w_project = jnp.concatenate([w_query, w_key, w_value], axis=1)
    scale = 1.0 / math.sqrt(HD)
    fast = rows == 2 and cols == 4 and lax.axis_size("dp") % 2 == 0 and mine == 4 * span
    if fast:
        (
            states, normed_one, query_raw, query_use, key_sent, pair, mixed_f, logs, hidden,
            normed_two, w_project, w_out_all, gate_other, up_other, gains,
        ) = front(
            tokens, w_project, w_out, jnp.stack([norm1_gain, norm2_gain]), w_gate, w_up,
            cosine, sine, query_gain[:, None], key_gain[:, None],
        )
        states = states.astype(F32)
        inverse_one, inverse_two = rms(states), rms(hidden)
        gain_one, gain_two = gains[:, 0].reshape(D), gains[:, 1].reshape(D)
        mixed_f = mixed_f.reshape(KVH, REP, HD, mine)
        mixed = mixed_f.reshape(QH * HD, mine).astype(BF)
        w_project = w_project.reshape(cols, D, -1)
        ffn_weights = [w_gate, gate_other, w_up, up_other, w_down]
    else:
        states = to_members(tokens).astype(F32)
        gain_one = gather_rows(norm1_gain, 0)
        gain_two = gather_rows(norm2_gain, 0)
        w_project = gather_rows(w_project, 0)
        w_project = lax.all_gather(w_project, ("group", "side"), axis=0)
        w_out_all = gather_rows(w_out, 1)
        w_out_all = lax.all_gather(w_out_all, ("group", "side"), axis=0, tiled=True)
        def halves(block, axis):
            if rows == 2:
                return [block, from_row(block, 1)]
            return jnp.split(gather_rows(block, axis), 2, axis=axis)

        ffn_weights = halves(w_gate, 0) + halves(w_up, 0) + halves(w_down, 1)
        inverse_one = rms(states)
        normed_one = (states * inverse_one * gain_one).astype(BF)
        projected = dot(w_project, normed_one, ((1,), (1,)))
        query_raw = projected[:, :q_width].reshape(QH, HD, mine)
        key_sent = projected[:, q_width : q_width + k_width].reshape(KVH, HD, mine).astype(BF)
        value_sent = projected[:, q_width + k_width :].reshape(KVH, HD, mine).astype(BF)
        query_rot, query_back = jax.vjp(
            lambda raw, gain: prepare(raw, gain, cosine, sine), query_raw, query_gain
        )
        key_rot, key_back = jax.vjp(
            lambda raw, gain: prepare(raw, gain, cosine, sine), key_sent.astype(F32), key_gain
        )
        query_use = (query_rot.astype(BF) * BF(scale)).reshape(KVH, REP, HD, mine)
        pair = jnp.stack([key_rot.astype(BF), value_sent])
        pair = lax.all_gather(pair, ("row", "side"), axis=0)

        def natural(stacked):
            lead = stacked.shape[1:-1]
            parts = stacked.reshape((members,) + lead + (cores, 2, span))
            low, high = parts[..., 0, :], parts[..., 1, :]
            both = jnp.concatenate([low, high[::-1]], axis=0)
            return jnp.moveaxis(both, 0, -2).reshape(lead + (GROUP,))

        pair = natural(pair)
        key_t, value_t = pair[0], pair[1]
        key_n = key_t.transpose(0, 2, 1)
        value_one = jnp.concatenate([value_t, jnp.ones((KVH, 16, GROUP), BF)], axis=1)
        mixed_f, logs = attend(first_tokens, query_use, key_n, value_one)
        mixed = mixed_f.reshape(QH * HD, mine).astype(BF)
        hidden = states + dot(mixed, w_out_all, ((0,), (0,)))

        inverse_two = rms(hidden)
        normed_two = (hidden * inverse_two * gain_two).astype(BF)

    total_tokens = shard * cols * lax.axis_size("dp")
    loss_scale = total_tokens / token_count[0].astype(F32)
    if fast:
        normed_all, _, _, activated, _, d_low, d_gate_up, d_result, d_normed, block_out = feed(
            normed_two, ffn_weights, teacher, hidden, loss_scale[None]
        )
        d_result = d_result.reshape(mine, D)
    else:
        normed_all, gate, up, activated, ffn_out = spread(True, normed_two, ffn_weights)
        result = hidden + ffn_out.reshape(mine, D)
        d_result = loss_scale * (result - to_members(teacher).astype(F32))
        d_low, d_gate_up, d_normed = spread(False, d_result.astype(BF), ffn_weights, gate, up)
        block_out = from_members(result.astype(BF))
    d_normed = d_normed.reshape(mine, D)
    d_low, normed_all = d_low.reshape(-1, D), normed_all.reshape(-1, D)
    activated, d_gate_up = activated.reshape(-1, ff), d_gate_up.reshape(-1, 2 * ff)

    norm_two_part = jnp.sum(d_normed * hidden * inverse_two, axis=0)
    d_hidden = d_result + norm_back(hidden, inverse_two, gain_two, d_normed)
    d_hidden, d_hidden_low = lax.optimization_barrier((d_hidden, d_hidden.astype(BF)))
    grad_out = dot(mixed, d_hidden_low, ((1,), (0,))).astype(BF)
    d_mixed = dot(w_out_all, d_hidden_low, ((1,), (1,))).astype(BF)
    d_mixed = d_mixed.reshape(KVH, REP, HD, mine)
    delta = jnp.sum(d_mixed.astype(F32) * mixed_f, axis=2)
    if fast:
        d_projected, query_gain_part, key_gain_part = back(
            query_use, d_mixed.reshape(QH, HD, mine), logs, delta, pair, query_raw, key_sent,
            cosine, sine, query_gain[:, None], key_gain[:, None],
        )
        query_gain_part, key_gain_part = query_gain_part[:, 0], key_gain_part[:, 0]
    else:
        d_query, d_key_n, d_value_n = attend_back(
            first_tokens, query_use, d_mixed, logs, delta, key_t, value_t
        )
        d_pair = dealt(jnp.stack([d_key_n, d_value_n])).astype(BF)
        d_pair = lax.psum_scatter(d_pair, ("row", "side"), scatter_dimension=0, tiled=True)[0]
        d_pair = d_pair.astype(F32).transpose(0, 1, 3, 2)
        d_query_raw, query_gain_part = query_back(d_query.reshape(QH, HD, mine) * scale)
        d_key_raw, key_gain_part = key_back(d_pair[0])
        d_projected = jnp.concatenate(
            [
                d_query_raw.reshape(cols, q_width, mine),
                d_key_raw.reshape(cols, k_width, mine),
                d_pair[1].reshape(cols, k_width, mine),
            ],
            axis=1,
        ).astype(BF)
    d_normed_one = dot(d_projected, w_project, ((0, 1), (0, 2)))
    grad_input = d_hidden + norm_back(states, inverse_one, gain_one, d_normed_one)
    norm_one_part = jnp.sum(d_normed_one * states * inverse_one, axis=0)

    grad_project = lax.dot_general(
        d_projected, normed_one, (((2,), (0,)), ((), ())), preferred_element_type=F32
    )
    grad_project = grad_project.astype(BF)
    grad_out = grad_out.reshape(cols, q_width, D)
    norm_one_part = jnp.roll(norm_one_part.reshape(rows, width), row_index, 0).reshape(D)
    norm_two_part = jnp.roll(norm_two_part.reshape(rows, width), row_index, 0).reshape(D)
    small = jnp.concatenate([norm_one_part, norm_two_part, query_gain_part, key_gain_part])
    if fast and lax.axis_size("dp") == 4:
        padded = jnp.pad(small, (0, SMALL * 128 - small.shape[0])).reshape(SMALL, 128)
        grad_gate_up, grad_out, grad_project, grad_down, small, grad_input = reduce_all(
            4, normed_all, d_gate_up, activated, d_low, grad_out, grad_project, padded, grad_input.astype(BF)
        )
        grad_input = grad_input.astype(F32)
        small = small.reshape(-1)[: 2 * D + 2 * HD]
    else:
        grad_input = from_members(grad_input)
        small = lax.psum(small, ("dp", "row", "group", "side"))
        col_axes = ("group", "side")
        grad_project = lax.psum_scatter(grad_project, col_axes, scatter_dimension=0, tiled=True)
        grad_out = lax.psum_scatter(grad_out, col_axes, scatter_dimension=0, tiled=True)
        grad_down = dot(activated, d_low, ((0,), (0,))).astype(BF)
        grad_gate_up = dot(normed_all, d_gate_up, ((0,), (0,))).astype(BF)
        grad_down = sum_planes(scatter_rows(grad_down, 1), 2)
        grad_gate_up = sum_planes(scatter_rows(grad_gate_up, 0), 4)
        grad_out = sum_planes(scatter_rows(grad_out[0], 1), 1)
        grad_project = sum_planes(scatter_rows(grad_project[0], 1), 2)
    grad_norm1 = lax.dynamic_slice_in_dim(small, row_index * width, width, 0)
    grad_norm2 = lax.dynamic_slice_in_dim(small, D + row_index * width, width, 0)
    grad_project = grad_project.astype(F32).T
    return (
        block_out,
        grad_input,
        grad_norm1,
        grad_project[:, :q_width],
        grad_project[:, q_width : q_width + k_width],
        grad_project[:, q_width + k_width :],
        small[2 * D : 2 * D + HD],
        small[2 * D + HD :],
        grad_out.astype(F32),
        grad_norm2,
        grad_gate_up[:, :ff].astype(F32),
        grad_gate_up[:, ff:].astype(F32),
        grad_down.astype(F32),
    )


def solution(mesh):
    dp, row, col = mesh.shape["dp"], mesh.shape["row"], mesh.shape["col"]

    def call(*args):
        side = GROUP * dp * col // args[0].shape[0]
        fine = Mesh(
            mesh.devices.reshape(dp, row, col // side, side), ("dp", "row", "group", "side")
        )
        col_axes = ("group", "side")
        token_spec = P(("dp", "group", "side"), "row")
        wide = P("row", col_axes)
        tall = P(col_axes, "row")
        return jax.shard_map(
            body,
            mesh=fine,
            in_specs=(
                token_spec,
                P("row"),
                wide,
                wide,
                wide,
                P(),
                P(),
                tall,
                P("row"),
                wide,
                wide,
                tall,
                token_spec,
                P("dp"),
                P(),
            ),
            out_specs=(
                token_spec,
                token_spec,
                P("row"),
                wide,
                wide,
                wide,
                P(),
                P(),
                tall,
                P("row"),
                wide,
                wide,
                tall,
            ),
            check_vma=False,
        )(*args)

    return call
```

```python
import functools
import math

import jax
import jax.numpy as jnp
from jax import lax
from jax.experimental import pallas as pl
from jax.experimental.pallas import tpu as pltpu
from jax.sharding import Mesh
from jax.sharding import PartitionSpec as P

D = 2048
QH = 20
KVH = 5
HD = 64
PROMPT = 1024
CONT = 128
NCONT = 8
GROUP = PROMPT + NCONT * CONT
REP = QH // KVH
KEYS = 256

EPSILON = 1e-06
BF = jnp.bfloat16
F32 = jnp.float32


def dot(left, right, dims=((1,), (0,))):
    return lax.dot_general(left, right, (dims, ((), ())), preferred_element_type=F32)


def rms(values):
    return lax.rsqrt(jnp.mean(values * values, axis=1, keepdims=True) + EPSILON)


def norm_back(states, inverse, gain, d_normed):
    mean = jnp.mean(states * gain * d_normed, axis=1, keepdims=True)
    return inverse * gain * d_normed - states * inverse**3 * mean


def prepare(raw, gain, cosine, sine):
    values = raw * lax.rsqrt(jnp.mean(raw * raw, axis=1, keepdims=True) + EPSILON)
    values = values * gain[None, :, None]
    half = HD // 2
    first, second = values[:, :half], values[:, half:]
    return jnp.concatenate(
        [first * cosine - second * sine, second * cosine + first * sine], axis=1
    )


def allowed(first_query, first_key, span, rows):
    key = first_key + lax.broadcasted_iota(jnp.int32, (KEYS, rows), 0)
    query = first_query + lax.broadcasted_iota(jnp.int32, (KEYS, rows), 1) % span
    return (key <= query) & ((key < PROMPT) | (key // CONT == query // CONT))


def side_by_side(ref, index, span):
    return jnp.concatenate(
        [ref[0, head, :, index * span : (index + 1) * span] for head in range(REP)], axis=1
    )


def tiles_of(first_query):
    last = first_query // KEYS
    return jnp.minimum(last, PROMPT // KEYS), last


def attend_kernel(chunks, span, first_ref, query_ref, key_ref, value_ref, out_ref, log_ref):
    rows = REP * span
    for index in range(chunks):
        query = side_by_side(query_ref, index, span)
        first_query = first_ref[index]
        full, last = tiles_of(first_query)

        def tile(where, accum, masked):
            first_key = pl.multiple_of(where * KEYS, KEYS)
            scores = dot(key_ref[0, pl.ds(first_key, KEYS), :], query)
            expo = jnp.exp(scores)
            if masked:
                expo = jnp.where(allowed(first_query, first_key, span, rows), expo, 0.0)
            return accum + dot(value_ref[0, :, pl.ds(first_key, KEYS)], expo.astype(BF))

        accum = tile(last, jnp.zeros((value_ref.shape[1], rows), F32), True)
        accum = lax.fori_loop(0, full, lambda where, total: tile(where, total, False), accum)
        total = accum[HD : HD + 1]
        mixed = accum[:HD] / total
        logs = jnp.log(total)
        for head in range(REP):
            cut = slice(head * span, (head + 1) * span)
            out_ref[0, head, :, index * span : (index + 1) * span] = mixed[:, cut]
            log_ref[0, head : head + 1, index * span : (index + 1) * span] = logs[:, cut]


def attend_back_kernel(
    chunks,
    span,
    first_ref,
    query_ref,
    d_out_ref,
    log_ref,
    delta_ref,
    key_t_ref,
    value_t_ref,
    d_query_ref,
    d_key_ref,
    d_value_ref,
    key_ref,
    value_ref,
):
    rows = REP * span
    key_ref[...] = key_t_ref[0].T
    value_ref[...] = value_t_ref[0].T
    d_key_ref[...] = jnp.zeros_like(d_key_ref)
    d_value_ref[...] = jnp.zeros_like(d_value_ref)
    for index in range(chunks):
        query = side_by_side(query_ref, index, span)
        d_out = side_by_side(d_out_ref, index, span)
        query_t = query.T
        d_out_t = d_out.T
        cut = slice(index * span, (index + 1) * span)
        logs = jnp.concatenate([log_ref[0, h : h + 1, cut] for h in range(REP)], axis=1)
        delta = jnp.concatenate([delta_ref[0, h : h + 1, cut] for h in range(REP)], axis=1)
        first_query = first_ref[index]
        full, last = tiles_of(first_query)

        def tile(where, accum, masked):
            first_key = pl.multiple_of(where * KEYS, KEYS)
            here = pl.ds(first_key, KEYS)
            probs = jnp.exp(dot(key_ref[here, :], query) - logs)
            if masked:
                probs = jnp.where(allowed(first_query, first_key, span, rows), probs, 0.0)
            d_probs = dot(value_ref[here, :], d_out)
            d_scores = (probs * (d_probs - delta)).astype(BF)
            d_value_ref[0, here, :] += dot(probs.astype(BF), d_out_t)
            d_key_ref[0, here, :] += dot(d_scores, query_t)
            return accum + dot(key_t_ref[0, :, here], d_scores)

        accum = tile(last, jnp.zeros((HD, rows), F32), True)
        accum = lax.fori_loop(0, full, lambda where, total: tile(where, total, False), accum)
        for head in range(REP):
            part = accum[:, head * span : (head + 1) * span]
            d_query_ref[0, head, :, cut] = part


def per_head(shape):
    return pl.BlockSpec((1,) + shape, lambda head, first: (head,) + (0,) * len(shape))


def attend(first, query, key, value_t):
    tokens = query.shape[-1]
    chunks = first.shape[0]
    return pl.pallas_call(
        functools.partial(attend_kernel, chunks, tokens // chunks),
        out_shape=(
            jax.ShapeDtypeStruct((KVH, REP, HD, tokens), F32),
            jax.ShapeDtypeStruct((KVH, REP, tokens), F32),
        ),
        grid_spec=pltpu.PrefetchScalarGridSpec(
            num_scalar_prefetch=1,
            grid=(KVH,),
            in_specs=[
                per_head((REP, HD, tokens)),
                per_head((GROUP, HD)),
                per_head((value_t.shape[1], GROUP)),
            ],
            out_specs=[per_head((REP, HD, tokens)), per_head((REP, tokens))],
        ),
        compiler_params=pltpu.CompilerParams(vmem_limit_bytes=32 * 1024 * 1024),
        name="attend",
    )(first, query, key, value_t)


def attend_back(first, query, d_out, logs, delta, key_t, value_t):
    tokens = query.shape[-1]
    chunks = first.shape[0]
    return pl.pallas_call(
        functools.partial(attend_back_kernel, chunks, tokens // chunks),
        out_shape=(
            jax.ShapeDtypeStruct((KVH, REP, HD, tokens), F32),
            jax.ShapeDtypeStruct((KVH, GROUP, HD), F32),
            jax.ShapeDtypeStruct((KVH, GROUP, HD), F32),
        ),
        grid_spec=pltpu.PrefetchScalarGridSpec(
            num_scalar_prefetch=1,
            grid=(KVH,),
            in_specs=[
                per_head((REP, HD, tokens)),
                per_head((REP, HD, tokens)),
                per_head((REP, tokens)),
                per_head((REP, tokens)),
                per_head((HD, GROUP)),
                per_head((HD, GROUP)),
            ],
            out_specs=[
                per_head((REP, HD, tokens)),
                per_head((GROUP, HD)),
                per_head((GROUP, HD)),
            ],
            scratch_shapes=[pltpu.VMEM((GROUP, HD), BF), pltpu.VMEM((GROUP, HD), BF)],
        ),
        compiler_params=pltpu.CompilerParams(vmem_limit_bytes=32 * 1024 * 1024),
        name="attend_back",
    )(first, query, d_out, logs, delta, key_t, value_t)


AHEAD = 4
SLOTS = AHEAD + 2
FAR_LAG, WIDE_LAG, LAG = 1, 2, 4
SMALL = 40


class Part:
    def __init__(self, axis, rows, cols, count, base, col):
        self.axis, self.rows, self.cols = axis, rows, cols
        self.count, self.base, self.col = count, base, col

    def cut(self, ref, index, half, lead=()):
        first = pl.ds(index * self.rows, self.rows)
        if self.axis == 0:
            first = pl.ds((half * self.count + index) * self.rows, self.rows)
            return ref.at[(*lead, first, slice(None))]
        return ref.at[(*lead, first, pl.ds(half * self.cols, self.cols))]


def reduce_kernel(parts, planes, *refs):
    count = len(parts)
    refs = list(refs)

    def take(number):
        taken = refs[:number]
        del refs[:number]
        return taken

    col_parts = [j for j in range(count) if parts[j].col]
    normed_ref, d_gate_up_ref, act_ref, d_low_ref = take(4)
    grads = dict(zip(col_parts, take(len(col_parts))))
    (small_ref, mine_ref) = take(2)
    outs = take(count)
    (small_out, dealt_ref) = take(2)
    near, far, own = take(count), take(count), take(count)
    made = [j for j in range(count) if not parts[j].col]
    leaving = dict(zip(made, take(len(made))))
    mate_in = dict(zip(col_parts, take(len(col_parts))))
    far_in = dict(zip(col_parts, take(len(col_parts))))
    right, left, left_t, right_sem, left_sem, free_sem = take(6)
    out_sem, row_send, row_recv, in_send, far_recv, mid_send, wide_recv = take(7)
    col_own, col_send, col_recv, x_send, x_recv, small_local, small_send, small_recv = take(8)
    small_in, small_sum, deal_send, deal_recv, deal_local = take(5)
    plane, row = lax.axis_index("dp"), lax.axis_index("row")
    group, side = lax.axis_index("group"), lax.axis_index("side")
    other_row, mate, far_dev = {"row": 1 - row}, {"side": 1 - side}, {"group": 1 - group}
    cross = {"row": 1 - row, "side": 1 - side}
    at_end = (plane == 0) | (plane == planes - 1)
    low = plane < planes // 2
    end_next = {"dp": jnp.where(low, 1, planes - 2)}
    mid_outer = {"dp": jnp.where(low, 0, planes - 1)}
    mid_other = {"dp": jnp.where(low, planes // 2, planes // 2 - 1)}

    def remote(source, target, send, recv, where):
        return pltpu.make_async_remote_copy(
            source, target, send, recv, device_id=where, device_id_type=pl.DeviceIdType.MESH
        )

    barrier = pltpu.get_barrier_semaphore()

    def greet(where):
        pl.semaphore_signal(barrier, 1, device_id=where, device_id_type=pl.DeviceIdType.MESH)

    for where in (other_row, mate, far_dev, cross):
        greet(where)

    @pl.when(at_end)
    def _():
        greet(end_next)
        pl.semaphore_wait(barrier, 5)

    @pl.when(jnp.logical_not(at_end))
    def _():
        greet(mid_outer)
        greet(mid_other)
        pl.semaphore_wait(barrier, 6)

    def col_slot(j, half, index):
        before = sum(2 * parts[i].count for i in col_parts if i < j)
        return before + half * parts[j].count + index

    def col_own_copy(j, half, index, target):
        return pltpu.make_async_copy(
            parts[j].cut(grads[j], index, half, (2 * target + side,)),
            own[j].at[target, half, index],
            col_own.at[target, col_slot(j, half, index)],
        )

    def col_copy(j, half, index, target):
        slot = col_slot(j, half, index)
        return remote(
            parts[j].cut(grads[j], index, half, (2 * target + 1 - side,)),
            mate_in[j].at[target, half, index],
            col_send.at[target, slot],
            col_recv.at[target, slot],
            mate,
        )

    def x_copy(j, half, index):
        slot = col_slot(j, half, index)
        return remote(
            mate_in[j].at[1 - group, half, index],
            far_in[j].at[half, index],
            x_send.at[slot],
            x_recv.at[slot],
            far_dev,
        )

    def take_col(j, half, index):
        for target in range(2):
            col_own_copy(j, half, index, target).wait()
            col_copy(j, half, index, target).wait_recv()
            mate_in[j][target, half, index] = mate_in[j][target, half, index] + own[j][target, half, index]
        x_copy(j, half, index).start()

    def take_x(j, half, index):
        x_copy(j, half, index).wait_recv()
        far_in[j][half, index] = far_in[j][half, index] + mate_in[j][group, half, index]

    half_depth = normed_ref.shape[1] // 2
    gate_up, down = made
    units = parts[gate_up].count // 2

    def left_copies(unit, of_down):
        if of_down:
            source = act_ref.at[:, pl.ds(pl.multiple_of(unit * 256, 256), 256)]
            slot = (units + unit) % 2
            return [pltpu.make_async_copy(source, left.at[slot], left_sem.at[slot, 0])]
        slot = unit % 2
        copies = []
        for half in range(2):
            first = pl.multiple_of(half * half_depth + unit * 128, 128)
            target = left.at[slot, :, pl.ds(half * 128, 128)]
            copies.append(
                pltpu.make_async_copy(normed_ref.at[:, pl.ds(first, 128)], target, left_sem.at[slot, half])
            )
        return copies

    d_low_load = pltpu.make_async_copy(d_low_ref, right.at[:, pl.ds(0, d_low_ref.shape[1])], right_sem.at[1])
    d_gate_up_load = pltpu.make_async_copy(d_gate_up_ref, right, right_sem.at[0])

    def start_unit(j, unit):
        of_down = j == down
        part = parts[j]
        for copy in left_copies(unit, of_down):
            copy.wait()

        @pl.when(unit + 1 < part.count // 2)
        def _():
            for copy in left_copies(unit + 1, of_down):
                copy.start()

        if not of_down:
            @pl.when(unit + 1 == units)
            def _():
                for copy in left_copies(0, True):
                    copy.start()

        @pl.when(unit == 0)
        def _():
            (d_low_load if of_down else d_gate_up_load).wait()

        for chunk in range(2):
            index = 2 * unit + chunk

            @pl.when(index >= SLOTS)
            def _(index=index):
                row_copy(j, jnp.maximum(index - SLOTS, 0)).wait_send()

        slot = ((units + unit) if of_down else unit) % 2

        @pl.loop(0, left.shape[1] // 256)
        def _(block):
            here = pl.ds(pl.multiple_of(block * 256, 256), 256)
            left_t[:, here] = left[slot, here, :].T

    def tile(j, unit, number, targets):
        rows = parts[j].rows
        where = pl.ds(pl.multiple_of(number * 256, 256), 256)
        product = dot(left_t[...], right[:, where]).astype(BF)
        for place, (target, chunk, first_tile) in enumerate(targets):
            to = pl.ds(pl.multiple_of((number - first_tile) * 256, 256), 256)
            target[j][(2 * unit + chunk) % SLOTS, :, to] = product[place * rows : (place + 1) * rows]

    def make(j, unit, second):
        part = parts[j]
        if not second:
            start_unit(j, unit)
        if j == down:
            tiles = part.cols // 256
            first, target = (0, own) if second else (tiles, leaving)
            targets = [(target, 0, first), (target, 1, first)]
            pl.loop(first, first + tiles)(lambda number: tile(j, unit, number, targets))
        else:
            tiles = part.cols // 256
            targets = [(own, 0, 0), (own, 1, 0), (leaving, 0, 0), (leaving, 1, 0)]
            bounds = (tiles // 2, tiles) if second else (0, tiles // 2)
            pl.loop(*bounds)(lambda number: tile(j, unit, number, targets))
        if second and j != down:
            @pl.when(unit + 1 == units)
            def _():
                d_low_load.start()

        if second != (j == down):
            for chunk in range(2):
                row_copy(j, 2 * unit + chunk).start()

    def row_copy(j, index):
        slot = parts[j].base + index
        source = far_in[j].at[1, index] if parts[j].col else leaving[j].at[index % SLOTS]
        return remote(source, near[j].at[index], row_send.at[slot], row_recv.at[slot], other_row)

    def in_copy(j, index):
        slot = parts[j].base + index
        return remote(near[j].at[index], far[j].at[index], in_send.at[slot], far_recv.at[slot], end_next)

    def mid_copy(j, index):
        slot = parts[j].base + index
        return remote(far[j].at[index], near[j].at[index], mid_send.at[slot], wide_recv.at[slot], mid_other)

    def back_copy(j, index):
        slot = parts[j].base + index
        return remote(near[j].at[index], far[j].at[index], in_send.at[slot], far_recv.at[slot], mid_outer)

    def out_copy(j, index, source):
        slot = parts[j].base + index
        return pltpu.make_async_copy(source[j].at[index], parts[j].cut(outs[j], index, 0), out_sem.at[slot])

    def each(step, action):
        for j, part in enumerate(parts):
            index = step - part.base

            @pl.when((index >= 0) & (index < part.count))
            def _(j=j, index=index):
                action(j, index)

    def send_row(j, index):
        if parts[j].col:
            row_copy(j, index).start()
        else:
            @pl.when(index % 2 == 0)
            def _():
                make(j, index // 2, False)

            @pl.when(index % 2 == 1)
            def _():
                make(j, index // 2, True)

    def take_row(j, index):
        row_copy(j, index).wait_recv()
        mine = far_in[j][0, index] if parts[j].col else own[j][index % SLOTS]
        near[j][index] = near[j][index] + mine

        @pl.when(at_end)
        def _():
            in_copy(j, index).start()

    def take_far(j, index):
        back_copy(j, index).wait_recv()
        far[j][index] = far[j][index] + near[j][index]
        pl.semaphore_signal(free_sem, 1, device_id=mid_other, device_id_type=pl.DeviceIdType.MESH)
        pl.semaphore_wait(free_sem, 1)
        mid_copy(j, index).start()

    def take_wide(j, index):
        mid_copy(j, index).wait_recv()
        near[j][index] = near[j][index] + far[j][index]
        back_copy(j, index).start()
        out_copy(j, index, near).start()

    def take_back(j, index):
        in_copy(j, index).wait_recv()
        out_copy(j, index, far).start()

    def row_sent(j, index):
        @pl.when(jnp.logical_or(parts[j].col, index >= parts[j].count - SLOTS))
        def _():
            row_copy(j, index).wait_send()

    def finish_end(j, index):
        row_sent(j, index)
        in_copy(j, index).wait_send()
        out_copy(j, index, far).wait()

    def finish_mid(j, index):
        row_sent(j, index)
        mid_copy(j, index).wait_send()
        back_copy(j, index).wait_send()
        out_copy(j, index, near).wait()

    def small_copy(stage, source, where):
        return remote(small_sum.at[source], small_in.at[stage], small_send.at[stage], small_recv.at[stage], where)

    plane_hops = [small_copy(0, 0, mate), small_copy(1, 1, far_dev), small_copy(2, 2, other_row)]
    small_end = small_copy(3, 3, end_next)
    small_mid = small_copy(4, 4, mid_other)
    small_back = small_copy(3, 5, mid_outer)
    small_load = pltpu.make_async_copy(small_ref, small_sum.at[0], small_local.at[0])
    small_store = pltpu.make_async_copy(small_sum.at[5], small_out, small_local.at[1])

    span, width = mine_ref.shape[0] // 4, mine_ref.shape[1] // 2
    member = 2 * row + side
    dealt = []
    for index, (to_row, to_side, where) in enumerate(
        [(1 - row, side, other_row), (1 - row, 1 - side, cross), (row, 1 - side, mate), (row, side, None)]
    ):
        for high in range(2):
            piece = 7 - member if high else member
            first = pl.multiple_of(to_side * 2 * span + high * span, span)
            source = mine_ref.at[pl.ds(first, span), pl.ds((0 if index >= 2 else 1) * width, width)]
            target = dealt_ref.at[pl.ds(pl.multiple_of(piece * span, span), span), :]
            if where is None:
                dealt.append(pltpu.make_async_copy(source, target, deal_local.at[high]))
            else:
                dealt.append(remote(source, target, deal_send.at[index, high], deal_recv.at[index, high], where))

    total = sum(part.count for part in parts)
    for copy in left_copies(0, False):
        copy.start()
    d_gate_up_load.start()
    small_load.start()
    for copy in dealt[4:]:
        copy.start()
    for j in col_parts:
        for half in (1, 0):
            for index in range(parts[j].count):
                for target in range(2):
                    col_own_copy(j, half, index, target).start()
                    col_copy(j, half, index, target).start()

    @pl.loop(0, AHEAD)
    def _(step):
        each(step, send_row)

    pieces = [(j, half, index) for j in col_parts for half in (1, 0) for index in range(parts[j].count)]

    @pl.loop(0, total + LAG)
    def _(step):
        each(step + AHEAD, send_row)
        each(step, take_row)

        @pl.when(at_end)
        def _():
            each(step - LAG, take_back)

        @pl.when(jnp.logical_not(at_end))
        def _():
            each(step - FAR_LAG, take_far)
            each(step - WIDE_LAG, take_wide)

        @pl.when(step == total - AHEAD)
        def _():
            for copy in dealt[:4]:
                copy.start()

        for place, piece in enumerate(pieces):
            @pl.when(step == place + 1)
            def _(piece=piece):
                take_col(*piece)

            @pl.when(step == place + 5)
            def _(piece=piece):
                take_x(*piece)

        @pl.when(step == 0)
        def _():
            small_load.wait()
            plane_hops[0].start()

        for hop in range(3):
            @pl.when(step == hop + 1)
            def _(hop=hop):
                plane_hops[hop].wait_recv()
                small_sum[hop + 1] = small_sum[hop] + small_in[hop]
                if hop < 2:
                    plane_hops[hop + 1].start()

        @pl.when(at_end & (step == 3))
        def _():
            small_end.start()

        @pl.when(at_end & (step == 10))
        def _():
            small_end.wait_recv()
            small_sum[5] = small_in[3]
            small_store.start()

        @pl.when(jnp.logical_not(at_end) & (step == 5))
        def _():
            small_back.wait_recv()
            small_sum[4] = small_sum[3] + small_in[3]
            small_mid.start()

        @pl.when(jnp.logical_not(at_end) & (step == 7))
        def _():
            small_mid.wait_recv()
            small_sum[5] = small_sum[4] + small_in[4]
            small_back.start()
            small_store.start()

    for copy in plane_hops:
        copy.wait_send()
    small_store.wait()
    for copy in dealt:
        copy.wait()
    for j, half, index in pieces:
        for target in range(2):
            col_copy(j, half, index, target).wait_send()
        x_copy(j, half, index).wait_send()

    @pl.when(at_end)
    def _():
        small_end.wait_send()

        @pl.loop(0, total)
        def _(step):
            each(step, finish_end)

    @pl.when(jnp.logical_not(at_end))
    def _():
        small_mid.wait_send()
        small_back.wait_send()

        @pl.loop(0, total)
        def _(step):
            each(step, finish_mid)


def reduce_all(planes, normed, d_gate_up, act, d_low, grad_out, grad_project, small, mine):
    depth, width = normed.shape[1], act.shape[1]
    parts = [Part(0, 64, d_gate_up.shape[1], depth // 128, 0, False)]
    for rows, height, col in ((grad_out.shape[1] // 2, grad_out.shape[1], True),
                              (grad_project.shape[1] // 2, grad_project.shape[1], True), (128, width, False)):
        parts.append(Part(1, rows, depth // 2, height // rows, parts[-1].base + parts[-1].count, col))
    base = parts[-1].base + parts[-1].count
    shapes = [(part.count, part.rows, part.cols) for part in parts]
    col_shapes = [(2, *shape) for part, shape in zip(parts, shapes) if part.col]
    made_shapes = [(SLOTS, *shape[1:]) for part, shape in zip(parts, shapes) if not part.col]
    pieces = sum(shape[1] * 2 for shape in col_shapes)
    own_shapes = [
        (2, 2, *shape) if part.col else (SLOTS, *shape[1:]) for part, shape in zip(parts, shapes)
    ]
    anywhere = pl.BlockSpec(memory_space=pl.ANY)
    dma = pltpu.SemaphoreType.DMA
    tokens = normed.shape[0]
    inputs = (normed, d_gate_up, act, d_low, grad_out, grad_project, small, mine)
    return pl.pallas_call(
        functools.partial(reduce_kernel, parts, planes),
        out_shape=[jax.ShapeDtypeStruct((n * r, c), BF) for n, r, c in shapes]
        + [
            jax.ShapeDtypeStruct(small.shape, F32),
            jax.ShapeDtypeStruct((2 * mine.shape[0], mine.shape[1] // 2), BF),
        ],
        in_specs=[anywhere] * len(inputs),
        out_specs=[anywhere] * (len(parts) + 2),
        scratch_shapes=[pltpu.VMEM(shape, BF) for _ in range(2) for shape in shapes]
        + [pltpu.VMEM(shape, BF) for shape in own_shapes + made_shapes]
        + [pltpu.VMEM((2, *shape), BF) for shape in col_shapes]
        + [pltpu.VMEM(shape, BF) for shape in col_shapes]
        + [
            pltpu.VMEM((tokens, d_gate_up.shape[1]), BF),
            pltpu.VMEM((2, tokens, 256), BF),
            pltpu.VMEM((256, tokens), BF),
            dma((2,)),
            dma((2, 2)),
            pltpu.SemaphoreType.REGULAR,
        ]
        + [dma((base,)) for _ in range(7)]
        + [dma((2, pieces)), dma((2, pieces)), dma((2, pieces)), dma((pieces,)), dma((pieces,))]
        + [dma((2,)), dma((5,)), dma((5,))]
        + [pltpu.VMEM((5, *small.shape), F32), pltpu.VMEM((6, *small.shape), F32)]
        + [dma((3, 2)), dma((3, 2)), dma((2,))],
        compiler_params=pltpu.CompilerParams(
            collective_id=0, has_side_effects=True, vmem_limit_bytes=60 * 1024 * 1024
        ),
        name="reduce_grads",
    )(*inputs)


TILE = 256
STEPS = 8


def spread_kernel(forward, *refs):
    if forward:
        mine_ref, *weights = refs[:7]
        all_ref, gate_ref, up_ref, act_ref, out_ref = refs[7:12]
        rest = refs[12:]
    else:
        mine_ref, *weights = refs[:7]
        gate_ref, up_ref = refs[7:9]
        all_ref, d_gate_up_ref, out_ref = refs[9:12]
        rest = refs[12:]
    block, w_gate, w_up, w_down, kept, to_mate, from_mate, far_part, to_far, from_mate_far, far_sum, from_far = rest[:12]
    (
        weight_sem, block_sem, out_sem, mate_send, mate_recv, x_send, x_recv, pass_send, pass_recv,
        sum_send, sum_recv, part_send, part_recv, back_send, back_recv,
    ) = rest[12:27]
    stage = rest[27:]
    tokens, depth = mine_ref.shape
    quarter = tokens // 4
    width = w_gate.shape[1]
    group, side = lax.axis_index("group"), lax.axis_index("side")
    mate, far = {"side": 1 - side}, {"group": 1 - group}

    def remote(source, target, send, recv, where):
        return pltpu.make_async_remote_copy(
            source, target, send, recv, device_id=where, device_id_type=pl.DeviceIdType.MESH
        )

    barrier = pltpu.get_barrier_semaphore()
    for where in (mate, far):
        pl.semaphore_signal(barrier, 1, device_id=where, device_id_type=pl.DeviceIdType.MESH)

    half = depth // 2
    loads = []
    for index, (source, target) in enumerate(
        [
            (weights[0], w_gate.at[pl.ds(0, half), :]),
            (weights[1], w_gate.at[pl.ds(half, half), :]),
            (weights[2], w_up.at[pl.ds(0, half), :]),
            (weights[3], w_up.at[pl.ds(half, half), :]),
            (weights[4], w_down.at[:, pl.ds(0, half)]),
            (weights[5], w_down.at[:, pl.ds(half, half)]),
        ]
    ):
        loads.append(pltpu.make_async_copy(source, target, weight_sem.at[index]))
    order = loads if forward else loads[4:] + loads[:4]
    mine_copies = [
        pltpu.make_async_copy(
            mine_ref.at[pl.ds(i * 2 * quarter, 2 * quarter), :], block.at[i], block_sem.at[i]
        )
        for i in range(2)
    ]
    for copy in mine_copies:
        copy.start()
    for copy in order:
        copy.start()
    pl.semaphore_wait(barrier, 2)

    def piece(index):
        return mine_ref.at[pl.ds(index * quarter, quarter), :]

    def mate_copy(index):
        return remote(
            piece(index),
            block.at[2 + index // 2, pl.ds(index % 2 * quarter, quarter), :],
            mate_send.at[index],
            mate_recv.at[index],
            mate,
        )

    def x_copy(index):
        return remote(
            piece(index), block.at[4 + index, pl.ds(0, quarter), :], x_send.at[index], x_recv.at[index], far
        )

    def pass_copy(index):
        return remote(
            block.at[4 + index, pl.ds(0, quarter), :],
            block.at[4 + index, pl.ds(quarter, quarter), :],
            pass_send.at[index],
            pass_recv.at[index],
            mate,
        )

    def sum_copy(index):
        return remote(to_mate.at[index], from_mate.at[index], sum_send.at[index], sum_recv.at[index], mate)

    def part_copy(index):
        return remote(to_far.at[index], from_mate_far.at[index], part_send.at[index], part_recv.at[index], mate)

    def back_copy(index):
        return remote(far_sum.at[index], from_far.at[index], back_send.at[index], back_recv.at[index], far)

    x_copy(0).start()
    for index in range(4):
        mate_copy(index).start()
    x_copy(1).start()
    for copy in mine_copies:
        copy.wait()

    def emit(step, where, part):
        @pl.when(step < 2)
        def _():
            kept[jnp.minimum(step, 1), :, where] = part

        @pl.when((step >= 2) & (step < 4))
        def _():
            to_mate[jnp.clip(step - 2, 0, 1), :, where] = part.astype(BF)

        @pl.when(step >= 4)
        def _():
            far_part[jnp.maximum(step - 4, 0), :, where] = part[:quarter]
            to_far[jnp.maximum(step - 4, 0), :, where] = part[quarter:].astype(BF)

    def all_copy(step):
        return pltpu.make_async_copy(block.at[step], all_ref.at[step], out_sem.at[0, step])

    if forward:
        stage_gate, stage_up, stage_act = stage

        def saves(step):
            slot = step % 2
            return [
                pltpu.make_async_copy(stage_gate.at[slot], gate_ref.at[step], out_sem.at[1, step]),
                pltpu.make_async_copy(stage_up.at[slot], up_ref.at[step], out_sem.at[2, step]),
                pltpu.make_async_copy(stage_act.at[slot], act_ref.at[step], out_sem.at[3, step]),
            ]

        def fetches(step):
            return []

        def first_loads():
            for copy in loads[:4]:
                copy.wait()

        def second_loads():
            for copy in loads[4:]:
                copy.wait()

        def first_half(step):
            slot = step % 2

            @pl.loop(0, width // TILE)
            def _(tile):
                where = pl.ds(pl.multiple_of(tile * TILE, TILE), TILE)
                gate = dot(block[step], w_gate[:, where])
                up = dot(block[step], w_up[:, where])
                stage_gate[slot, :, where] = gate.astype(BF)
                stage_up[slot, :, where] = up.astype(BF)
                stage_act[slot, :, where] = (gate * up / (1.0 + jnp.exp(-gate))).astype(BF)

        def second_half(step):
            slot = step % 2

            @pl.loop(0, depth // TILE)
            def _(tile):
                where = pl.ds(pl.multiple_of(tile * TILE, TILE), TILE)
                emit(step, where, dot(stage_act[slot], w_down[:, where]))

    else:
        stage_gate, stage_up, stage_d, fetch_sem = stage

        def saves(step):
            return [
                pltpu.make_async_copy(stage_d.at[step % 2], d_gate_up_ref.at[step], out_sem.at[1, step])
            ]

        def fetches(step):
            slot = step % 2
            return [
                pltpu.make_async_copy(gate_ref.at[step], stage_gate.at[slot], fetch_sem.at[0, step]),
                pltpu.make_async_copy(up_ref.at[step], stage_up.at[slot], fetch_sem.at[1, step]),
            ]

        def first_loads():
            for copy in loads[4:]:
                copy.wait()

        def second_loads():
            for copy in loads[:4]:
                copy.wait()

        def first_half(step):
            slot = step % 2

            @pl.loop(0, width // TILE)
            def _(tile):
                first = pl.multiple_of(tile * TILE, TILE)
                where = pl.ds(first, TILE)
                d_act = dot(block[step], w_down[where, :], ((1,), (1,)))
                gate = stage_gate[slot, :, where].astype(F32)
                up = stage_up[slot, :, where].astype(F32)
                sig = 1.0 / (1.0 + jnp.exp(-gate))
                d_gate = d_act * up * sig * (1.0 + gate * (1.0 - sig))
                stage_d[slot, :, where] = d_gate.astype(BF)
                stage_d[slot, :, pl.ds(pl.multiple_of(width + first, TILE), TILE)] = (d_act * gate * sig).astype(BF)

        def second_half(step):
            slot = step % 2

            @pl.loop(0, depth // TILE)
            def _(tile):
                where = pl.ds(pl.multiple_of(tile * TILE, TILE), TILE)
                part = dot(stage_d[slot, :, :width], w_gate[where, :], ((1,), (1,)))
                part += dot(stage_d[slot, :, width:], w_up[where, :], ((1,), (1,)))
                emit(step, where, part)

    def finish_far(index):
        part_copy(index).wait_recv()
        total = far_part[index] + from_mate_far[index].astype(F32)
        far_sum[index] = total.astype(BF)
        back_copy(index).start()

    for copy in fetches(0):
        copy.start()

    @pl.loop(0, STEPS)
    def _(step):
        @pl.when((step == 2) | (step == 3))
        def _():
            index = jnp.clip(2 * (step - 2), 0, 2)
            mate_copy(index).wait_recv()
            mate_copy(index + 1).wait_recv()

        @pl.when(step >= 4)
        def _():
            index = jnp.maximum(step - 4, 0)
            x_copy(index).wait_recv()
            pass_copy(index).start()
            pass_copy(index).wait_recv()

        all_copy(step).start()
        for copy in fetches(step):
            copy.wait()

        if not forward:
            @pl.when(step < STEPS - 1)
            def _():
                for copy in fetches(jnp.minimum(step + 1, STEPS - 1)):
                    copy.start()

        @pl.when(step == 0)
        def _():
            first_loads()

        @pl.when(step >= 2)
        def _():
            for copy in saves(jnp.maximum(step - 2, 0)):
                copy.wait()

        first_half(step)

        @pl.when(step == 0)
        def _():
            second_loads()

        second_half(step)
        for copy in saves(step):
            copy.start()

        @pl.when((step == 1) | (step == 3))
        def _():
            x_copy(2 + step // 2).start()

        @pl.when((step >= 2) & (step < 4))
        def _():
            sum_copy(jnp.clip(step - 2, 0, 1)).start()

        @pl.when(step >= 4)
        def _():
            part_copy(jnp.maximum(step - 4, 0)).start()

        @pl.when(step >= 5)
        def _():
            finish_far(jnp.maximum(step - 5, 0))

    finish_far(3)
    for index in range(2):
        sum_copy(index).wait_recv()
        kept[index] = kept[index] + from_mate[index].astype(F32)
    results = []
    for index in range(4):
        back_copy(index).wait_recv()
        rows = pl.ds(index % 2 * quarter, quarter)
        kept[index // 2, rows, :] = kept[index // 2, rows, :] + from_far[index].astype(F32)
        if index % 2:
            copy = pltpu.make_async_copy(kept.at[index // 2], out_ref.at[index // 2], block_sem.at[index // 2])
            copy.start()
            results.append(copy)
    for copy in results:
        copy.wait()

    @pl.loop(0, STEPS)
    def _(step):
        all_copy(step).wait()

        @pl.when(step >= STEPS - 2)
        def _():
            for copy in saves(step):
                copy.wait()

        @pl.when(step < 4)
        def _():
            index = jnp.minimum(step, 3)
            mate_copy(index).wait_send()
            x_copy(index).wait_send()
            pass_copy(index).wait_send()
            part_copy(index).wait_send()
            back_copy(index).wait_send()

        @pl.when(step < 2)
        def _():
            sum_copy(jnp.minimum(step, 1)).wait_send()


def spread(forward, mine, weights, *kept):
    tokens, depth = mine.shape
    quarter, double = tokens // 4, tokens // 2
    width = weights[0].shape[1]
    anywhere = pl.BlockSpec(memory_space=pl.ANY)
    wide = jax.ShapeDtypeStruct((STEPS, double, width), BF)
    whole = jax.ShapeDtypeStruct((STEPS, double, depth), BF)
    out = jax.ShapeDtypeStruct((2, double, depth), F32)
    if forward:
        outs = [whole, wide, wide, wide, out]
        stage = [pltpu.VMEM((2, double, width), BF) for _ in range(3)]
    else:
        outs = [whole, jax.ShapeDtypeStruct((STEPS, double, 2 * width), BF), out]
        stage = [
            pltpu.VMEM((2, double, width), BF),
            pltpu.VMEM((2, double, width), BF),
            pltpu.VMEM((2, double, 2 * width), BF),
            pltpu.SemaphoreType.DMA((2, STEPS)),
        ]
    result = pl.pallas_call(
        functools.partial(spread_kernel, forward),
        out_shape=outs,
        in_specs=[anywhere] * (7 + len(kept)),
        out_specs=[anywhere] * len(outs),
        scratch_shapes=[
            pltpu.VMEM((STEPS, double, depth), BF),
            pltpu.VMEM((depth, width), BF),
            pltpu.VMEM((depth, width), BF),
            pltpu.VMEM((width, depth), BF),
            pltpu.VMEM((2, double, depth), F32),
            pltpu.VMEM((2, double, depth), BF),
            pltpu.VMEM((2, double, depth), BF),
            pltpu.VMEM((4, quarter, depth), F32),
            pltpu.VMEM((4, quarter, depth), BF),
            pltpu.VMEM((4, quarter, depth), BF),
            pltpu.VMEM((4, quarter, depth), BF),
            pltpu.VMEM((4, quarter, depth), BF),
            pltpu.SemaphoreType.DMA((6,)),
            pltpu.SemaphoreType.DMA((2,)),
            pltpu.SemaphoreType.DMA((4, STEPS)),
        ]
        + [pltpu.SemaphoreType.DMA((4,)) for _ in range(6)]
        + [pltpu.SemaphoreType.DMA((2,)) for _ in range(2)]
        + [pltpu.SemaphoreType.DMA((4,)) for _ in range(4)]
        + stage,
        compiler_params=pltpu.CompilerParams(
            collective_id=5 if forward else 2,
            has_side_effects=True,
            vmem_limit_bytes=60 * 1024 * 1024,
        ),
        name="spread" if forward else "spread_back",
    )(mine, *weights, *kept)
    return result


def feed_kernel(*refs):
    refs = list(refs)

    def take(number):
        taken = refs[:number]
        del refs[:number]
        return taken

    mine_ref, *weights = take(6)
    teacher_ref, hidden_ref, scale_ref = take(3)
    all_ref, gate_ref, up_ref, act_ref, target_ref = take(5)
    all_low_ref, d_gate_up_ref, d_result_ref, out_ref, block_out_ref = take(5)
    block, w_gate, w_up, w_down, kept, to_mate, from_mate, far_part, to_far, from_mate_far, far_sum, from_far = take(12)
    stage_gate, stage_up, stage_act = take(3)
    weight_sem, block_sem, out_sem, fetch_sem, result_sem = take(5)
    mate_send, mate_recv, x_send, x_recv, pass_send, pass_recv, sum_send, sum_recv = take(8)
    part_send, part_recv, back_send, back_recv = take(4)
    deal_send, deal_recv, deal_local, row_send, row_recv, plane_send, plane_recv = take(7)
    tokens, depth = mine_ref.shape
    quarter = tokens // 4
    width = w_gate.shape[1]
    half = depth // 2
    row = lax.axis_index("row")
    group, side = lax.axis_index("group"), lax.axis_index("side")
    mate, far = {"side": 1 - side}, {"group": 1 - group}
    other_row, cross = {"row": 1 - row}, {"row": 1 - row, "side": 1 - side}
    parity = lax.axis_index("dp") % 2
    next_plane = {"dp": lax.axis_index("dp") + 1 - 2 * parity}
    member = 2 * row + side

    def remote(source, target, send, recv, where):
        return pltpu.make_async_remote_copy(
            source, target, send, recv, device_id=where, device_id_type=pl.DeviceIdType.MESH
        )

    def local(source, target, sem):
        return pltpu.make_async_copy(source, target, sem)

    barrier = pltpu.get_barrier_semaphore()
    greeted = [mate, far, other_row, cross, next_plane]
    for where in greeted:
        pl.semaphore_signal(barrier, 1, device_id=where, device_id_type=pl.DeviceIdType.MESH)

    mine_copies = [
        local(mine_ref.at[pl.ds(i * 2 * quarter, 2 * quarter), :], block.at[i], block_sem.at[i]) for i in range(2)
    ]
    loads = [
        local(weights[0], w_gate.at[pl.ds(0, half), :], weight_sem.at[0]),
        local(weights[1], w_gate.at[pl.ds(half, half), :], weight_sem.at[1]),
        local(weights[2], w_up.at[pl.ds(0, half), :], weight_sem.at[2]),
        local(weights[3], w_up.at[pl.ds(half, half), :], weight_sem.at[3]),
        local(weights[4], w_down.at[:, pl.ds(0, half)], weight_sem.at[4]),
    ]
    for copy in mine_copies + loads:
        copy.start()

    down_chunks = []
    rows = width // 8
    for index in range(4):
        here = pl.ds(pl.multiple_of((4 * parity + index) * rows, 16), rows)
        place = w_down.at[here, pl.ds(half, half)]
        down_chunks.append(
            (
                remote(weights[4].at[here, :], place, row_send.at[index], row_recv.at[index], other_row),
                remote(place, place, plane_send.at[index], plane_recv.at[index], next_plane),
            )
        )

    def deals(outward):
        sent, own = [], []
        for index, (to_row, to_side, where) in enumerate(
            [(1 - row, side, other_row), (1 - row, 1 - side, cross), (row, 1 - side, mate), (row, side, None)]
        ):
            slot = 0 if index >= 2 else 1
            there = 2 * to_row + to_side if outward == 0 else member
            for high in range(2):
                piece = 7 - there if high else there
                whole = pl.ds(pl.multiple_of(piece * quarter, quarter), quarter), slice(None)
                columns = pl.ds(slot * half, half)
                if outward == 0:
                    first = pl.multiple_of(side * 2 * quarter + high * quarter, quarter)
                    source, target = teacher_ref.at[whole], target_ref.at[pl.ds(first, quarter), columns]
                else:
                    source = to_mate.at[to_side, pl.ds(high * quarter, quarter), columns]
                    target = block_out_ref.at[whole]
                if where is None:
                    own.append(local(source, target, deal_local.at[outward, high]))
                else:
                    sems = deal_send.at[outward, index, high], deal_recv.at[outward, index, high]
                    sent.append(remote(source, target, *sems, where))
        return sent, own

    teacher_sent, teacher_own = deals(0)
    result_sent, result_own = deals(1)

    def piece(phase, index):
        if phase == 0:
            return mine_ref.at[pl.ds(index * quarter, quarter), :]
        return block.at[index // 2, pl.ds(index % 2 * quarter, quarter), :]

    def mate_copy(phase, index):
        target = block.at[2 + index // 2, pl.ds(index % 2 * quarter, quarter), :]
        return remote(piece(phase, index), target, mate_send.at[phase, index], mate_recv.at[phase, index], mate)

    def x_copy(phase, index):
        target = block.at[4 + index, pl.ds(0, quarter), :]
        return remote(piece(phase, index), target, x_send.at[phase, index], x_recv.at[phase, index], far)

    def pass_copy(phase, index):
        return remote(
            block.at[4 + index, pl.ds(0, quarter), :],
            block.at[4 + index, pl.ds(quarter, quarter), :],
            pass_send.at[phase, index],
            pass_recv.at[phase, index],
            mate,
        )

    def sum_copy(phase, index):
        return remote(
            to_mate.at[index], from_mate.at[index], sum_send.at[phase, index], sum_recv.at[phase, index], mate
        )

    def part_copy(phase, index):
        return remote(
            to_far.at[index], from_mate_far.at[index], part_send.at[phase, index], part_recv.at[phase, index], mate
        )

    def back_copy(phase, index):
        return remote(
            far_sum.at[index], from_far.at[index], back_send.at[phase, index], back_recv.at[phase, index], far
        )

    def all_copy(phase, step):
        return local(block.at[step], (all_ref, all_low_ref)[phase].at[step], out_sem.at[4 * phase, step])

    def saves(step):
        return [
            local(stage_gate.at[step % 2], gate_ref.at[step], out_sem.at[1, step]),
            local(stage_up.at[step % 2], up_ref.at[step], out_sem.at[2, step]),
            local(stage_act.at[step], act_ref.at[step], out_sem.at[3, step]),
        ]

    def back_saves(step):
        slot = 2 * (step % 2)
        return [
            local(stage_act.at[slot + i], d_gate_up_ref.at[step, :, pl.ds(i * width, width)], out_sem.at[5 + i, step])
            for i in range(2)
        ]

    def fetches(step):
        return [
            local(gate_ref.at[step], stage_gate.at[step % 2], fetch_sem.at[0, step]),
            local(up_ref.at[step], stage_up.at[step % 2], fetch_sem.at[1, step]),
        ]

    def emit(step, where, part):
        @pl.when(step < 2)
        def _():
            kept[jnp.minimum(step, 1), :, where] = part

        @pl.when((step >= 2) & (step < 4))
        def _():
            to_mate[jnp.clip(step - 2, 0, 1), :, where] = part.astype(BF)

        @pl.when(step >= 4)
        def _():
            far_part[jnp.maximum(step - 4, 0), :, where] = part[:quarter]
            to_far[jnp.maximum(step - 4, 0), :, where] = part[quarter:].astype(BF)

    def tiles(first, last, action):
        @pl.loop(first, last)
        def _(tile):
            action(pl.ds(pl.multiple_of(tile * TILE, TILE), TILE), pl.multiple_of(tile * TILE, TILE))

    def multiply_in(step):
        slot = step % 2

        def action(where, first):
            gate = dot(block[step], w_gate[:, where])
            up = dot(block[step], w_up[:, where])
            stage_gate[slot, :, where] = gate.astype(BF)
            stage_up[slot, :, where] = up.astype(BF)
            stage_act[step, :, where] = (gate * up / (1.0 + jnp.exp(-gate))).astype(BF)

        tiles(0, width // TILE, action)

    def multiply_out(step, first=0, last=depth // TILE):
        tiles(first, last, lambda where, _: emit(step, where, dot(stage_act[step], w_down[:, where])))

    def multiply_back_in(step):
        slot = step % 2

        def action(where, first):
            d_act = dot(block[step], w_down[where, :], ((1,), (1,)))
            gate = stage_gate[slot, :, where].astype(F32)
            up = stage_up[slot, :, where].astype(F32)
            sig = 1.0 / (1.0 + jnp.exp(-gate))
            d_gate = d_act * up * sig * (1.0 + gate * (1.0 - sig))
            stage_act[2 * slot, :, where] = d_gate.astype(BF)
            stage_act[2 * slot + 1, :, where] = (d_act * gate * sig).astype(BF)

        tiles(0, width // TILE, action)

    def multiply_back_out(step):
        slot = 2 * (step % 2)

        def action(where, first):
            part = dot(stage_act[slot], w_gate[where, :], ((1,), (1,)))
            part += dot(stage_act[slot + 1], w_up[where, :], ((1,), (1,)))
            emit(step, where, part)

        tiles(0, depth // TILE, action)

    def finish_far(phase, index):
        part_copy(phase, index).wait_recv()
        total = far_part[index] + from_mate_far[index].astype(F32)
        far_sum[index] = total.astype(BF)
        if phase == 0:
            all_copy(0, 4 + index).wait()
            pass_copy(0, index).wait_send()
        back_copy(phase, index).start()

    def arrive(phase, step):
        @pl.when((step == 2) | (step == 3))
        def _():
            index = jnp.clip(2 * (step - 2), 0, 2)
            mate_copy(phase, index).wait_recv()
            mate_copy(phase, index + 1).wait_recv()

        @pl.when(step >= 4)
        def _():
            index = jnp.maximum(step - 4, 0)
            x_copy(phase, index).wait_recv()
            pass_copy(phase, index).start()
            pass_copy(phase, index).wait_recv()

        all_copy(phase, step).start()

    pl.semaphore_wait(barrier, len(greeted))
    for over_row, _ in down_chunks:
        over_row.start()
    x_copy(0, 0).start()
    for index in range(4):
        mate_copy(0, index).start()
    x_copy(0, 1).start()
    for copy in teacher_sent + teacher_own:
        copy.start()
    for copy in mine_copies:
        copy.wait()

    @pl.loop(0, STEPS)
    def _(step):
        @pl.when(step == 7)
        def _():
            finish_far(0, 2)

        arrive(0, step)

        @pl.when(step == 0)
        def _():
            for copy in loads:
                copy.wait()

        @pl.when(step >= 2)
        def _():
            for copy in saves(jnp.maximum(step - 2, 0)):
                copy.wait()

        multiply_in(step)

        @pl.when(step < 6)
        def _():
            multiply_out(step, 0, half // TILE)

        for index in range(4):
            @pl.when(step == index + 1)
            def _(index=index):
                down_chunks[index][0].wait_recv()
                down_chunks[index][1].start()

        @pl.when(step == 5)
        def _():
            for _, over_planes in down_chunks:
                over_planes.wait_recv()
            pl.loop(4, 6)(lambda early: multiply_out(early, half // TILE))
            part_copy(0, 0).start()
            part_copy(0, 1).start()
            pl.loop(2, 4)(lambda early: multiply_out(early, half // TILE))
            for index in range(2):
                all_copy(0, 2 + index).wait()
                sum_copy(0, index).start()
            finish_far(0, 0)
            finish_far(0, 1)
            pl.loop(0, 2)(lambda early: multiply_out(early, half // TILE))

        @pl.when(step >= 6)
        def _():
            multiply_out(step)
            part_copy(0, jnp.maximum(step - 4, 0)).start()

        for copy in saves(step):
            copy.start()

        @pl.when((step == 1) | (step == 3))
        def _():
            x_copy(0, 2 + step // 2).start()

    for copy in teacher_own:
        copy.wait()
    for copy in teacher_sent:
        copy.wait_recv()
    result_loads = []
    for index in range(4):
        if index == 3:
            finish_far(0, 3)
        part_copy(0, index).wait_send()
        here = pl.ds(index * quarter, quarter)
        result_loads.append(
            [
                local(target_ref.at[here, :], to_far.at[index], result_sem.at[0, index]),
                local(hidden_ref.at[here, :], far_part.at[index], result_sem.at[1, index]),
            ]
        )
        for copy in result_loads[-1]:
            copy.start()
    for index in range(2):
        all_copy(0, index).wait()
        sum_copy(0, index).wait()
    for step in (STEPS - 2, STEPS - 1):
        for copy in saves(step):
            copy.wait()
    for copy in fetches(0):
        copy.start()
    scale = scale_ref[0]
    d_result_saves = []
    for index in range(4):
        back_copy(0, index).wait_recv()
        for copy in result_loads[index]:
            copy.wait()
        here = pl.ds(index % 2 * quarter, quarter)

        def action(where, first):
            total = kept[index // 2, here, where] + from_mate[index // 2, here, where].astype(F32)
            total = total + from_far[index, :, where].astype(F32)
            result = far_part[index, :, where] + total
            d_result = scale * (result - to_far[index, :, where].astype(F32))
            to_mate[index // 2, here, where] = result.astype(BF)
            kept[index // 2, here, where] = d_result
            block[index // 2, here, where] = d_result.astype(BF)

        tiles(0, depth // TILE, action)
        x_copy(1, index).start()
        mate_copy(1, index).start()
        if index % 2:
            copy = local(kept.at[index // 2], d_result_ref.at[index // 2], block_sem.at[index // 2])
            copy.start()
            d_result_saves.append(copy)
    for copy in result_sent + result_own:
        copy.start()
    for index in range(4):
        mate_copy(0, index).wait_send()
        x_copy(0, index).wait_send()
        back_copy(0, index).wait_send()

    @pl.loop(0, STEPS)
    def _(step):
        @pl.when(step >= 5)
        def _():
            finish_far(1, jnp.maximum(step - 5, 0))

        arrive(1, step)
        for copy in fetches(step):
            copy.wait()

        @pl.when(step < STEPS - 1)
        def _():
            for copy in fetches(jnp.minimum(step + 1, STEPS - 1)):
                copy.start()

        @pl.when(step >= 2)
        def _():
            for copy in back_saves(jnp.maximum(step - 2, 0)):
                copy.wait()

        multiply_back_in(step)

        @pl.when(step == 0)
        def _():
            for copy in d_result_saves:
                copy.wait()

        @pl.when(step == 2)
        def _():
            for copy in result_own:
                copy.wait()
            for copy in result_sent:
                copy.wait_send()

        multiply_back_out(step)
        for copy in back_saves(step):
            copy.start()

        @pl.when((step >= 2) & (step < 4))
        def _():
            sum_copy(1, jnp.clip(step - 2, 0, 1)).start()

        @pl.when(step >= 4)
        def _():
            part_copy(1, jnp.maximum(step - 4, 0)).start()

    finish_far(1, 3)
    for index in range(2):
        sum_copy(1, index).wait_recv()
        kept[index] = kept[index] + from_mate[index].astype(F32)
    results = []
    for index in range(4):
        back_copy(1, index).wait_recv()
        here = pl.ds(index % 2 * quarter, quarter)
        kept[index // 2, here, :] = kept[index // 2, here, :] + from_far[index].astype(F32)
        if index % 2:
            results.append(local(kept.at[index // 2], out_ref.at[index // 2], block_sem.at[index // 2]))
            results[-1].start()
    for copy in results:
        copy.wait()
    for copy in result_sent:
        copy.wait_recv()
    for copy in teacher_sent:
        copy.wait_send()
    for over_row, over_planes in down_chunks:
        over_row.wait_send()
        over_planes.wait_send()

    @pl.loop(0, STEPS)
    def _(step):
        all_copy(1, step).wait()

        @pl.when(step >= STEPS - 2)
        def _():
            for copy in back_saves(step):
                copy.wait()

        @pl.when(step < 4)
        def _():
            index = jnp.minimum(step, 3)
            for copy in (mate_copy, x_copy, pass_copy, part_copy, back_copy):
                copy(1, index).wait_send()

        @pl.when(step < 2)
        def _():
            sum_copy(1, jnp.minimum(step, 1)).wait_send()


def feed(mine, weights, teacher, hidden, scale):
    tokens, depth = mine.shape
    quarter, double = tokens // 4, tokens // 2
    width = weights[0].shape[1]
    anywhere = pl.BlockSpec(memory_space=pl.ANY)
    shape = jax.ShapeDtypeStruct
    wide, whole = shape((STEPS, double, width), BF), shape((STEPS, double, depth), BF)
    own = shape((2, double, depth), F32)
    outs = [
        whole, wide, wide, wide, shape((tokens, depth), BF),
        whole, shape((STEPS, double, 2 * width), BF), own, own, shape((2 * tokens, depth // 2), BF),
    ]
    dma = pltpu.SemaphoreType.DMA
    return pl.pallas_call(
        feed_kernel,
        out_shape=outs,
        in_specs=[anywhere] * 8 + [pl.BlockSpec(memory_space=pltpu.SMEM)],
        out_specs=[anywhere] * len(outs),
        scratch_shapes=[
            pltpu.VMEM((STEPS, double, depth), BF),
            pltpu.VMEM((depth, width), BF),
            pltpu.VMEM((depth, width), BF),
            pltpu.VMEM((width, depth), BF),
            pltpu.VMEM((2, double, depth), F32),
            pltpu.VMEM((2, double, depth), BF),
            pltpu.VMEM((2, double, depth), BF),
            pltpu.VMEM((4, quarter, depth), F32),
            pltpu.VMEM((4, quarter, depth), BF),
            pltpu.VMEM((4, quarter, depth), BF),
            pltpu.VMEM((4, quarter, depth), BF),
            pltpu.VMEM((4, quarter, depth), BF),
            pltpu.VMEM((2, double, width), BF),
            pltpu.VMEM((2, double, width), BF),
            pltpu.VMEM((STEPS, double, width), BF),
            dma((5,)), dma((2,)), dma((7, STEPS)), dma((2, STEPS)), dma((2, 4)),
            dma((2, 4)), dma((2, 4)), dma((2, 4)), dma((2, 4)), dma((2, 4)), dma((2, 4)), dma((2, 2)), dma((2, 2)),
            dma((2, 4)), dma((2, 4)), dma((2, 4)), dma((2, 4)),
            dma((2, 3, 2)), dma((2, 3, 2)), dma((2, 2)), dma((4,)), dma((4,)), dma((4,)), dma((4,)),
        ],
        compiler_params=pltpu.CompilerParams(
            collective_id=1, has_side_effects=True, vmem_limit_bytes=60 * 1024 * 1024
        ),
        name="feed_forward",
    )(mine, *weights, teacher, hidden, scale)


def front_kernel(*refs):
    refs = list(refs)

    def take(number):
        taken = refs[:number]
        del refs[:number]
        return taken

    tokens_ref, w_project_ref, w_out_ref, gains_ref, gate_ref, up_ref = take(6)
    cos_ref, sin_ref, query_gain_ref, key_gain_ref = take(4)
    (
        states_out, normed_out, raw_out, query_out, key_out, pair_out, mixed_out, logs_out, hidden_out, normed_two_out,
        w_project_out, w_out_out, gate_out, up_out, gains_out,
    ) = take(15)
    states, normed, w_project, raw, key_raw, query, pair_own, pair, key_n, mixed_t, logs, mixed = take(12)
    w_out, hidden, gains = take(3)
    token_send, token_recv, token_local = take(3)
    project_send, project_recv, out_send, out_recv, gain_send, gain_recv = take(6)
    pair_send, pair_recv, row_send, row_recv, plane_send, plane_recv, local, store = take(8)

    plane, row = lax.axis_index("dp"), lax.axis_index("row")
    group, side = lax.axis_index("group"), lax.axis_index("side")
    other_row, mate, far = {"row": 1 - row}, {"side": 1 - side}, {"group": 1 - group}
    cross = {"row": 1 - row, "side": 1 - side}
    parity = plane % 2
    next_plane = {"dp": plane + 1 - 2 * parity}
    shard, width = tokens_ref.shape
    mine, depth = states.shape
    pieces = 8
    span = shard // pieces
    member = 2 * row + side
    kv_rows = key_raw.shape[0]

    def remote(source, target, send, recv, where):
        return pltpu.make_async_remote_copy(
            source, target, send, recv, device_id=where, device_id_type=pl.DeviceIdType.MESH
        )

    barrier = pltpu.get_barrier_semaphore()
    for where in (other_row, mate, far, cross, next_plane):
        pl.semaphore_signal(barrier, 1, device_id=where, device_id_type=pl.DeviceIdType.MESH)

    def token_copies(to_row, to_side, index, where):
        target_member = 2 * to_row + to_side
        slot = 1 if to_row is not row else 0
        copies = []
        for high in range(2):
            piece = pieces - 1 - target_member if high else target_member
            source = tokens_ref.at[pl.ds(pl.multiple_of(piece * span, span), span), :]
            first = pl.multiple_of(side * 2 * span + high * span, span)
            target = states.at[pl.ds(first, span), pl.ds(slot * width, width)]
            if where is None:
                copies.append(pltpu.make_async_copy(source, target, token_local.at[high]))
            else:
                sems = token_send.at[index, high], token_recv.at[index, high]
                copies.append(remote(source, target, *sems, where))
        return copies

    own_tokens = token_copies(row, side, 0, None)
    other = 1 - row
    sent_tokens = token_copies(other, side, 0, other_row)
    sent_tokens += token_copies(other, 1 - side, 1, cross)
    sent_tokens += token_copies(row, 1 - side, 2, mate)

    me, far_col = 2 * group + side, 2 * (1 - group) + side

    class Spread:
        def __init__(self, source, place, send, recv):
            self.copies = []

            def add(origin, target, where):
                index = len(self.copies)
                self.copies.append(remote(origin, target, send.at[index], recv.at[index], where))
                return self.copies[-1]

            here, there = parity, 1 - parity
            rows = source.shape[0] // 2
            first_half = source.at[pl.ds(pl.multiple_of(here * rows, 16), rows), :]
            self.to_row = add(first_half, place(me, 1, here), other_row)
            self.to_plane = add(place(me, 1, here), place(me, 1, here), next_plane)
            self.to_far = [add(source, place(me, 0, None), far)]
            self.to_far += [add(place(me, 1, half), place(me, 1, half), far) for half in (here, there)]
            self.to_mate = [add(source, place(me, 0, None), mate)]
            self.to_mate += [add(place(me, 1, half), place(me, 1, half), mate) for half in (here, there)]
            self.to_mate += [add(place(far_col, 0, None), place(far_col, 0, None), mate)]
            self.to_mate += [
                add(place(far_col, 1, half), place(far_col, 1, half), mate) for half in (here, there)
            ]

        def first(self):
            self.to_row.start()
            self.to_far[0].start()
            self.to_mate[0].start()

        def row_in(self):
            self.to_row.wait_recv()
            for copy in (self.to_plane, self.to_far[1], self.to_mate[1]):
                copy.start()

        def plane_in(self):
            self.to_plane.wait_recv()
            self.to_far[2].start()
            self.to_mate[2].start()

        def far_in(self, index):
            self.to_far[index].wait_recv()
            self.to_mate[3 + index].start()

        def mate_in(self, first, last):
            for copy in self.to_mate[first:last]:
                copy.wait_recv()

        def sent(self):
            for copy in self.copies:
                copy.wait_send()

    q_width = w_out_ref.shape[0]

    def project_place(col, slot, half):
        if half is None:
            return w_project.at[col, slot]
        return w_project.at[col, slot, pl.ds(pl.multiple_of(half * (width // 2), 16), width // 2), :]

    def out_place(col, slot, half):
        first, rows = col * q_width, q_width
        if half is not None:
            rows = q_width // 2
            first = first + half * rows
        return w_out.at[pl.ds(pl.multiple_of(first, 16), rows), pl.ds(slot * width, width)]

    project = Spread(w_project_ref, project_place, project_send, project_recv)
    output = Spread(w_out_ref, out_place, out_send, out_recv)
    own_project = pltpu.make_async_copy(w_project_ref, w_project.at[me, 0], local.at[0])
    own_output = pltpu.make_async_copy(w_out_ref, out_place(me, 0, None), local.at[1])
    own_gains = pltpu.make_async_copy(gains_ref, gains.at[0], local.at[2])
    sent_gains = remote(gains_ref, gains.at[1], gain_send.at[0], gain_recv.at[0], other_row)

    chunks = []
    for index, (source, target) in enumerate([(gate_ref, gate_out), (up_ref, up_out)]):
        rows = source.shape[0] // 4
        for part in range(2):
            here = pl.ds(pl.multiple_of((2 * parity + part) * rows, 64), rows)
            slot = 2 * index + part
            over_row = remote(source.at[here, :], target.at[here, :], row_send.at[slot], row_recv.at[slot], other_row)
            over_planes = remote(
                target.at[here, :], target.at[here, :], plane_send.at[slot], plane_recv.at[slot], next_plane
            )
            chunks.append((over_row, over_planes))

    def pass_on(index):
        chunks[index][0].wait_recv()
        chunks[index][1].start()

    own_copies = [own_gains, *own_tokens, own_project, own_output]
    for copy in own_copies:
        copy.start()
    pl.semaphore_wait(barrier, 5)
    sent_gains.start()
    project.first()
    for copy in sent_tokens:
        copy.start()
    output.to_row.start()
    chunks[0][0].start()
    for copy in own_copies:
        copy.wait()
    sent_gains.wait_recv()
    project.row_in()
    for copy in sent_tokens:
        copy.wait_recv()

    stores = []

    def save(source, target):
        copy = pltpu.make_async_copy(source, target, store.at[len(stores)])
        copy.start()
        stores.append(copy)
        return copy

    block = mine // 4

    @pl.loop(0, 4)
    def _(index):
        here = pl.ds(pl.multiple_of(index * block, block), block)
        values = states[here, :].astype(F32)
        inverse = lax.rsqrt(jnp.mean(values * values, axis=1, keepdims=True) + EPSILON)
        for slot in range(2):
            part = values[:, slot * width : (slot + 1) * width] * inverse
            normed[here, slot * width : (slot + 1) * width] = (part * gains[slot, 0:1, :]).astype(BF)

    save(states, states_out)
    normed_saved = save(normed, normed_out)
    save(gains, gains_out)

    def project_col(col):
        part = dot(normed[:, :width], w_project[col, 0]) + dot(normed[:, width:], w_project[col, 1])
        part = part.T
        heads = q_width // HD
        for head in range(heads):
            raw[col * heads + head] = part[head * HD : (head + 1) * HD]
        k_width = kv_rows // 4
        first = pl.multiple_of(col * k_width, 16)
        key_raw[pl.ds(first, k_width), :] = part[q_width : q_width + k_width].astype(BF)
        first = pl.multiple_of(kv_rows + col * k_width, 16)
        pair_own[pl.ds(first, k_width), :] = part[q_width + k_width :].astype(BF)

    project.plane_in()
    project.far_in(0)
    project_col(me)
    project.mate_in(0, 3)
    project_col(2 * group + 1 - side)
    project.far_in(1)
    project.far_in(2)
    project_col(far_col)
    project.mate_in(3, 6)
    project_col(2 * (1 - group) + 1 - side)
    save(raw, raw_out)
    save(key_raw, key_out)
    save(w_project, w_project_out)

    cosine, sine = cos_ref[...], sin_ref[...]

    def turned(values, gain):
        values = values * lax.rsqrt(jnp.mean(values * values, axis=0, keepdims=True) + EPSILON) * gain
        first, second = values[: HD // 2], values[HD // 2 :]
        return jnp.concatenate([first * cosine - second * sine, second * cosine + first * sine], axis=0)

    for head in range(kv_rows // HD):
        cut = slice(head * HD, (head + 1) * HD)
        pair_own[cut, :] = turned(key_raw[cut, :].astype(F32), key_gain_ref[...]).astype(BF)

    def places(who):
        starts = [who, pieces - 1 - who, pieces + who, 2 * pieces - 1 - who]
        return [pair.at[:, pl.ds(pl.multiple_of(start * span, span), span)] for start in starts]

    for index, place in enumerate(places(member)):
        place[...] = pair_own[:, index * span : (index + 1) * span]
    to_mate, to_row, passed = [], [], []
    for index, place in enumerate(places(member)):
        to_row.append(remote(place, place, pair_send.at[0, index], pair_recv.at[0, index], other_row))
        to_mate.append(remote(place, place, pair_send.at[1, index], pair_recv.at[1, index], mate))
    for index, place in enumerate(places(2 * (1 - row) + side)):
        passed.append(remote(place, place, pair_send.at[2, index], pair_recv.at[2, index], mate))
    for copy in to_row + to_mate:
        copy.start()
    output.to_far[0].start()
    output.to_mate[0].start()
    chunks[1][0].start()
    output.row_in()

    @pl.loop(0, raw.shape[0])
    def _(head):
        values = turned(raw[head], query_gain_ref[...]).astype(BF)
        query[head] = values * BF(1.0 / math.sqrt(HD))

    for index in range(4):
        to_row[index].wait_recv()
        passed[index].start()
    chunks[2][0].start()
    output.plane_in()
    pass_on(0)
    for index in range(4):
        to_mate[index].wait_recv()
        passed[index].wait_recv()
    chunks[3][0].start()
    output.far_in(0)
    output.far_in(1)

    firsts = [member, pieces - 1 - member, pieces + member, 2 * pieces - 1 - member]
    rows = REP * span
    ones = jnp.ones((16, KEYS), BF)

    @pl.loop(0, kv_rows // HD)
    def _(head):
        key_n[...] = pair[pl.ds(pl.multiple_of(head * HD, HD), HD), :].T
        value_rows = pl.ds(pl.multiple_of(kv_rows + head * HD, HD), HD)
        for index in range(4):
            cut = slice(index * span, (index + 1) * span)
            query_here = jnp.concatenate([query[head * REP + rep, :, cut] for rep in range(REP)], axis=1)
            first_query = firsts[index] * span
            full, last = tiles_of(first_query)

            def tile(where, accum, masked):
                first_key = pl.multiple_of(where * KEYS, KEYS)
                expo = jnp.exp(dot(key_n[pl.ds(first_key, KEYS), :], query_here))
                if masked:
                    expo = jnp.where(allowed(first_query, first_key, span, rows), expo, 0.0)
                value = jnp.concatenate([pair[value_rows, pl.ds(first_key, KEYS)], ones], axis=0)
                return accum + dot(value, expo.astype(BF))

            accum = tile(last, jnp.zeros((HD + 16, rows), F32), True)
            least = (0, PROMPT // KEYS // 2, PROMPT // KEYS, PROMPT // KEYS)[index]
            for where in range(least):
                accum = tile(where, accum, False)
            if index < 2:
                accum = lax.fori_loop(least, full, lambda where, total: tile(where, total, False), accum)
            total = accum[HD : HD + 1]
            result = accum[:HD] / total
            log = jnp.log(total)
            for rep in range(REP):
                part = slice(rep * span, (rep + 1) * span)
                mixed_t[pl.ds(pl.multiple_of((head * REP + rep) * HD, HD), HD), cut] = result[:, part]
                logs[head, rep : rep + 1, cut] = log[:, part]

        @pl.when(head == 2)
        def _():
            output.far_in(2)

        for number, index in ((1, 1), (3, 2)):
            @pl.when(head == number)
            def _(index=index):
                pass_on(index)

    save(query, query_out)
    save(mixed_t, mixed_out)
    save(logs, logs_out)
    save(pair, pair_out)
    pass_on(3)
    output.mate_in(0, 6)
    save(w_out, w_out_out)

    @pl.loop(0, mixed_t.shape[0] // 128)
    def _(index):
        here = pl.ds(pl.multiple_of(index * 128, 128), 128)
        mixed[:, here] = mixed_t[here, :].astype(BF).T

    @pl.loop(0, depth // TILE)
    def _(index):
        here = pl.ds(pl.multiple_of(index * TILE, TILE), TILE)
        hidden[:, here] = states[:, here].astype(F32) + dot(mixed[...], w_out[:, here])

    normed_saved.wait()

    @pl.loop(0, 4)
    def _(index):
        here = pl.ds(pl.multiple_of(index * block, block), block)
        values = hidden[here, :]
        inverse = lax.rsqrt(jnp.mean(values * values, axis=1, keepdims=True) + EPSILON)
        for slot in range(2):
            part = values[:, slot * width : (slot + 1) * width] * inverse
            normed[here, slot * width : (slot + 1) * width] = (part * gains[slot, 1:2, :]).astype(BF)

    save(hidden, hidden_out)
    save(normed, normed_two_out)
    for copy in stores:
        if copy is not normed_saved:
            copy.wait()
    sent_gains.wait_send()
    for copy in sent_tokens + to_row + to_mate + passed:
        copy.wait_send()
    project.sent()
    output.sent()
    for over_row, over_planes in chunks:
        over_row.wait_send()
        over_planes.wait_recv()
        over_planes.wait_send()


def front(tokens, w_project, w_out, gains, w_gate, w_up, cosine, sine, query_gain, key_gain):
    shard, width = tokens.shape
    mine, depth = shard // 2, 2 * width
    q_width, columns = w_out.shape[0], w_project.shape[1]
    kv_rows = KVH * HD
    anywhere = pl.BlockSpec(memory_space=pl.ANY)
    inside = pl.BlockSpec(memory_space=pltpu.VMEM)
    dma = pltpu.SemaphoreType.DMA
    shape = jax.ShapeDtypeStruct
    return pl.pallas_call(
        front_kernel,
        out_shape=[
            shape((mine, depth), BF),
            shape((mine, depth), BF),
            shape((QH, HD, mine), F32),
            shape((QH, HD, mine), BF),
            shape((kv_rows, mine), BF),
            shape((2 * kv_rows, GROUP), BF),
            shape((QH * HD, mine), F32),
            shape((KVH, REP, mine), F32),
            shape((mine, depth), F32),
            shape((mine, depth), BF),
            shape((4, 2, width, columns), BF),
            shape((4 * q_width, depth), BF),
            shape(w_gate.shape, BF),
            shape(w_up.shape, BF),
            shape((2, 2, width), F32),
        ],
        in_specs=[anywhere] * 6 + [inside] * 4,
        out_specs=[anywhere] * 15,
        scratch_shapes=[
            pltpu.VMEM((mine, depth), BF),
            pltpu.VMEM((mine, depth), BF),
            pltpu.VMEM((4, 2, width, columns), BF),
            pltpu.VMEM((QH, HD, mine), F32),
            pltpu.VMEM((kv_rows, mine), BF),
            pltpu.VMEM((QH, HD, mine), BF),
            pltpu.VMEM((2 * kv_rows, mine), BF),
            pltpu.VMEM((2 * kv_rows, GROUP), BF),
            pltpu.VMEM((GROUP, HD), BF),
            pltpu.VMEM((QH * HD, mine), F32),
            pltpu.VMEM((KVH, REP, mine), F32),
            pltpu.VMEM((mine, QH * HD), BF),
            pltpu.VMEM((4 * q_width, depth), BF),
            pltpu.VMEM((mine, depth), F32),
            pltpu.VMEM((2, 2, width), F32),
            dma((3, 2)), dma((3, 2)), dma((2,)),
            dma((11,)), dma((11,)), dma((11,)), dma((11,)), dma((1,)), dma((1,)),
            dma((3, 4)), dma((3, 4)), dma((4,)), dma((4,)), dma((4,)), dma((4,)), dma((3,)), dma((13,)),
        ],
        compiler_params=pltpu.CompilerParams(
            collective_id=3, has_side_effects=True, vmem_limit_bytes=56 * 1024 * 1024
        ),
        name="front",
    )(tokens, w_project, w_out, gains, w_gate, w_up, cosine, sine, query_gain, key_gain)


def back_kernel(*refs):
    query, d_out, logs_ref, delta_ref, pair, raw, key_raw, cos_ref, sin_ref, query_gain, key_gain = refs[:11]
    d_project, query_gain_out, key_gain_out = refs[11:14]
    key_n, value_n, d_key, d_value, both_t, staged, come, gain_sum, send_sem, recv_sem = refs[14:]
    row, side = lax.axis_index("row"), lax.axis_index("side")
    others = [
        (2 * (1 - row) + side, {"row": 1 - row}),
        (2 * (1 - row) + 1 - side, {"row": 1 - row, "side": 1 - side}),
        (2 * row + 1 - side, {"side": 1 - side}),
    ]
    member = 2 * row + side
    pieces = 8
    span = query.shape[2] // 4
    rows = REP * span
    kv_rows = key_raw.shape[0]
    half = HD // 2

    barrier = pltpu.get_barrier_semaphore()
    for _, where in others:
        pl.semaphore_signal(barrier, 1, device_id=where, device_id_type=pl.DeviceIdType.MESH)
    pl.semaphore_wait(barrier, 3)

    def sent(index, head):
        return pltpu.make_async_remote_copy(
            staged.at[index, head],
            come.at[index, head],
            send_sem.at[index, head],
            recv_sem.at[index, head],
            device_id=others[index][1],
            device_id_type=pl.DeviceIdType.MESH,
        )

    def starts(who):
        return [who, pieces - 1 - who, pieces + who, 2 * pieces - 1 - who]

    def through_norm(values, gain, cosine, sine, d_turned):
        first, second = d_turned[:half], d_turned[half:]
        d_scaled = jnp.concatenate([first * cosine + second * sine, second * cosine - first * sine], axis=0)
        inverse = lax.rsqrt(jnp.mean(values * values, axis=0, keepdims=True) + EPSILON)
        d_normed = d_scaled * gain
        mean = jnp.mean(values * d_normed, axis=0, keepdims=True)
        return inverse * d_normed - values * inverse**3 * mean, d_scaled * values * inverse

    gain_sum[...] = jnp.zeros_like(gain_sum)
    scale = 1.0 / math.sqrt(HD)

    @pl.loop(0, KVH)
    def _(head):
        key_rows = pl.ds(pl.multiple_of(head * HD, HD), HD)
        value_rows = pl.ds(pl.multiple_of(kv_rows + head * HD, HD), HD)
        key_n[...] = pair[key_rows, :].T
        value_n[...] = pair[value_rows, :].T
        d_key[...] = jnp.zeros_like(d_key)
        d_value[...] = jnp.zeros_like(d_value)
        for index, start in enumerate(starts(member)):
            cut = slice(index * span, (index + 1) * span)

            def beside(ref):
                return jnp.concatenate([ref[head * REP + rep, :, cut] for rep in range(REP)], axis=1)

            query_here, d_out_here = beside(query), beside(d_out)
            query_t, d_out_t = query_here.T, d_out_here.T
            logs = jnp.concatenate([logs_ref[head, rep : rep + 1, cut] for rep in range(REP)], axis=1)
            delta = jnp.concatenate([delta_ref[head, rep : rep + 1, cut] for rep in range(REP)], axis=1)
            first_query = start * span
            full, last = tiles_of(first_query)

            def tile(where, accum, masked):
                first_key = pl.multiple_of(where * KEYS, KEYS)
                here = pl.ds(first_key, KEYS)
                probs = jnp.exp(dot(key_n[here, :], query_here) - logs)
                if masked:
                    probs = jnp.where(allowed(first_query, first_key, span, rows), probs, 0.0)
                d_probs = dot(value_n[here, :], d_out_here)
                d_scores = (probs * (d_probs - delta)).astype(BF)
                d_value[here, :] += dot(probs.astype(BF), d_out_t)
                d_key[here, :] += dot(d_scores, query_t)
                return accum + dot(pair[key_rows, here], d_scores)

            accum = tile(last, jnp.zeros((HD, rows), F32), True)
            least = (0, PROMPT // KEYS // 2, PROMPT // KEYS, PROMPT // KEYS)[index]
            for where in range(least):
                accum = tile(where, accum, False)
            if index < 2:
                accum = lax.fori_loop(least, full, lambda where, total: tile(where, total, False), accum)
            cosine = jnp.concatenate([cos_ref[:, cut]] * REP, axis=1)
            sine = jnp.concatenate([sin_ref[:, cut]] * REP, axis=1)
            d_raw, part = through_norm(beside(raw), query_gain[...], cosine, sine, accum * scale)
            gain_sum[0] += part
            for rep in range(REP):
                which = head * REP + rep
                place = pl.ds(pl.multiple_of(which % KVH * HD, HD), HD)
                d_project[which // KVH, place, cut] = d_raw[:, rep * span : (rep + 1) * span].astype(BF)
        both_t[:HD, :] = d_key[...].T.astype(BF)
        both_t[HD:, :] = d_value[...].T.astype(BF)
        for index, who in enumerate([who for who, _ in others] + [member]):
            for number, start in enumerate(starts(who)):
                part = both_t[:, pl.ds(pl.multiple_of(start * span, span), span)]
                staged[index, head, :, number * span : (number + 1) * span] = part
            if index < 3:
                sent(index, head).start()

    cosine, sine = cos_ref[...], sin_ref[...]
    width = kv_rows // 4
    for head in range(KVH):
        total = staged[3, head].astype(F32)
        for index in range(3):
            sent(index, head).wait_recv()
            total += come[index, head].astype(F32)
        values = key_raw[head * HD : (head + 1) * HD, :].astype(F32)
        d_raw, part = through_norm(values, key_gain[...], cosine, sine, total[:HD])
        gain_sum[1] += part
        for offset, result in ((0, d_raw.astype(BF)), (width, total[HD:].astype(BF))):
            first = head * HD
            while first < (head + 1) * HD:
                col, inside = first // width, first % width
                size = min(width - inside, (head + 1) * HD - first)
                place = d_project.shape[1] - 2 * width + offset + inside
                d_project[col, place : place + size, :] = result[first - head * HD : first - head * HD + size]
                first += size
    query_gain_out[...] = jnp.sum(gain_sum[0], axis=1, keepdims=True)
    key_gain_out[...] = jnp.sum(gain_sum[1], axis=1, keepdims=True)
    for head in range(KVH):
        for index in range(3):
            sent(index, head).wait_send()


def back(query, d_out, logs, delta, pair, raw, key_raw, cosine, sine, query_gain, key_gain):
    mine = query.shape[2]
    inside = pl.BlockSpec(memory_space=pltpu.VMEM)
    dma = pltpu.SemaphoreType.DMA
    shape = jax.ShapeDtypeStruct
    columns = (QH + 2 * KVH) * HD // 4
    return pl.pallas_call(
        back_kernel,
        out_shape=[shape((4, columns, mine), BF), shape((HD, 1), F32), shape((HD, 1), F32)],
        in_specs=[inside] * 11,
        out_specs=[inside] * 3,
        scratch_shapes=[
            pltpu.VMEM((GROUP, HD), BF),
            pltpu.VMEM((GROUP, HD), BF),
            pltpu.VMEM((GROUP, HD), F32),
            pltpu.VMEM((GROUP, HD), F32),
            pltpu.VMEM((2 * HD, GROUP), BF),
            pltpu.VMEM((4, KVH, 2 * HD, mine), BF),
            pltpu.VMEM((3, KVH, 2 * HD, mine), BF),
            pltpu.VMEM((2, HD, mine), F32),
            dma((3, KVH)),
            dma((3, KVH)),
        ],
        compiler_params=pltpu.CompilerParams(
            collective_id=4, has_side_effects=True, vmem_limit_bytes=48 * 1024 * 1024
        ),
        name="attend_back",
    )(query, d_out, logs, delta, pair, raw, key_raw, cosine, sine, query_gain, key_gain)


def body(
    tokens,
    norm1_gain,
    w_query,
    w_key,
    w_value,
    query_gain,
    key_gain,
    w_out,
    norm2_gain,
    w_gate,
    w_up,
    w_down,
    teacher,
    positions,
    token_count,
):
    rows = lax.axis_size("row")
    cores = lax.axis_size("side")
    cols = lax.axis_size("group") * cores
    row_index = lax.axis_index("row")
    group_index = lax.axis_index("group")
    members = rows * cores
    member = row_index * cores + lax.axis_index("side")
    shard, width = tokens.shape
    pieces = 2 * members
    span = shard // pieces
    mine = shard // members * cores
    q_width, k_width = w_query.shape[1], w_key.shape[1]
    ff = w_gate.shape[1]

    def from_row(block, ahead):
        pairs = [((r + ahead) % rows, r) for r in range(rows)]
        return lax.ppermute(block, "row", pairs)

    def gather_rows(block, axis):
        parts = [block] + [from_row(block, ahead) for ahead in range(1, rows)]
        return jnp.concatenate(parts, axis=axis)

    def scatter_rows(block, axis):
        size = block.shape[axis] // rows
        total = lax.slice_in_dim(block, 0, size, axis=axis).astype(F32)
        for ahead in range(1, rows):
            part = lax.slice_in_dim(block, ahead * size, (ahead + 1) * size, axis=axis)
            total = total + from_row(part, rows - ahead).astype(F32)
        return total.astype(BF)

    def sum_planes(block, cuts):
        planes = lax.axis_size("dp")
        plane = lax.axis_index("dp")
        half = planes // 2
        edge = jnp.minimum(plane, planes - 1 - plane)
        done = []
        for part in jnp.split(block, cuts, axis=0):
            for step in range(half - 1):
                pairs = [(step, step + 1), (planes - 1 - step, planes - 2 - step)]
                come = lax.ppermute(part, "dp", pairs)
                part = (part.astype(F32) + come.astype(F32)).astype(BF)
            come = lax.ppermute(part, "dp", [(half - 1, half), (half, half - 1)])
            part = (part.astype(F32) + come.astype(F32)).astype(BF)
            for step in reversed(range(half - 1)):
                pairs = [(step + 1, step), (planes - 2 - step, planes - 1 - step)]
                come = lax.ppermute(part, "dp", pairs)
                part = jnp.where(edge == step, come, part)
            done.append(part)
        return jnp.concatenate(done, axis=0)

    def to_members(block):
        parts = block.reshape(pieces, span, width)
        parts = jnp.stack([parts[:members], parts[members:][::-1]], axis=1)
        moved = lax.all_to_all(parts, ("row", "side"), 0, 0, tiled=True)
        moved = jnp.roll(moved.reshape(rows, cores, 2 * span, width), -row_index, 0)
        moved = moved.transpose(1, 2, 0, 3)
        return moved.reshape(mine, rows * width)

    def from_members(block):
        parts = block.reshape(cores, 2, span, rows, width).transpose(3, 0, 1, 2, 4)
        parts = jnp.roll(parts, row_index, 0).reshape(members, 2, span, width)
        moved = lax.all_to_all(parts, ("row", "side"), 0, 0, tiled=True)
        moved = jnp.concatenate([moved[:, 0], moved[:, 1][::-1]], axis=0)
        return moved.reshape(shard, width)

    def pick(values):
        part = lax.dynamic_slice_in_dim(values.reshape(-1, cores, pieces, span), group_index, 1, 0)[0]
        low = lax.dynamic_slice_in_dim(part, member, 1, 1)
        high = lax.dynamic_slice_in_dim(part, pieces - 1 - member, 1, 1)
        return jnp.concatenate([low, high], axis=1).reshape(-1)

    first_tokens = (
        jnp.array([0, 0, shard, shard], jnp.int32)
        + jnp.stack([member, pieces - 1 - member] * 2).astype(jnp.int32) * span
    )

    half = HD // 2
    freq = jnp.exp(jnp.arange(half, dtype=F32) * (-2.0 * math.log(10000.0) / HD))
    angle = freq[:, None] * pick(positions).astype(F32)[None, :]
    cosine, sine = jnp.cos(angle), jnp.sin(angle)
    def dealt(full):
        lead, entry = full.shape[:-2], full.shape[-1]
        parts = full.reshape(lead + (cores, pieces, span, entry))
        low = parts[..., :members, :, :]
        high = parts[..., members:, :, :][..., ::-1, :, :]
        both = jnp.stack([low, high], axis=-3)
        both = jnp.moveaxis(both, -4, 0)
        return both.reshape((members,) + lead + (mine, entry))

    w_project = jnp.concatenate([w_query, w_key, w_value], axis=1)
    scale = 1.0 / math.sqrt(HD)
    fast = rows == 2 and cols == 4 and lax.axis_size("dp") % 2 == 0 and mine == 4 * span
    if fast:
        (
            states, normed_one, query_raw, query_use, key_sent, pair, mixed_f, logs, hidden,
            normed_two, w_project, w_out_all, gate_other, up_other, gains,
        ) = front(
            tokens, w_project, w_out, jnp.stack([norm1_gain, norm2_gain]), w_gate, w_up,
            cosine, sine, query_gain[:, None], key_gain[:, None],
        )
        states = states.astype(F32)
        inverse_one, inverse_two = rms(states), rms(hidden)
        gain_one, gain_two = gains[:, 0].reshape(D), gains[:, 1].reshape(D)
        mixed_f = mixed_f.reshape(KVH, REP, HD, mine)
        mixed = mixed_f.reshape(QH * HD, mine).astype(BF)
        w_project = w_project.reshape(cols, D, -1)
        ffn_weights = [w_gate, gate_other, w_up, up_other, w_down]
    else:
        states = to_members(tokens).astype(F32)
        gain_one = gather_rows(norm1_gain, 0)
        gain_two = gather_rows(norm2_gain, 0)
        w_project = gather_rows(w_project, 0)
        w_project = lax.all_gather(w_project, ("group", "side"), axis=0)
        w_out_all = gather_rows(w_out, 1)
        w_out_all = lax.all_gather(w_out_all, ("group", "side"), axis=0, tiled=True)
        def halves(block, axis):
            if rows == 2:
                return [block, from_row(block, 1)]
            return jnp.split(gather_rows(block, axis), 2, axis=axis)

        ffn_weights = halves(w_gate, 0) + halves(w_up, 0) + halves(w_down, 1)
        inverse_one = rms(states)
        normed_one = (states * inverse_one * gain_one).astype(BF)
        projected = dot(w_project, normed_one, ((1,), (1,)))
        query_raw = projected[:, :q_width].reshape(QH, HD, mine)
        key_sent = projected[:, q_width : q_width + k_width].reshape(KVH, HD, mine).astype(BF)
        value_sent = projected[:, q_width + k_width :].reshape(KVH, HD, mine).astype(BF)
        query_rot, query_back = jax.vjp(
            lambda raw, gain: prepare(raw, gain, cosine, sine), query_raw, query_gain
        )
        key_rot, key_back = jax.vjp(
            lambda raw, gain: prepare(raw, gain, cosine, sine), key_sent.astype(F32), key_gain
        )
        query_use = (query_rot.astype(BF) * BF(scale)).reshape(KVH, REP, HD, mine)
        pair = jnp.stack([key_rot.astype(BF), value_sent])
        pair = lax.all_gather(pair, ("row", "side"), axis=0)

        def natural(stacked):
            lead = stacked.shape[1:-1]
            parts = stacked.reshape((members,) + lead + (cores, 2, span))
            low, high = parts[..., 0, :], parts[..., 1, :]
            both = jnp.concatenate([low, high[::-1]], axis=0)
            return jnp.moveaxis(both, 0, -2).reshape(lead + (GROUP,))

        pair = natural(pair)
        key_t, value_t = pair[0], pair[1]
        key_n = key_t.transpose(0, 2, 1)
        value_one = jnp.concatenate([value_t, jnp.ones((KVH, 16, GROUP), BF)], axis=1)
        mixed_f, logs = attend(first_tokens, query_use, key_n, value_one)
        mixed = mixed_f.reshape(QH * HD, mine).astype(BF)
        hidden = states + dot(mixed, w_out_all, ((0,), (0,)))

        inverse_two = rms(hidden)
        normed_two = (hidden * inverse_two * gain_two).astype(BF)

    total_tokens = shard * cols * lax.axis_size("dp")
    loss_scale = total_tokens / token_count[0].astype(F32)
    if fast:
        normed_all, _, _, activated, _, d_low, d_gate_up, d_result, d_normed, block_out = feed(
            normed_two, ffn_weights, teacher, hidden, loss_scale[None]
        )
        d_result = d_result.reshape(mine, D)
    else:
        normed_all, gate, up, activated, ffn_out = spread(True, normed_two, ffn_weights)
        result = hidden + ffn_out.reshape(mine, D)
        d_result = loss_scale * (result - to_members(teacher).astype(F32))
        d_low, d_gate_up, d_normed = spread(False, d_result.astype(BF), ffn_weights, gate, up)
        block_out = from_members(result.astype(BF))
    d_normed = d_normed.reshape(mine, D)
    d_low, normed_all = d_low.reshape(-1, D), normed_all.reshape(-1, D)
    activated, d_gate_up = activated.reshape(-1, ff), d_gate_up.reshape(-1, 2 * ff)

    norm_two_part = jnp.sum(d_normed * hidden * inverse_two, axis=0)
    d_hidden = d_result + norm_back(hidden, inverse_two, gain_two, d_normed)
    d_hidden, d_hidden_low = lax.optimization_barrier((d_hidden, d_hidden.astype(BF)))
    grad_out = dot(mixed, d_hidden_low, ((1,), (0,))).astype(BF)
    d_mixed = dot(w_out_all, d_hidden_low, ((1,), (1,))).astype(BF)
    d_mixed = d_mixed.reshape(KVH, REP, HD, mine)
    delta = jnp.sum(d_mixed.astype(F32) * mixed_f, axis=2)
    if fast:
        d_projected, query_gain_part, key_gain_part = back(
            query_use, d_mixed.reshape(QH, HD, mine), logs, delta, pair, query_raw, key_sent,
            cosine, sine, query_gain[:, None], key_gain[:, None],
        )
        query_gain_part, key_gain_part = query_gain_part[:, 0], key_gain_part[:, 0]
    else:
        d_query, d_key_n, d_value_n = attend_back(
            first_tokens, query_use, d_mixed, logs, delta, key_t, value_t
        )
        d_pair = dealt(jnp.stack([d_key_n, d_value_n])).astype(BF)
        d_pair = lax.psum_scatter(d_pair, ("row", "side"), scatter_dimension=0, tiled=True)[0]
        d_pair = d_pair.astype(F32).transpose(0, 1, 3, 2)
        d_query_raw, query_gain_part = query_back(d_query.reshape(QH, HD, mine) * scale)
        d_key_raw, key_gain_part = key_back(d_pair[0])
        d_projected = jnp.concatenate(
            [
                d_query_raw.reshape(cols, q_width, mine),
                d_key_raw.reshape(cols, k_width, mine),
                d_pair[1].reshape(cols, k_width, mine),
            ],
            axis=1,
        ).astype(BF)
    d_normed_one = dot(d_projected, w_project, ((0, 1), (0, 2)))
    grad_input = d_hidden + norm_back(states, inverse_one, gain_one, d_normed_one)
    norm_one_part = jnp.sum(d_normed_one * states * inverse_one, axis=0)

    grad_project = lax.dot_general(
        d_projected, normed_one, (((2,), (0,)), ((), ())), preferred_element_type=F32
    )
    grad_project = grad_project.astype(BF)
    grad_out = grad_out.reshape(cols, q_width, D)
    norm_one_part = jnp.roll(norm_one_part.reshape(rows, width), row_index, 0).reshape(D)
    norm_two_part = jnp.roll(norm_two_part.reshape(rows, width), row_index, 0).reshape(D)
    small = jnp.concatenate([norm_one_part, norm_two_part, query_gain_part, key_gain_part])
    if fast and lax.axis_size("dp") == 4:
        padded = jnp.pad(small, (0, SMALL * 128 - small.shape[0])).reshape(SMALL, 128)
        grad_gate_up, grad_out, grad_project, grad_down, small, grad_input = reduce_all(
            4, normed_all, d_gate_up, activated, d_low, grad_out, grad_project, padded, grad_input.astype(BF)
        )
        grad_input = grad_input.astype(F32)
        small = small.reshape(-1)[: 2 * D + 2 * HD]
    else:
        grad_input = from_members(grad_input)
        small = lax.psum(small, ("dp", "row", "group", "side"))
        col_axes = ("group", "side")
        grad_project = lax.psum_scatter(grad_project, col_axes, scatter_dimension=0, tiled=True)
        grad_out = lax.psum_scatter(grad_out, col_axes, scatter_dimension=0, tiled=True)
        grad_down = dot(activated, d_low, ((0,), (0,))).astype(BF)
        grad_gate_up = dot(normed_all, d_gate_up, ((0,), (0,))).astype(BF)
        grad_down = sum_planes(scatter_rows(grad_down, 1), 2)
        grad_gate_up = sum_planes(scatter_rows(grad_gate_up, 0), 4)
        grad_out = sum_planes(scatter_rows(grad_out[0], 1), 1)
        grad_project = sum_planes(scatter_rows(grad_project[0], 1), 2)
    grad_norm1 = lax.dynamic_slice_in_dim(small, row_index * width, width, 0)
    grad_norm2 = lax.dynamic_slice_in_dim(small, D + row_index * width, width, 0)
    grad_project = grad_project.astype(F32).T
    return (
        block_out,
        grad_input,
        grad_norm1,
        grad_project[:, :q_width],
        grad_project[:, q_width : q_width + k_width],
        grad_project[:, q_width + k_width :],
        small[2 * D : 2 * D + HD],
        small[2 * D + HD :],
        grad_out.astype(F32),
        grad_norm2,
        grad_gate_up[:, :ff].astype(F32),
        grad_gate_up[:, ff:].astype(F32),
        grad_down.astype(F32),
    )


def solution(mesh):
    dp, row, col = mesh.shape["dp"], mesh.shape["row"], mesh.shape["col"]

    def call(*args):
        side = GROUP * dp * col // args[0].shape[0]
        fine = Mesh(
            mesh.devices.reshape(dp, row, col // side, side), ("dp", "row", "group", "side")
        )
        col_axes = ("group", "side")
        token_spec = P(("dp", "group", "side"), "row")
        wide = P("row", col_axes)
        tall = P(col_axes, "row")
        return jax.shard_map(
            body,
            mesh=fine,
            in_specs=(
                token_spec,
                P("row"),
                wide,
                wide,
                wide,
                P(),
                P(),
                tall,
                P("row"),
                wide,
                wide,
                tall,
                token_spec,
                P("dp"),
                P(),
            ),
            out_specs=(
                token_spec,
                token_spec,
                P("row"),
                wide,
                wide,
                wide,
                P(),
                P(),
                tall,
                P("row"),
                wide,
                wide,
                tall,
            ),
            check_vma=False,
        )(*args)

    return call
```
